128 devices in a mesh: gx: 8 (over x, core), gy: 16 (over z, y).
Axes of the slice: x: 4, y: 4, z: 4, core: 2. Of those that a mesh axis runs over, the one named last changes fastest.
Arguments:
- local_pos: float32 [8192, 3, 128], P(('gx', 'gy')), may hold values from -1 to 1
- charges: float32 [8192, 8, 128], P(('gx', 'gy')), may hold values from -0.6 to 0.6
- counts: int32 [8192], P(('gx', 'gy')), may hold values from 1 to 128, as said below
- box_centers: float32 [3, 8192], P(None, ('gx', 'gy')), may hold values from -1 to 65
- far_list: int32 [8192, 8], P(('gx', 'gy')), may hold values from 0 to 8191, as said below
- near_list: int32 [8192, 9], P(('gx', 'gy')), may hold values from 0 to 8191, as said below
Outputs:
- product: float32 [8192, 8, 128], P(('gx', 'gy'))
- curvature: float32 [8], replicated
The draws below stay inside these ranges and needn't reach their ends.
Inputs may be any that keep to these rules, and one draw needn't show every extreme that they name: `counts`: boxes of devices whose index along gx+gy is a multiple of 4 hold at least 64 points; box 0 holds 128. `far_list`: the 64 boxes of each device name together exactly 4 entries held on each device (its own included), box b being held by device b // 64. Entry 0 of near_list[b] is b. The other entries of the 64 boxes of each device name together exactly 4 entries held on each device (its own included), box b being held by device b // 64.
All inputs are finite; a program needn't handle non-finite values.
Results may differ from the reference program's by a relative error of at most 0.0003.
Values sent between devices are 32-bit elements; how exact they have to be, the bound alone decides.
No kernel may reach another device: no remote copies, remote signals or barrier semaphores. Data moves between devices by JAX's collectives and lax.ppermute only.
A program may use at most 64 MiB of HBM per device.

```python
import math
import jax
import jax.numpy as jnp
from jax import lax

BOX_DEV = 64
CAP = 128
RHS = 8
NODES = 4
FARN = 8
NEARN = 9
NDEV = 128
BOXES = 8192


def peer_table(key, width):
    total = BOX_DEV * width
    keys = jax.random.split(key, NDEV)
    perms = jax.vmap(lambda single: jax.random.permutation(single, total))(keys)
    return (perms % NDEV).reshape(NDEV, BOX_DEV, width)


def draw_far_list(key, part):
    key = jax.random.fold_in(key, 11)
    first, second, third = jax.random.split(key, 3)
    peers = peer_table(first, FARN)
    clusters = BOX_DEV // 2
    slot = jnp.arange(BOX_DEV)[None, :, None]
    step = 2 * jax.random.randint(second, peers.shape, 0, 2) - 1
    target = (slot // 2 + step + clusters) % clusters
    pick = 2 * target + jax.random.randint(third, peers.shape, 0, 2)
    return (peers * BOX_DEV + pick).reshape(BOXES, FARN).astype(jnp.int32)


def draw_near_list(key, part):
    key = jax.random.fold_in(key, 12)
    first, second = jax.random.split(key)
    others = NEARN - 1
    peers = peer_table(first, others)
    slot = jnp.arange(BOX_DEV)[None, :, None]
    device = jnp.arange(NDEV)[:, None, None]
    other_pick = 2 * (slot // 2) + jax.random.randint(second, peers.shape, 0, 2)
    partner = slot + 1 - 2 * (slot % 2)
    pick = jnp.where(peers == device, partner, other_pick)
    named = (peers * BOX_DEV + pick).reshape(BOXES, others)
    itself = jnp.arange(BOXES)[:, None]
    return jnp.concatenate([itself, named], axis=1).astype(jnp.int32)


def draw_counts(key, part):
    key = jax.random.fold_in(key, 13)
    first, second = jax.random.split(key)
    heavy = (jnp.arange(NDEV) % 4 == 0)[:, None]
    full = jax.random.randint(first, (NDEV, BOX_DEV), CAP // 2, CAP + 1)
    light = jax.random.randint(second, (NDEV, BOX_DEV), 1, CAP // 2 + 1)
    result = jnp.where(heavy, full, light).reshape(NDEV * BOX_DEV)
    return result.at[0].set(CAP).astype(jnp.int32)


def draw_box_centers(key, part):
    key = jax.random.fold_in(key, 14)
    clusters = BOX_DEV // 2
    radius = 2.5 * clusters / (2.0 * math.pi)
    cluster = (jnp.arange(BOXES) % BOX_DEV // 2).astype(jnp.float32)
    angle = cluster * (2.0 * math.pi / clusters)
    base = jnp.stack([radius * (1.0 + jnp.cos(angle)), radius * (1.0 + jnp.sin(angle)), jnp.full(angle.shape, 0.5, jnp.float32)])
    jitter = jax.random.uniform(key, (3, BOXES), jnp.float32, -0.5, 0.5)
    return (base + jitter).astype(jnp.float32)


def block_levels(key, shape, shards, least, high):
    loudness, own = 1.0, jax.random.fold_in(key, 6)
    for dim, shards_of in shards:
        heights = jnp.exp(jax.random.uniform(jax.random.fold_in(own, dim), (shards_of,), jnp.float32, least / len(shards), high / len(shards)))
        loudness = loudness * jnp.repeat(heights, shape[dim] // shards_of).reshape([-1 if axis == dim else 1 for axis in range(len(shape))])
    return loudness


def bell_draw(stream_key, shape, scale, most, cuts=(), held_as=jnp.bfloat16):
    level = block_levels(stream_key, shape, cuts, -0.22, 0.18) if cuts else 1.0
    entries = jax.random.normal(stream_key, shape, jnp.float32) * scale * level
    return jnp.minimum(jnp.maximum(entries, -most), most).astype(held_as)


def setup_inputs(seed: int = 0) -> dict:
    splits = jax.random.split(jax.random.key(seed), 7)
    return {
        "local_pos": jnp.clip(jax.random.uniform(splits[0], (BOXES, 3, CAP), jnp.float32, -1.0, 1.0) * block_levels(splits[0], (BOXES, 3, CAP), ((0, 128),), -0.4, 0.0), -1.0, 1.0),
        "charges": bell_draw(splits[1], (BOXES, RHS, CAP), 0.1, 0.6, ((0, 128),), jnp.float32),
        "counts": draw_counts(jax.random.fold_in(splits[6], 71), 0),
        "box_centers": draw_box_centers(jax.random.fold_in(splits[6], 71), 0),
        "far_list": draw_far_list(jax.random.fold_in(splits[6], 71), 0),
        "near_list": draw_near_list(jax.random.fold_in(splits[6], 71), 0),
    }


HALF = 0.5
ELL = 1.0
NOISE = 1.0
ROOT3 = 1.7320508075688772

def matern(dist2):
    scaled = ROOT3 * jnp.sqrt(dist2) / ELL
    return (1.0 + scaled) * jnp.exp(-scaled)

def node_values(order):
    theta = (2.0 * jnp.arange(order, dtype=jnp.float32) + 1.0) * (math.pi / (2.0 * order))
    return theta

def cheb_table(local_pos, order):
    theta = node_values(order)
    poly = [jnp.ones_like(local_pos), local_pos]
    for level in range(2, order):
        poly.append(2.0 * local_pos * poly[-1] - poly[-2])
    accum = jnp.full(local_pos.shape[:1] + (order,) + local_pos.shape[1:], 1.0 / order, jnp.float32)
    for level in range(1, order):
        accum = accum + 2.0 / order * jnp.cos(level * theta)[None, :, None, None] * poly[level][:, None, :, :]
    full = jnp.einsum('bip,bjp,blp->bijlp', accum[:, :, 0], accum[:, :, 1], accum[:, :, 2])
    return full.reshape(local_pos.shape[0], order ** 3, local_pos.shape[2])

def node_coords(order):
    nodes = jnp.cos(node_values(order))
    index = jnp.arange(order ** 3)
    return jnp.stack([nodes[index // (order * order)], nodes[index // order % order], nodes[index % order]])

def one_box(tgt_pos, tgt_center, table, q_tgt, far_w, far_center, near_pos, near_q, near_center, nodes):
    gap = tgt_center[None, :] - far_center
    spread = HALF * (nodes[:, :, None] - nodes[:, None, :])
    dist2 = jnp.zeros((far_w.shape[0],) + spread.shape[1:], jnp.float32)
    for dim in range(3):
        dist2 = dist2 + (gap[:, dim][:, None, None] + spread[dim][None]) ** 2
    local_w = jnp.einsum('frn,fmn->rm', far_w, matern(dist2), precision=lax.Precision.HIGHEST)
    far_out = jnp.dot(local_w, table, precision=lax.Precision.HIGHEST)
    tgt_abs = tgt_center[:, None] + HALF * tgt_pos
    src_abs = near_center[:, :, None] + HALF * near_pos
    near2 = jnp.zeros((near_pos.shape[0], tgt_pos.shape[1], near_pos.shape[2]), jnp.float32)
    for dim in range(3):
        near2 = near2 + (tgt_abs[dim][None, :, None] - src_abs[:, dim][:, None, :]) ** 2
    near_out = jnp.einsum('fpq,frq->rp', matern(near2), near_q, precision=lax.Precision.HIGHEST)
    return far_out + near_out + NOISE * q_tgt

def reference(local_pos, charges, counts, box_centers, far_list, near_list):
    slots = local_pos.shape[2]
    nboxes = local_pos.shape[0]
    live = (jnp.arange(slots)[None, :] < counts[:, None]).astype(jnp.float32)
    masked = charges * live[:, None, :]
    table = cheb_table(local_pos, NODES)
    weights = jnp.einsum('brp,bkp->brk', masked, table, precision=lax.Precision.HIGHEST)
    centers = box_centers.T
    nodes = node_coords(NODES)
    block = math.gcd(nboxes, 16)
    steps_count = nboxes // block

    def run_block(index):
        start = index * block
        sl = lambda arr: lax.dynamic_slice_in_dim(arr, start, block, 0)
        far_ids = sl(far_list)
        near_ids = sl(near_list)
        return jax.vmap(one_box, in_axes=(0, 0, 0, 0, 0, 0, 0, 0, 0, None))(sl(local_pos), sl(centers), sl(table), sl(masked), weights[far_ids], centers[far_ids], local_pos[near_ids], masked[near_ids], centers[near_ids], nodes)
    result = lax.map(run_block, jnp.arange(steps_count, dtype=jnp.int32))
    product = result.reshape(masked.shape) * live[:, None, :]
    curvature = lax.optimization_barrier(jnp.sum(masked * product, axis=(0, 2))) / (nboxes * slots)
    return (product, curvature)
```

```python
import functools
import math

import jax
import jax.numpy as jnp
import numpy as np
from jax import lax
from jax.experimental import pallas as pl
from jax.experimental.pallas import tpu as pltpu
from jax.sharding import PartitionSpec as P

AXES = ("gx", "gy")
NODES = 4
ROOT3 = 1.7320508075688772
BF = jnp.bfloat16
F32 = jnp.float32
NODE = [math.cos((2 * i + 1) * math.pi / 8) for i in range(NODES)]
NT = (((1,), (1,)), ((), ()))
TN = (((0,), (0,)), ((), ()))
VMEM_LIMIT = 56 * 1024 * 1024


def iota(shape, dim):
    return lax.broadcasted_iota(jnp.int32, shape, dim)


def dot(a, b, dims=None):
    if dims is None:
        return jnp.dot(a, b, preferred_element_type=F32)
    return lax.dot_general(a, b, dims, preferred_element_type=F32)


def split(x):
    high = x.astype(BF)
    return high, (x - high.astype(F32)).astype(BF)


def planes(rel, source):
    sub = iota(rel.shape, 0) % 4
    last = sub == 3
    rel = jnp.where(last, 0.0, rel)
    high = rel.astype(BF).astype(F32)
    low = (rel - high).astype(BF).astype(F32)
    square = high * (high + 2.0 * low)
    norm = pltpu.roll(square, 1, 0) + pltpu.roll(square, 2, 0) + pltpu.roll(square, 3, 0)
    one = norm.astype(BF).astype(F32)
    rest = norm - one
    two = rest.astype(BF).astype(F32)
    three = (rest - two).astype(BF).astype(F32)
    if source:
        parts = [
            jnp.where(last, one, high),
            jnp.where(last, two, high),
            jnp.where(last, 1.0, low),
            jnp.where(last, three, jnp.where(sub < 2, 1.0, 0.0)),
        ]
    else:
        parts = [
            jnp.where(last, 1.0, -2.0 * high),
            jnp.where(last, 1.0, -2.0 * low),
            jnp.where(last, one, -2.0 * high),
            jnp.where(
                sub == 0,
                pltpu.roll(two, 5, 0),
                jnp.where(sub == 1, pltpu.roll(three, 6, 0), jnp.where(last, 1.0, 0.0)),
            ),
        ]
    return parts


def matern(dist2):
    safe = jnp.maximum(dist2, 1e-12)
    scaled = safe * lax.rsqrt(safe)
    decay = jnp.exp(-scaled)
    return decay + scaled * decay


def stack_kernel(value):
    high, low = split(value)
    return jnp.concatenate([high, low], axis=0)


def fold(x):
    return x[0:8] + x[8:16]


def ids_kernel(far_ref, near_ref, want_ref):
    boxes = far_ref.shape[0]
    slots = far_ref.shape[1]
    total = boxes * slots
    lane = iota((total, 128), 1)
    box = iota((total, 128), 0) % boxes
    tri = (iota((total, total), 0) > iota((total, total), 1)).astype(F32).astype(BF)
    result = jnp.zeros((128, 128), F32)
    for ref, first, base in ((near_ref, 1, 0), (far_ref, 0, 4)):
        flat = jnp.concatenate([ref[:, first + j : first + j + 1] for j in range(slots)], axis=0)
        flat = jnp.broadcast_to(flat, (total, 128))
        hit = (flat // boxes) == lane
        onehot = hit.astype(F32).astype(BF)
        before = dot(tri, onehot)
        rank = jnp.sum(jnp.where(hit, before, 0.0), axis=1, keepdims=True).astype(jnp.int32)
        mine = rank == (lane % 4)
        within = jnp.where((lane >= base) & (lane < base + 4), flat % boxes, 0)
        owner = jnp.where((lane >= base + 16) & (lane < base + 20), box, 0)
        value = jnp.where(mine, within + owner, 0).astype(F32).astype(BF)
        result = result + dot(onehot, value, TN)
    want_ref[...] = result.astype(jnp.int32)


def table_kernel(pos_ref, charge_ref, count_ref, cen_ref, q_ref, w_ref, p_ref, f_ref, base_ref, t_ref):
    step = pl.program_id(0)
    group = pos_ref.shape[0]
    sub = iota((8, 128), 0)
    lane = iota((8, 128), 1)

    def body(b, carry):
        box = step * group + b
        live = lane < count_ref[box]
        q = jnp.where(live, charge_ref[b], 0.0)
        q_ref[b] = q
        pos = pos_ref[b]
        zero1 = jnp.zeros((1, 128), F32)
        x4 = jnp.concatenate([pos, zero1], axis=0)
        x = jnp.concatenate([x4, x4], axis=0)
        second = 2.0 * x * x - 1.0
        third = 2.0 * x * second - x
        basis = []
        for i in range(NODES):
            theta = (2 * i + 1) * math.pi / 8
            basis.append(0.25 + 0.5 * (math.cos(theta) * x + math.cos(2 * theta) * second + math.cos(3 * theta) * third))
        row = lambda i, d: jnp.broadcast_to(basis[i][d : d + 1], (8, 128))
        sub4 = sub % 4
        zs = jnp.where(sub4 == 0, row(0, 2), jnp.where(sub4 == 1, row(1, 2), jnp.where(sub4 == 2, row(2, 2), row(3, 2))))
        ys = [jnp.where(sub < 4, row(0, 1), row(1, 1)) * zs, jnp.where(sub < 4, row(2, 1), row(3, 1)) * zs]
        table = jnp.concatenate([row(i, 0) * ys[j] for i in range(NODES) for j in range(2)], axis=0)
        both = stack_kernel(table)
        t_ref[b] = both
        qs = jnp.concatenate(split(q), axis=0)
        weight = fold(dot(qs, both, NT))
        w_ref[b] = weight + pltpu.roll(weight, 64, 1)
        cx, cy, cz = cen_ref[0, box], cen_ref[1, box], cen_ref[2, box]
        lane4 = lane % 4
        far = jnp.where(lane4 == 0, cx, jnp.where(lane4 == 1, cy, cz))
        center = jnp.where(sub4 == 0, cx, jnp.where(sub4 == 1, cy, cz))
        p_ref[b] = jnp.where(sub4 == 3, far, center + 0.5 * x)
        rel = (0.5 * ROOT3) * x
        tgt = planes(rel, False)
        for unit in range(2):
            f_ref[b, unit] = jnp.concatenate([jnp.where(sub // 4 == unit, part, 0.0) for part in tgt], axis=0).astype(BF)
        src = jnp.concatenate(planes(rel, True) + [jnp.zeros((96, 128), F32)], axis=0).T.astype(BF)
        dist2 = dot(src[:, :32], f_ref[b, 0])
        value = stack_kernel(matern(dist2))
        near = fold(dot(jnp.concatenate([qs, qs], axis=1), value))
        base_ref[b] = near + q
        return carry

    lax.fori_loop(0, group, body, 0, unroll=4)


def gather_kernel(ids_ref, q_ref, w_ref, p_ref, out_ref):
    step = pl.program_id(0)
    group = out_ref.shape[0]
    sub4 = iota((8, 128), 0) % 4
    top = iota((8, 128), 0) < 4
    lane = iota((8, 128), 1)
    left = lane < 64

    def body(k, carry):
        peer = step * group + k
        near = [ids_ref[peer, j] for j in range(4)]
        far = [ids_ref[peer, 4 + j] for j in range(4)]
        for j in range(4):
            out_ref[k, 8 * j : 8 * j + 8] = q_ref[near[j]]
        w = [w_ref[far[j]] for j in range(4)]
        out_ref[k, 32:40] = jnp.where(left, w[0], w[2])
        out_ref[k, 40:48] = jnp.where(left, w[1], w[3])
        c = [p_ref[far[j]] for j in range(4)]
        centers = jnp.where(
            left, jnp.where(lane < 4, c[0], c[2]), jnp.where(lane < 68, c[1], c[3])
        )
        s = [p_ref[near[j]] for j in range(4)]
        out_ref[k, 48:56] = jnp.where(sub4 == 3, centers, jnp.where(top, s[0], s[1]))
        out_ref[k, 56:64] = jnp.where(sub4 == 3, centers, jnp.where(top, s[2], s[3]))
        return carry

    lax.fori_loop(0, group, body, 0, unroll=4)


def pair_kernel(
    tgt_ref, count_ref, got_ref, nc_ref, fc_ref, f_ref, fn_ref, base_ref, q_ref, t_ref, out_ref, term_ref, near_acc, far_acc
):
    step = pl.program_id(0)
    steps = pl.num_programs(0)
    group = got_ref.shape[0]
    boxes = f_ref.shape[0]
    sub = iota((8, 128), 0)
    lane = iota((8, 128), 1)
    left = lane < 64

    @pl.when(step == 0)
    def _():
        near_acc[...] = base_ref[...]
        far_acc[...] = jnp.zeros_like(far_acc)

    spread = (iota((128, 128), 0) // 64 == iota((128, 128), 1) // 64).astype(F32).astype(BF)

    def body(k, carry):
        peer = step * group + k
        tn = [tgt_ref[peer, j] for j in range(4)]
        tf = [tgt_ref[peer, 4 + j] for j in range(4)]
        points = [got_ref[k, 48:56], got_ref[k, 56:64]]
        feats = []
        for v in range(2):
            feats += planes((points[v] - nc_ref[k, 8 * v : 8 * v + 8]) * ROOT3, True)
        src = jnp.concatenate(feats + [jnp.zeros((64, 128), F32)], axis=0).T.astype(BF)
        for j in range(4):
            dist2 = dot(src[:, 32 * (j // 2) : 32 * (j // 2) + 32], f_ref[tn[j], j % 2])
            value = stack_kernel(matern(dist2))
            qs = jnp.concatenate(split(got_ref[k, 8 * j : 8 * j + 8]), axis=0)
            near_acc[tn[j]] += fold(dot(jnp.concatenate([qs, qs], axis=1), value))
        row = jnp.broadcast_to(points[0][3:4], (8, 128))
        row = jnp.where(lane % 64 == sub, row, 0.0)
        high = row.astype(BF)
        rest = row - high.astype(F32)
        mid = rest.astype(BF)
        low = (rest - mid.astype(F32)).astype(BF)
        cen = dot(jnp.concatenate([high, mid, low], axis=0), spread)
        rel = (fc_ref[k] - (cen[0:8] + cen[8:16] + cen[16:24])) * ROOT3
        tgt = jnp.concatenate(planes(rel, False), axis=0).astype(BF)
        value = stack_kernel(matern(dot(fn_ref[...], tgt)))
        ws = []
        for h in range(2):
            w = got_ref[k, 32 + 8 * h : 40 + 8 * h]
            for part in (jnp.where(left, w, 0.0), jnp.where(left, 0.0, w)):
                ws += list(split(part))
        ws = jnp.concatenate(ws, axis=0)
        locs = dot(jnp.concatenate([ws, ws], axis=1), value)
        for h in range(2):
            for u in range(2):
                at = 32 * h + 16 * u
                new = fold(locs[at : at + 16])
                far_acc[tf[2 * u + h]] += jnp.where(left if h == 0 else jnp.logical_not(left), new, 0.0)
        return carry

    lax.fori_loop(0, group, body, 0, unroll=2)

    @pl.when(step == steps - 1)
    def _():
        def finish(b, total):
            ls = jnp.concatenate(split(far_acc[b]), axis=0)
            both = t_ref[b]
            high, low = both[0:64], both[64:128]
            table = jnp.concatenate([high, high, low, low], axis=0)
            far = fold(dot(jnp.concatenate([ls, ls], axis=1), table))
            live = lane < count_ref[b]
            product = jnp.where(live, near_acc[b] + far, 0.0)
            out_ref[b] = product
            return total + product * q_ref[b]

        total = lax.fori_loop(0, boxes, finish, jnp.zeros((8, 128), F32), unroll=4)
        ones = jnp.ones((128, 128), F32)
        sums = lax.dot_general(ones, total, NT, precision=lax.Precision.HIGHEST, preferred_element_type=F32)
        term_ref[...] = jnp.concatenate([sums, jnp.zeros((128, 120), F32)], axis=1)


def far_sources():
    x = np.zeros((8, 128), np.float32)
    for n in range(64):
        for d, value in enumerate((NODE[n // 16], NODE[n // 4 % 4], NODE[n % 4])):
            for u in range(2):
                x[4 * u + d, 64 * u + n] = 0.5 * ROOT3 * value
    bf = lambda a: a.astype(jnp.bfloat16).astype(np.float32)
    high = bf(x)
    low = bf(x - high)
    norm = np.zeros_like(x)
    square = high * (high + 2 * low)
    for u in range(2):
        norm[4 * u + 3] = square[4 * u] + square[4 * u + 1] + square[4 * u + 2]
    one = bf(norm)
    two = bf(norm - one)
    three = bf(norm - one - two)
    sub = np.arange(8)[:, None] % 4
    unit = (np.arange(8)[:, None] // 4) == (np.arange(128)[None, :] // 64)
    parts = [
        np.where(sub == 3, one, high),
        np.where(sub == 3, two, high),
        np.where(sub == 3, 1.0, low),
        np.where(sub == 3, three, np.where(sub < 2, 1.0, 0.0)),
    ]
    return np.concatenate([np.where(unit, part, 0.0) for part in parts], axis=0).T.astype(np.float32)


def node_rows():
    out = np.zeros((8, 128), np.float32)
    for m in range(128):
        n = m % 64
        for u in range(2):
            for d, value in enumerate((NODE[n // 16], NODE[n // 4 % 4], NODE[n % 4])):
                out[4 * u + d, m] = 0.5 * value
    return out


def vmem(shape=None, index=None):
    if shape is None:
        return pl.BlockSpec(memory_space=pltpu.VMEM)
    return pl.BlockSpec(shape, index, memory_space=pltpu.VMEM)


SMEM = pl.BlockSpec(memory_space=pltpu.SMEM)


def params():
    return pltpu.CompilerParams(vmem_limit_bytes=VMEM_LIMIT)


def exchange(x):
    return lax.all_to_all(x, AXES, split_axis=0, concat_axis=0, tiled=True)


def on_device(local_pos, charges, counts, box_centers, far_list, near_list):
    devices = lax.axis_size("gx") * lax.axis_size("gy")
    boxes, _, slots = local_pos.shape
    struct = jax.ShapeDtypeStruct
    want = pl.pallas_call(
        ids_kernel,
        out_shape=struct((devices, 128), jnp.int32),
        in_specs=[vmem(), vmem()],
        out_specs=vmem(),
        compiler_params=params(),
        name="ids",
    )(far_list, near_list)
    served = exchange(want.reshape(devices, 1, 128)).reshape(devices, 128)

    group = 16
    lead = lambda shape: vmem((group,) + shape, lambda i: (i,) + (0,) * len(shape))
    q_tab, w_tab, p_tab, f_tab, base, table = pl.pallas_call(
        table_kernel,
        grid=(boxes // group,),
        out_shape=(
            struct((boxes, 8, 128), F32),
            struct((boxes, 8, 128), F32),
            struct((boxes, 8, 128), F32),
            struct((boxes, 2, 32, 128), BF),
            struct((boxes, 8, 128), F32),
            struct((boxes, 128, 128), BF),
        ),
        in_specs=[lead((3, 128)), lead((8, 128)), SMEM, SMEM],
        out_specs=(lead((8, 128)), lead((8, 128)), lead((8, 128)), lead((2, 32, 128)), lead((8, 128)), lead((128, 128))),
        compiler_params=params(),
        cost_estimate=pl.CostEstimate(flops=200_000_000, bytes_accessed=6_000_000, transcendentals=2_000_000),
        name="tables",
    )(local_pos, charges, counts, box_centers)

    send = pl.pallas_call(
        gather_kernel,
        grid=(devices // group,),
        out_shape=struct((devices, 64, 128), F32),
        in_specs=[SMEM, vmem(), vmem(), vmem()],
        out_specs=lead((64, 128)),
        compiler_params=params(),
        name="gather",
    )(served, q_tab, w_tab, p_tab)
    got = exchange(send)

    tgt = want[:, 16:24]
    centers = box_centers.T
    near_cen = jnp.pad(centers[tgt[:, :4]], ((0, 0), (0, 0), (0, 1))).reshape(devices, 16, 1)
    near_cen = jnp.broadcast_to(near_cen, (devices, 16, 128))
    far_cen = jnp.pad(centers[tgt[:, 4:]], ((0, 0), (0, 0), (0, 1))).reshape(devices, 2, 2, 4)
    far_cen = far_cen.transpose(0, 1, 3, 2).reshape(devices, 8, 2, 1)
    far_cen = jnp.broadcast_to(far_cen, (devices, 8, 2, 64)).reshape(devices, 8, 128) + node_rows()[None]

    product, term = pl.pallas_call(
        pair_kernel,
        grid=(devices // group,),
        out_shape=(struct((boxes, 8, 128), F32), struct((devices, 128), F32)),
        in_specs=[
            SMEM,
            SMEM,
            lead((64, 128)),
            lead((16, 128)),
            lead((8, 128)),
            vmem(),
            vmem(),
            vmem(),
            vmem(),
            vmem(),
        ],
        out_specs=(vmem(), vmem()),
        scratch_shapes=[pltpu.VMEM((boxes, 8, 128), F32), pltpu.VMEM((boxes, 8, 128), F32)],
        compiler_params=params(),
        cost_estimate=pl.CostEstimate(flops=1_000_000_000, bytes_accessed=12_000_000, transcendentals=20_000_000),
        name="pairs",
    )(tgt, counts, got, near_cen, far_cen, f_tab, jnp.asarray(far_sources(), BF), base, q_tab, table)

    terms = exchange(term.reshape(devices, 1, 128))[:, 0, :8]
    curvature = jnp.sum(terms, axis=0) / (devices * boxes * slots)
    return (product, curvature)


def solution(mesh):
    in_specs = (
        P(AXES, None, None),
        P(AXES, None, None),
        P(AXES),
        P(None, AXES),
        P(AXES, None),
        P(AXES, None),
    )
    out_specs = (P(AXES, None, None), P())
    return jax.shard_map(on_device, mesh=mesh, in_specs=in_specs, out_specs=out_specs, check_vma=False)
```

```python
import functools
import math

import jax
import jax.numpy as jnp
import numpy as np
from jax import lax
from jax.experimental import pallas as pl
from jax.experimental.pallas import tpu as pltpu
from jax.sharding import PartitionSpec as P

AXES = ("gx", "gy")
NODES = 4
ROOT3 = 1.7320508075688772
BF = jnp.bfloat16
F32 = jnp.float32
NODE = [math.cos((2 * i + 1) * math.pi / 8) for i in range(NODES)]
NT = (((1,), (1,)), ((), ()))
TN = (((0,), (0,)), ((), ()))
VMEM_LIMIT = 56 * 1024 * 1024


def iota(shape, dim):
    return lax.broadcasted_iota(jnp.int32, shape, dim)


def dot(a, b, dims=None):
    if dims is None:
        return jnp.dot(a, b, preferred_element_type=F32)
    return lax.dot_general(a, b, dims, preferred_element_type=F32)


def split(x):
    high = x.astype(BF)
    return high, (x - high.astype(F32)).astype(BF)


def planes(rel, source):
    axis = rel.ndim - 2
    sub = iota(rel.shape, axis) % 4
    last = sub == 3
    rel = jnp.where(last, 0.0, rel)
    high = rel.astype(BF).astype(F32)
    low = (rel - high).astype(BF).astype(F32)
    square = high * (high + 2.0 * low)
    norm = pltpu.roll(square, 1, axis) + pltpu.roll(square, 2, axis) + pltpu.roll(square, 3, axis)
    one = norm.astype(BF).astype(F32)
    rest = norm - one
    two = rest.astype(BF).astype(F32)
    three = (rest - two).astype(BF).astype(F32)
    if source:
        parts = [
            jnp.where(last, one, high),
            jnp.where(last, two, high),
            jnp.where(last, 1.0, low),
            jnp.where(last, three, jnp.where(sub < 2, 1.0, 0.0)),
        ]
    else:
        parts = [
            jnp.where(last, 1.0, -2.0 * high),
            jnp.where(last, 1.0, -2.0 * low),
            jnp.where(last, one, -2.0 * high),
            jnp.where(
                sub == 0,
                pltpu.roll(two, 5, axis),
                jnp.where(sub == 1, pltpu.roll(three, 6, axis), jnp.where(last, 1.0, 0.0)),
            ),
        ]
    return parts


def matern(dist2):
    safe = jnp.maximum(dist2, 1e-12)
    scaled = safe * lax.rsqrt(safe)
    decay = jnp.exp(-scaled)
    return decay + scaled * decay


def stack_kernel(value):
    high, low = split(value)
    return jnp.concatenate([high, low], axis=0)


def fold(x):
    return x[0:8] + x[8:16]


def ids_kernel(far_ref, near_ref, want_ref):
    boxes = far_ref.shape[0]
    slots = far_ref.shape[1]
    total = boxes * slots
    lane = iota((total, 128), 1)
    box = iota((total, 128), 0) % boxes
    tri = (iota((total, total), 0) > iota((total, total), 1)).astype(F32).astype(BF)
    result = jnp.zeros((128, 128), F32)
    for ref, first, base in ((near_ref, 1, 0), (far_ref, 0, 4)):
        flat = jnp.concatenate([ref[:, first + j : first + j + 1] for j in range(slots)], axis=0)
        flat = jnp.broadcast_to(flat, (total, 128))
        hit = (flat // boxes) == lane
        onehot = hit.astype(F32).astype(BF)
        before = dot(tri, onehot)
        rank = jnp.sum(jnp.where(hit, before, 0.0), axis=1, keepdims=True).astype(jnp.int32)
        mine = rank == (lane % 4)
        within = jnp.where((lane >= base) & (lane < base + 4), flat % boxes, 0)
        owner = jnp.where((lane >= base + 16) & (lane < base + 20), box, 0)
        value = jnp.where(mine, within + owner, 0).astype(F32).astype(BF)
        result = result + dot(onehot, value, TN)
    want_ref[...] = result.astype(jnp.int32)


def table_kernel(pos_ref, charge_ref, count_ref, cen_ref, q_ref, w_ref, p_ref, f_ref, base_ref, t_ref):
    step = pl.program_id(0)
    group = pos_ref.shape[0]
    sub = iota((8, 128), 0)
    lane = iota((8, 128), 1)

    def body(b, carry):
        box = step * group + b
        live = lane < count_ref[box]
        q = jnp.where(live, charge_ref[b], 0.0)
        q_ref[b] = q
        pos = pos_ref[b]
        zero1 = jnp.zeros((1, 128), F32)
        x4 = jnp.concatenate([pos, zero1], axis=0)
        x = jnp.concatenate([x4, x4], axis=0)
        second = 2.0 * x * x - 1.0
        third = 2.0 * x * second - x
        basis = []
        for i in range(NODES):
            theta = (2 * i + 1) * math.pi / 8
            basis.append(0.25 + 0.5 * (math.cos(theta) * x + math.cos(2 * theta) * second + math.cos(3 * theta) * third))
        row = lambda i, d: jnp.broadcast_to(basis[i][d : d + 1], (8, 128))
        sub4 = sub % 4
        zs = jnp.where(sub4 == 0, row(0, 2), jnp.where(sub4 == 1, row(1, 2), jnp.where(sub4 == 2, row(2, 2), row(3, 2))))
        ys = [jnp.where(sub < 4, row(0, 1), row(1, 1)) * zs, jnp.where(sub < 4, row(2, 1), row(3, 1)) * zs]
        table = jnp.concatenate([row(i, 0) * ys[j] for i in range(NODES) for j in range(2)], axis=0)
        both = stack_kernel(table)
        t_ref[b] = both
        qs = jnp.concatenate(split(q), axis=0)
        weight = fold(dot(qs, both, NT))
        w_ref[b] = weight + pltpu.roll(weight, 64, 1)
        cx, cy, cz = cen_ref[0, box], cen_ref[1, box], cen_ref[2, box]
        lane4 = lane % 4
        far = jnp.where(lane4 == 0, cx, jnp.where(lane4 == 1, cy, cz))
        center = jnp.where(sub4 == 0, cx, jnp.where(sub4 == 1, cy, cz))
        p_ref[b] = jnp.where(sub4 == 3, far, center + 0.5 * x)
        rel = (0.5 * ROOT3) * x
        tgt = planes(rel, False)
        for unit in range(2):
            f_ref[b, unit] = jnp.concatenate([jnp.where(sub // 4 == unit, part, 0.0) for part in tgt], axis=0).astype(BF)
        src = jnp.concatenate(planes(rel, True) + [jnp.zeros((96, 128), F32)], axis=0).T.astype(BF)
        dist2 = dot(src[:, :32], f_ref[b, 0])
        value = stack_kernel(matern(dist2))
        near = fold(dot(jnp.concatenate([qs, qs], axis=1), value))
        base_ref[b] = near + q
        return carry

    lax.fori_loop(0, group, body, 0, unroll=4)


def gather_kernel(ids_ref, q_ref, w_ref, p_ref, out_ref):
    step = pl.program_id(0)
    group = out_ref.shape[0]
    sub4 = iota((8, 128), 0) % 4
    top = iota((8, 128), 0) < 4
    lane = iota((8, 128), 1)
    left = lane < 64

    def body(k, carry):
        peer = step * group + k
        near = [ids_ref[peer, j] for j in range(4)]
        far = [ids_ref[peer, 4 + j] for j in range(4)]
        for j in range(4):
            out_ref[k, 8 * j : 8 * j + 8] = q_ref[near[j]]
        w = [w_ref[far[j]] for j in range(4)]
        out_ref[k, 32:40] = jnp.where(left, w[0], w[2])
        out_ref[k, 40:48] = jnp.where(left, w[1], w[3])
        c = [p_ref[far[j]] for j in range(4)]
        centers = jnp.where(
            left, jnp.where(lane < 4, c[0], c[2]), jnp.where(lane < 68, c[1], c[3])
        )
        s = [p_ref[near[j]] for j in range(4)]
        out_ref[k, 48:56] = jnp.where(sub4 == 3, centers, jnp.where(top, s[0], s[1]))
        out_ref[k, 56:64] = jnp.where(sub4 == 3, centers, jnp.where(top, s[2], s[3]))
        return carry

    lax.fori_loop(0, group, body, 0, unroll=4)


def pair_kernel(
    tgt_ref, count_ref, got_ref, nc_ref, fc_ref, f_ref, fn_ref, base_ref, q_ref, t_ref, out_ref, term_ref, near_acc, far_acc
):
    step = pl.program_id(0)
    steps = pl.num_programs(0)
    group = got_ref.shape[0]
    boxes = f_ref.shape[0]
    sub = iota((8, 128), 0)
    lane = iota((8, 128), 1)
    left = lane < 64

    @pl.when(step == 0)
    def _():
        near_acc[...] = base_ref[...]
        far_acc[...] = jnp.zeros_like(far_acc)

    spread = (iota((128, 128), 0) // 64 == iota((128, 128), 1) // 64).astype(F32).astype(BF)

    def body(k, carry):
        peer = step * group + k
        tn = [tgt_ref[peer, j] for j in range(4)]
        tf = [tgt_ref[peer, 4 + j] for j in range(4)]
        points = [got_ref[k, 48:56], got_ref[k, 56:64]]
        feats = []
        for v in range(2):
            feats += planes((points[v] - nc_ref[k, 8 * v : 8 * v + 8]) * ROOT3, True)
        src = jnp.concatenate(feats + [jnp.zeros((64, 128), F32)], axis=0).T.astype(BF)
        for j in range(4):
            dist2 = dot(src[:, 32 * (j // 2) : 32 * (j // 2) + 32], f_ref[tn[j], j % 2])
            value = stack_kernel(matern(dist2))
            qs = jnp.concatenate(split(got_ref[k, 8 * j : 8 * j + 8]), axis=0)
            near_acc[tn[j]] += fold(dot(jnp.concatenate([qs, qs], axis=1), value))
        row = jnp.broadcast_to(points[0][3:4], (8, 128))
        row = jnp.where(lane % 64 == sub, row, 0.0)
        high = row.astype(BF)
        rest = row - high.astype(F32)
        mid = rest.astype(BF)
        low = (rest - mid.astype(F32)).astype(BF)
        cen = dot(jnp.concatenate([high, mid, low], axis=0), spread)
        rel = (fc_ref[k] - (cen[0:8] + cen[8:16] + cen[16:24])) * ROOT3
        tgt = jnp.concatenate(planes(rel, False), axis=0).astype(BF)
        value = stack_kernel(matern(dot(fn_ref[...], tgt)))
        ws = []
        for h in range(2):
            w = got_ref[k, 32 + 8 * h : 40 + 8 * h]
            for part in (jnp.where(left, w, 0.0), jnp.where(left, 0.0, w)):
                ws += list(split(part))
        ws = jnp.concatenate(ws, axis=0)
        locs = dot(jnp.concatenate([ws, ws], axis=1), value)
        for h in range(2):
            for u in range(2):
                at = 32 * h + 16 * u
                new = fold(locs[at : at + 16])
                far_acc[tf[2 * u + h]] += jnp.where(left if h == 0 else jnp.logical_not(left), new, 0.0)
        return carry

    lax.fori_loop(0, group, body, 0, unroll=2)

    @pl.when(step == steps - 1)
    def _():
        def finish(b, total):
            ls = jnp.concatenate(split(far_acc[b]), axis=0)
            both = t_ref[b]
            high, low = both[0:64], both[64:128]
            table = jnp.concatenate([high, high, low, low], axis=0)
            far = fold(dot(jnp.concatenate([ls, ls], axis=1), table))
            live = lane < count_ref[b]
            product = jnp.where(live, near_acc[b] + far, 0.0)
            out_ref[b] = product
            return total + product * q_ref[b]

        total = lax.fori_loop(0, boxes, finish, jnp.zeros((8, 128), F32), unroll=4)
        ones = jnp.ones((128, 128), F32)
        sums = lax.dot_general(ones, total, NT, precision=lax.Precision.HIGHEST, preferred_element_type=F32)
        term_ref[...] = jnp.concatenate([sums, jnp.zeros((128, 120), F32)], axis=1)


def far_sources():
    x = np.zeros((8, 128), np.float32)
    for n in range(64):
        for d, value in enumerate((NODE[n // 16], NODE[n // 4 % 4], NODE[n % 4])):
            for u in range(2):
                x[4 * u + d, 64 * u + n] = 0.5 * ROOT3 * value
    bf = lambda a: a.astype(jnp.bfloat16).astype(np.float32)
    high = bf(x)
    low = bf(x - high)
    norm = np.zeros_like(x)
    square = high * (high + 2 * low)
    for u in range(2):
        norm[4 * u + 3] = square[4 * u] + square[4 * u + 1] + square[4 * u + 2]
    one = bf(norm)
    two = bf(norm - one)
    three = bf(norm - one - two)
    sub = np.arange(8)[:, None] % 4
    unit = (np.arange(8)[:, None] // 4) == (np.arange(128)[None, :] // 64)
    parts = [
        np.where(sub == 3, one, high),
        np.where(sub == 3, two, high),
        np.where(sub == 3, 1.0, low),
        np.where(sub == 3, three, np.where(sub < 2, 1.0, 0.0)),
    ]
    return np.concatenate([np.where(unit, part, 0.0) for part in parts], axis=0).T.astype(np.float32)


def node_rows():
    out = np.zeros((8, 128), np.float32)
    for m in range(128):
        n = m % 64
        for u in range(2):
            for d, value in enumerate((NODE[n // 16], NODE[n // 4 % 4], NODE[n % 4])):
                out[4 * u + d, m] = 0.5 * value
    return out


def vmem(shape=None, index=None):
    if shape is None:
        return pl.BlockSpec(memory_space=pltpu.VMEM)
    return pl.BlockSpec(shape, index, memory_space=pltpu.VMEM)


SMEM = pl.BlockSpec(memory_space=pltpu.SMEM)


def params():
    return pltpu.CompilerParams(vmem_limit_bytes=VMEM_LIMIT)


def exchange(x):
    return lax.all_to_all(x, AXES, split_axis=0, concat_axis=0, tiled=True)


def general(local_pos, charges, counts, box_centers, far_list, near_list):
    devices = lax.axis_size("gx") * lax.axis_size("gy")
    boxes, _, slots = local_pos.shape
    struct = jax.ShapeDtypeStruct
    want = pl.pallas_call(
        ids_kernel,
        out_shape=struct((devices, 128), jnp.int32),
        in_specs=[vmem(), vmem()],
        out_specs=vmem(),
        compiler_params=params(),
        name="ids",
    )(far_list, near_list)
    served = exchange(want.reshape(devices, 1, 128)).reshape(devices, 128)

    group = 16
    lead = lambda shape: vmem((group,) + shape, lambda i: (i,) + (0,) * len(shape))
    q_tab, w_tab, p_tab, f_tab, base, table = pl.pallas_call(
        table_kernel,
        grid=(boxes // group,),
        out_shape=(
            struct((boxes, 8, 128), F32),
            struct((boxes, 8, 128), F32),
            struct((boxes, 8, 128), F32),
            struct((boxes, 2, 32, 128), BF),
            struct((boxes, 8, 128), F32),
            struct((boxes, 128, 128), BF),
        ),
        in_specs=[lead((3, 128)), lead((8, 128)), SMEM, SMEM],
        out_specs=(lead((8, 128)), lead((8, 128)), lead((8, 128)), lead((2, 32, 128)), lead((8, 128)), lead((128, 128))),
        compiler_params=params(),
        cost_estimate=pl.CostEstimate(flops=200_000_000, bytes_accessed=6_000_000, transcendentals=2_000_000),
        name="tables",
    )(local_pos, charges, counts, box_centers)

    send = pl.pallas_call(
        gather_kernel,
        grid=(devices // group,),
        out_shape=struct((devices, 64, 128), F32),
        in_specs=[SMEM, vmem(), vmem(), vmem()],
        out_specs=lead((64, 128)),
        compiler_params=params(),
        name="gather",
    )(served, q_tab, w_tab, p_tab)
    got = exchange(send)

    tgt = want[:, 16:24]
    centers = box_centers.T
    near_cen = jnp.pad(centers[tgt[:, :4]], ((0, 0), (0, 0), (0, 1))).reshape(devices, 16, 1)
    near_cen = jnp.broadcast_to(near_cen, (devices, 16, 128))
    far_cen = jnp.pad(centers[tgt[:, 4:]], ((0, 0), (0, 0), (0, 1))).reshape(devices, 2, 2, 4)
    far_cen = far_cen.transpose(0, 1, 3, 2).reshape(devices, 8, 2, 1)
    far_cen = jnp.broadcast_to(far_cen, (devices, 8, 2, 64)).reshape(devices, 8, 128) + node_rows()[None]

    product, term = pl.pallas_call(
        pair_kernel,
        grid=(devices // group,),
        out_shape=(struct((boxes, 8, 128), F32), struct((devices, 128), F32)),
        in_specs=[
            SMEM,
            SMEM,
            lead((64, 128)),
            lead((16, 128)),
            lead((8, 128)),
            vmem(),
            vmem(),
            vmem(),
            vmem(),
            vmem(),
        ],
        out_specs=(vmem(), vmem()),
        scratch_shapes=[pltpu.VMEM((boxes, 8, 128), F32), pltpu.VMEM((boxes, 8, 128), F32)],
        compiler_params=params(),
        cost_estimate=pl.CostEstimate(flops=1_000_000_000, bytes_accessed=12_000_000, transcendentals=20_000_000),
        name="pairs",
    )(tgt, counts, got, near_cen, far_cen, f_tab, jnp.asarray(far_sources(), BF), base, q_tab, table)

    terms = exchange(term.reshape(devices, 1, 128))[:, 0, :8]
    curvature = jnp.sum(terms, axis=0) / (devices * boxes * slots)
    return (product, curvature)


HALF = 64
ROWS = 48


def start_kernel(far_ref, near_ref, most_ref, pos_ref, charge_ref, count_ref, cen_ref, want_ref, ex_ref):
    boxes = far_ref.shape[1]
    slots = far_ref.shape[0]
    sub = iota((8, 128), 0)
    lane = iota((8, 128), 1)
    left = lane < HALF

    def body(b, carry):
        live = lane < count_ref[b]
        q = pltpu.roll(jnp.where(live, charge_ref[b], 0.0), HALF, 1)
        point = jnp.zeros((8, 128), F32)
        for d in range(3):
            row = jnp.broadcast_to(pos_ref[d, pl.ds(b, 1), :], (8, 128))
            point = jnp.where(sub == d, cen_ref[d, b] + 0.5 * row, point)
        ex_ref[b] = jnp.where(left, q, point)
        return carry

    lax.fori_loop(0, boxes, body, 0, unroll=8)

    peer = iota((128, 128), 0)
    line = iota((128, 128), 1)
    tri = (peer < line).astype(F32).astype(BF)
    row32 = iota((32, 128), 0)
    boxrow = iota((32, 128), 1) % boxes
    result = jnp.zeros((128, 32), F32)
    for ref, first, base in ((near_ref, 1, 0), (far_ref, 0, 4)):
        seen = jnp.zeros((128, 1), F32)
        for j in range(0, slots, 2):
            flat = jnp.concatenate([ref[first + j : first + j + 1, :], ref[first + j + 1 : first + j + 2, :]], axis=1)
            hit = jnp.broadcast_to(flat // boxes, (128, 128)) == peer
            ones = hit.astype(F32)
            onehot = ones.astype(BF)
            before = dot(onehot, tri) + seen
            rank = jnp.sum(jnp.where(hit, before, 0.0), axis=0, keepdims=True).astype(jnp.int32)
            seen = seen + jnp.sum(ones, axis=1, keepdims=True)
            within = jnp.broadcast_to(flat % boxes, (32, 128))
            mine = row32 % 4 == jnp.broadcast_to(rank, (32, 128))
            value = jnp.where(row32 // 4 == base // 4, within, jnp.where(row32 // 4 == base // 4 + 4, boxrow, 0))
            value = jnp.where(mine, value, 0).astype(F32).astype(BF)
            result = result + dot(onehot, value, NT)
    result = jnp.concatenate([result, jnp.zeros((128, 96), F32)], axis=1)
    extra = jnp.zeros((128, 1), F32)
    member = iota((128, 1), 0) % 4
    for y in range(4):
        column = result[:, y : y + 1]
        column = pltpu.roll(jnp.broadcast_to(column, (128, 128)), y, 0)[:, 0:1] if y else column
        extra = jnp.where(member == y, column, extra)
    result = jnp.where(line == 8, jnp.broadcast_to(extra, (128, 128)), result)
    most = jnp.max(most_ref[...], axis=1, keepdims=True)
    want_ref[...] = jnp.where(line == 9, jnp.broadcast_to(most, (128, 128)), result.astype(jnp.int32))


def cheb_rows(x):
    sub = iota((8, 128), 0)
    second = 2.0 * x * x - 1.0
    third = 2.0 * x * second - x
    basis = []
    for i in range(NODES):
        theta = (2 * i + 1) * math.pi / 8
        basis.append(0.25 + 0.5 * (math.cos(theta) * x + math.cos(2 * theta) * second + math.cos(3 * theta) * third))
    row = lambda i, d: jnp.broadcast_to(basis[i][d : d + 1], (8, 128))
    sub4 = sub % 4
    zs = jnp.where(sub4 == 0, row(0, 2), jnp.where(sub4 == 1, row(1, 2), jnp.where(sub4 == 2, row(2, 2), row(3, 2))))
    ys = [jnp.where(sub < 4, row(0, 1), row(1, 1)) * zs, jnp.where(sub < 4, row(2, 1), row(3, 1)) * zs]
    return jnp.concatenate([row(i, 0) * ys[j] for i in range(NODES) for j in range(2)], axis=0)


def point_rows(pos_ref, b):
    sub4 = iota((8, 128), 0) % 4
    x = jnp.zeros((8, 128), F32)
    for d in range(3):
        x = jnp.where(sub4 == d, jnp.broadcast_to(pos_ref[d, pl.ds(b, 1), :], (8, 128)), x)
    return x


def doubled(x):
    return jnp.where(iota((8, 128), 1) < HALF, x, pltpu.roll(x, HALF, 1))


def send_table_kernel(pos_ref, charge_ref, count_ref, cen_ref, q_ref, w_ref, p_ref):
    boxes = charge_ref.shape[0]
    lane = iota((8, 128), 1)
    sub4 = iota((8, 128), 0) % 4

    def body(b, carry):
        q = jnp.where(lane < count_ref[b], charge_ref[b], 0.0)
        q_ref[b] = doubled(q)
        x = point_rows(pos_ref, b)
        qs = jnp.concatenate(split(q), axis=0)
        weight = fold(dot(qs, stack_kernel(cheb_rows(x)), NT))
        w_ref[b] = weight + pltpu.roll(weight, 64, 1)
        cx, cy, cz = cen_ref[0, b], cen_ref[1, b], cen_ref[2, b]
        far = jnp.where(lane % 4 == 0, cx, jnp.where(lane % 4 == 1, cy, cz))
        center = jnp.where(sub4 == 0, cx, jnp.where(sub4 == 1, cy, cz))
        p_ref[b] = jnp.where(sub4 == 3, far, doubled(center + 0.5 * x))
        return carry

    lax.fori_loop(0, boxes, body, 0, unroll=8)


def own_table_kernel(pos_ref, charge_ref, count_ref, q_ref, f_ref, base_ref, t_ref):
    boxes = charge_ref.shape[0]
    sub = iota((8, 128), 0)
    lane = iota((8, 128), 1)

    def body(b, carry):
        q = jnp.where(lane < count_ref[b], charge_ref[b], 0.0)
        q_ref[b] = q
        x = point_rows(pos_ref, b)
        t_ref[b] = stack_kernel(cheb_rows(x))
        rel = (0.5 * ROOT3) * x
        tgt = planes(rel, False)
        for unit in range(2):
            f_ref[b, unit] = jnp.concatenate([jnp.where(sub // 4 == unit, part, 0.0) for part in tgt], axis=0).astype(BF)
        zero = jnp.zeros((96, 128), F32)
        src = jnp.concatenate(planes(rel, True) + [zero], axis=0).T.astype(BF)
        first = jnp.concatenate([jnp.where(sub < 4, part, 0.0) for part in tgt] + [zero], axis=0).astype(BF)
        value = stack_kernel(matern(dot(src, first)))
        qs = jnp.concatenate(split(q), axis=0)
        base_ref[b] = fold(dot(jnp.concatenate([qs, qs], axis=1), value)) + q
        return carry

    lax.fori_loop(0, boxes, body, 0, unroll=4)


def send_kernel(ids_ref, q_ref, w_ref, p_ref, ex_ref, out_ref):
    step = pl.program_id(0)
    group = out_ref.shape[0]
    sub4 = iota((8, 128), 0) % 4
    top = iota((8, 128), 0) < 4
    lane = iota((8, 128), 1)
    left = lane < HALF

    def body(k, carry):
        peer = step * group + k
        near = [ids_ref[peer, j] for j in range(4)]
        far = [ids_ref[peer, 4 + j] for j in range(4)]
        q = [q_ref[n] for n in near]
        out_ref[k, 0:8] = jnp.where(left, q[0], q[1])
        out_ref[k, 8:16] = jnp.where(left, q[2], q[3])
        w = [w_ref[n] for n in far]
        out_ref[k, 16:24] = jnp.where(left, w[0], w[2])
        out_ref[k, 24:32] = jnp.where(left, w[1], w[3])
        out_ref[k, 32:40] = ex_ref[ids_ref[peer, 8]]
        c = [p_ref[n] for n in far]
        centers = jnp.where(left, jnp.where(lane < 4, c[0], c[2]), jnp.where(lane < 68, c[1], c[3]))
        s = [p_ref[n] for n in near]
        points = jnp.where(top, jnp.where(left, s[0], s[1]), jnp.where(left, s[2], s[3]))
        out_ref[k, 40:48] = jnp.where(sub4 == 3, centers, points)
        return carry

    lax.fori_loop(0, group, body, 0, unroll=8)


def duo_kernel(
    tgt_ref, count_ref, got_ref, nc_ref, ec_ref, fc_ref, f_ref, fn_ref, base_ref, q_ref, t_ref, out_ref, term_ref,
    near_acc, far_acc, ft_ref, xt_ref, *bufs
):
    dist_refs, value_refs = bufs[:7], bufs[7:]
    peers = got_ref.shape[0]
    duos = peers // 2
    boxes = f_ref.shape[0]
    sub = iota((8, 128), 0)
    lane = iota((8, 128), 1)
    left = lane < HALF
    near_acc[...] = base_ref[...]
    far_acc[...] = jnp.zeros_like(far_acc)
    xt_ref[...] = jnp.zeros_like(xt_ref)
    for ref in dist_refs:
        ref[...] = jnp.zeros_like(ref)
    for ref in value_refs:
        ref[...] = jnp.zeros_like(ref)
    spread = (iota((128, 128), 0) // 64 == iota((128, 128), 1) // 64).astype(F32).astype(BF)

    batch = 16
    mask = iota((batch, 8, 128), 2) % 64 == iota((batch, 8, 128), 1)

    def far_body(g, carry):
        at = pl.ds(g * batch, batch)
        rows = got_ref[at, 40:48, :]
        rows = jnp.where(mask, jnp.broadcast_to(rows[:, 3:4, :], rows.shape), 0.0).reshape(batch * 8, 128)
        high = rows.astype(BF)
        rest = rows - high.astype(F32)
        mid = rest.astype(BF)
        low = (rest - mid.astype(F32)).astype(BF)
        cen = dot(high, spread) + dot(mid, spread) + dot(low, spread)
        rel = (fc_ref[at] - cen.reshape(batch, 8, 128)) * ROOT3
        ft_ref[at] = jnp.concatenate(planes(rel, False), axis=1).astype(BF)
        return carry

    lax.fori_loop(0, peers // batch, far_body, 0, unroll=2)

    def extra(duo):
        return got_ref[2 * duo, 32:40], got_ref[2 * duo + 1, 32:40]

    def body(i, carry):
        duo = jnp.maximum(i - 3, 0)
        go = jnp.broadcast_to(i, (8, 128)) >= 3
        ex = extra(duo)
        tiles = [got_ref[2 * duo + k // 2, 8 * (k % 2) : 8 * (k % 2) + 8] for k in range(4)]
        tiles.append(jnp.where(left, ex[0], pltpu.roll(ex[1], HALF, 1)))
        goals = [(tgt_ref[2 * duo + k // 2, 2 * (k % 2)], tgt_ref[2 * duo + k // 2, 2 * (k % 2) + 1]) for k in range(4)]
        goals.append((tgt_ref[2 * duo, 8], tgt_ref[2 * duo + 1, 8]))
        for k in range(5):
            q = jnp.where(go, tiles[k], 0.0)
            qs = split(jnp.where(left, q, 0.0)) + split(jnp.where(left, 0.0, q))
            qs = jnp.concatenate(qs, axis=0)
            new = dot(jnp.concatenate([qs, qs], axis=1), value_refs[k][...])
            near_acc[goals[k][0]] += fold(new[0:16])
            near_acc[goals[k][1]] += fold(new[16:32])
        for a in range(2):
            ws = []
            for h in range(2):
                w = jnp.where(go, got_ref[2 * duo + a, 16 + 8 * h : 24 + 8 * h], 0.0)
                ws += list(split(jnp.where(left, w, 0.0)) + split(jnp.where(left, 0.0, w)))
            ws = jnp.concatenate(ws, axis=0)
            new = dot(jnp.concatenate([ws, ws], axis=1), value_refs[5 + a][...])
            for h in range(2):
                for u in range(2):
                    at = 32 * h + 16 * u
                    part = fold(new[at : at + 16])
                    far_acc[tgt_ref[2 * duo + a, 4 + 2 * u + h]] += jnp.where(left if h == 0 else jnp.logical_not(left), part, 0.0)

        for k in range(7):
            value_refs[k][...] = stack_kernel(matern(dist_refs[k][...]))

        duo = jnp.clip(i - 1, 0, duos - 1)
        upper, lower = xt_ref[0:64, :], xt_ref[64:128, :]
        goals = [(tgt_ref[2 * duo + k // 2, 2 * (k % 2)], tgt_ref[2 * duo + k // 2, 2 * (k % 2) + 1]) for k in range(4)]
        goals.append((tgt_ref[2 * duo, 8], tgt_ref[2 * duo + 1, 8]))
        for k in range(5):
            v, u = k // 2, k % 2
            for half, part in enumerate((upper, lower)):
                pieces = [jnp.zeros((32 * v, 128), BF)] if v else []
                pieces += [f_ref[goals[k][half], u], jnp.zeros((96 - 32 * v, 128), BF)]
                dist_refs[k][64 * half : 64 * half + 64, :] = dot(part, jnp.concatenate(pieces, axis=0))
        for a in range(2):
            dist_refs[5 + a][...] = dot(fn_ref[...], ft_ref[2 * duo + a])

        duo = jnp.minimum(i, duos - 1)
        ex = extra(duo)
        feats = []
        for a in range(2):
            feats += planes((got_ref[2 * duo + a, 40:48] - nc_ref[2 * duo + a]) * ROOT3, True)
        point = jnp.where(left, pltpu.roll(ex[0], HALF, 1), ex[1])
        feats += planes((point - ec_ref[duo]) * ROOT3, True)
        feats.append(jnp.zeros((32, 128), F32))
        xt_ref[...] = jnp.concatenate(feats, axis=0).T.astype(BF)
        return carry

    lax.fori_loop(0, duos + 3, body, 0)

    def finish(b, total):
        ls = jnp.concatenate(split(far_acc[b]), axis=0)
        both = t_ref[b]
        high, low = both[0:64], both[64:128]
        table = jnp.concatenate([high, high, low, low], axis=0)
        far = fold(dot(jnp.concatenate([ls, ls], axis=1), table))
        product = jnp.where(lane < count_ref[b], near_acc[b] + far, 0.0)
        out_ref[b] = product
        return total + product * q_ref[b]

    total = lax.fori_loop(0, boxes, finish, jnp.zeros((8, 128), F32), unroll=8)
    ones = jnp.ones((128, 128), F32)
    sums = lax.dot_general(ones, total, NT, precision=lax.Precision.HIGHEST, preferred_element_type=F32)
    term_ref[...] = jnp.concatenate([sums, jnp.zeros((128, 120), F32)], axis=1)


def center_rows(centers, goals, halves=2):
    n, units = goals.shape[:2]
    rows = jnp.pad(centers[goals], ((0, 0), (0, 2 - units), (0, 0), (0, 1)))
    rows = rows.transpose(0, 1, 3, 2).reshape(n, 8, 2, 1)
    return jnp.broadcast_to(rows, (n, 8, 2, HALF)).reshape(n, 8, 128)


def on_device(local_pos, charges, counts, box_centers, far_list, near_list):
    devices = lax.axis_size("gx") * lax.axis_size("gy")
    boxes, _, slots = local_pos.shape
    struct = jax.ShapeDtypeStruct
    pos = jnp.transpose(local_pos, (1, 0, 2))
    table = struct((boxes, 8, 128), F32)
    want, ex_own = pl.pallas_call(
        start_kernel,
        out_shape=(struct((devices, 128), jnp.int32), table),
        in_specs=[vmem(), vmem(), vmem(), vmem(), vmem(), SMEM, SMEM],
        out_specs=(vmem(), vmem()),
        compiler_params=params(),
        name="start",
    )(far_list.T, near_list.T, counts.reshape(1, boxes), pos, charges, counts, box_centers)
    moved = [lax.ppermute(ex_own, "gy", [(4 * z, 4 * z + k) for z in range(4)]) for k in range(1, 4)]
    ex_tab = moved[0] + moved[1] + moved[2] + jnp.where(lax.axis_index("gy") % 4 == 0, ex_own, 0.0)
    served = exchange(want.reshape(devices, 1, 128)).reshape(devices, 128)

    q2_tab, w_tab, p_tab = pl.pallas_call(
        send_table_kernel,
        out_shape=(table, table, table),
        in_specs=[vmem(), vmem(), SMEM, SMEM],
        out_specs=(vmem(), vmem(), vmem()),
        compiler_params=params(),
        cost_estimate=pl.CostEstimate(flops=50_000_000, bytes_accessed=1_200_000, transcendentals=0),
        name="send_tables",
    )(pos, charges, counts, box_centers)

    group = 16
    lead = lambda shape: vmem((group,) + shape, lambda i: (i,) + (0,) * len(shape))
    send = pl.pallas_call(
        send_kernel,
        grid=(devices // group,),
        out_shape=struct((devices, ROWS, 128), F32),
        in_specs=[SMEM, vmem(), vmem(), vmem(), vmem()],
        out_specs=lead((ROWS, 128)),
        compiler_params=params(),
        name="send",
    )(served, q2_tab, w_tab, p_tab, ex_tab)
    got = exchange(send)

    q_tab, f_tab, base, cheb = pl.pallas_call(
        own_table_kernel,
        out_shape=(table, struct((boxes, 2, 32, 128), BF), table, struct((boxes, 128, 128), BF)),
        in_specs=[vmem(), vmem(), SMEM],
        out_specs=(vmem(), vmem(), vmem(), vmem()),
        compiler_params=params(),
        cost_estimate=pl.CostEstimate(flops=200_000_000, bytes_accessed=4_000_000, transcendentals=2_000_000),
        name="own_tables",
    )(pos, charges, counts)

    centers = box_centers.T
    goal = want[:, 16:24]
    more = goal.reshape(devices // 4, 4, 8)[:, 0, :4].reshape(devices, 1)
    tgt = jnp.concatenate([goal, more], axis=1)
    near_cen = center_rows(centers, goal[:, :4].reshape(devices, 2, 2))
    far_cen = center_rows(centers, goal[:, 4:].reshape(devices, 2, 2)) + node_rows()[None]
    ex_cen = center_rows(centers, more.reshape(devices // 2, 1, 2))

    big = lambda dtype, rows: pltpu.VMEM((rows, 128), dtype)
    product, term = pl.pallas_call(
        duo_kernel,
        out_shape=(table, struct((devices, 128), F32)),
        in_specs=[SMEM, SMEM] + [vmem()] * 9,
        out_specs=(vmem(), vmem()),
        scratch_shapes=[
            pltpu.VMEM((boxes, 8, 128), F32),
            pltpu.VMEM((boxes, 8, 128), F32),
            pltpu.VMEM((devices, 32, 128), BF),
            big(BF, 128),
        ]
        + [big(F32, 128)] * 7
        + [big(BF, 256)] * 7,
        compiler_params=params(),
        cost_estimate=pl.CostEstimate(flops=1_000_000_000, bytes_accessed=12_000_000, transcendentals=20_000_000),
        name="pairs",
    )(tgt, counts, got, near_cen, ex_cen, far_cen, f_tab, jnp.asarray(far_sources(), BF), base, q_tab, cheb)

    terms = exchange(term.reshape(devices, 1, 128))[:, 0, :8]
    curvature = jnp.sum(terms, axis=0) / (devices * boxes * slots)
    over = jnp.any((served[:, 9] > HALF) & (jnp.arange(devices) % 4 != 0))
    whole = (local_pos, charges, counts, box_centers, far_list, near_list)
    return lax.cond(over, lambda: general(*whole), lambda: (product, curvature))


def solution(mesh):
    in_specs = (
        P(AXES, None, None),
        P(AXES, None, None),
        P(AXES),
        P(None, AXES),
        P(AXES, None),
        P(AXES, None),
    )
    out_specs = (P(AXES, None, None), P())
    return jax.shard_map(on_device, mesh=mesh, in_specs=in_specs, out_specs=out_specs, check_vma=False)
```

```python
import functools
import math

import jax
import jax.numpy as jnp
import numpy as np
from jax import lax
from jax.experimental import pallas as pl
from jax.experimental.pallas import tpu as pltpu
from jax.sharding import PartitionSpec as P

AXES = ("gx", "gy")
NODES = 4
ROOT3 = 1.7320508075688772
LOG2E = 1.4426950408889634
BF = jnp.bfloat16
F32 = jnp.float32
NODE = [math.cos((2 * i + 1) * math.pi / 8) for i in range(NODES)]
NT = (((1,), (1,)), ((), ()))
TN = (((0,), (0,)), ((), ()))


def iota(shape, dim):
    return lax.broadcasted_iota(jnp.int32, shape, dim)


def dot(a, b, dims=None):
    if dims is None:
        return jnp.dot(a, b, preferred_element_type=F32)
    return lax.dot_general(a, b, dims, preferred_element_type=F32)


def split(x):
    high = x.astype(BF)
    return high, (x - high.astype(F32)).astype(BF)


def planes(rel, source):
    axis = rel.ndim - 2
    sub = iota(rel.shape, axis) % 4
    last = sub == 3
    rel = jnp.where(last, 0.0, rel)
    high = rel.astype(BF).astype(F32)
    low = (rel - high).astype(BF).astype(F32)
    square = high * (high + 2.0 * low)
    norm = pltpu.roll(square, 1, axis) + pltpu.roll(square, 2, axis) + pltpu.roll(square, 3, axis)
    one = norm.astype(BF).astype(F32)
    rest = norm - one
    two = rest.astype(BF).astype(F32)
    three = (rest - two).astype(BF).astype(F32)
    if source:
        parts = [
            jnp.where(last, one, high),
            jnp.where(last, two, high),
            jnp.where(last, 1.0, low),
            jnp.where(last, three, jnp.where(sub < 2, 1.0, 0.0)),
        ]
    else:
        parts = [
            jnp.where(last, 1.0, -2.0 * high),
            jnp.where(last, 1.0, -2.0 * low),
            jnp.where(last, one, -2.0 * high),
            jnp.where(
                sub == 0,
                pltpu.roll(two, 5, axis),
                jnp.where(sub == 1, pltpu.roll(three, 6, axis), jnp.where(last, 1.0, 0.0)),
            ),
        ]
    return parts


def matern(dist2):
    safe = jnp.maximum(dist2, 1e-12)
    scaled = safe * lax.rsqrt(safe)
    decay = jnp.exp2(scaled * (-LOG2E))
    return decay + scaled * decay


def stack_kernel(value):
    high, low = split(value)
    return jnp.concatenate([high, low], axis=0)


def fold(x):
    return x[0:8] + x[8:16]


def ids_kernel(far_ref, near_ref, want_ref):
    boxes = far_ref.shape[0]
    slots = far_ref.shape[1]
    total = boxes * slots
    lane = iota((total, 128), 1)
    box = iota((total, 128), 0) % boxes
    tri = (iota((total, total), 0) > iota((total, total), 1)).astype(F32).astype(BF)
    result = jnp.zeros((128, 128), F32)
    for ref, first, base in ((near_ref, 1, 0), (far_ref, 0, 4)):
        flat = jnp.concatenate([ref[:, first + j : first + j + 1] for j in range(slots)], axis=0)
        flat = jnp.broadcast_to(flat, (total, 128))
        hit = (flat // boxes) == lane
        onehot = hit.astype(F32).astype(BF)
        before = dot(tri, onehot)
        rank = jnp.sum(jnp.where(hit, before, 0.0), axis=1, keepdims=True).astype(jnp.int32)
        mine = rank == (lane % 4)
        within = jnp.where((lane >= base) & (lane < base + 4), flat % boxes, 0)
        owner = jnp.where((lane >= base + 16) & (lane < base + 20), box, 0)
        value = jnp.where(mine, within + owner, 0).astype(F32).astype(BF)
        result = result + dot(onehot, value, TN)
    want_ref[...] = result.astype(jnp.int32)


def table_kernel(pos_ref, charge_ref, count_ref, cen_ref, q_ref, w_ref, p_ref, f_ref, base_ref, t_ref):
    step = pl.program_id(0)
    group = pos_ref.shape[0]
    sub = iota((8, 128), 0)
    lane = iota((8, 128), 1)

    def body(b, carry):
        box = step * group + b
        live = lane < count_ref[box]
        q = jnp.where(live, charge_ref[b], 0.0)
        q_ref[b] = q
        pos = pos_ref[b]
        zero1 = jnp.zeros((1, 128), F32)
        x4 = jnp.concatenate([pos, zero1], axis=0)
        x = jnp.concatenate([x4, x4], axis=0)
        second = 2.0 * x * x - 1.0
        third = 2.0 * x * second - x
        basis = []
        for i in range(NODES):
            theta = (2 * i + 1) * math.pi / 8
            basis.append(0.25 + 0.5 * (math.cos(theta) * x + math.cos(2 * theta) * second + math.cos(3 * theta) * third))
        row = lambda i, d: jnp.broadcast_to(basis[i][d : d + 1], (8, 128))
        sub4 = sub % 4
        zs = jnp.where(sub4 == 0, row(0, 2), jnp.where(sub4 == 1, row(1, 2), jnp.where(sub4 == 2, row(2, 2), row(3, 2))))
        ys = [jnp.where(sub < 4, row(0, 1), row(1, 1)) * zs, jnp.where(sub < 4, row(2, 1), row(3, 1)) * zs]
        table = jnp.concatenate([row(i, 0) * ys[j] for i in range(NODES) for j in range(2)], axis=0)
        both = stack_kernel(table)
        t_ref[b] = both
        qs = jnp.concatenate(split(q), axis=0)
        weight = fold(dot(qs, both, NT))
        w_ref[b] = weight + pltpu.roll(weight, 64, 1)
        cx, cy, cz = cen_ref[0, box], cen_ref[1, box], cen_ref[2, box]
        lane4 = lane % 4
        far = jnp.where(lane4 == 0, cx, jnp.where(lane4 == 1, cy, cz))
        center = jnp.where(sub4 == 0, cx, jnp.where(sub4 == 1, cy, cz))
        p_ref[b] = jnp.where(sub4 == 3, far, center + 0.5 * x)
        rel = (0.5 * ROOT3) * x
        tgt = planes(rel, False)
        for unit in range(2):
            f_ref[b, unit] = jnp.concatenate([jnp.where(sub // 4 == unit, part, 0.0) for part in tgt], axis=0).astype(BF)
        src = jnp.concatenate(planes(rel, True) + [jnp.zeros((96, 128), F32)], axis=0).T.astype(BF)
        dist2 = dot(src[:, :32], f_ref[b, 0])
        value = stack_kernel(matern(dist2))
        near = fold(dot(jnp.concatenate([qs, qs], axis=1), value))
        base_ref[b] = near + q
        return carry

    lax.fori_loop(0, group, body, 0, unroll=4)


def gather_kernel(ids_ref, q_ref, w_ref, p_ref, out_ref):
    step = pl.program_id(0)
    group = out_ref.shape[0]
    sub4 = iota((8, 128), 0) % 4
    top = iota((8, 128), 0) < 4
    lane = iota((8, 128), 1)
    left = lane < 64

    def body(k, carry):
        peer = step * group + k
        near = [ids_ref[peer, j] for j in range(4)]
        far = [ids_ref[peer, 4 + j] for j in range(4)]
        for j in range(4):
            out_ref[k, 8 * j : 8 * j + 8] = q_ref[near[j]]
        w = [w_ref[far[j]] for j in range(4)]
        out_ref[k, 32:40] = jnp.where(left, w[0], w[2])
        out_ref[k, 40:48] = jnp.where(left, w[1], w[3])
        c = [p_ref[far[j]] for j in range(4)]
        centers = jnp.where(
            left, jnp.where(lane < 4, c[0], c[2]), jnp.where(lane < 68, c[1], c[3])
        )
        s = [p_ref[near[j]] for j in range(4)]
        out_ref[k, 48:56] = jnp.where(sub4 == 3, centers, jnp.where(top, s[0], s[1]))
        out_ref[k, 56:64] = jnp.where(sub4 == 3, centers, jnp.where(top, s[2], s[3]))
        return carry

    lax.fori_loop(0, group, body, 0, unroll=4)


def pair_kernel(
    tgt_ref, count_ref, got_ref, nc_ref, fc_ref, f_ref, fn_ref, base_ref, q_ref, t_ref, out_ref, term_ref, near_acc, far_acc
):
    step = pl.program_id(0)
    steps = pl.num_programs(0)
    group = got_ref.shape[0]
    boxes = f_ref.shape[0]
    sub = iota((8, 128), 0)
    lane = iota((8, 128), 1)
    left = lane < 64

    @pl.when(step == 0)
    def _():
        near_acc[...] = base_ref[...]
        far_acc[...] = jnp.zeros_like(far_acc)

    spread = (iota((128, 128), 0) // 64 == iota((128, 128), 1) // 64).astype(F32).astype(BF)

    def body(k, carry):
        peer = step * group + k
        tn = [tgt_ref[peer, j] for j in range(4)]
        tf = [tgt_ref[peer, 4 + j] for j in range(4)]
        points = [got_ref[k, 48:56], got_ref[k, 56:64]]
        feats = []
        for v in range(2):
            feats += planes((points[v] - nc_ref[k, 8 * v : 8 * v + 8]) * ROOT3, True)
        src = jnp.concatenate(feats + [jnp.zeros((64, 128), F32)], axis=0).T.astype(BF)
        for j in range(4):
            dist2 = dot(src[:, 32 * (j // 2) : 32 * (j // 2) + 32], f_ref[tn[j], j % 2])
            value = stack_kernel(matern(dist2))
            qs = jnp.concatenate(split(got_ref[k, 8 * j : 8 * j + 8]), axis=0)
            near_acc[tn[j]] += fold(dot(jnp.concatenate([qs, qs], axis=1), value))
        row = jnp.broadcast_to(points[0][3:4], (8, 128))
        row = jnp.where(lane % 64 == sub, row, 0.0)
        high = row.astype(BF)
        rest = row - high.astype(F32)
        mid = rest.astype(BF)
        low = (rest - mid.astype(F32)).astype(BF)
        cen = dot(jnp.concatenate([high, mid, low], axis=0), spread)
        rel = (fc_ref[k] - (cen[0:8] + cen[8:16] + cen[16:24])) * ROOT3
        tgt = jnp.concatenate(planes(rel, False), axis=0).astype(BF)
        value = stack_kernel(matern(dot(fn_ref[...], tgt)))
        ws = []
        for h in range(2):
            w = got_ref[k, 32 + 8 * h : 40 + 8 * h]
            for part in (jnp.where(left, w, 0.0), jnp.where(left, 0.0, w)):
                ws += list(split(part))
        ws = jnp.concatenate(ws, axis=0)
        locs = dot(jnp.concatenate([ws, ws], axis=1), value)
        for h in range(2):
            for u in range(2):
                at = 32 * h + 16 * u
                new = fold(locs[at : at + 16])
                far_acc[tf[2 * u + h]] += jnp.where(left if h == 0 else jnp.logical_not(left), new, 0.0)
        return carry

    lax.fori_loop(0, group, body, 0, unroll=2)

    @pl.when(step == steps - 1)
    def _():
        def finish(b, total):
            ls = jnp.concatenate(split(far_acc[b]), axis=0)
            both = t_ref[b]
            high, low = both[0:64], both[64:128]
            table = jnp.concatenate([high, high, low, low], axis=0)
            far = fold(dot(jnp.concatenate([ls, ls], axis=1), table))
            live = lane < count_ref[b]
            product = jnp.where(live, near_acc[b] + far, 0.0)
            out_ref[b] = product
            return total + product * q_ref[b]

        total = lax.fori_loop(0, boxes, finish, jnp.zeros((8, 128), F32), unroll=4)
        ones = jnp.ones((128, 128), F32)
        sums = lax.dot_general(ones, total, NT, precision=lax.Precision.HIGHEST, preferred_element_type=F32)
        term_ref[...] = jnp.concatenate([sums, jnp.zeros((128, 120), F32)], axis=1)


def far_sources():
    x = np.zeros((8, 128), np.float32)
    for n in range(64):
        for d, value in enumerate((NODE[n // 16], NODE[n // 4 % 4], NODE[n % 4])):
            for u in range(2):
                x[4 * u + d, 64 * u + n] = 0.5 * ROOT3 * value
    bf = lambda a: a.astype(jnp.bfloat16).astype(np.float32)
    high = bf(x)
    low = bf(x - high)
    norm = np.zeros_like(x)
    square = high * (high + 2 * low)
    for u in range(2):
        norm[4 * u + 3] = square[4 * u] + square[4 * u + 1] + square[4 * u + 2]
    one = bf(norm)
    two = bf(norm - one)
    three = bf(norm - one - two)
    sub = np.arange(8)[:, None] % 4
    unit = (np.arange(8)[:, None] // 4) == (np.arange(128)[None, :] // 64)
    parts = [
        np.where(sub == 3, one, high),
        np.where(sub == 3, two, high),
        np.where(sub == 3, 1.0, low),
        np.where(sub == 3, three, np.where(sub < 2, 1.0, 0.0)),
    ]
    return np.concatenate([np.where(unit, part, 0.0) for part in parts], axis=0).T.astype(np.float32)


def node_rows():
    out = np.zeros((8, 128), np.float32)
    for m in range(128):
        n = m % 64
        for u in range(2):
            for d, value in enumerate((NODE[n // 16], NODE[n // 4 % 4], NODE[n % 4])):
                out[4 * u + d, m] = 0.5 * value
    return out


def vmem(shape=None, index=None):
    if shape is None:
        return pl.BlockSpec(memory_space=pltpu.VMEM)
    return pl.BlockSpec(shape, index, memory_space=pltpu.VMEM)


SMEM = pl.BlockSpec(memory_space=pltpu.SMEM)


def params(mebibytes=56):
    return pltpu.CompilerParams(vmem_limit_bytes=mebibytes * 1024 * 1024)


def exchange(x):
    return lax.all_to_all(x, AXES, split_axis=0, concat_axis=0, tiled=True)


def general(local_pos, charges, counts, box_centers, far_list, near_list):
    devices = lax.axis_size("gx") * lax.axis_size("gy")
    boxes, _, slots = local_pos.shape
    struct = jax.ShapeDtypeStruct
    want = pl.pallas_call(
        ids_kernel,
        out_shape=struct((devices, 128), jnp.int32),
        in_specs=[vmem(), vmem()],
        out_specs=vmem(),
        compiler_params=params(),
        name="ids",
    )(far_list, near_list)
    served = exchange(want.reshape(devices, 1, 128)).reshape(devices, 128)

    group = 16
    lead = lambda shape: vmem((group,) + shape, lambda i: (i,) + (0,) * len(shape))
    q_tab, w_tab, p_tab, f_tab, base, table = pl.pallas_call(
        table_kernel,
        grid=(boxes // group,),
        out_shape=(
            struct((boxes, 8, 128), F32),
            struct((boxes, 8, 128), F32),
            struct((boxes, 8, 128), F32),
            struct((boxes, 2, 32, 128), BF),
            struct((boxes, 8, 128), F32),
            struct((boxes, 128, 128), BF),
        ),
        in_specs=[lead((3, 128)), lead((8, 128)), SMEM, SMEM],
        out_specs=(lead((8, 128)), lead((8, 128)), lead((8, 128)), lead((2, 32, 128)), lead((8, 128)), lead((128, 128))),
        compiler_params=params(),
        cost_estimate=pl.CostEstimate(flops=200_000_000, bytes_accessed=6_000_000, transcendentals=2_000_000),
        name="tables",
    )(local_pos, charges, counts, box_centers)

    send = pl.pallas_call(
        gather_kernel,
        grid=(devices // group,),
        out_shape=struct((devices, 64, 128), F32),
        in_specs=[SMEM, vmem(), vmem(), vmem()],
        out_specs=lead((64, 128)),
        compiler_params=params(),
        name="gather",
    )(served, q_tab, w_tab, p_tab)
    got = exchange(send)

    tgt = want[:, 16:24]
    centers = box_centers.T
    near_cen = jnp.pad(centers[tgt[:, :4]], ((0, 0), (0, 0), (0, 1))).reshape(devices, 16, 1)
    near_cen = jnp.broadcast_to(near_cen, (devices, 16, 128))
    far_cen = jnp.pad(centers[tgt[:, 4:]], ((0, 0), (0, 0), (0, 1))).reshape(devices, 2, 2, 4)
    far_cen = far_cen.transpose(0, 1, 3, 2).reshape(devices, 8, 2, 1)
    far_cen = jnp.broadcast_to(far_cen, (devices, 8, 2, 64)).reshape(devices, 8, 128) + node_rows()[None]

    product, term = pl.pallas_call(
        pair_kernel,
        grid=(devices // group,),
        out_shape=(struct((boxes, 8, 128), F32), struct((devices, 128), F32)),
        in_specs=[
            SMEM,
            SMEM,
            lead((64, 128)),
            lead((16, 128)),
            lead((8, 128)),
            vmem(),
            vmem(),
            vmem(),
            vmem(),
            vmem(),
        ],
        out_specs=(vmem(), vmem()),
        scratch_shapes=[pltpu.VMEM((boxes, 8, 128), F32), pltpu.VMEM((boxes, 8, 128), F32)],
        compiler_params=params(),
        cost_estimate=pl.CostEstimate(flops=1_000_000_000, bytes_accessed=12_000_000, transcendentals=20_000_000),
        name="pairs",
    )(tgt, counts, got, near_cen, far_cen, f_tab, jnp.asarray(far_sources(), BF), base, q_tab, table)

    terms = exchange(term.reshape(devices, 1, 128))[:, 0, :8]
    curvature = jnp.sum(terms, axis=0) / (devices * boxes * slots)
    return (product, curvature)


HALF = 64
ROWS = 48
UNROLL = 4


def start_kernel(far_ref, near_ref, most_ref, pos_ref, charge_ref, count_ref, cen_ref, want_ref, ex_ref):
    boxes = far_ref.shape[1]
    slots = far_ref.shape[0]
    sub = iota((8, 128), 0)
    lane = iota((8, 128), 1)
    left = lane < HALF

    def body(b, carry):
        live = lane < count_ref[b]
        q = pltpu.roll(jnp.where(live, charge_ref[b], 0.0), HALF, 1)
        point = jnp.zeros((8, 128), F32)
        for d in range(3):
            row = jnp.broadcast_to(pos_ref[d, pl.ds(b, 1), :], (8, 128))
            point = jnp.where(sub == d, cen_ref[d, b] + 0.5 * row, point)
        ex_ref[b] = jnp.where(left, q, point)
        return carry

    lax.fori_loop(0, boxes, body, 0, unroll=8)

    peer = iota((128, 128), 0)
    line = iota((128, 128), 1)
    tri = (peer < line).astype(F32).astype(BF)
    row32 = iota((32, 128), 0)
    boxrow = iota((32, 128), 1) % boxes
    result = jnp.zeros((128, 32), F32)
    for ref, first, base in ((near_ref, 1, 0), (far_ref, 0, 4)):
        seen = jnp.zeros((128, 1), F32)
        for j in range(0, slots, 2):
            flat = jnp.concatenate([ref[first + j : first + j + 1, :], ref[first + j + 1 : first + j + 2, :]], axis=1)
            hit = jnp.broadcast_to(flat // boxes, (128, 128)) == peer
            ones = hit.astype(F32)
            onehot = ones.astype(BF)
            before = dot(onehot, tri) + seen
            rank = jnp.sum(jnp.where(hit, before, 0.0), axis=0, keepdims=True).astype(jnp.int32)
            seen = seen + jnp.sum(ones, axis=1, keepdims=True)
            within = jnp.broadcast_to(flat % boxes * 16, (32, 128))
            mine = row32 % 4 == jnp.broadcast_to(rank, (32, 128))
            value = jnp.where(row32 // 4 == base // 4, within, jnp.where(row32 // 4 == base // 4 + 4, boxrow, 0))
            value = jnp.where(mine, value, 0).astype(F32).astype(BF)
            result = result + dot(onehot, value, NT)
    result = jnp.concatenate([result, jnp.zeros((128, 96), F32)], axis=1)
    member = peer % 4
    moved = [result] + [pltpu.roll(result, y, 0) for y in range(1, 4)]
    for at, base, scale in ((8, 0, 0.5), (24, 16, 1.0)):
        extra = jnp.zeros((128, 1), F32)
        for y in range(4):
            extra = jnp.where(member[:, 0:1] == y, moved[y][:, base + y : base + y + 1], extra)
        result = jnp.where(line == at, jnp.broadcast_to(scale * extra, (128, 128)), result)
    most = jnp.max(most_ref[...], axis=1, keepdims=True)
    want_ref[...] = jnp.where(line == 9, jnp.broadcast_to(most, (128, 128)), result.astype(jnp.int32))


def cheb_rows(x):
    sub = iota((8, 128), 0)
    second = 2.0 * x * x - 1.0
    third = 2.0 * x * second - x
    basis = []
    for i in range(NODES):
        theta = (2 * i + 1) * math.pi / 8
        basis.append(0.25 + 0.5 * (math.cos(theta) * x + math.cos(2 * theta) * second + math.cos(3 * theta) * third))
    row = lambda i, d: jnp.broadcast_to(basis[i][d : d + 1], (8, 128))
    sub4 = sub % 4
    zs = jnp.where(sub4 == 0, row(0, 2), jnp.where(sub4 == 1, row(1, 2), jnp.where(sub4 == 2, row(2, 2), row(3, 2))))
    ys = [jnp.where(sub < 4, row(0, 1), row(1, 1)) * zs, jnp.where(sub < 4, row(2, 1), row(3, 1)) * zs]
    return jnp.concatenate([row(i, 0) * ys[j] for i in range(NODES) for j in range(2)], axis=0)


def point_rows(pos_ref, b):
    sub4 = iota((8, 128), 0) % 4
    x = jnp.zeros((8, 128), F32)
    for d in range(3):
        x = jnp.where(sub4 == d, jnp.broadcast_to(pos_ref[d, pl.ds(b, 1), :], (8, 128)), x)
    return x


def doubled(x):
    return jnp.where(iota((8, 128), 1) < HALF, x, pltpu.roll(x, HALF, 1))


def send_table_kernel(pos_ref, charge_ref, count_ref, cen_ref, near_ref, far_ref):
    boxes = charge_ref.shape[0]
    lane = iota((8, 128), 1)
    sub4 = iota((8, 128), 0) % 4

    def body(b, carry):
        q = jnp.where(lane < count_ref[b], charge_ref[b], 0.0)
        near_ref[b, 0:8] = doubled(q)
        x = point_rows(pos_ref, b)
        cx, cy, cz = cen_ref[0, b], cen_ref[1, b], cen_ref[2, b]
        center = jnp.where(sub4 == 0, cx, jnp.where(sub4 == 1, cy, cz))
        near_ref[b, 8:16] = doubled(center + 0.5 * x)
        qs = jnp.concatenate(split(q), axis=0)
        weight = fold(dot(qs, stack_kernel(cheb_rows(x)), NT))
        far_ref[b, 0:8] = weight + pltpu.roll(weight, 64, 1)
        far_ref[b, 8:16] = jnp.where(lane % 4 == 0, cx, jnp.where(lane % 4 == 1, cy, cz))
        return carry

    lax.fori_loop(0, boxes, body, 0, unroll=8)


def own_table_kernel(pos_ref, charge_ref, count_ref, q_ref, f_ref, base_ref, t_ref):
    boxes = charge_ref.shape[0]
    sub = iota((8, 128), 0)
    lane = iota((8, 128), 1)

    def body(b, carry):
        q = jnp.where(lane < count_ref[b], charge_ref[b], 0.0)
        q_ref[b] = q
        x = point_rows(pos_ref, b)
        t_ref[b] = stack_kernel(cheb_rows(x))
        rel = (0.5 * ROOT3) * x
        tgt = planes(rel, False)
        for unit in range(2):
            f_ref[b, unit] = jnp.concatenate([jnp.where(sub // 4 == unit, part, 0.0) for part in tgt], axis=0).astype(BF)
        zero = jnp.zeros((96, 128), F32)
        src = jnp.concatenate(planes(rel, True) + [zero], axis=0).T.astype(BF)
        first = jnp.concatenate([jnp.where(sub < 4, part, 0.0) for part in tgt] + [zero], axis=0).astype(BF)
        value = stack_kernel(matern(dot(src, first)))
        qs = jnp.concatenate(split(q), axis=0)
        base_ref[b] = fold(dot(jnp.concatenate([qs, qs], axis=1), value)) + q
        return carry

    lax.fori_loop(0, boxes, body, 0, unroll=4)


def goal_kernel(want_ref, cen_ref, node_ref, nc_ref, fc_ref, ec_ref, odd_ref):
    lane = iota((128, 128), 1)
    left = lane < HALF
    boxes = cen_ref.shape[1]
    cen = jnp.concatenate([cen_ref[...], jnp.zeros((5, boxes), F32)], axis=0)
    cen = jnp.concatenate([cen, jnp.zeros((8, 128 - boxes), F32)], axis=1)
    cen = jnp.concatenate([cen, jnp.zeros((120, 128), F32)], axis=0).T
    high, rest = split(cen)
    rest = cen - high.astype(F32)
    mid, low = split(rest)
    parts = jnp.concatenate([high, mid, low], axis=0)
    want = want_ref[...]

    def centers(at):
        goal = jnp.broadcast_to(want[:, at : at + 1], (128, 128))
        onehot = (goal == lane).astype(F32).astype(BF)
        found = dot(jnp.concatenate([onehot] * 3, axis=1), parts)
        return [jnp.broadcast_to(found[:, d : d + 1], (128, 128)) for d in range(3)]

    nc_ref[...] = jnp.zeros_like(nc_ref)
    fc_ref[...] = jnp.zeros_like(fc_ref)
    ec_ref[...] = jnp.zeros_like(ec_ref)
    for ref, base in ((nc_ref, 16), (fc_ref, 20)):
        for u in range(2):
            first, second = centers(base + 2 * u), centers(base + 2 * u + 1)
            for d in range(3):
                row = jnp.where(left, first[d], second[d])
                if base == 20:
                    row = row + node_ref[d : d + 1, :]
                ref[pl.ds(4 * u + d, 128, stride=8), :] = row
    extra = centers(24)
    for d in range(3):
        odd_ref[...] = extra[d]
        even, odd = odd_ref[pl.ds(0, 64, stride=2), :], odd_ref[pl.ds(1, 64, stride=2), :]
        ec_ref[pl.ds(d, 64, stride=8), :] = jnp.where(left[:64], even, odd)


def send_kernel(member_ref, served_ref, near_ref, far_ref, own_ref, *refs):
    moved, (out_ref, ids_ref, ex_ref, sem) = refs[:3], refs[3:]
    step = pl.program_id(0)
    group = out_ref.shape[0]
    sub4 = iota((8, 128), 0) % 4
    top = iota((8, 128), 0) < 4
    lane = iota((8, 128), 1)
    left = lane < HALF

    @pl.when(step == 0)
    def _():
        copy = pltpu.make_async_copy(served_ref, ids_ref, sem)
        copy.start()
        ex_ref[...] = moved[0][...] + moved[1][...] + moved[2][...]

        @pl.when(member_ref[0] == 0)
        def _():
            ex_ref[...] = own_ref[...]

        copy.wait()

    def body(k, carry):
        peer = step * group + k
        rows = lambda ref, j, at, size: ref[pl.ds(pl.multiple_of(ids_ref[peer, j], size) + at, 8), :]
        q = [rows(near_ref, j, 0, 16) for j in range(4)]
        s = [rows(near_ref, j, 8, 16) for j in range(4)]
        w = [rows(far_ref, 4 + j, 0, 16) for j in range(4)]
        c = [rows(far_ref, 4 + j, 8, 16) for j in range(4)]
        out_ref[k, 0:8] = jnp.where(left, q[0], q[1])
        out_ref[k, 8:16] = jnp.where(left, q[2], q[3])
        out_ref[k, 16:24] = jnp.where(left, w[0], w[2])
        out_ref[k, 24:32] = jnp.where(left, w[1], w[3])
        out_ref[k, 32:40] = rows(ex_ref, 8, 0, 8)
        centers = jnp.where(left, jnp.where(lane < 4, c[0], c[2]), jnp.where(lane < 68, c[1], c[3]))
        points = jnp.where(top, jnp.where(left, s[0], s[1]), jnp.where(left, s[2], s[3]))
        out_ref[k, 40:48] = jnp.where(sub4 == 3, centers, points)
        return carry

    lax.fori_loop(0, group, body, 0, unroll=16)


def duo_kernel(
    got_ref, fn_ref, want_hbm, nc_hbm, ec_hbm, fc_hbm, f_hbm, base_hbm, q_hbm, w_hbm, near_hbm, far_hbm, term_ref,
    tgt_ref, nc_ref, ec_ref, fc_ref, f_ref, base_ref, q_ref, w_ref, near_ref, far_ref, sems, ft_ref, *bufs
):
    whole = [(fc_hbm, fc_ref), (want_hbm, tgt_ref), (nc_hbm, nc_ref), (ec_hbm, ec_ref), (f_hbm, f_ref)]
    whole += [(base_hbm, base_ref), (q_hbm, q_ref), (w_hbm, w_ref)]
    loads = [pltpu.make_async_copy(source, target, sems.at[i]) for i, (source, target) in enumerate(whole)]
    for copy in loads:
        copy.start()
    xt_refs, dist_refs, value_refs = bufs[:2], (bufs[2:9], bufs[9:16]), (bufs[16:23], bufs[23:30])
    near_accs, far_accs = bufs[30:32], bufs[32:34]
    peers = got_ref.shape[0]
    duos = peers // 2
    boxes = f_ref.shape[0]
    sub = iota((8, 128), 0)
    lane = iota((8, 128), 1)
    left = lane < HALF
    for ref in value_refs[1] + near_accs + far_accs:
        ref[...] = jnp.zeros_like(ref)
    for ref in dist_refs[1]:
        ref[...] = jnp.full(ref.shape, 1e6, F32)
    spread = (iota((128, 128), 0) // 64 == iota((128, 128), 1) // 64).astype(F32).astype(BF)

    batch = 16
    mask = iota((batch, 8, 128), 2) % 64 == iota((batch, 8, 128), 1)

    def far_body(g, carry):
        at = pl.ds(g * batch, batch)
        rows = got_ref[at, 40:48, :]
        rows = jnp.where(mask, jnp.broadcast_to(rows[:, 3:4, :], rows.shape), 0.0).reshape(batch * 8, 128)
        high = rows.astype(BF)
        rest = rows - high.astype(F32)
        mid = rest.astype(BF)
        low = (rest - mid.astype(F32)).astype(BF)
        cen = dot(high, spread) + dot(mid, spread) + dot(low, spread)
        rel = (fc_ref[at] - cen.reshape(batch, 8, 128)) * ROOT3
        ft_ref[at] = jnp.concatenate(planes(rel, False), axis=1).astype(BF)
        return carry

    loads[0].wait()
    lax.fori_loop(0, peers // batch, far_body, 0, unroll=2)

    def extra(duo):
        return got_ref[2 * duo, 32:40], got_ref[2 * duo + 1, 32:40]

    def goals(duo):
        pairs = [(tgt_ref[2 * duo + k // 2, 16 + 2 * (k % 2)], tgt_ref[2 * duo + k // 2, 17 + 2 * (k % 2)]) for k in range(4)]
        return pairs + [(tgt_ref[2 * duo, 24], tgt_ref[2 * duo + 1, 24])]

    def halves(x):
        high = x.astype(BF).astype(F32)
        both = [high, x - high]
        return [jnp.where(left, part, 0.0) for part in both] + [jnp.where(left, 0.0, part) for part in both]

    def products(duo, value):
        ex = extra(duo)
        tiles = [got_ref[2 * duo + k // 2, 8 * (k % 2) : 8 * (k % 2) + 8] for k in range(4)]
        tiles.append(jnp.where(left, ex[0], pltpu.roll(ex[1], HALF, 1)))
        for k, goal in enumerate(goals(duo)):
            qs = jnp.concatenate(halves(tiles[k]), axis=0).astype(BF)
            new = dot(jnp.concatenate([qs, qs], axis=1), value[k][...])
            for h in range(2):
                near_accs[h][goal[h]] += fold(new[16 * h : 16 * h + 16])
        for a in range(2):
            ws = []
            for h in range(2):
                ws += halves(got_ref[2 * duo + a, 16 + 8 * h : 24 + 8 * h])
            ws = jnp.concatenate(ws, axis=0).astype(BF)
            new = dot(jnp.concatenate([ws, ws], axis=1), value[5 + a][...])
            for h in range(2):
                for u in range(2):
                    at = 32 * h + 16 * u
                    far_accs[h][tgt_ref[2 * duo + a, 20 + 2 * u + h]] += fold(new[at : at + 16])

    def values(dist, value):
        for k in range(7):
            value[k][...] = stack_kernel(matern(dist[k][...]))

    def distances(duo, xt, dist):
        for k, goal in enumerate(goals(duo)):
            v, u = k // 2, k % 2
            for half in range(2):
                pieces = [jnp.zeros((32 * v, 128), BF)] if v else []
                pieces += [f_ref[goal[half], u], jnp.zeros((96 - 32 * v, 128), BF)]
                at = slice(64 * half, 64 * half + 64)
                dist[k][at, :] = dot(xt[at, :], jnp.concatenate(pieces, axis=0))
        for a in range(2):
            dist[5 + a][...] = dot(fn_ref[...], ft_ref[2 * duo + a])

    def features(duo, xt):
        ex = extra(duo)
        feats = []
        for a in range(2):
            feats += planes((got_ref[2 * duo + a, 40:48] - nc_ref[2 * duo + a]) * ROOT3, True)
        point = jnp.where(left, pltpu.roll(ex[0], HALF, 1), ex[1])
        feats += planes((point - ec_ref[duo]) * ROOT3, True)
        feats.append(jnp.zeros((32, 128), F32))
        xt[...] = jnp.concatenate(feats, axis=0).T.astype(BF)

    def body(i, carry):
        for s in range(UNROLL):
            now, was = s % 2, 1 - s % 2
            step = UNROLL * i + s
            products(jnp.maximum(step - 2, 0), value_refs[was])
            values(dist_refs[was], value_refs[now])
            distances(step, xt_refs[was], dist_refs[now])
            features(jnp.minimum(step + 1, duos - 1), xt_refs[now])
        return carry

    for copy in loads[1:5]:
        copy.wait()
    features(0, xt_refs[1])
    lax.fori_loop(0, duos // UNROLL, body, 0)
    products(duos - 2, value_refs[1])
    values(dist_refs[1], value_refs[0])
    products(duos - 1, value_refs[0])

    for copy in loads[5:]:
        copy.wait()

    def finish(b, total):
        near = near_accs[0][b] + near_accs[1][b] + base_ref[b]
        far = jnp.where(left, far_accs[0][b], far_accs[1][b])
        near_ref[b] = near
        far_ref[b] = far
        return total + near * q_ref[b] + far * w_ref[b, 0:8]

    total = jnp.zeros((8, 128), F32)
    stores = []
    quarter = boxes // 4
    for part in range(4):
        total = lax.fori_loop(part * quarter, part * quarter + quarter, finish, total, unroll=16)
        at = pl.ds(part * quarter, quarter)
        for source, target, sem in ((near_ref, near_hbm, 8 + part), (far_ref, far_hbm, 12 + part)):
            copy = pltpu.make_async_copy(source.at[at], target.at[at], sems.at[sem])
            copy.start()
            stores.append(copy)
    ones = jnp.ones((128, 128), F32)
    sums = lax.dot_general(ones, total, NT, precision=lax.Precision.HIGHEST, preferred_element_type=F32)
    term_ref[...] = jnp.concatenate([sums, jnp.zeros((128, 120), F32)], axis=1)
    for copy in stores:
        copy.wait()


def finish_kernel(count_ref, near_ref, far_ref, t_ref, out_ref):
    boxes = near_ref.shape[0]
    lane = iota((8, 128), 1)

    def body(b, carry):
        ls = jnp.concatenate(split(far_ref[b]), axis=0)
        high, low = t_ref[b, 0:64], t_ref[b, 64:128]
        far = fold(dot(jnp.concatenate([ls, ls], axis=1), jnp.concatenate([high, high, low, low], axis=0)))
        out_ref[b] = jnp.where(lane < count_ref[b], near_ref[b] + far, 0.0)
        return carry

    lax.fori_loop(0, boxes, body, 0, unroll=16)


def on_device(local_pos, charges, counts, box_centers, far_list, near_list):
    devices = lax.axis_size("gx") * lax.axis_size("gy")
    boxes, _, slots = local_pos.shape
    struct = jax.ShapeDtypeStruct
    pos = jnp.transpose(local_pos, (1, 0, 2))
    table = struct((boxes, 8, 128), F32)
    hbm = pltpu.HBM
    stay = lambda x: pltpu.with_memory_space_constraint(x, pltpu.HBM)
    anywhere = pl.BlockSpec(memory_space=pltpu.HBM)
    wide = struct((boxes, 16, 128), F32)
    member = (lax.axis_index("gy") % 4).astype(jnp.int32).reshape(1)
    want, ex_own = pl.pallas_call(
        start_kernel,
        out_shape=(struct((devices, 128), jnp.int32), table),
        in_specs=[vmem(), vmem(), vmem(), vmem(), vmem(), SMEM, SMEM],
        out_specs=(vmem(), vmem()),
        compiler_params=params(8),
        name="start",
    )(far_list.T, near_list.T, counts.reshape(1, boxes), pos, charges, counts, box_centers)
    moved = [lax.ppermute(ex_own, "gy", [(4 * z, 4 * z + k) for z in range(4)]) for k in range(1, 4)]
    served = exchange(want.reshape(devices, 1, 128)).reshape(devices, 128)

    near_tab, far_tab = pl.pallas_call(
        send_table_kernel,
        out_shape=(wide, wide),
        in_specs=[vmem(), vmem(), SMEM, SMEM],
        out_specs=(vmem(), vmem()),
        compiler_params=params(8),
        cost_estimate=pl.CostEstimate(flops=50_000_000, bytes_accessed=1_200_000, transcendentals=0),
        name="send_tables",
    )(pos, charges, counts, box_centers)

    group = 64
    flat = lambda x: x.reshape(-1, 128)
    send = pl.pallas_call(
        send_kernel,
        grid=(devices // group,),
        out_shape=struct((devices, ROWS, 128), F32),
        in_specs=[SMEM, pl.BlockSpec(memory_space=pl.ANY)] + [vmem()] * 6,
        out_specs=vmem((group, ROWS, 128), lambda i: (i, 0, 0)),
        scratch_shapes=[
            pltpu.SMEM((devices, 128), jnp.int32),
            pltpu.VMEM((boxes * 8, 128), F32),
            pltpu.SemaphoreType.DMA(()),
        ],
        compiler_params=params(12),
        name="send",
    )(member, served, flat(near_tab), flat(far_tab), flat(ex_own), *[flat(x) for x in moved])
    got = exchange(send)

    q_tab, f_tab, base, cheb = pl.pallas_call(
        own_table_kernel,
        out_shape=(
            hbm((boxes, 8, 128), F32),
            hbm((boxes, 2, 32, 128), BF),
            hbm((boxes, 8, 128), F32),
            hbm((boxes, 128, 128), BF),
        ),
        in_specs=[vmem(), vmem(), SMEM],
        out_specs=(vmem(), vmem(), vmem(), vmem()),
        compiler_params=params(8),
        cost_estimate=pl.CostEstimate(flops=200_000_000, bytes_accessed=4_000_000, transcendentals=2_000_000),
        name="own_tables",
    )(pos, charges, counts)

    near_cen, far_cen, ex_cen = pl.pallas_call(
        goal_kernel,
        out_shape=(hbm((devices * 8, 128), F32), hbm((devices * 8, 128), F32), hbm((devices * 4, 128), F32)),
        in_specs=[vmem()] * 3,
        out_specs=(vmem(), vmem(), vmem()),
        scratch_shapes=[pltpu.VMEM((128, 128), F32)],
        compiler_params=params(8),
        cost_estimate=pl.CostEstimate(flops=50_000_000, bytes_accessed=2_000_000, transcendentals=0),
        name="goals",
    )(want, box_centers, jnp.asarray(node_rows()))
    near_cen, far_cen, ex_cen = [x.reshape(-1, 8, 128) for x in (near_cen, far_cen, ex_cen)]

    big = lambda dtype, rows: pltpu.VMEM((rows, 128), dtype)
    near, far, term = pl.pallas_call(
        duo_kernel,
        out_shape=(hbm((boxes, 8, 128), F32), hbm((boxes, 8, 128), F32), struct((devices, 128), F32)),
        in_specs=[vmem()] * 2 + [anywhere] * 8,
        out_specs=(anywhere, anywhere, vmem()),
        scratch_shapes=[
            pltpu.SMEM((devices, 128), jnp.int32),
            pltpu.VMEM((devices, 8, 128), F32),
            pltpu.VMEM((devices // 2, 8, 128), F32),
            pltpu.VMEM((devices, 8, 128), F32),
            pltpu.VMEM((boxes, 2, 32, 128), BF),
            pltpu.VMEM((boxes, 8, 128), F32),
            pltpu.VMEM((boxes, 8, 128), F32),
            pltpu.VMEM((boxes, 16, 128), F32),
            pltpu.VMEM((boxes, 8, 128), F32),
            pltpu.VMEM((boxes, 8, 128), F32),
            pltpu.SemaphoreType.DMA((16,)),
            pltpu.VMEM((devices, 32, 128), BF),
        ]
        + [big(BF, 128)] * 2
        + [big(F32, 128)] * 14
        + [big(BF, 256)] * 14
        + [pltpu.VMEM((boxes, 8, 128), F32)] * 4,
        compiler_params=params(20),
        cost_estimate=pl.CostEstimate(flops=1_000_000_000, bytes_accessed=12_000_000, transcendentals=20_000_000),
        name="pairs",
    )(got, jnp.asarray(far_sources(), BF), *[stay(x) for x in (want, near_cen, ex_cen, far_cen, f_tab, base, q_tab, far_tab)])

    terms = exchange(term.reshape(devices, 1, 128))[:, 0, :8]
    curvature = jnp.sum(terms, axis=0) / (devices * boxes * slots)
    product = pl.pallas_call(
        finish_kernel,
        out_shape=table,
        in_specs=[SMEM] + [vmem()] * 3,
        out_specs=vmem(),
        compiler_params=params(8),
        cost_estimate=pl.CostEstimate(flops=50_000_000, bytes_accessed=3_000_000, transcendentals=0),
        name="finish",
    )(counts, stay(near), stay(far), stay(cheb))
    over = jnp.any((served[:, 9] > HALF) & (jnp.arange(devices) % 4 != 0))
    whole = (local_pos, charges, counts, box_centers, far_list, near_list)
    return lax.cond(over, lambda: general(*whole), lambda: (product, curvature))


def solution(mesh):
    in_specs = (
        P(AXES, None, None),
        P(AXES, None, None),
        P(AXES),
        P(None, AXES),
        P(AXES, None),
        P(AXES, None),
    )
    out_specs = (P(AXES, None, None), P())
    return jax.shard_map(on_device, mesh=mesh, in_specs=in_specs, out_specs=out_specs, check_vma=False)
```

```python
import functools
import math

import jax
import jax.numpy as jnp
import numpy as np
from jax import lax
from jax.experimental import pallas as pl
from jax.experimental.pallas import tpu as pltpu
from jax.sharding import PartitionSpec as P

AXES = ("gx", "gy")
NODES = 4
ROOT3 = 1.7320508075688772
LOG2E = 1.4426950408889634
BF = jnp.bfloat16
F32 = jnp.float32
NODE = [math.cos((2 * i + 1) * math.pi / 8) for i in range(NODES)]
NT = (((1,), (1,)), ((), ()))
TN = (((0,), (0,)), ((), ()))


def iota(shape, dim):
    return lax.broadcasted_iota(jnp.int32, shape, dim)


def dot(a, b, dims=None):
    if dims is None:
        return jnp.dot(a, b, preferred_element_type=F32)
    return lax.dot_general(a, b, dims, preferred_element_type=F32)


def split(x):
    high = x.astype(BF)
    return high, (x - high.astype(F32)).astype(BF)


def planes(rel, source):
    axis = rel.ndim - 2
    sub = iota(rel.shape, axis) % 4
    last = sub == 3
    rel = jnp.where(last, 0.0, rel)
    high = rel.astype(BF).astype(F32)
    low = (rel - high).astype(BF).astype(F32)
    square = high * (high + 2.0 * low)
    norm = pltpu.roll(square, 1, axis) + pltpu.roll(square, 2, axis) + pltpu.roll(square, 3, axis)
    one = norm.astype(BF).astype(F32)
    rest = norm - one
    two = rest.astype(BF).astype(F32)
    three = (rest - two).astype(BF).astype(F32)
    if source:
        parts = [
            jnp.where(last, one, high),
            jnp.where(last, two, high),
            jnp.where(last, 1.0, low),
            jnp.where(last, three, jnp.where(sub < 2, 1.0, 0.0)),
        ]
    else:
        parts = [
            jnp.where(last, 1.0, -2.0 * high),
            jnp.where(last, 1.0, -2.0 * low),
            jnp.where(last, one, -2.0 * high),
            jnp.where(
                sub == 0,
                pltpu.roll(two, 5, axis),
                jnp.where(sub == 1, pltpu.roll(three, 6, axis), jnp.where(last, 1.0, 0.0)),
            ),
        ]
    return parts


def matern(dist2):
    safe = jnp.maximum(dist2, 1e-12)
    scaled = safe * lax.rsqrt(safe)
    decay = jnp.exp2(scaled * (-LOG2E))
    return decay + scaled * decay


def stack_kernel(value):
    high, low = split(value)
    return jnp.concatenate([high, low], axis=0)


def fold(x):
    return x[0:8] + x[8:16]


def ids_kernel(far_ref, near_ref, want_ref):
    boxes = far_ref.shape[0]
    slots = far_ref.shape[1]
    total = boxes * slots
    lane = iota((total, 128), 1)
    box = iota((total, 128), 0) % boxes
    tri = (iota((total, total), 0) > iota((total, total), 1)).astype(F32).astype(BF)
    result = jnp.zeros((128, 128), F32)
    for ref, first, base in ((near_ref, 1, 0), (far_ref, 0, 4)):
        flat = jnp.concatenate([ref[:, first + j : first + j + 1] for j in range(slots)], axis=0)
        flat = jnp.broadcast_to(flat, (total, 128))
        hit = (flat // boxes) == lane
        onehot = hit.astype(F32).astype(BF)
        before = dot(tri, onehot)
        rank = jnp.sum(jnp.where(hit, before, 0.0), axis=1, keepdims=True).astype(jnp.int32)
        mine = rank == (lane % 4)
        within = jnp.where((lane >= base) & (lane < base + 4), flat % boxes, 0)
        owner = jnp.where((lane >= base + 16) & (lane < base + 20), box, 0)
        value = jnp.where(mine, within + owner, 0).astype(F32).astype(BF)
        result = result + dot(onehot, value, TN)
    want_ref[...] = result.astype(jnp.int32)


def table_kernel(pos_ref, charge_ref, count_ref, cen_ref, q_ref, w_ref, p_ref, f_ref, base_ref, t_ref):
    step = pl.program_id(0)
    group = pos_ref.shape[0]
    sub = iota((8, 128), 0)
    lane = iota((8, 128), 1)

    def body(b, carry):
        box = step * group + b
        live = lane < count_ref[box]
        q = jnp.where(live, charge_ref[b], 0.0)
        q_ref[b] = q
        pos = pos_ref[b]
        zero1 = jnp.zeros((1, 128), F32)
        x4 = jnp.concatenate([pos, zero1], axis=0)
        x = jnp.concatenate([x4, x4], axis=0)
        second = 2.0 * x * x - 1.0
        third = 2.0 * x * second - x
        basis = []
        for i in range(NODES):
            theta = (2 * i + 1) * math.pi / 8
            basis.append(0.25 + 0.5 * (math.cos(theta) * x + math.cos(2 * theta) * second + math.cos(3 * theta) * third))
        row = lambda i, d: jnp.broadcast_to(basis[i][d : d + 1], (8, 128))
        sub4 = sub % 4
        zs = jnp.where(sub4 == 0, row(0, 2), jnp.where(sub4 == 1, row(1, 2), jnp.where(sub4 == 2, row(2, 2), row(3, 2))))
        ys = [jnp.where(sub < 4, row(0, 1), row(1, 1)) * zs, jnp.where(sub < 4, row(2, 1), row(3, 1)) * zs]
        table = jnp.concatenate([row(i, 0) * ys[j] for i in range(NODES) for j in range(2)], axis=0)
        both = stack_kernel(table)
        t_ref[b] = both
        qs = jnp.concatenate(split(q), axis=0)
        weight = fold(dot(qs, both, NT))
        w_ref[b] = weight + pltpu.roll(weight, 64, 1)
        cx, cy, cz = cen_ref[0, box], cen_ref[1, box], cen_ref[2, box]
        lane4 = lane % 4
        far = jnp.where(lane4 == 0, cx, jnp.where(lane4 == 1, cy, cz))
        center = jnp.where(sub4 == 0, cx, jnp.where(sub4 == 1, cy, cz))
        p_ref[b] = jnp.where(sub4 == 3, far, center + 0.5 * x)
        rel = (0.5 * ROOT3) * x
        tgt = planes(rel, False)
        for unit in range(2):
            f_ref[b, unit] = jnp.concatenate([jnp.where(sub // 4 == unit, part, 0.0) for part in tgt], axis=0).astype(BF)
        src = jnp.concatenate(planes(rel, True) + [jnp.zeros((96, 128), F32)], axis=0).T.astype(BF)
        dist2 = dot(src[:, :32], f_ref[b, 0])
        value = stack_kernel(matern(dist2))
        near = fold(dot(jnp.concatenate([qs, qs], axis=1), value))
        base_ref[b] = near + q
        return carry

    lax.fori_loop(0, group, body, 0, unroll=4)


def gather_kernel(ids_ref, q_ref, w_ref, p_ref, out_ref):
    step = pl.program_id(0)
    group = out_ref.shape[0]
    sub4 = iota((8, 128), 0) % 4
    top = iota((8, 128), 0) < 4
    lane = iota((8, 128), 1)
    left = lane < 64

    def body(k, carry):
        peer = step * group + k
        near = [ids_ref[peer, j] for j in range(4)]
        far = [ids_ref[peer, 4 + j] for j in range(4)]
        for j in range(4):
            out_ref[k, 8 * j : 8 * j + 8] = q_ref[near[j]]
        w = [w_ref[far[j]] for j in range(4)]
        out_ref[k, 32:40] = jnp.where(left, w[0], w[2])
        out_ref[k, 40:48] = jnp.where(left, w[1], w[3])
        c = [p_ref[far[j]] for j in range(4)]
        centers = jnp.where(
            left, jnp.where(lane < 4, c[0], c[2]), jnp.where(lane < 68, c[1], c[3])
        )
        s = [p_ref[near[j]] for j in range(4)]
        out_ref[k, 48:56] = jnp.where(sub4 == 3, centers, jnp.where(top, s[0], s[1]))
        out_ref[k, 56:64] = jnp.where(sub4 == 3, centers, jnp.where(top, s[2], s[3]))
        return carry

    lax.fori_loop(0, group, body, 0, unroll=4)


def pair_kernel(
    tgt_ref, count_ref, got_ref, nc_ref, fc_ref, f_ref, fn_ref, base_ref, q_ref, t_ref, out_ref, term_ref, near_acc, far_acc
):
    step = pl.program_id(0)
    steps = pl.num_programs(0)
    group = got_ref.shape[0]
    boxes = f_ref.shape[0]
    sub = iota((8, 128), 0)
    lane = iota((8, 128), 1)
    left = lane < 64

    @pl.when(step == 0)
    def _():
        near_acc[...] = base_ref[...]
        far_acc[...] = jnp.zeros_like(far_acc)

    spread = (iota((128, 128), 0) // 64 == iota((128, 128), 1) // 64).astype(F32).astype(BF)

    def body(k, carry):
        peer = step * group + k
        tn = [tgt_ref[peer, j] for j in range(4)]
        tf = [tgt_ref[peer, 4 + j] for j in range(4)]
        points = [got_ref[k, 48:56], got_ref[k, 56:64]]
        feats = []
        for v in range(2):
            feats += planes((points[v] - nc_ref[k, 8 * v : 8 * v + 8]) * ROOT3, True)
        src = jnp.concatenate(feats + [jnp.zeros((64, 128), F32)], axis=0).T.astype(BF)
        for j in range(4):
            dist2 = dot(src[:, 32 * (j // 2) : 32 * (j // 2) + 32], f_ref[tn[j], j % 2])
            value = stack_kernel(matern(dist2))
            qs = jnp.concatenate(split(got_ref[k, 8 * j : 8 * j + 8]), axis=0)
            near_acc[tn[j]] += fold(dot(jnp.concatenate([qs, qs], axis=1), value))
        row = jnp.broadcast_to(points[0][3:4], (8, 128))
        row = jnp.where(lane % 64 == sub, row, 0.0)
        high = row.astype(BF)
        rest = row - high.astype(F32)
        mid = rest.astype(BF)
        low = (rest - mid.astype(F32)).astype(BF)
        cen = dot(jnp.concatenate([high, mid, low], axis=0), spread)
        rel = (fc_ref[k] - (cen[0:8] + cen[8:16] + cen[16:24])) * ROOT3
        tgt = jnp.concatenate(planes(rel, False), axis=0).astype(BF)
        value = stack_kernel(matern(dot(fn_ref[...], tgt)))
        ws = []
        for h in range(2):
            w = got_ref[k, 32 + 8 * h : 40 + 8 * h]
            for part in (jnp.where(left, w, 0.0), jnp.where(left, 0.0, w)):
                ws += list(split(part))
        ws = jnp.concatenate(ws, axis=0)
        locs = dot(jnp.concatenate([ws, ws], axis=1), value)
        for h in range(2):
            for u in range(2):
                at = 32 * h + 16 * u
                new = fold(locs[at : at + 16])
                far_acc[tf[2 * u + h]] += jnp.where(left if h == 0 else jnp.logical_not(left), new, 0.0)
        return carry

    lax.fori_loop(0, group, body, 0, unroll=2)

    @pl.when(step == steps - 1)
    def _():
        def finish(b, total):
            ls = jnp.concatenate(split(far_acc[b]), axis=0)
            both = t_ref[b]
            high, low = both[0:64], both[64:128]
            table = jnp.concatenate([high, high, low, low], axis=0)
            far = fold(dot(jnp.concatenate([ls, ls], axis=1), table))
            live = lane < count_ref[b]
            product = jnp.where(live, near_acc[b] + far, 0.0)
            out_ref[b] = product
            return total + product * q_ref[b]

        total = lax.fori_loop(0, boxes, finish, jnp.zeros((8, 128), F32), unroll=4)
        ones = jnp.ones((128, 128), F32)
        sums = lax.dot_general(ones, total, NT, precision=lax.Precision.HIGHEST, preferred_element_type=F32)
        term_ref[...] = jnp.concatenate([sums, jnp.zeros((128, 120), F32)], axis=1)


def far_sources():
    x = np.zeros((8, 128), np.float32)
    for n in range(64):
        for d, value in enumerate((NODE[n // 16], NODE[n // 4 % 4], NODE[n % 4])):
            for u in range(2):
                x[4 * u + d, 64 * u + n] = 0.5 * ROOT3 * value
    bf = lambda a: a.astype(jnp.bfloat16).astype(np.float32)
    high = bf(x)
    low = bf(x - high)
    norm = np.zeros_like(x)
    square = high * (high + 2 * low)
    for u in range(2):
        norm[4 * u + 3] = square[4 * u] + square[4 * u + 1] + square[4 * u + 2]
    one = bf(norm)
    two = bf(norm - one)
    three = bf(norm - one - two)
    sub = np.arange(8)[:, None] % 4
    unit = (np.arange(8)[:, None] // 4) == (np.arange(128)[None, :] // 64)
    parts = [
        np.where(sub == 3, one, high),
        np.where(sub == 3, two, high),
        np.where(sub == 3, 1.0, low),
        np.where(sub == 3, three, np.where(sub < 2, 1.0, 0.0)),
    ]
    return np.concatenate([np.where(unit, part, 0.0) for part in parts], axis=0).T.astype(np.float32)


def node_rows():
    out = np.zeros((8, 128), np.float32)
    for m in range(128):
        n = m % 64
        for u in range(2):
            for d, value in enumerate((NODE[n // 16], NODE[n // 4 % 4], NODE[n % 4])):
                out[4 * u + d, m] = 0.5 * value
    return out


def vmem(shape=None, index=None):
    if shape is None:
        return pl.BlockSpec(memory_space=pltpu.VMEM)
    return pl.BlockSpec(shape, index, memory_space=pltpu.VMEM)


SMEM = pl.BlockSpec(memory_space=pltpu.SMEM)


def params(mebibytes=56):
    return pltpu.CompilerParams(vmem_limit_bytes=mebibytes * 1024 * 1024)


def exchange(x):
    return lax.all_to_all(x, AXES, split_axis=0, concat_axis=0, tiled=True)


def general(local_pos, charges, counts, box_centers, far_list, near_list):
    devices = lax.axis_size("gx") * lax.axis_size("gy")
    boxes, _, slots = local_pos.shape
    struct = jax.ShapeDtypeStruct
    want = pl.pallas_call(
        ids_kernel,
        out_shape=struct((devices, 128), jnp.int32),
        in_specs=[vmem(), vmem()],
        out_specs=vmem(),
        compiler_params=params(),
        name="ids",
    )(far_list, near_list)
    served = exchange(want.reshape(devices, 1, 128)).reshape(devices, 128)

    group = 16
    lead = lambda shape: vmem((group,) + shape, lambda i: (i,) + (0,) * len(shape))
    q_tab, w_tab, p_tab, f_tab, base, table = pl.pallas_call(
        table_kernel,
        grid=(boxes // group,),
        out_shape=(
            struct((boxes, 8, 128), F32),
            struct((boxes, 8, 128), F32),
            struct((boxes, 8, 128), F32),
            struct((boxes, 2, 32, 128), BF),
            struct((boxes, 8, 128), F32),
            struct((boxes, 128, 128), BF),
        ),
        in_specs=[lead((3, 128)), lead((8, 128)), SMEM, SMEM],
        out_specs=(lead((8, 128)), lead((8, 128)), lead((8, 128)), lead((2, 32, 128)), lead((8, 128)), lead((128, 128))),
        compiler_params=params(),
        cost_estimate=pl.CostEstimate(flops=200_000_000, bytes_accessed=6_000_000, transcendentals=2_000_000),
        name="tables",
    )(local_pos, charges, counts, box_centers)

    send = pl.pallas_call(
        gather_kernel,
        grid=(devices // group,),
        out_shape=struct((devices, 64, 128), F32),
        in_specs=[SMEM, vmem(), vmem(), vmem()],
        out_specs=lead((64, 128)),
        compiler_params=params(),
        name="gather",
    )(served, q_tab, w_tab, p_tab)
    got = exchange(send)

    tgt = want[:, 16:24]
    centers = box_centers.T
    near_cen = jnp.pad(centers[tgt[:, :4]], ((0, 0), (0, 0), (0, 1))).reshape(devices, 16, 1)
    near_cen = jnp.broadcast_to(near_cen, (devices, 16, 128))
    far_cen = jnp.pad(centers[tgt[:, 4:]], ((0, 0), (0, 0), (0, 1))).reshape(devices, 2, 2, 4)
    far_cen = far_cen.transpose(0, 1, 3, 2).reshape(devices, 8, 2, 1)
    far_cen = jnp.broadcast_to(far_cen, (devices, 8, 2, 64)).reshape(devices, 8, 128) + node_rows()[None]

    product, term = pl.pallas_call(
        pair_kernel,
        grid=(devices // group,),
        out_shape=(struct((boxes, 8, 128), F32), struct((devices, 128), F32)),
        in_specs=[
            SMEM,
            SMEM,
            lead((64, 128)),
            lead((16, 128)),
            lead((8, 128)),
            vmem(),
            vmem(),
            vmem(),
            vmem(),
            vmem(),
        ],
        out_specs=(vmem(), vmem()),
        scratch_shapes=[pltpu.VMEM((boxes, 8, 128), F32), pltpu.VMEM((boxes, 8, 128), F32)],
        compiler_params=params(),
        cost_estimate=pl.CostEstimate(flops=1_000_000_000, bytes_accessed=12_000_000, transcendentals=20_000_000),
        name="pairs",
    )(tgt, counts, got, near_cen, far_cen, f_tab, jnp.asarray(far_sources(), BF), base, q_tab, table)

    terms = exchange(term.reshape(devices, 1, 128))[:, 0, :8]
    curvature = jnp.sum(terms, axis=0) / (devices * boxes * slots)
    return (product, curvature)


HALF = 64
ROWS = 44
NEAR_ROWS = 24
UNROLL = 4


def start_kernel(far_ref, near_ref, most_ref, pos_ref, charge_ref, count_ref, cen_ref, row_ref, msg_ref, want_ref, ex_ref):
    boxes = far_ref.shape[1]
    slots = far_ref.shape[0]
    lane = iota((8, 128), 1)
    left = lane < HALF
    for d in range(3):
        center = jnp.concatenate([row_ref[...], jnp.zeros((5, boxes), F32)], axis=0)
        center = jnp.concatenate([center, jnp.zeros((8, 128 - boxes), F32)], axis=1)
        center = jnp.concatenate([center, jnp.zeros((120, 128), F32)], axis=0).T[:boxes, d : d + 1]
        ex_ref[pl.ds(d, boxes, stride=8), :] = center + 0.5 * pos_ref[d]
    for d in range(3, 8):
        ex_ref[pl.ds(d, boxes, stride=8), :] = jnp.zeros((boxes, 128), F32)

    def body(b, carry):
        q = pltpu.roll(jnp.where(lane < count_ref[b], charge_ref[b], 0.0), HALF, 1)
        at = pl.ds(pl.multiple_of(8 * b, 8), 8)
        ex_ref[at, :] = jnp.where(left, q, ex_ref[at, :])
        return carry

    lax.fori_loop(0, boxes, body, 0, unroll=16)

    peer = iota((128, 128), 0)
    line = iota((128, 128), 1)
    tri = (peer < line).astype(F32).astype(BF)
    full = jnp.ones((128, 128), BF)
    row32 = iota((32, 128), 0)
    kind = row32 // 4
    boxrow = iota((32, 128), 1) % boxes
    result = jnp.zeros((128, 32), F32)
    for ref, first, group in ((near_ref, 1, 0), (far_ref, 0, 1)):
        seen = jnp.zeros((128, 128), F32)
        for j in range(0, slots, 2):
            flat = jnp.concatenate([ref[first + j : first + j + 1, :], ref[first + j + 1 : first + j + 2, :]], axis=1)
            hit = jnp.broadcast_to(flat // boxes, (128, 128)) == peer
            onehot = hit.astype(F32).astype(BF)
            before = dot(onehot, tri) + seen
            rank = jnp.sum(jnp.where(hit, before, 0.0), axis=0, keepdims=True).astype(jnp.int32)
            if j + 2 < slots:
                seen = seen + dot(onehot, full)
            within = jnp.broadcast_to(flat % boxes, (32, 128))
            if group == 0:
                value = jnp.where(kind == 0, within * NEAR_ROWS, jnp.where(kind == 2, within * 8, 0))
            else:
                value = jnp.where(kind == 1, within * 8, 0)
            value = jnp.where(kind == 4 + group, boxrow, value)
            value = jnp.where(row32 % 4 == jnp.broadcast_to(rank, (32, 128)), value, 0).astype(F32).astype(BF)
            result = result + dot(onehot, value, NT)
    result = jnp.concatenate([result, jnp.zeros((128, 96), F32)], axis=1)
    heavy = (line == peer - peer % 4).astype(F32).astype(BF)
    first = dot(heavy, result.astype(BF))
    for at, base in ((8, 8), (24, 16)):
        extra = dot(jnp.where(line == base + peer % 4, first, 0.0).astype(BF), full)
        result = jnp.where(line == at, extra, result)
    most = jnp.max(most_ref[...], axis=1, keepdims=True).astype(F32)
    result = jnp.where(line == 9, jnp.broadcast_to(most, (128, 128)), result)
    want_ref[...] = result.astype(jnp.int32)
    rows = [jnp.concatenate([row_ref[d : d + 1, :]] * 2, axis=1) for d in range(3)]
    rows = [jnp.broadcast_to(row, (128, 128)) for row in rows]
    msg_ref[pl.ds(0, 128, stride=2), :] = jnp.where(line < HALF, result, rows[2])
    msg_ref[pl.ds(1, 128, stride=2), :] = jnp.where(line < HALF, rows[0], rows[1])


def cheb_rows(x):
    sub = iota((8, 128), 0)
    second = 2.0 * x * x - 1.0
    third = 2.0 * x * second - x
    basis = []
    for i in range(NODES):
        theta = (2 * i + 1) * math.pi / 8
        basis.append(0.25 + 0.5 * (math.cos(theta) * x + math.cos(2 * theta) * second + math.cos(3 * theta) * third))
    row = lambda i, d: jnp.broadcast_to(basis[i][d : d + 1], (8, 128))
    sub4 = sub % 4
    zs = jnp.where(sub4 == 0, row(0, 2), jnp.where(sub4 == 1, row(1, 2), jnp.where(sub4 == 2, row(2, 2), row(3, 2))))
    ys = [jnp.where(sub < 4, row(0, 1), row(1, 1)) * zs, jnp.where(sub < 4, row(2, 1), row(3, 1)) * zs]
    return jnp.concatenate([row(i, 0) * ys[j] for i in range(NODES) for j in range(2)], axis=0)


def point_rows(pos_ref, b):
    sub4 = iota((8, 128), 0) % 4
    x = jnp.zeros((8, 128), F32)
    for d in range(3):
        x = jnp.where(sub4 == d, jnp.broadcast_to(pos_ref[d, pl.ds(b, 1), :], (8, 128)), x)
    return x


def doubled(x):
    return jnp.where(iota((8, 128), 1) < HALF, x, pltpu.roll(x, HALF, 1))


def send_table_kernel(pos_ref, charge_ref, count_ref, cen_ref, near_ref, far_ref, basis_ref):
    boxes = charge_ref.shape[0]
    lane = iota((8, 128), 1)
    sub = iota((8, 128), 0)
    for d in range(3):
        x = pos_ref[d]
        second = 2.0 * x * x - 1.0
        third = 2.0 * x * second - x
        for i in range(NODES):
            theta = (2 * i + 1) * math.pi / 8
            value = math.cos(theta) * x + math.cos(2 * theta) * second + math.cos(3 * theta) * third
            basis_ref[4 * d + i] = 0.25 + 0.5 * value

    def body(b, carry):
        q = jnp.where(lane < count_ref[b], charge_ref[b], 0.0)
        near_ref[b, 0:8] = doubled(q)
        x, y, z = [doubled(cen_ref[d, b] + 0.5 * jnp.broadcast_to(pos_ref[d, pl.ds(b, 1), :], (8, 128))) for d in range(3)]
        near_ref[b, 8:16] = jnp.where(sub == 4, x, jnp.where(sub == 5, y, z))
        near_ref[b, 16:24] = jnp.where(sub == 7, x, jnp.where((sub == 3) | (sub == 5), y, z))
        row = lambda i, d: jnp.broadcast_to(basis_ref[4 * d + i, pl.ds(b, 1), :], (8, 128))
        sub4 = sub % 4
        zs = jnp.where(sub4 == 0, row(0, 2), jnp.where(sub4 == 1, row(1, 2), jnp.where(sub4 == 2, row(2, 2), row(3, 2))))
        ys = [jnp.where(sub < 4, row(0, 1), row(1, 1)) * zs, jnp.where(sub < 4, row(2, 1), row(3, 1)) * zs]
        table = jnp.concatenate([row(i, 0) * ys[j] for i in range(NODES) for j in range(2)], axis=0)
        qs = jnp.concatenate(split(q), axis=0)
        weight = fold(dot(qs, stack_kernel(table), NT))
        far_ref[b] = weight + pltpu.roll(weight, 64, 1)
        return carry

    lax.fori_loop(0, boxes, body, 0, unroll=8)


def own_table_kernel(pos_ref, charge_ref, count_ref, q_ref, f_ref, base_ref, t_ref):
    boxes = charge_ref.shape[0]
    sub = iota((8, 128), 0)
    lane = iota((8, 128), 1)

    def body(b, carry):
        q = jnp.where(lane < count_ref[b], charge_ref[b], 0.0)
        q_ref[b] = q
        x = point_rows(pos_ref, b)
        t_ref[b] = stack_kernel(cheb_rows(x))
        rel = (0.5 * ROOT3) * x
        tgt = planes(rel, False)
        for unit in range(2):
            f_ref[b, unit] = jnp.concatenate([jnp.where(sub // 4 == unit, part, 0.0) for part in tgt], axis=0).astype(BF)
        zero = jnp.zeros((96, 128), F32)
        src = jnp.concatenate(planes(rel, True) + [zero], axis=0).T.astype(BF)
        first = jnp.concatenate([jnp.where(sub < 4, part, 0.0) for part in tgt] + [zero], axis=0).astype(BF)
        value = stack_kernel(matern(dot(src, first)))
        qs = jnp.concatenate(split(q), axis=0)
        base_ref[b] = fold(dot(jnp.concatenate([qs, qs], axis=1), value)) + q
        return carry

    lax.fori_loop(0, boxes, body, 0, unroll=4)


def goal_kernel(want_ref, served_ref, cen_ref, node_ref, nc_ref, fc_ref, ec_ref, odd_ref):
    lane = iota((128, 128), 1)
    left = lane < HALF
    boxes = cen_ref.shape[1]
    cen = jnp.concatenate([cen_ref[...], jnp.zeros((5, boxes), F32)], axis=0)
    cen = jnp.concatenate([cen, jnp.zeros((8, 128 - boxes), F32)], axis=1)
    cen = jnp.concatenate([cen, jnp.zeros((120, 128), F32)], axis=0).T

    def split3(x, axis):
        high = x.astype(BF)
        rest = x - high.astype(F32)
        mid = rest.astype(BF)
        return jnp.concatenate([high, mid, (rest - mid.astype(F32)).astype(BF)], axis=axis)

    parts = split3(cen, 0)
    want = want_ref[...]
    sources = [served_ref[pl.ds(1, 128, stride=2), :], served_ref[pl.ds(0, 128, stride=2), :]]
    halves = [jnp.concatenate([(iota((128, 128), 0) // HALF == h).astype(F32).astype(BF)] * 3, axis=0) for h in range(2)]

    def column(at):
        return jnp.broadcast_to(want[:, at : at + 1], (128, 128))

    def centers(at):
        onehot = (column(at) == lane).astype(F32).astype(BF)
        found = dot(jnp.concatenate([onehot] * 3, axis=1), parts)
        return [jnp.broadcast_to(found[:, d : d + 1], (128, 128)) for d in range(3)]

    def gaps(j):
        mine = lane % HALF == column(4 + j) // 8
        both = [split3(jnp.where(mine, source, 0.0), 1) for source in sources]
        theirs = [dot(both[0], halves[0]), dot(both[0], halves[1]), dot(both[1], halves[1])]
        return [a - b for a, b in zip(centers(20 + j), theirs)]

    nc_ref[...] = jnp.zeros_like(nc_ref)
    fc_ref[...] = jnp.zeros_like(fc_ref)
    ec_ref[...] = jnp.zeros_like(ec_ref)
    for u in range(2):
        first, second = centers(16 + 2 * u), centers(17 + 2 * u)
        for d in range(3):
            nc_ref[pl.ds(4 * u + d, 128, stride=8), :] = jnp.where(left, first[d], second[d])
        first, second = gaps(2 * u), gaps(2 * u + 1)
        for d in range(3):
            fc_ref[pl.ds(4 * u + d, 128, stride=8), :] = jnp.where(left, first[d], second[d]) + node_ref[d : d + 1, :]
    extra = centers(24)
    for d in range(3):
        odd_ref[...] = extra[d]
        even, odd = odd_ref[pl.ds(0, 64, stride=2), :], odd_ref[pl.ds(1, 64, stride=2), :]
        ec_ref[pl.ds(d, 64, stride=8), :] = jnp.where(left[:64], even, odd)


def far_kernel(fc_ref, fn_ref, out_ref):
    group = fc_ref.shape[0]
    tgt = jnp.concatenate(planes(fc_ref[...] * ROOT3, False), axis=1).astype(BF)
    for k in range(group):
        out_ref[k] = stack_kernel(matern(dot(fn_ref[...], tgt[k])))


def send_kernel(member_ref, served_ref, near_ref, far_ref, own_ref, *refs):
    moved, (out_ref, ids_ref, int_ref, ex_ref, buf_ref, sems) = refs[:3], refs[3:]
    peers = ids_ref.shape[0]
    sub = iota((8, 128), 0)
    lane = iota((8, 128), 1)
    left = lane < HALF
    keep = left | (sub < 3)
    second = sub < 5
    int_ref[...] = served_ref[pl.ds(0, peers, stride=2), :].astype(jnp.int32)
    copy = pltpu.make_async_copy(int_ref, ids_ref, sems.at[0])
    copy.start()
    ex_ref[...] = moved[0][...] + moved[1][...] + moved[2][...]

    @pl.when(member_ref[0] == 0)
    def _():
        ex_ref[...] = own_ref[...]

    copy.wait()

    def body(i, carry):
        base = pl.multiple_of(i * 2 * ROWS, 8)
        for k in range(2):
            peer = 2 * i + k
            at = lambda row: pl.ds(base + (k * ROWS + row), 8)
            rows = lambda ref, j, row: ref[pl.ds(pl.multiple_of(ids_ref[peer, j], 8) + row, 8), :]
            q = [rows(near_ref, j, 0) for j in range(4)]
            w = [rows(far_ref, 4 + j, 0) for j in range(4)]
            p = [rows(near_ref, j, 16 if j < 2 else 8) for j in range(4)]
            buf_ref[at(0), :] = jnp.where(left, q[0], q[1])
            buf_ref[at(8), :] = jnp.where(left, q[2], q[3])
            buf_ref[at(16), :] = jnp.where(left, w[0], w[2])
            buf_ref[at(24), :] = jnp.where(left, w[1], w[3])
            buf_ref[at(36), :] = jnp.where(sub == 7, jnp.where(left, p[0], p[1]), jnp.where(left, p[2], p[3]))
            buf_ref[at(32), :] = jnp.where(keep, rows(ex_ref, 8, 0), jnp.where(second, p[1], p[0]))
        return carry

    chunks = 4
    each = peers // chunks
    stores = []
    for c in range(chunks):
        lax.fori_loop(c * each // 2, (c + 1) * each // 2, body, 0, unroll=8)
        at = pl.ds(c * each * ROWS, each * ROWS)
        stores.append(pltpu.make_async_copy(buf_ref.at[at], out_ref.at[at], sems.at[1 + c]))
        stores[-1].start()
    for copy in stores:
        copy.wait()


def duo_kernel(
    got_ref, want_hbm, nc_hbm, ec_hbm, f_hbm, base_hbm, q_hbm, w_hbm, v_hbm, near_hbm, far_hbm, term_ref,
    tgt_ref, nc_ref, ec_ref, f_ref, base_ref, q_ref, w_ref, v_ref, near_ref, far_ref, sems, *bufs
):
    whole = [(want_hbm, tgt_ref), (nc_hbm, nc_ref), (ec_hbm, ec_ref), (f_hbm, f_ref)]
    whole += [(base_hbm, base_ref), (q_hbm, q_ref), (w_hbm, w_ref)]
    loads = [pltpu.make_async_copy(source, target, sems.at[i]) for i, (source, target) in enumerate(whole)]
    for copy in loads[:4]:
        copy.start()
    chunk = v_ref.shape[0] // 4

    def far_values(c):
        at = pl.ds(c * chunk, chunk)
        return pltpu.make_async_copy(v_hbm.at[at], v_ref.at[at], sems.at[16 + c])

    for c in range(4):
        far_values(c).start()
    for copy in loads[4:]:
        copy.start()
    xt_refs, dist_refs, value_refs = bufs[:2], (bufs[2:7], bufs[7:12]), (bufs[12:17], bufs[17:22])
    near_accs, far_accs = bufs[22:24], bufs[24:26]
    duos = ec_ref.shape[0]
    boxes = f_ref.shape[0]
    sub = iota((8, 128), 0)
    lane = iota((8, 128), 1)
    left = lane < HALF
    for ref in value_refs[1] + near_accs + far_accs:
        ref[...] = jnp.zeros_like(ref)
    for ref in dist_refs[1]:
        ref[...] = jnp.full(ref.shape, 1e6, F32)
    def tile(duo, a, row):
        return got_ref[pl.ds(pl.multiple_of(duo * 2 * ROWS, 8) + (a * ROWS + row), 8), :]

    def extra(duo):
        return tile(duo, 0, 32), tile(duo, 1, 32)

    def goals(duo):
        pairs = [(tgt_ref[2 * duo + k // 2, 16 + 2 * (k % 2)], tgt_ref[2 * duo + k // 2, 17 + 2 * (k % 2)]) for k in range(4)]
        return pairs + [(tgt_ref[2 * duo, 24], tgt_ref[2 * duo + 1, 24])]

    def halves(x):
        high = x.astype(BF).astype(F32)
        both = [high, x - high]
        return [jnp.where(left, part, 0.0) for part in both] + [jnp.where(left, 0.0, part) for part in both]

    def products(duo, value):
        ex = extra(duo)
        tiles = [tile(duo, k // 2, 8 * (k % 2)) for k in range(4)]
        tiles.append(jnp.where(left, ex[0], pltpu.roll(ex[1], HALF, 1)))
        for k, goal in enumerate(goals(duo)):
            qs = jnp.concatenate(halves(tiles[k]), axis=0).astype(BF)
            new = dot(jnp.concatenate([qs, qs], axis=1), value[k][...])
            for h in range(2):
                near_accs[h][goal[h]] += fold(new[16 * h : 16 * h + 16])

    def far_products(duo):
        for a in range(2):
            ws = []
            for h in range(2):
                ws += halves(tile(duo, a, 16 + 8 * h))
            ws = jnp.concatenate(ws, axis=0).astype(BF)
            new = dot(jnp.concatenate([ws, ws], axis=1), v_ref[2 * duo + a])
            for h in range(2):
                for u in range(2):
                    at = 32 * h + 16 * u
                    far_accs[h][tgt_ref[2 * duo + a, 20 + 2 * u + h]] += fold(new[at : at + 16])

    def values(dist, value):
        for k in range(5):
            value[k][...] = stack_kernel(matern(dist[k][...]))

    def distances(duo, xt, dist):
        for k, goal in enumerate(goals(duo)):
            v, u = k // 2, k % 2
            for half in range(2):
                pieces = [jnp.zeros((32 * v, 128), BF)] if v else []
                pieces += [f_ref[goal[half], u], jnp.zeros((96 - 32 * v, 128), BF)]
                at = slice(64 * half, 64 * half + 64)
                dist[k][at, :] = dot(xt[at, :], jnp.concatenate(pieces, axis=0))

    def features(duo, xt):
        ex = extra(duo)
        turned = [pltpu.roll(x, HALF, 1) for x in ex]
        feats = []
        for a in range(2):
            full = tile(duo, a, 36)
            split_rows = jnp.where(left, pltpu.roll(turned[a], 4, 0), pltpu.roll(ex[a], 6, 0))
            point = jnp.where(sub >= 4, full, jnp.where(sub == 0, pltpu.roll(full, 1, 0), split_rows))
            feats += planes((point - nc_ref[2 * duo + a]) * ROOT3, True)
        point = jnp.where(left, turned[0], ex[1])
        feats += planes((point - ec_ref[duo]) * ROOT3, True)
        feats.append(jnp.zeros((32, 128), F32))
        xt[...] = jnp.concatenate(feats, axis=0).T.astype(BF)

    turns = duos // UNROLL

    def body(i, carry):
        @pl.when(i % (turns // 4) == 0)
        def _():
            far_values(i // (turns // 4)).wait()

        for s in range(UNROLL):
            now, was = s % 2, 1 - s % 2
            step = UNROLL * i + s
            products(jnp.maximum(step - 2, 0), value_refs[was])
            far_products(step)
            values(dist_refs[was], value_refs[now])
            distances(step, xt_refs[was], dist_refs[now])
            features(jnp.minimum(step + 1, duos - 1), xt_refs[now])
        return carry

    for copy in loads[:4]:
        copy.wait()
    features(0, xt_refs[1])
    lax.fori_loop(0, turns, body, 0)
    products(duos - 2, value_refs[1])
    values(dist_refs[1], value_refs[0])
    products(duos - 1, value_refs[0])

    for copy in loads[4:]:
        copy.wait()

    def finish(b, total):
        near = near_accs[0][b] + near_accs[1][b] + base_ref[b]
        far = jnp.where(left, far_accs[0][b], far_accs[1][b])
        near_ref[b] = near
        far_ref[b] = far
        return total + near * q_ref[b] + far * w_ref[b]

    total = jnp.zeros((8, 128), F32)
    stores = []
    quarter = boxes // 4
    for part in range(4):
        total = lax.fori_loop(part * quarter, part * quarter + quarter, finish, total, unroll=16)
        at = pl.ds(part * quarter, quarter)
        for source, target, sem in ((near_ref, near_hbm, 8 + part), (far_ref, far_hbm, 12 + part)):
            copy = pltpu.make_async_copy(source.at[at], target.at[at], sems.at[sem])
            copy.start()
            stores.append(copy)
    ones = jnp.ones((128, 128), F32)
    sums = lax.dot_general(ones, total, NT, precision=lax.Precision.HIGHEST, preferred_element_type=F32)
    term_ref[...] = jnp.concatenate([sums, jnp.zeros((128, 120), F32)], axis=1)
    for copy in stores:
        copy.wait()


def finish_kernel(count_ref, near_ref, far_ref, t_ref, out_ref):
    boxes = near_ref.shape[0]
    lane = iota((8, 128), 1)

    def body(b, carry):
        ls = jnp.concatenate(split(far_ref[b]), axis=0)
        high, low = t_ref[b, 0:64], t_ref[b, 64:128]
        far = fold(dot(jnp.concatenate([ls, ls], axis=1), jnp.concatenate([high, high, low, low], axis=0)))
        out_ref[b] = jnp.where(lane < count_ref[b], near_ref[b] + far, 0.0)
        return carry

    lax.fori_loop(0, boxes, body, 0, unroll=16)


def on_device(local_pos, charges, counts, box_centers, far_list, near_list):
    devices = lax.axis_size("gx") * lax.axis_size("gy")
    boxes, _, slots = local_pos.shape
    struct = jax.ShapeDtypeStruct
    hbm = pltpu.HBM
    stay = lambda x: pltpu.with_memory_space_constraint(x, pltpu.HBM)
    anywhere = pl.BlockSpec(memory_space=pltpu.HBM)
    pos = jnp.transpose(local_pos, (1, 0, 2))
    table = struct((boxes, 8, 128), F32)
    flat = lambda x: x.reshape(-1, 128)
    member = (lax.axis_index("gy") % 4).astype(jnp.int32).reshape(1)
    msg, want, ex_own = pl.pallas_call(
        start_kernel,
        out_shape=(struct((devices * 2, 128), F32), struct((devices, 128), jnp.int32), struct((boxes * 8, 128), F32)),
        in_specs=[vmem()] * 5 + [SMEM, SMEM, vmem()],
        out_specs=(vmem(), vmem(), vmem()),
        compiler_params=params(8),
        name="start",
    )(far_list.T, near_list.T, counts.reshape(1, boxes), pos, charges, counts, box_centers, box_centers)
    moved = [lax.ppermute(ex_own, "gy", [(4 * z, 4 * z + k) for z in range(4)]) for k in range(1, 4)]
    served = flat(exchange(msg.reshape(devices, 2, 128)))

    near_tab, far_tab = pl.pallas_call(
        send_table_kernel,
        out_shape=(struct((boxes, NEAR_ROWS, 128), F32), table),
        in_specs=[vmem(), vmem(), SMEM, SMEM],
        out_specs=(vmem(), vmem()),
        scratch_shapes=[pltpu.VMEM((12, boxes, 128), F32)],
        compiler_params=params(8),
        cost_estimate=pl.CostEstimate(flops=50_000_000, bytes_accessed=1_200_000, transcendentals=0),
        name="send_tables",
    )(pos, charges, counts, box_centers)

    send = pl.pallas_call(
        send_kernel,
        out_shape=hbm((devices * ROWS, 128), F32),
        in_specs=[SMEM] + [vmem()] * 7,
        out_specs=anywhere,
        scratch_shapes=[
            pltpu.SMEM((devices, 128), jnp.int32),
            pltpu.VMEM((devices, 128), jnp.int32),
            pltpu.VMEM((boxes * 8, 128), F32),
            pltpu.VMEM((devices * ROWS, 128), F32),
            pltpu.SemaphoreType.DMA((5,)),
        ],
        compiler_params=params(12),
        name="send",
    )(member, served, flat(near_tab), flat(far_tab), ex_own, *moved)
    got = flat(exchange(send.reshape(devices, ROWS // 4, 4, 128)))

    q_tab, f_tab, base, cheb = pl.pallas_call(
        own_table_kernel,
        out_shape=(
            hbm((boxes, 8, 128), F32),
            hbm((boxes, 2, 32, 128), BF),
            hbm((boxes, 8, 128), F32),
            hbm((boxes, 128, 128), BF),
        ),
        in_specs=[vmem(), vmem(), SMEM],
        out_specs=(vmem(), vmem(), vmem(), vmem()),
        compiler_params=params(8),
        cost_estimate=pl.CostEstimate(flops=200_000_000, bytes_accessed=4_000_000, transcendentals=2_000_000),
        name="own_tables",
    )(pos, charges, counts)

    near_cen, far_gap, ex_cen = pl.pallas_call(
        goal_kernel,
        out_shape=(hbm((devices * 8, 128), F32), hbm((devices * 8, 128), F32), hbm((devices * 4, 128), F32)),
        in_specs=[vmem()] * 4,
        out_specs=(vmem(), vmem(), vmem()),
        scratch_shapes=[pltpu.VMEM((128, 128), F32)],
        compiler_params=params(8),
        cost_estimate=pl.CostEstimate(flops=50_000_000, bytes_accessed=2_000_000, transcendentals=0),
        name="goals",
    )(want, served, box_centers, jnp.asarray(node_rows()))
    near_cen, far_gap, ex_cen = [x.reshape(-1, 8, 128) for x in (near_cen, far_gap, ex_cen)]
    group = 8
    far_value = pl.pallas_call(
        far_kernel,
        grid=(devices // group,),
        out_shape=hbm((devices, 256, 128), BF),
        in_specs=[vmem((group, 8, 128), lambda i: (i, 0, 0)), vmem()],
        out_specs=vmem((group, 256, 128), lambda i: (i, 0, 0)),
        compiler_params=params(8),
        cost_estimate=pl.CostEstimate(flops=200_000_000, bytes_accessed=9_000_000, transcendentals=4_000_000),
        name="far_values",
    )(far_gap, jnp.asarray(far_sources(), BF))

    big = lambda dtype, rows: pltpu.VMEM((rows, 128), dtype)
    near, far, term = pl.pallas_call(
        duo_kernel,
        out_shape=(hbm((boxes, 8, 128), F32), hbm((boxes, 8, 128), F32), struct((devices, 128), F32)),
        in_specs=[vmem()] + [anywhere] * 8,
        out_specs=(anywhere, anywhere, vmem()),
        scratch_shapes=[
            pltpu.SMEM((devices, 128), jnp.int32),
            pltpu.VMEM((devices, 8, 128), F32),
            pltpu.VMEM((devices // 2, 8, 128), F32),
            pltpu.VMEM((boxes, 2, 32, 128), BF),
            pltpu.VMEM((boxes, 8, 128), F32),
            pltpu.VMEM((boxes, 8, 128), F32),
            pltpu.VMEM((boxes, 8, 128), F32),
            pltpu.VMEM((devices, 256, 128), BF),
            pltpu.VMEM((boxes, 8, 128), F32),
            pltpu.VMEM((boxes, 8, 128), F32),
            pltpu.SemaphoreType.DMA((20,)),
        ]
        + [big(BF, 128)] * 2
        + [big(F32, 128)] * 10
        + [big(BF, 256)] * 10
        + [pltpu.VMEM((boxes, 8, 128), F32)] * 4,
        compiler_params=params(28),
        cost_estimate=pl.CostEstimate(flops=1_000_000_000, bytes_accessed=12_000_000, transcendentals=20_000_000),
        name="pairs",
    )(got, *[stay(x) for x in (want, near_cen, ex_cen, f_tab, base, q_tab, far_tab, far_value)])

    terms = exchange(term.reshape(devices, 1, 128))[:, 0, :8]
    curvature = jnp.sum(terms, axis=0) / (devices * boxes * slots)
    product = pl.pallas_call(
        finish_kernel,
        out_shape=table,
        in_specs=[SMEM] + [vmem()] * 3,
        out_specs=vmem(),
        compiler_params=params(8),
        cost_estimate=pl.CostEstimate(flops=50_000_000, bytes_accessed=3_000_000, transcendentals=0),
        name="finish",
    )(counts, stay(near), stay(far), stay(cheb))
    over = jnp.any((served.reshape(devices, 2, 128)[:, 0, 9] > HALF) & (jnp.arange(devices) % 4 != 0))
    whole = (local_pos, charges, counts, box_centers, far_list, near_list)
    return lax.cond(over, lambda: general(*whole), lambda: (product, curvature))


def solution(mesh):
    in_specs = (
        P(AXES, None, None),
        P(AXES, None, None),
        P(AXES),
        P(None, AXES),
        P(AXES, None),
        P(AXES, None),
    )
    out_specs = (P(AXES, None, None), P())
    return jax.shard_map(on_device, mesh=mesh, in_specs=in_specs, out_specs=out_specs, check_vma=False)
```

```python
import functools
import math

import jax
import jax.numpy as jnp
import numpy as np
from jax import lax
from jax.experimental import pallas as pl
from jax.experimental.pallas import tpu as pltpu
from jax.sharding import PartitionSpec as P

AXES = ("gx", "gy")
NODES = 4
ROOT3 = 1.7320508075688772
LOG2E = 1.4426950408889634
BF = jnp.bfloat16
F32 = jnp.float32
NODE = [math.cos((2 * i + 1) * math.pi / 8) for i in range(NODES)]
NT = (((1,), (1,)), ((), ()))
TN = (((0,), (0,)), ((), ()))


def iota(shape, dim):
    return lax.broadcasted_iota(jnp.int32, shape, dim)


def dot(a, b, dims=None):
    if dims is None:
        return jnp.dot(a, b, preferred_element_type=F32)
    return lax.dot_general(a, b, dims, preferred_element_type=F32)


def split(x):
    high = x.astype(BF)
    return high, (x - high.astype(F32)).astype(BF)


def planes(rel, source):
    axis = rel.ndim - 2
    sub = iota(rel.shape, axis) % 4
    last = sub == 3
    rel = jnp.where(last, 0.0, rel)
    high = rel.astype(BF).astype(F32)
    low = (rel - high).astype(BF).astype(F32)
    square = high * (high + 2.0 * low)
    norm = pltpu.roll(square, 1, axis) + pltpu.roll(square, 2, axis) + pltpu.roll(square, 3, axis)
    one = norm.astype(BF).astype(F32)
    rest = norm - one
    two = rest.astype(BF).astype(F32)
    three = (rest - two).astype(BF).astype(F32)
    if source:
        parts = [
            jnp.where(last, one, high),
            jnp.where(last, two, high),
            jnp.where(last, 1.0, low),
            jnp.where(last, three, jnp.where(sub < 2, 1.0, 0.0)),
        ]
    else:
        parts = [
            jnp.where(last, 1.0, -2.0 * high),
            jnp.where(last, 1.0, -2.0 * low),
            jnp.where(last, one, -2.0 * high),
            jnp.where(
                sub == 0,
                pltpu.roll(two, 5, axis),
                jnp.where(sub == 1, pltpu.roll(three, 6, axis), jnp.where(last, 1.0, 0.0)),
            ),
        ]
    return parts


def matern(dist2):
    safe = jnp.maximum(dist2, 1e-12)
    scaled = safe * lax.rsqrt(safe)
    decay = jnp.exp2(scaled * (-LOG2E))
    return decay + scaled * decay


def stack_kernel(value):
    high, low = split(value)
    return jnp.concatenate([high, low], axis=0)


def fold(x):
    return x[0:8] + x[8:16]


def ids_kernel(far_ref, near_ref, want_ref):
    boxes = far_ref.shape[0]
    slots = far_ref.shape[1]
    total = boxes * slots
    lane = iota((total, 128), 1)
    box = iota((total, 128), 0) % boxes
    tri = (iota((total, total), 0) > iota((total, total), 1)).astype(F32).astype(BF)
    result = jnp.zeros((128, 128), F32)
    for ref, first, base in ((near_ref, 1, 0), (far_ref, 0, 4)):
        flat = jnp.concatenate([ref[:, first + j : first + j + 1] for j in range(slots)], axis=0)
        flat = jnp.broadcast_to(flat, (total, 128))
        hit = (flat // boxes) == lane
        onehot = hit.astype(F32).astype(BF)
        before = dot(tri, onehot)
        rank = jnp.sum(jnp.where(hit, before, 0.0), axis=1, keepdims=True).astype(jnp.int32)
        mine = rank == (lane % 4)
        within = jnp.where((lane >= base) & (lane < base + 4), flat % boxes, 0)
        owner = jnp.where((lane >= base + 16) & (lane < base + 20), box, 0)
        value = jnp.where(mine, within + owner, 0).astype(F32).astype(BF)
        result = result + dot(onehot, value, TN)
    want_ref[...] = result.astype(jnp.int32)


def table_kernel(pos_ref, charge_ref, count_ref, cen_ref, q_ref, w_ref, p_ref, f_ref, base_ref, t_ref):
    step = pl.program_id(0)
    group = pos_ref.shape[0]
    sub = iota((8, 128), 0)
    lane = iota((8, 128), 1)

    def body(b, carry):
        box = step * group + b
        live = lane < count_ref[box]
        q = jnp.where(live, charge_ref[b], 0.0)
        q_ref[b] = q
        pos = pos_ref[b]
        zero1 = jnp.zeros((1, 128), F32)
        x4 = jnp.concatenate([pos, zero1], axis=0)
        x = jnp.concatenate([x4, x4], axis=0)
        second = 2.0 * x * x - 1.0
        third = 2.0 * x * second - x
        basis = []
        for i in range(NODES):
            theta = (2 * i + 1) * math.pi / 8
            basis.append(0.25 + 0.5 * (math.cos(theta) * x + math.cos(2 * theta) * second + math.cos(3 * theta) * third))
        row = lambda i, d: jnp.broadcast_to(basis[i][d : d + 1], (8, 128))
        sub4 = sub % 4
        zs = jnp.where(sub4 == 0, row(0, 2), jnp.where(sub4 == 1, row(1, 2), jnp.where(sub4 == 2, row(2, 2), row(3, 2))))
        ys = [jnp.where(sub < 4, row(0, 1), row(1, 1)) * zs, jnp.where(sub < 4, row(2, 1), row(3, 1)) * zs]
        table = jnp.concatenate([row(i, 0) * ys[j] for i in range(NODES) for j in range(2)], axis=0)
        both = stack_kernel(table)
        t_ref[b] = both
        qs = jnp.concatenate(split(q), axis=0)
        weight = fold(dot(qs, both, NT))
        w_ref[b] = weight + pltpu.roll(weight, 64, 1)
        cx, cy, cz = cen_ref[0, box], cen_ref[1, box], cen_ref[2, box]
        lane4 = lane % 4
        far = jnp.where(lane4 == 0, cx, jnp.where(lane4 == 1, cy, cz))
        center = jnp.where(sub4 == 0, cx, jnp.where(sub4 == 1, cy, cz))
        p_ref[b] = jnp.where(sub4 == 3, far, center + 0.5 * x)
        rel = (0.5 * ROOT3) * x
        tgt = planes(rel, False)
        for unit in range(2):
            f_ref[b, unit] = jnp.concatenate([jnp.where(sub // 4 == unit, part, 0.0) for part in tgt], axis=0).astype(BF)
        src = jnp.concatenate(planes(rel, True) + [jnp.zeros((96, 128), F32)], axis=0).T.astype(BF)
        dist2 = dot(src[:, :32], f_ref[b, 0])
        value = stack_kernel(matern(dist2))
        near = fold(dot(jnp.concatenate([qs, qs], axis=1), value))
        base_ref[b] = near + q
        return carry

    lax.fori_loop(0, group, body, 0, unroll=4)


def gather_kernel(ids_ref, q_ref, w_ref, p_ref, out_ref):
    step = pl.program_id(0)
    group = out_ref.shape[0]
    sub4 = iota((8, 128), 0) % 4
    top = iota((8, 128), 0) < 4
    lane = iota((8, 128), 1)
    left = lane < 64

    def body(k, carry):
        peer = step * group + k
        near = [ids_ref[peer, j] for j in range(4)]
        far = [ids_ref[peer, 4 + j] for j in range(4)]
        for j in range(4):
            out_ref[k, 8 * j : 8 * j + 8] = q_ref[near[j]]
        w = [w_ref[far[j]] for j in range(4)]
        out_ref[k, 32:40] = jnp.where(left, w[0], w[2])
        out_ref[k, 40:48] = jnp.where(left, w[1], w[3])
        c = [p_ref[far[j]] for j in range(4)]
        centers = jnp.where(
            left, jnp.where(lane < 4, c[0], c[2]), jnp.where(lane < 68, c[1], c[3])
        )
        s = [p_ref[near[j]] for j in range(4)]
        out_ref[k, 48:56] = jnp.where(sub4 == 3, centers, jnp.where(top, s[0], s[1]))
        out_ref[k, 56:64] = jnp.where(sub4 == 3, centers, jnp.where(top, s[2], s[3]))
        return carry

    lax.fori_loop(0, group, body, 0, unroll=4)


def pair_kernel(
    tgt_ref, count_ref, got_ref, nc_ref, fc_ref, f_ref, fn_ref, base_ref, q_ref, t_ref, out_ref, term_ref, near_acc, far_acc
):
    step = pl.program_id(0)
    steps = pl.num_programs(0)
    group = got_ref.shape[0]
    boxes = f_ref.shape[0]
    sub = iota((8, 128), 0)
    lane = iota((8, 128), 1)
    left = lane < 64

    @pl.when(step == 0)
    def _():
        near_acc[...] = base_ref[...]
        far_acc[...] = jnp.zeros_like(far_acc)

    spread = (iota((128, 128), 0) // 64 == iota((128, 128), 1) // 64).astype(F32).astype(BF)

    def body(k, carry):
        peer = step * group + k
        tn = [tgt_ref[peer, j] for j in range(4)]
        tf = [tgt_ref[peer, 4 + j] for j in range(4)]
        points = [got_ref[k, 48:56], got_ref[k, 56:64]]
        feats = []
        for v in range(2):
            feats += planes((points[v] - nc_ref[k, 8 * v : 8 * v + 8]) * ROOT3, True)
        src = jnp.concatenate(feats + [jnp.zeros((64, 128), F32)], axis=0).T.astype(BF)
        for j in range(4):
            dist2 = dot(src[:, 32 * (j // 2) : 32 * (j // 2) + 32], f_ref[tn[j], j % 2])
            value = stack_kernel(matern(dist2))
            qs = jnp.concatenate(split(got_ref[k, 8 * j : 8 * j + 8]), axis=0)
            near_acc[tn[j]] += fold(dot(jnp.concatenate([qs, qs], axis=1), value))
        row = jnp.broadcast_to(points[0][3:4], (8, 128))
        row = jnp.where(lane % 64 == sub, row, 0.0)
        high = row.astype(BF)
        rest = row - high.astype(F32)
        mid = rest.astype(BF)
        low = (rest - mid.astype(F32)).astype(BF)
        cen = dot(jnp.concatenate([high, mid, low], axis=0), spread)
        rel = (fc_ref[k] - (cen[0:8] + cen[8:16] + cen[16:24])) * ROOT3
        tgt = jnp.concatenate(planes(rel, False), axis=0).astype(BF)
        value = stack_kernel(matern(dot(fn_ref[...], tgt)))
        ws = []
        for h in range(2):
            w = got_ref[k, 32 + 8 * h : 40 + 8 * h]
            for part in (jnp.where(left, w, 0.0), jnp.where(left, 0.0, w)):
                ws += list(split(part))
        ws = jnp.concatenate(ws, axis=0)
        locs = dot(jnp.concatenate([ws, ws], axis=1), value)
        for h in range(2):
            for u in range(2):
                at = 32 * h + 16 * u
                new = fold(locs[at : at + 16])
                far_acc[tf[2 * u + h]] += jnp.where(left if h == 0 else jnp.logical_not(left), new, 0.0)
        return carry

    lax.fori_loop(0, group, body, 0, unroll=2)

    @pl.when(step == steps - 1)
    def _():
        def finish(b, total):
            ls = jnp.concatenate(split(far_acc[b]), axis=0)
            both = t_ref[b]
            high, low = both[0:64], both[64:128]
            table = jnp.concatenate([high, high, low, low], axis=0)
            far = fold(dot(jnp.concatenate([ls, ls], axis=1), table))
            live = lane < count_ref[b]
            product = jnp.where(live, near_acc[b] + far, 0.0)
            out_ref[b] = product
            return total + product * q_ref[b]

        total = lax.fori_loop(0, boxes, finish, jnp.zeros((8, 128), F32), unroll=4)
        ones = jnp.ones((128, 128), F32)
        sums = lax.dot_general(ones, total, NT, precision=lax.Precision.HIGHEST, preferred_element_type=F32)
        term_ref[...] = jnp.concatenate([sums, jnp.zeros((128, 120), F32)], axis=1)


def far_sources():
    x = np.zeros((8, 128), np.float32)
    for n in range(64):
        for d, value in enumerate((NODE[n // 16], NODE[n // 4 % 4], NODE[n % 4])):
            for u in range(2):
                x[4 * u + d, 64 * u + n] = 0.5 * ROOT3 * value
    bf = lambda a: a.astype(jnp.bfloat16).astype(np.float32)
    high = bf(x)
    low = bf(x - high)
    norm = np.zeros_like(x)
    square = high * (high + 2 * low)
    for u in range(2):
        norm[4 * u + 3] = square[4 * u] + square[4 * u + 1] + square[4 * u + 2]
    one = bf(norm)
    two = bf(norm - one)
    three = bf(norm - one - two)
    sub = np.arange(8)[:, None] % 4
    unit = (np.arange(8)[:, None] // 4) == (np.arange(128)[None, :] // 64)
    parts = [
        np.where(sub == 3, one, high),
        np.where(sub == 3, two, high),
        np.where(sub == 3, 1.0, low),
        np.where(sub == 3, three, np.where(sub < 2, 1.0, 0.0)),
    ]
    return np.concatenate([np.where(unit, part, 0.0) for part in parts], axis=0).T.astype(np.float32)


def node_rows():
    out = np.zeros((8, 128), np.float32)
    for m in range(128):
        n = m % 64
        for u in range(2):
            for d, value in enumerate((NODE[n // 16], NODE[n // 4 % 4], NODE[n % 4])):
                out[4 * u + d, m] = 0.5 * value
    return out


def vmem(shape=None, index=None):
    if shape is None:
        return pl.BlockSpec(memory_space=pltpu.VMEM)
    return pl.BlockSpec(shape, index, memory_space=pltpu.VMEM)


SMEM = pl.BlockSpec(memory_space=pltpu.SMEM)


def params(mebibytes=56):
    return pltpu.CompilerParams(vmem_limit_bytes=mebibytes * 1024 * 1024)


def exchange(x):
    return lax.all_to_all(x, AXES, split_axis=0, concat_axis=0, tiled=True)


def general(local_pos, charges, counts, box_centers, far_list, near_list):
    devices = lax.axis_size("gx") * lax.axis_size("gy")
    boxes, _, slots = local_pos.shape
    struct = jax.ShapeDtypeStruct
    want = pl.pallas_call(
        ids_kernel,
        out_shape=struct((devices, 128), jnp.int32),
        in_specs=[vmem(), vmem()],
        out_specs=vmem(),
        compiler_params=params(),
        name="ids",
    )(far_list, near_list)
    served = exchange(want.reshape(devices, 1, 128)).reshape(devices, 128)

    group = 16
    lead = lambda shape: vmem((group,) + shape, lambda i: (i,) + (0,) * len(shape))
    q_tab, w_tab, p_tab, f_tab, base, table = pl.pallas_call(
        table_kernel,
        grid=(boxes // group,),
        out_shape=(
            struct((boxes, 8, 128), F32),
            struct((boxes, 8, 128), F32),
            struct((boxes, 8, 128), F32),
            struct((boxes, 2, 32, 128), BF),
            struct((boxes, 8, 128), F32),
            struct((boxes, 128, 128), BF),
        ),
        in_specs=[lead((3, 128)), lead((8, 128)), SMEM, SMEM],
        out_specs=(lead((8, 128)), lead((8, 128)), lead((8, 128)), lead((2, 32, 128)), lead((8, 128)), lead((128, 128))),
        compiler_params=params(),
        cost_estimate=pl.CostEstimate(flops=200_000_000, bytes_accessed=6_000_000, transcendentals=2_000_000),
        name="tables",
    )(local_pos, charges, counts, box_centers)

    send = pl.pallas_call(
        gather_kernel,
        grid=(devices // group,),
        out_shape=struct((devices, 64, 128), F32),
        in_specs=[SMEM, vmem(), vmem(), vmem()],
        out_specs=lead((64, 128)),
        compiler_params=params(),
        name="gather",
    )(served, q_tab, w_tab, p_tab)
    got = exchange(send)

    tgt = want[:, 16:24]
    centers = box_centers.T
    near_cen = jnp.pad(centers[tgt[:, :4]], ((0, 0), (0, 0), (0, 1))).reshape(devices, 16, 1)
    near_cen = jnp.broadcast_to(near_cen, (devices, 16, 128))
    far_cen = jnp.pad(centers[tgt[:, 4:]], ((0, 0), (0, 0), (0, 1))).reshape(devices, 2, 2, 4)
    far_cen = far_cen.transpose(0, 1, 3, 2).reshape(devices, 8, 2, 1)
    far_cen = jnp.broadcast_to(far_cen, (devices, 8, 2, 64)).reshape(devices, 8, 128) + node_rows()[None]

    product, term = pl.pallas_call(
        pair_kernel,
        grid=(devices // group,),
        out_shape=(struct((boxes, 8, 128), F32), struct((devices, 128), F32)),
        in_specs=[
            SMEM,
            SMEM,
            lead((64, 128)),
            lead((16, 128)),
            lead((8, 128)),
            vmem(),
            vmem(),
            vmem(),
            vmem(),
            vmem(),
        ],
        out_specs=(vmem(), vmem()),
        scratch_shapes=[pltpu.VMEM((boxes, 8, 128), F32), pltpu.VMEM((boxes, 8, 128), F32)],
        compiler_params=params(),
        cost_estimate=pl.CostEstimate(flops=1_000_000_000, bytes_accessed=12_000_000, transcendentals=20_000_000),
        name="pairs",
    )(tgt, counts, got, near_cen, far_cen, f_tab, jnp.asarray(far_sources(), BF), base, q_tab, table)

    terms = exchange(term.reshape(devices, 1, 128))[:, 0, :8]
    curvature = jnp.sum(terms, axis=0) / (devices * boxes * slots)
    return (product, curvature)


HALF = 64
ROWS = 44
NEAR_ROWS = 24
UNROLL = 4
CHUNKS = 16
AHEAD = 4


def upper_kernel(pos_ref, charge_ref, count_ref, row_ref, ex_ref):
    half = charge_ref.shape[0] // 2
    lane = iota((8, 128), 1)
    left = lane < HALF
    center = jnp.concatenate([row_ref[...], jnp.zeros((5, 2 * half), F32)], axis=0)
    center = jnp.concatenate([center, jnp.zeros((8, 128 - 2 * half), F32)], axis=1)
    center = jnp.concatenate([center, jnp.zeros((120, 128), F32)], axis=0).T
    wide = iota((half, 128), 1) < HALF
    for d in range(3):
        first = center[:half, d : d + 1] + 0.5 * pos_ref[d, :half]
        second = center[half : 2 * half, d : d + 1] + 0.5 * pos_ref[d, half:]
        ex_ref[(8 + d) * half : (9 + d) * half, :] = jnp.where(wide, pltpu.roll(first, HALF, 1), second)

    def body(b, carry):
        first = pltpu.roll(jnp.where(lane < count_ref[b], charge_ref[b], 0.0), HALF, 1)
        second = jnp.where(lane < count_ref[b + half], charge_ref[b + half], 0.0)
        ex_ref[pl.ds(pl.multiple_of(8 * b, 8), 8), :] = jnp.where(left, first, second)
        return carry

    lax.fori_loop(0, half, body, 0, unroll=16)


def start_kernel(far_ref, near_ref, most_ref, row_ref, msg_ref, want_ref):
    boxes = far_ref.shape[1]
    slots = far_ref.shape[0]
    peer = iota((128, 128), 0)
    line = iota((128, 128), 1)
    tri = (peer < line).astype(F32).astype(BF)
    full = jnp.ones((128, 128), BF)
    row32 = iota((32, 128), 0)
    kind = row32 // 4
    boxrow = iota((32, 128), 1) % boxes
    result = jnp.zeros((128, 32), F32)
    for ref, first, group in ((near_ref, 1, 0), (far_ref, 0, 1)):
        seen = jnp.zeros((128, 128), F32)
        for j in range(0, slots, 2):
            flat = jnp.concatenate([ref[first + j : first + j + 1, :], ref[first + j + 1 : first + j + 2, :]], axis=1)
            hit = jnp.broadcast_to(flat // boxes, (128, 128)) == peer
            onehot = hit.astype(F32).astype(BF)
            before = dot(onehot, tri) + seen
            rank = jnp.sum(jnp.where(hit, before, 0.0), axis=0, keepdims=True).astype(jnp.int32)
            if j + 2 < slots:
                seen = seen + dot(onehot, full)
            within = jnp.broadcast_to(flat % boxes, (32, 128))
            if group == 0:
                value = jnp.where(kind == 0, within * NEAR_ROWS, jnp.where(kind == 2, within * 8, 0))
            else:
                value = jnp.where(kind == 1, within * 8, 0)
            value = jnp.where(kind == 4 + group, boxrow, value)
            value = jnp.where(row32 % 4 == jnp.broadcast_to(rank, (32, 128)), value, 0).astype(F32).astype(BF)
            result = result + dot(onehot, value, NT)
    result = jnp.concatenate([result, jnp.zeros((128, 96), F32)], axis=1)
    heavy = (line == peer - peer % 4).astype(F32).astype(BF)
    first = dot(heavy, result.astype(BF))
    for at, base in ((8, 8), (24, 16)):
        extra = dot(jnp.where(line == base + peer % 4, first, 0.0).astype(BF), full)
        result = jnp.where(line == at, extra, result)
    most = jnp.max(most_ref[...], axis=1, keepdims=True).astype(F32)
    result = jnp.where(line == 9, jnp.broadcast_to(most, (128, 128)), result)
    want_ref[...] = result.astype(jnp.int32)
    rows = [jnp.concatenate([row_ref[d : d + 1, :]] * 2, axis=1) for d in range(3)]
    rows = [jnp.broadcast_to(row, (128, 128)) for row in rows]
    msg_ref[pl.ds(0, 128, stride=2), :] = jnp.where(line < HALF, result, rows[2])
    msg_ref[pl.ds(1, 128, stride=2), :] = jnp.where(line < HALF, rows[0], rows[1])


def cheb_rows(x):
    sub = iota((8, 128), 0)
    second = 2.0 * x * x - 1.0
    third = 2.0 * x * second - x
    basis = []
    for i in range(NODES):
        theta = (2 * i + 1) * math.pi / 8
        basis.append(0.25 + 0.5 * (math.cos(theta) * x + math.cos(2 * theta) * second + math.cos(3 * theta) * third))
    row = lambda i, d: jnp.broadcast_to(basis[i][d : d + 1], (8, 128))
    sub4 = sub % 4
    zs = jnp.where(sub4 == 0, row(0, 2), jnp.where(sub4 == 1, row(1, 2), jnp.where(sub4 == 2, row(2, 2), row(3, 2))))
    ys = [jnp.where(sub < 4, row(0, 1), row(1, 1)) * zs, jnp.where(sub < 4, row(2, 1), row(3, 1)) * zs]
    return jnp.concatenate([row(i, 0) * ys[j] for i in range(NODES) for j in range(2)], axis=0)


def point_rows(pos_ref, b):
    sub4 = iota((8, 128), 0) % 4
    x = jnp.zeros((8, 128), F32)
    for d in range(3):
        x = jnp.where(sub4 == d, jnp.broadcast_to(pos_ref[d, pl.ds(b, 1), :], (8, 128)), x)
    return x


def doubled(x):
    return jnp.where(iota((8, 128), 1) < HALF, x, pltpu.roll(x, HALF, 1))


def send_table_kernel(pos_ref, charge_ref, count_ref, cen_ref, near_ref, far_ref, basis_ref):
    boxes = charge_ref.shape[0]
    lane = iota((8, 128), 1)
    sub = iota((8, 128), 0)
    for d in range(3):
        x = pos_ref[d]
        second = 2.0 * x * x - 1.0
        third = 2.0 * x * second - x
        for i in range(NODES):
            theta = (2 * i + 1) * math.pi / 8
            value = math.cos(theta) * x + math.cos(2 * theta) * second + math.cos(3 * theta) * third
            basis_ref[4 * d + i] = 0.25 + 0.5 * value

    def body(b, carry):
        q = jnp.where(lane < count_ref[b], charge_ref[b], 0.0)
        near_ref[b, 0:8] = doubled(q)
        x, y, z = [doubled(cen_ref[d, b] + 0.5 * jnp.broadcast_to(pos_ref[d, pl.ds(b, 1), :], (8, 128))) for d in range(3)]
        near_ref[b, 8:16] = jnp.where(sub == 4, x, jnp.where(sub == 5, y, z))
        near_ref[b, 16:24] = jnp.where(sub == 7, x, jnp.where((sub == 3) | (sub == 5), y, z))
        row = lambda i, d: jnp.broadcast_to(basis_ref[4 * d + i, pl.ds(b, 1), :], (8, 128))
        sub4 = sub % 4
        zs = jnp.where(sub4 == 0, row(0, 2), jnp.where(sub4 == 1, row(1, 2), jnp.where(sub4 == 2, row(2, 2), row(3, 2))))
        ys = [jnp.where(sub < 4, row(0, 1), row(1, 1)) * zs, jnp.where(sub < 4, row(2, 1), row(3, 1)) * zs]
        table = jnp.concatenate([row(i, 0) * ys[j] for i in range(NODES) for j in range(2)], axis=0)
        qs = jnp.concatenate(split(q), axis=0)
        weight = fold(dot(qs, stack_kernel(table), NT))
        far_ref[b] = weight + pltpu.roll(weight, 64, 1)
        return carry

    lax.fori_loop(0, boxes, body, 0, unroll=32)


def own_table_kernel(pos_ref, charge_ref, count_ref, q_ref, f_ref, base_ref, t_ref):
    boxes = charge_ref.shape[0]
    sub = iota((8, 128), 0)
    lane = iota((8, 128), 1)

    def body(b, carry):
        q = jnp.where(lane < count_ref[b], charge_ref[b], 0.0)
        q_ref[b] = q
        x = point_rows(pos_ref, b)
        t_ref[b] = stack_kernel(cheb_rows(x))
        rel = (0.5 * ROOT3) * x
        tgt = planes(rel, False)
        for unit in range(2):
            f_ref[b, unit] = jnp.concatenate([jnp.where(sub // 4 == unit, part, 0.0) for part in tgt], axis=0).astype(BF)
        zero = jnp.zeros((96, 128), F32)
        src = jnp.concatenate(planes(rel, True) + [zero], axis=0).T.astype(BF)
        first = jnp.concatenate([jnp.where(sub < 4, part, 0.0) for part in tgt] + [zero], axis=0).astype(BF)
        value = stack_kernel(matern(dot(src, first)))
        qs = jnp.concatenate(split(q), axis=0)
        base_ref[b] = fold(dot(jnp.concatenate([qs, qs], axis=1), value)) + q
        return carry

    lax.fori_loop(0, boxes, body, 0, unroll=4)


def goal_kernel(want_ref, served_ref, cen_ref, node_ref, nc_ref, fc_ref, ec_ref, goal_ref, odd_ref):
    lane = iota((128, 128), 1)
    left = lane < HALF
    boxes = cen_ref.shape[1]
    cen = jnp.concatenate([cen_ref[...], jnp.zeros((5, boxes), F32)], axis=0)
    cen = jnp.concatenate([cen, jnp.zeros((8, 128 - boxes), F32)], axis=1)
    cen = jnp.concatenate([cen, jnp.zeros((120, 128), F32)], axis=0).T

    def split3(x, axis):
        high = x.astype(BF)
        rest = x - high.astype(F32)
        mid = rest.astype(BF)
        return jnp.concatenate([high, mid, (rest - mid.astype(F32)).astype(BF)], axis=axis)

    parts = split3(cen, 0)
    want = want_ref[...]
    goal_ref[...] = want.astype(F32).T[16:32].astype(jnp.int32)
    sources = [served_ref[pl.ds(1, 128, stride=2), :], served_ref[pl.ds(0, 128, stride=2), :]]
    halves = [jnp.concatenate([(iota((128, 128), 0) // HALF == h).astype(F32).astype(BF)] * 3, axis=0) for h in range(2)]

    def column(at):
        return jnp.broadcast_to(want[:, at : at + 1], (128, 128))

    def centers(at):
        onehot = (column(at) == lane).astype(F32).astype(BF)
        found = dot(jnp.concatenate([onehot] * 3, axis=1), parts)
        return [jnp.broadcast_to(found[:, d : d + 1], (128, 128)) for d in range(3)]

    def gaps(j):
        mine = lane % HALF == column(4 + j) // 8
        both = [split3(jnp.where(mine, source, 0.0), 1) for source in sources]
        theirs = [dot(both[0], halves[0]), dot(both[0], halves[1]), dot(both[1], halves[1])]
        return [a - b for a, b in zip(centers(20 + j), theirs)]

    nc_ref[...] = jnp.zeros_like(nc_ref)
    fc_ref[...] = jnp.zeros_like(fc_ref)
    ec_ref[...] = jnp.zeros_like(ec_ref)
    for u in range(2):
        first, second = centers(16 + 2 * u), centers(17 + 2 * u)
        for d in range(3):
            nc_ref[pl.ds(4 * u + d, 128, stride=8), :] = jnp.where(left, first[d], second[d])
        first, second = gaps(2 * u), gaps(2 * u + 1)
        for d in range(3):
            fc_ref[pl.ds(4 * u + d, 128, stride=8), :] = jnp.where(left, first[d], second[d]) + node_ref[d : d + 1, :]
    extra = centers(24)
    for d in range(3):
        odd_ref[...] = extra[d]
        even, odd = odd_ref[pl.ds(0, 64, stride=2), :], odd_ref[pl.ds(1, 64, stride=2), :]
        ec_ref[pl.ds(d, 64, stride=8), :] = jnp.where(left[:64], even, odd)


def far_kernel(fc_ref, fn_ref, out_ref):
    group = fc_ref.shape[0]
    tgt = jnp.concatenate(planes(fc_ref[...] * ROOT3, False), axis=1).astype(BF)
    for k in range(group):
        out_ref[k] = stack_kernel(matern(dot(fn_ref[...], tgt[k])))


def send_kernel(member_ref, served_ref, near_ref, far_ref, own_ref, *refs):
    moved, (out_ref, ids_ref, int_ref, ex_ref, buf_ref, sems) = refs[:3], refs[3:]
    peers = ids_ref.shape[1]
    sub = iota((8, 128), 0)
    lane = iota((8, 128), 1)
    left = lane < HALF
    keep = left | (sub < 3)
    second = sub < 5
    int_ref[...] = served_ref[pl.ds(0, peers, stride=2), :].T[:16].astype(jnp.int32)
    copy = pltpu.make_async_copy(int_ref, ids_ref, sems.at[0])
    copy.start()
    half = ex_ref.shape[0] // 16
    packed = moved[0][...] + moved[1][...] + moved[2][...]
    packed = jnp.where(member_ref[0] == 0, own_ref[...], packed)
    for d in range(3):
        rows = packed[(8 + d) * half : (9 + d) * half]
        ex_ref[pl.ds(d, half, stride=8), :] = pltpu.roll(rows, HALF, 1)
        ex_ref[pl.ds(8 * half + d, half, stride=8), :] = rows
    for b in range(half):
        tile = packed[8 * b : 8 * b + 8]
        for at, part in ((8 * b, tile), (8 * (b + half), pltpu.roll(tile, HALF, 1))):
            ex_ref[at : at + 8, :] = jnp.where(left, part, jnp.where(sub < 3, ex_ref[at : at + 8, :], 0.0))
    copy.wait()

    def body(i, carry):
        base = pl.multiple_of(i * 2 * ROWS, 8)
        for k in range(2):
            peer = 2 * i + k
            at = lambda row: pl.ds(base + (k * ROWS + row), 8)
            rows = lambda ref, j, row: ref[pl.ds(pl.multiple_of(ids_ref[j, peer], 8) + row, 8), :]
            q = [rows(near_ref, j, 0) for j in range(4)]
            w = [rows(far_ref, 4 + j, 0) for j in range(4)]
            p = [rows(near_ref, j, 16 if j < 2 else 8) for j in range(4)]
            buf_ref[at(0), :] = jnp.where(left, q[0], q[1])
            buf_ref[at(8), :] = jnp.where(left, q[2], q[3])
            buf_ref[at(16), :] = jnp.where(left, w[0], w[2])
            buf_ref[at(24), :] = jnp.where(left, w[1], w[3])
            buf_ref[at(36), :] = jnp.where(sub == 7, jnp.where(left, p[0], p[1]), jnp.where(left, p[2], p[3]))
            buf_ref[at(32), :] = jnp.where(keep, rows(ex_ref, 8, 0), jnp.where(second, p[1], p[0]))
        return carry

    chunks = 4
    each = peers // chunks
    stores = []
    for c in range(chunks):
        lax.fori_loop(c * each // 2, (c + 1) * each // 2, body, 0, unroll=8)
        at = pl.ds(c * each * ROWS, each * ROWS)
        stores.append(pltpu.make_async_copy(buf_ref.at[at], out_ref.at[at], sems.at[1 + c]))
        stores[-1].start()
    for copy in stores:
        copy.wait()


def duo_kernel(
    scale, got_ref, want_hbm, nc_hbm, ec_hbm, f_hbm, base_hbm, q_hbm, w_hbm, v_hbm, near_hbm, far_hbm, term_ref,
    tgt_ref, nc_ref, ec_ref, f_ref, base_ref, q_ref, w_ref, v_ref, near_ref, far_ref, sems, *bufs
):
    whole = [(want_hbm, tgt_ref), (nc_hbm, nc_ref), (ec_hbm, ec_ref), (f_hbm, f_ref)]
    whole += [(base_hbm, base_ref), (q_hbm, q_ref), (w_hbm, w_ref)]
    loads = [pltpu.make_async_copy(source, target, sems.at[i]) for i, (source, target) in enumerate(whole)]
    for copy in loads[:4]:
        copy.start()
    chunk = v_ref.shape[0] // CHUNKS

    def far_values(c):
        at = pl.ds(c * chunk, chunk)
        return pltpu.make_async_copy(v_hbm.at[at], v_ref.at[at], sems.at[16 + c % AHEAD])

    for c in range(AHEAD):
        far_values(c).start()
    xt_refs, dist_refs, value_refs = bufs[:2], (bufs[2:7], bufs[7:12]), (bufs[12:17], bufs[17:22])
    near_accs, far_accs = bufs[22:24], bufs[24:26]
    duos = ec_ref.shape[0]
    boxes = f_ref.shape[0]
    sub = iota((8, 128), 0)
    lane = iota((8, 128), 1)
    left = lane < HALF
    for ref in value_refs[1] + near_accs + far_accs:
        ref[...] = jnp.zeros_like(ref)
    for ref in dist_refs[1]:
        ref[...] = jnp.full(ref.shape, 1e6, F32)
    def tile(duo, a, row):
        return got_ref[pl.ds(pl.multiple_of(duo * 2 * ROWS, 8) + (a * ROWS + row), 8), :]

    def extra(duo):
        return tile(duo, 0, 32), tile(duo, 1, 32)

    def goals(duo):
        pairs = [(tgt_ref[2 * (k % 2), 2 * duo + k // 2], tgt_ref[2 * (k % 2) + 1, 2 * duo + k // 2]) for k in range(4)]
        return pairs + [(tgt_ref[8, 2 * duo], tgt_ref[8, 2 * duo + 1])]

    def halves(x):
        high = x.astype(BF).astype(F32)
        both = [high, x - high]
        return [jnp.where(left, part, 0.0) for part in both] + [jnp.where(left, 0.0, part) for part in both]

    def products(duo, value):
        ex = extra(duo)
        tiles = [tile(duo, k // 2, 8 * (k % 2)) for k in range(4)]
        tiles.append(jnp.where(left, ex[0], pltpu.roll(ex[1], HALF, 1)))
        for k, goal in enumerate(goals(duo)):
            qs = jnp.concatenate(halves(tiles[k]), axis=0).astype(BF)
            new = dot(jnp.concatenate([qs, qs], axis=1), value[k][...])
            for h in range(2):
                near_accs[h][goal[h]] += fold(new[16 * h : 16 * h + 16])

    def far_products(duo):
        for a in range(2):
            ws = []
            for h in range(2):
                ws += halves(tile(duo, a, 16 + 8 * h))
            ws = jnp.concatenate(ws, axis=0).astype(BF)
            new = dot(jnp.concatenate([ws, ws], axis=1), v_ref[2 * duo + a])
            for h in range(2):
                for u in range(2):
                    at = 32 * h + 16 * u
                    far_accs[h][tgt_ref[4 + 2 * u + h, 2 * duo + a]] += fold(new[at : at + 16])

    def values(dist, value):
        for k in range(5):
            value[k][...] = stack_kernel(matern(dist[k][...]))

    def distances(duo, xt, dist):
        for k, goal in enumerate(goals(duo)):
            v, u = k // 2, k % 2
            for half in range(2):
                pieces = [jnp.zeros((32 * v, 128), BF)] if v else []
                pieces += [f_ref[goal[half], u], jnp.zeros((96 - 32 * v, 128), BF)]
                at = slice(64 * half, 64 * half + 64)
                dist[k][at, :] = dot(xt[at, :], jnp.concatenate(pieces, axis=0))

    def features(duo, xt):
        ex = extra(duo)
        turned = [pltpu.roll(x, HALF, 1) for x in ex]
        feats = []
        for a in range(2):
            full = tile(duo, a, 36)
            split_rows = jnp.where(left, pltpu.roll(turned[a], 4, 0), pltpu.roll(ex[a], 6, 0))
            point = jnp.where(sub >= 4, full, jnp.where(sub == 0, pltpu.roll(full, 1, 0), split_rows))
            feats += planes((point - nc_ref[2 * duo + a]) * ROOT3, True)
        point = jnp.where(left, turned[0], ex[1])
        feats += planes((point - ec_ref[duo]) * ROOT3, True)
        feats.append(jnp.zeros((32, 128), F32))
        xt[...] = jnp.concatenate(feats, axis=0).T.astype(BF)

    turns = duos // UNROLL
    assert turns == CHUNKS

    def body(i, carry):
        far_values(i).wait()

        @pl.when(i + AHEAD < CHUNKS)
        def _():
            far_values(i + AHEAD).start()

        for s in range(UNROLL):
            now, was = s % 2, 1 - s % 2
            step = UNROLL * i + s
            products(jnp.maximum(step - 2, 0), value_refs[was])
            far_products(step)
            values(dist_refs[was], value_refs[now])
            distances(step, xt_refs[was], dist_refs[now])
            features(jnp.minimum(step + 1, duos - 1), xt_refs[now])
        return carry

    for copy in loads[:4]:
        copy.wait()
    features(0, xt_refs[1])
    for copy in loads[4:]:
        copy.start()
    lax.fori_loop(0, turns, body, 0)
    products(duos - 2, value_refs[1])
    values(dist_refs[1], value_refs[0])
    products(duos - 1, value_refs[0])

    for copy in loads[4:]:
        copy.wait()

    def finish(b, total):
        near = near_accs[0][b] + near_accs[1][b] + base_ref[b]
        far = jnp.where(left, far_accs[0][b], far_accs[1][b])
        near_ref[b] = near
        far_ref[b] = far
        return total + near * q_ref[b] + far * w_ref[b]

    total = jnp.zeros((8, 128), F32)
    stores = []
    quarter = boxes // 4
    for part in range(4):
        total = lax.fori_loop(part * quarter, part * quarter + quarter, finish, total, unroll=16)
        at = pl.ds(part * quarter, quarter)
        for source, target, sem in ((near_ref, near_hbm, 8 + part), (far_ref, far_hbm, 12 + part)):
            copy = pltpu.make_async_copy(source.at[at], target.at[at], sems.at[sem])
            copy.start()
            stores.append(copy)
    ones = jnp.ones((128, 128), F32)
    sums = lax.dot_general(ones, total, NT, precision=lax.Precision.HIGHEST, preferred_element_type=F32)
    term_ref[...] = jnp.concatenate([sums * scale, jnp.zeros((128, 120), F32)], axis=1)
    for copy in stores:
        copy.wait()


def finish_kernel(count_ref, near_ref, far_ref, t_ref, out_ref):
    boxes = near_ref.shape[0]
    lane = iota((8, 128), 1)

    def body(b, carry):
        ls = jnp.concatenate(split(far_ref[b]), axis=0)
        high, low = t_ref[b, 0:64], t_ref[b, 64:128]
        far = fold(dot(jnp.concatenate([ls, ls], axis=1), jnp.concatenate([high, high, low, low], axis=0)))
        out_ref[b] = jnp.where(lane < count_ref[b], near_ref[b] + far, 0.0)
        return carry

    lax.fori_loop(0, boxes, body, 0, unroll=16)


def on_device(local_pos, charges, counts, box_centers, far_list, near_list):
    devices = lax.axis_size("gx") * lax.axis_size("gy")
    boxes, _, slots = local_pos.shape
    struct = jax.ShapeDtypeStruct
    hbm = pltpu.HBM
    stay = lambda x: pltpu.with_memory_space_constraint(x, pltpu.HBM)
    anywhere = pl.BlockSpec(memory_space=pltpu.HBM)
    pos = jnp.transpose(local_pos, (1, 0, 2))
    table = struct((boxes, 8, 128), F32)
    flat = lambda x: x.reshape(-1, 128)
    member = (lax.axis_index("gy") % 4).astype(jnp.int32).reshape(1)
    ex_own = pl.pallas_call(
        upper_kernel,
        out_shape=struct((boxes * 11 // 2, 128), F32),
        in_specs=[vmem(), vmem(), SMEM, vmem()],
        out_specs=vmem(),
        compiler_params=params(8),
        name="upper_halves",
    )(pos, charges, counts, box_centers)
    msg, want = pl.pallas_call(
        start_kernel,
        out_shape=(struct((devices * 2, 128), F32), struct((devices, 128), jnp.int32)),
        in_specs=[vmem()] * 4,
        out_specs=(vmem(), vmem()),
        compiler_params=params(8),
        name="start",
    )(far_list.T, near_list.T, counts.reshape(1, boxes), box_centers)
    moved = [lax.ppermute(ex_own, "gy", [(4 * z, 4 * z + k) for z in range(4)]) for k in range(1, 4)]
    served = flat(exchange(msg.reshape(devices, 2, 128)))

    near_tab, far_tab = pl.pallas_call(
        send_table_kernel,
        out_shape=(struct((boxes, NEAR_ROWS, 128), F32), table),
        in_specs=[vmem(), vmem(), SMEM, SMEM],
        out_specs=(vmem(), vmem()),
        scratch_shapes=[pltpu.VMEM((12, boxes, 128), F32)],
        compiler_params=params(8),
        cost_estimate=pl.CostEstimate(flops=50_000_000, bytes_accessed=1_200_000, transcendentals=0),
        name="send_tables",
    )(pos, charges, counts, box_centers)

    send = pl.pallas_call(
        send_kernel,
        out_shape=hbm((devices * ROWS, 128), F32),
        in_specs=[SMEM] + [vmem()] * 7,
        out_specs=anywhere,
        scratch_shapes=[
            pltpu.SMEM((16, devices), jnp.int32),
            pltpu.VMEM((16, devices), jnp.int32),
            pltpu.VMEM((boxes * 8, 128), F32),
            pltpu.VMEM((devices * ROWS, 128), F32),
            pltpu.SemaphoreType.DMA((5,)),
        ],
        compiler_params=params(12),
        name="send",
    )(member, served, flat(near_tab), flat(far_tab), ex_own, *moved)
    got = flat(exchange(send.reshape(devices, ROWS // 4, 4, 128)))

    q_tab, f_tab, base, cheb = pl.pallas_call(
        own_table_kernel,
        out_shape=(
            hbm((boxes, 8, 128), F32),
            hbm((boxes, 2, 32, 128), BF),
            hbm((boxes, 8, 128), F32),
            hbm((boxes, 128, 128), BF),
        ),
        in_specs=[vmem(), vmem(), SMEM],
        out_specs=(vmem(), vmem(), vmem(), vmem()),
        compiler_params=params(8),
        cost_estimate=pl.CostEstimate(flops=200_000_000, bytes_accessed=4_000_000, transcendentals=2_000_000),
        name="own_tables",
    )(pos, charges, counts)

    near_cen, far_gap, ex_cen, goals = pl.pallas_call(
        goal_kernel,
        out_shape=(
            hbm((devices * 8, 128), F32),
            hbm((devices * 8, 128), F32),
            hbm((devices * 4, 128), F32),
            hbm((16, devices), jnp.int32),
        ),
        in_specs=[vmem()] * 4,
        out_specs=(vmem(),) * 4,
        scratch_shapes=[pltpu.VMEM((128, 128), F32)],
        compiler_params=params(8),
        cost_estimate=pl.CostEstimate(flops=50_000_000, bytes_accessed=2_000_000, transcendentals=0),
        name="goals",
    )(want, served, box_centers, jnp.asarray(node_rows()))
    near_cen, far_gap, ex_cen = [x.reshape(-1, 8, 128) for x in (near_cen, far_gap, ex_cen)]
    group = 8
    far_value = pl.pallas_call(
        far_kernel,
        grid=(devices // group,),
        out_shape=hbm((devices, 256, 128), BF),
        in_specs=[vmem((group, 8, 128), lambda i: (i, 0, 0)), vmem()],
        out_specs=vmem((group, 256, 128), lambda i: (i, 0, 0)),
        compiler_params=params(8),
        cost_estimate=pl.CostEstimate(flops=200_000_000, bytes_accessed=9_000_000, transcendentals=4_000_000),
        name="far_values",
    )(far_gap, jnp.asarray(far_sources(), BF))

    big = lambda dtype, rows: pltpu.VMEM((rows, 128), dtype)
    near, far, term = pl.pallas_call(
        functools.partial(duo_kernel, 1.0 / (devices * boxes * slots)),
        out_shape=(hbm((boxes, 8, 128), F32), hbm((boxes, 8, 128), F32), struct((devices, 128), F32)),
        in_specs=[vmem()] + [anywhere] * 8,
        out_specs=(anywhere, anywhere, vmem()),
        scratch_shapes=[
            pltpu.SMEM((16, devices), jnp.int32),
            pltpu.VMEM((devices, 8, 128), F32),
            pltpu.VMEM((devices // 2, 8, 128), F32),
            pltpu.VMEM((boxes, 2, 32, 128), BF),
            pltpu.VMEM((boxes, 8, 128), F32),
            pltpu.VMEM((boxes, 8, 128), F32),
            pltpu.VMEM((boxes, 8, 128), F32),
            pltpu.VMEM((devices, 256, 128), BF),
            pltpu.VMEM((boxes, 8, 128), F32),
            pltpu.VMEM((boxes, 8, 128), F32),
            pltpu.SemaphoreType.DMA((20,)),
        ]
        + [big(BF, 128)] * 2
        + [big(F32, 128)] * 10
        + [big(BF, 256)] * 10
        + [pltpu.VMEM((boxes, 8, 128), F32)] * 4,
        compiler_params=params(28),
        cost_estimate=pl.CostEstimate(flops=1_000_000_000, bytes_accessed=12_000_000, transcendentals=20_000_000),
        name="pairs",
    )(got, *[stay(x) for x in (goals, near_cen, ex_cen, f_tab, base, q_tab, far_tab, far_value)])

    terms = exchange(term.reshape(devices, 1, 128))[:, 0, :8]
    curvature = jnp.sum(terms, axis=0)
    product = pl.pallas_call(
        finish_kernel,
        out_shape=table,
        in_specs=[SMEM] + [vmem()] * 3,
        out_specs=vmem(),
        compiler_params=params(8),
        cost_estimate=pl.CostEstimate(flops=50_000_000, bytes_accessed=3_000_000, transcendentals=0),
        name="finish",
    )(counts, stay(near), stay(far), stay(cheb))
    over = jnp.any((served.reshape(devices, 2, 128)[:, 0, 9] > HALF) & (jnp.arange(devices) % 4 != 0))
    whole = (local_pos, charges, counts, box_centers, far_list, near_list)
    return lax.cond(over, lambda: general(*whole), lambda: (product, curvature))


def solution(mesh):
    in_specs = (
        P(AXES, None, None),
        P(AXES, None, None),
        P(AXES),
        P(None, AXES),
        P(AXES, None),
        P(AXES, None),
    )
    out_specs = (P(AXES, None, None), P())
    return jax.shard_map(on_device, mesh=mesh, in_specs=in_specs, out_specs=out_specs, check_vma=False)
```

```python
import functools
import math

import jax
import jax.numpy as jnp
import numpy as np
from jax import lax
from jax.experimental import pallas as pl
from jax.experimental.pallas import tpu as pltpu
from jax.sharding import PartitionSpec as P

AXES = ("gx", "gy")
NODES = 4
ROOT3 = 1.7320508075688772
LOG2E = 1.4426950408889634
BF = jnp.bfloat16
F32 = jnp.float32
NODE = [math.cos((2 * i + 1) * math.pi / 8) for i in range(NODES)]
NT = (((1,), (1,)), ((), ()))
TN = (((0,), (0,)), ((), ()))


def iota(shape, dim):
    return lax.broadcasted_iota(jnp.int32, shape, dim)


def dot(a, b, dims=None):
    if dims is None:
        return jnp.dot(a, b, preferred_element_type=F32)
    return lax.dot_general(a, b, dims, preferred_element_type=F32)


def split(x):
    high = x.astype(BF)
    return high, (x - high.astype(F32)).astype(BF)


def planes(rel, source):
    axis = rel.ndim - 2
    sub = iota(rel.shape, axis) % 4
    last = sub == 3
    rel = jnp.where(last, 0.0, rel)
    high = rel.astype(BF).astype(F32)
    low = (rel - high).astype(BF).astype(F32)
    square = high * (high + 2.0 * low)
    norm = pltpu.roll(square, 1, axis) + pltpu.roll(square, 2, axis) + pltpu.roll(square, 3, axis)
    one = norm.astype(BF).astype(F32)
    rest = norm - one
    two = rest.astype(BF).astype(F32)
    three = (rest - two).astype(BF).astype(F32)
    if source:
        parts = [
            jnp.where(last, one, high),
            jnp.where(last, two, high),
            jnp.where(last, 1.0, low),
            jnp.where(last, three, jnp.where(sub < 2, 1.0, 0.0)),
        ]
    else:
        parts = [
            jnp.where(last, 1.0, -2.0 * high),
            jnp.where(last, 1.0, -2.0 * low),
            jnp.where(last, one, -2.0 * high),
            jnp.where(
                sub == 0,
                pltpu.roll(two, 5, axis),
                jnp.where(sub == 1, pltpu.roll(three, 6, axis), jnp.where(last, 1.0, 0.0)),
            ),
        ]
    return parts


def matern(dist2):
    safe = jnp.maximum(dist2, 1e-12)
    scaled = safe * lax.rsqrt(safe)
    decay = jnp.exp2(scaled * (-LOG2E))
    return decay + scaled * decay


def stack_kernel(value):
    high, low = split(value)
    return jnp.concatenate([high, low], axis=0)


def fold(x):
    return x[0:8] + x[8:16]


def ids_kernel(far_ref, near_ref, want_ref):
    boxes = far_ref.shape[0]
    slots = far_ref.shape[1]
    total = boxes * slots
    lane = iota((total, 128), 1)
    box = iota((total, 128), 0) % boxes
    tri = (iota((total, total), 0) > iota((total, total), 1)).astype(F32).astype(BF)
    result = jnp.zeros((128, 128), F32)
    for ref, first, base in ((near_ref, 1, 0), (far_ref, 0, 4)):
        flat = jnp.concatenate([ref[:, first + j : first + j + 1] for j in range(slots)], axis=0)
        flat = jnp.broadcast_to(flat, (total, 128))
        hit = (flat // boxes) == lane
        onehot = hit.astype(F32).astype(BF)
        before = dot(tri, onehot)
        rank = jnp.sum(jnp.where(hit, before, 0.0), axis=1, keepdims=True).astype(jnp.int32)
        mine = rank == (lane % 4)
        within = jnp.where((lane >= base) & (lane < base + 4), flat % boxes, 0)
        owner = jnp.where((lane >= base + 16) & (lane < base + 20), box, 0)
        value = jnp.where(mine, within + owner, 0).astype(F32).astype(BF)
        result = result + dot(onehot, value, TN)
    want_ref[...] = result.astype(jnp.int32)


def table_kernel(pos_ref, charge_ref, count_ref, cen_ref, q_ref, w_ref, p_ref, f_ref, base_ref, t_ref):
    step = pl.program_id(0)
    group = pos_ref.shape[0]
    sub = iota((8, 128), 0)
    lane = iota((8, 128), 1)

    def body(b, carry):
        box = step * group + b
        live = lane < count_ref[box]
        q = jnp.where(live, charge_ref[b], 0.0)
        q_ref[b] = q
        pos = pos_ref[b]
        zero1 = jnp.zeros((1, 128), F32)
        x4 = jnp.concatenate([pos, zero1], axis=0)
        x = jnp.concatenate([x4, x4], axis=0)
        second = 2.0 * x * x - 1.0
        third = 2.0 * x * second - x
        basis = []
        for i in range(NODES):
            theta = (2 * i + 1) * math.pi / 8
            basis.append(0.25 + 0.5 * (math.cos(theta) * x + math.cos(2 * theta) * second + math.cos(3 * theta) * third))
        row = lambda i, d: jnp.broadcast_to(basis[i][d : d + 1], (8, 128))
        sub4 = sub % 4
        zs = jnp.where(sub4 == 0, row(0, 2), jnp.where(sub4 == 1, row(1, 2), jnp.where(sub4 == 2, row(2, 2), row(3, 2))))
        ys = [jnp.where(sub < 4, row(0, 1), row(1, 1)) * zs, jnp.where(sub < 4, row(2, 1), row(3, 1)) * zs]
        table = jnp.concatenate([row(i, 0) * ys[j] for i in range(NODES) for j in range(2)], axis=0)
        both = stack_kernel(table)
        t_ref[b] = both
        qs = jnp.concatenate(split(q), axis=0)
        weight = fold(dot(qs, both, NT))
        w_ref[b] = weight + pltpu.roll(weight, 64, 1)
        cx, cy, cz = cen_ref[0, box], cen_ref[1, box], cen_ref[2, box]
        lane4 = lane % 4
        far = jnp.where(lane4 == 0, cx, jnp.where(lane4 == 1, cy, cz))
        center = jnp.where(sub4 == 0, cx, jnp.where(sub4 == 1, cy, cz))
        p_ref[b] = jnp.where(sub4 == 3, far, center + 0.5 * x)
        rel = (0.5 * ROOT3) * x
        tgt = planes(rel, False)
        for unit in range(2):
            f_ref[b, unit] = jnp.concatenate([jnp.where(sub // 4 == unit, part, 0.0) for part in tgt], axis=0).astype(BF)
        src = jnp.concatenate(planes(rel, True) + [jnp.zeros((96, 128), F32)], axis=0).T.astype(BF)
        dist2 = dot(src[:, :32], f_ref[b, 0])
        value = stack_kernel(matern(dist2))
        near = fold(dot(jnp.concatenate([qs, qs], axis=1), value))
        base_ref[b] = near + q
        return carry

    lax.fori_loop(0, group, body, 0, unroll=4)


def gather_kernel(ids_ref, q_ref, w_ref, p_ref, out_ref):
    step = pl.program_id(0)
    group = out_ref.shape[0]
    sub4 = iota((8, 128), 0) % 4
    top = iota((8, 128), 0) < 4
    lane = iota((8, 128), 1)
    left = lane < 64

    def body(k, carry):
        peer = step * group + k
        near = [ids_ref[peer, j] for j in range(4)]
        far = [ids_ref[peer, 4 + j] for j in range(4)]
        for j in range(4):
            out_ref[k, 8 * j : 8 * j + 8] = q_ref[near[j]]
        w = [w_ref[far[j]] for j in range(4)]
        out_ref[k, 32:40] = jnp.where(left, w[0], w[2])
        out_ref[k, 40:48] = jnp.where(left, w[1], w[3])
        c = [p_ref[far[j]] for j in range(4)]
        centers = jnp.where(
            left, jnp.where(lane < 4, c[0], c[2]), jnp.where(lane < 68, c[1], c[3])
        )
        s = [p_ref[near[j]] for j in range(4)]
        out_ref[k, 48:56] = jnp.where(sub4 == 3, centers, jnp.where(top, s[0], s[1]))
        out_ref[k, 56:64] = jnp.where(sub4 == 3, centers, jnp.where(top, s[2], s[3]))
        return carry

    lax.fori_loop(0, group, body, 0, unroll=4)


def pair_kernel(
    tgt_ref, count_ref, got_ref, nc_ref, fc_ref, f_ref, fn_ref, base_ref, q_ref, t_ref, out_ref, term_ref, near_acc, far_acc
):
    step = pl.program_id(0)
    steps = pl.num_programs(0)
    group = got_ref.shape[0]
    boxes = f_ref.shape[0]
    sub = iota((8, 128), 0)
    lane = iota((8, 128), 1)
    left = lane < 64

    @pl.when(step == 0)
    def _():
        near_acc[...] = base_ref[...]
        far_acc[...] = jnp.zeros_like(far_acc)

    spread = (iota((128, 128), 0) // 64 == iota((128, 128), 1) // 64).astype(F32).astype(BF)

    def body(k, carry):
        peer = step * group + k
        tn = [tgt_ref[peer, j] for j in range(4)]
        tf = [tgt_ref[peer, 4 + j] for j in range(4)]
        points = [got_ref[k, 48:56], got_ref[k, 56:64]]
        feats = []
        for v in range(2):
            feats += planes((points[v] - nc_ref[k, 8 * v : 8 * v + 8]) * ROOT3, True)
        src = jnp.concatenate(feats + [jnp.zeros((64, 128), F32)], axis=0).T.astype(BF)
        for j in range(4):
            dist2 = dot(src[:, 32 * (j // 2) : 32 * (j // 2) + 32], f_ref[tn[j], j % 2])
            value = stack_kernel(matern(dist2))
            qs = jnp.concatenate(split(got_ref[k, 8 * j : 8 * j + 8]), axis=0)
            near_acc[tn[j]] += fold(dot(jnp.concatenate([qs, qs], axis=1), value))
        row = jnp.broadcast_to(points[0][3:4], (8, 128))
        row = jnp.where(lane % 64 == sub, row, 0.0)
        high = row.astype(BF)
        rest = row - high.astype(F32)
        mid = rest.astype(BF)
        low = (rest - mid.astype(F32)).astype(BF)
        cen = dot(jnp.concatenate([high, mid, low], axis=0), spread)
        rel = (fc_ref[k] - (cen[0:8] + cen[8:16] + cen[16:24])) * ROOT3
        tgt = jnp.concatenate(planes(rel, False), axis=0).astype(BF)
        value = stack_kernel(matern(dot(fn_ref[...], tgt)))
        ws = []
        for h in range(2):
            w = got_ref[k, 32 + 8 * h : 40 + 8 * h]
            for part in (jnp.where(left, w, 0.0), jnp.where(left, 0.0, w)):
                ws += list(split(part))
        ws = jnp.concatenate(ws, axis=0)
        locs = dot(jnp.concatenate([ws, ws], axis=1), value)
        for h in range(2):
            for u in range(2):
                at = 32 * h + 16 * u
                new = fold(locs[at : at + 16])
                far_acc[tf[2 * u + h]] += jnp.where(left if h == 0 else jnp.logical_not(left), new, 0.0)
        return carry

    lax.fori_loop(0, group, body, 0, unroll=2)

    @pl.when(step == steps - 1)
    def _():
        def finish(b, total):
            ls = jnp.concatenate(split(far_acc[b]), axis=0)
            both = t_ref[b]
            high, low = both[0:64], both[64:128]
            table = jnp.concatenate([high, high, low, low], axis=0)
            far = fold(dot(jnp.concatenate([ls, ls], axis=1), table))
            live = lane < count_ref[b]
            product = jnp.where(live, near_acc[b] + far, 0.0)
            out_ref[b] = product
            return total + product * q_ref[b]

        total = lax.fori_loop(0, boxes, finish, jnp.zeros((8, 128), F32), unroll=4)
        ones = jnp.ones((128, 128), F32)
        sums = lax.dot_general(ones, total, NT, precision=lax.Precision.HIGHEST, preferred_element_type=F32)
        term_ref[...] = jnp.concatenate([sums, jnp.zeros((128, 120), F32)], axis=1)


def far_sources():
    x = np.zeros((8, 128), np.float32)
    for n in range(64):
        for d, value in enumerate((NODE[n // 16], NODE[n // 4 % 4], NODE[n % 4])):
            for u in range(2):
                x[4 * u + d, 64 * u + n] = 0.5 * ROOT3 * value
    bf = lambda a: a.astype(jnp.bfloat16).astype(np.float32)
    high = bf(x)
    low = bf(x - high)
    norm = np.zeros_like(x)
    square = high * (high + 2 * low)
    for u in range(2):
        norm[4 * u + 3] = square[4 * u] + square[4 * u + 1] + square[4 * u + 2]
    one = bf(norm)
    two = bf(norm - one)
    three = bf(norm - one - two)
    sub = np.arange(8)[:, None] % 4
    unit = (np.arange(8)[:, None] // 4) == (np.arange(128)[None, :] // 64)
    parts = [
        np.where(sub == 3, one, high),
        np.where(sub == 3, two, high),
        np.where(sub == 3, 1.0, low),
        np.where(sub == 3, three, np.where(sub < 2, 1.0, 0.0)),
    ]
    return np.concatenate([np.where(unit, part, 0.0) for part in parts], axis=0).T.astype(np.float32)


def node_rows():
    out = np.zeros((8, 128), np.float32)
    for m in range(128):
        n = m % 64
        for u in range(2):
            for d, value in enumerate((NODE[n // 16], NODE[n // 4 % 4], NODE[n % 4])):
                out[4 * u + d, m] = 0.5 * value
    return out


def vmem(shape=None, index=None):
    if shape is None:
        return pl.BlockSpec(memory_space=pltpu.VMEM)
    return pl.BlockSpec(shape, index, memory_space=pltpu.VMEM)


SMEM = pl.BlockSpec(memory_space=pltpu.SMEM)


def params(mebibytes=56):
    return pltpu.CompilerParams(vmem_limit_bytes=mebibytes * 1024 * 1024)


def exchange(x):
    return lax.all_to_all(x, AXES, split_axis=0, concat_axis=0, tiled=True)


def general(local_pos, charges, counts, box_centers, far_list, near_list):
    devices = lax.axis_size("gx") * lax.axis_size("gy")
    boxes, _, slots = local_pos.shape
    struct = jax.ShapeDtypeStruct
    want = pl.pallas_call(
        ids_kernel,
        out_shape=struct((devices, 128), jnp.int32),
        in_specs=[vmem(), vmem()],
        out_specs=vmem(),
        compiler_params=params(),
        name="ids",
    )(far_list, near_list)
    served = exchange(want.reshape(devices, 1, 128)).reshape(devices, 128)

    group = 16
    lead = lambda shape: vmem((group,) + shape, lambda i: (i,) + (0,) * len(shape))
    q_tab, w_tab, p_tab, f_tab, base, table = pl.pallas_call(
        table_kernel,
        grid=(boxes // group,),
        out_shape=(
            struct((boxes, 8, 128), F32),
            struct((boxes, 8, 128), F32),
            struct((boxes, 8, 128), F32),
            struct((boxes, 2, 32, 128), BF),
            struct((boxes, 8, 128), F32),
            struct((boxes, 128, 128), BF),
        ),
        in_specs=[lead((3, 128)), lead((8, 128)), SMEM, SMEM],
        out_specs=(lead((8, 128)), lead((8, 128)), lead((8, 128)), lead((2, 32, 128)), lead((8, 128)), lead((128, 128))),
        compiler_params=params(),
        cost_estimate=pl.CostEstimate(flops=200_000_000, bytes_accessed=6_000_000, transcendentals=2_000_000),
        name="tables",
    )(local_pos, charges, counts, box_centers)

    send = pl.pallas_call(
        gather_kernel,
        grid=(devices // group,),
        out_shape=struct((devices, 64, 128), F32),
        in_specs=[SMEM, vmem(), vmem(), vmem()],
        out_specs=lead((64, 128)),
        compiler_params=params(),
        name="gather",
    )(served, q_tab, w_tab, p_tab)
    got = exchange(send)

    tgt = want[:, 16:24]
    centers = box_centers.T
    near_cen = jnp.pad(centers[tgt[:, :4]], ((0, 0), (0, 0), (0, 1))).reshape(devices, 16, 1)
    near_cen = jnp.broadcast_to(near_cen, (devices, 16, 128))
    far_cen = jnp.pad(centers[tgt[:, 4:]], ((0, 0), (0, 0), (0, 1))).reshape(devices, 2, 2, 4)
    far_cen = far_cen.transpose(0, 1, 3, 2).reshape(devices, 8, 2, 1)
    far_cen = jnp.broadcast_to(far_cen, (devices, 8, 2, 64)).reshape(devices, 8, 128) + node_rows()[None]

    product, term = pl.pallas_call(
        pair_kernel,
        grid=(devices // group,),
        out_shape=(struct((boxes, 8, 128), F32), struct((devices, 128), F32)),
        in_specs=[
            SMEM,
            SMEM,
            lead((64, 128)),
            lead((16, 128)),
            lead((8, 128)),
            vmem(),
            vmem(),
            vmem(),
            vmem(),
            vmem(),
        ],
        out_specs=(vmem(), vmem()),
        scratch_shapes=[pltpu.VMEM((boxes, 8, 128), F32), pltpu.VMEM((boxes, 8, 128), F32)],
        compiler_params=params(),
        cost_estimate=pl.CostEstimate(flops=1_000_000_000, bytes_accessed=12_000_000, transcendentals=20_000_000),
        name="pairs",
    )(tgt, counts, got, near_cen, far_cen, f_tab, jnp.asarray(far_sources(), BF), base, q_tab, table)

    terms = exchange(term.reshape(devices, 1, 128))[:, 0, :8]
    curvature = jnp.sum(terms, axis=0) / (devices * boxes * slots)
    return (product, curvature)


HALF = 64
ROWS = 44
NEAR_ROWS = 24
UNROLL = 4
CHUNKS = 16
AHEAD = 4


def upper_kernel(pos_ref, charge_ref, count_ref, row_ref, ex_ref):
    half = charge_ref.shape[0] // 2
    lane = iota((8, 128), 1)
    left = lane < HALF
    center = jnp.concatenate([row_ref[...], jnp.zeros((5, 2 * half), F32)], axis=0)
    center = jnp.concatenate([center, jnp.zeros((8, 128 - 2 * half), F32)], axis=1)
    center = jnp.concatenate([center, jnp.zeros((120, 128), F32)], axis=0).T
    wide = iota((half, 128), 1) < HALF
    for d in range(3):
        first = center[:half, d : d + 1] + 0.5 * pos_ref[d, :half]
        second = center[half : 2 * half, d : d + 1] + 0.5 * pos_ref[d, half:]
        ex_ref[(8 + d) * half : (9 + d) * half, :] = jnp.where(wide, pltpu.roll(first, HALF, 1), second)

    def body(b, carry):
        first = pltpu.roll(jnp.where(lane < count_ref[b], charge_ref[b], 0.0), HALF, 1)
        second = jnp.where(lane < count_ref[b + half], charge_ref[b + half], 0.0)
        ex_ref[pl.ds(pl.multiple_of(8 * b, 8), 8), :] = jnp.where(left, first, second)
        return carry

    lax.fori_loop(0, half, body, 0, unroll=16)


def start_kernel(far_ref, near_ref, most_ref, row_ref, msg_ref, want_ref):
    boxes = far_ref.shape[1]
    slots = far_ref.shape[0]
    peer = iota((128, 128), 0)
    line = iota((128, 128), 1)
    tri = (peer < line).astype(F32).astype(BF)
    full = jnp.ones((128, 128), BF)
    row32 = iota((32, 128), 0)
    kind = row32 // 4
    boxrow = iota((32, 128), 1) % boxes
    result = jnp.zeros((128, 32), F32)
    for ref, first, group in ((near_ref, 1, 0), (far_ref, 0, 1)):
        seen = jnp.zeros((128, 128), F32)
        for j in range(0, slots, 2):
            flat = jnp.concatenate([ref[first + j : first + j + 1, :], ref[first + j + 1 : first + j + 2, :]], axis=1)
            hit = jnp.broadcast_to(flat // boxes, (128, 128)) == peer
            onehot = hit.astype(F32).astype(BF)
            before = dot(onehot, tri) + seen
            rank = jnp.sum(jnp.where(hit, before, 0.0), axis=0, keepdims=True).astype(jnp.int32)
            if j + 2 < slots:
                seen = seen + dot(onehot, full)
            within = jnp.broadcast_to(flat % boxes, (32, 128))
            if group == 0:
                value = jnp.where(kind == 0, within * NEAR_ROWS, jnp.where(kind == 2, within * 8, 0))
            else:
                value = jnp.where(kind == 1, within * 8, 0)
            value = jnp.where(kind == 4 + group, boxrow, value)
            value = jnp.where(row32 % 4 == jnp.broadcast_to(rank, (32, 128)), value, 0).astype(F32).astype(BF)
            result = result + dot(onehot, value, NT)
    result = jnp.concatenate([result, jnp.zeros((128, 96), F32)], axis=1)
    heavy = (line == peer - peer % 4).astype(F32).astype(BF)
    first = dot(heavy, result.astype(BF))
    for at, base in ((8, 8), (24, 16)):
        extra = dot(jnp.where(line == base + peer % 4, first, 0.0).astype(BF), full)
        result = jnp.where(line == at, extra, result)
    most = jnp.max(most_ref[...], axis=1, keepdims=True).astype(F32)
    result = jnp.where(line == 9, jnp.broadcast_to(most, (128, 128)), result)
    want_ref[...] = result.astype(jnp.int32)
    rows = [jnp.concatenate([row_ref[d : d + 1, :]] * 2, axis=1) for d in range(3)]
    rows = [jnp.broadcast_to(row, (128, 128)) for row in rows]
    msg_ref[pl.ds(0, 128, stride=2), :] = jnp.where(line < HALF, result, rows[2])
    msg_ref[pl.ds(1, 128, stride=2), :] = jnp.where(line < HALF, rows[0], rows[1])


def cheb_rows(x):
    sub = iota((8, 128), 0)
    second = 2.0 * x * x - 1.0
    third = 2.0 * x * second - x
    basis = []
    for i in range(NODES):
        theta = (2 * i + 1) * math.pi / 8
        basis.append(0.25 + 0.5 * (math.cos(theta) * x + math.cos(2 * theta) * second + math.cos(3 * theta) * third))
    row = lambda i, d: jnp.broadcast_to(basis[i][d : d + 1], (8, 128))
    sub4 = sub % 4
    zs = jnp.where(sub4 == 0, row(0, 2), jnp.where(sub4 == 1, row(1, 2), jnp.where(sub4 == 2, row(2, 2), row(3, 2))))
    ys = [jnp.where(sub < 4, row(0, 1), row(1, 1)) * zs, jnp.where(sub < 4, row(2, 1), row(3, 1)) * zs]
    return jnp.concatenate([row(i, 0) * ys[j] for i in range(NODES) for j in range(2)], axis=0)


def point_rows(pos_ref, b):
    sub4 = iota((8, 128), 0) % 4
    x = jnp.zeros((8, 128), F32)
    for d in range(3):
        x = jnp.where(sub4 == d, jnp.broadcast_to(pos_ref[d, pl.ds(b, 1), :], (8, 128)), x)
    return x


def doubled(x):
    return jnp.where(iota((8, 128), 1) < HALF, x, pltpu.roll(x, HALF, 1))


def fill_basis(pos_ref, basis_ref):
    for d in range(3):
        x = pos_ref[d]
        second = 2.0 * x * x - 1.0
        third = 2.0 * x * second - x
        for i in range(NODES):
            theta = (2 * i + 1) * math.pi / 8
            value = math.cos(theta) * x + math.cos(2 * theta) * second + math.cos(3 * theta) * third
            basis_ref[4 * d + i] = 0.25 + 0.5 * value


def basis_table(basis_ref, b):
    sub = iota((8, 128), 0)
    row = lambda i, d: jnp.broadcast_to(basis_ref[4 * d + i, pl.ds(b, 1), :], (8, 128))
    sub4 = sub % 4
    zs = jnp.where(sub4 == 0, row(0, 2), jnp.where(sub4 == 1, row(1, 2), jnp.where(sub4 == 2, row(2, 2), row(3, 2))))
    ys = [jnp.where(sub < 4, row(0, 1), row(1, 1)) * zs, jnp.where(sub < 4, row(2, 1), row(3, 1)) * zs]
    return jnp.concatenate([row(i, 0) * ys[j] for i in range(NODES) for j in range(2)], axis=0)


def send_table_kernel(pos_ref, charge_ref, count_ref, cen_ref, near_ref, far_ref, basis_ref):
    boxes = charge_ref.shape[0]
    lane = iota((8, 128), 1)
    sub = iota((8, 128), 0)
    fill_basis(pos_ref, basis_ref)

    def body(b, carry):
        q = jnp.where(lane < count_ref[b], charge_ref[b], 0.0)
        near_ref[b, 0:8] = doubled(q)
        x, y, z = [doubled(cen_ref[d, b] + 0.5 * jnp.broadcast_to(pos_ref[d, pl.ds(b, 1), :], (8, 128))) for d in range(3)]
        near_ref[b, 8:16] = jnp.where(sub == 4, x, jnp.where(sub == 5, y, z))
        near_ref[b, 16:24] = jnp.where(sub == 7, x, jnp.where((sub == 3) | (sub == 5), y, z))
        table = basis_table(basis_ref, b)
        qs = jnp.concatenate(split(q), axis=0)
        weight = fold(dot(qs, stack_kernel(table), NT))
        far_ref[b] = weight + pltpu.roll(weight, 64, 1)
        return carry

    lax.fori_loop(0, boxes, body, 0, unroll=32)


def own_table_kernel(pos_ref, charge_ref, count_ref, q_ref, f_ref, base_ref):
    boxes = charge_ref.shape[0]
    sub = iota((8, 128), 0)
    lane = iota((8, 128), 1)

    def body(b, carry):
        q = jnp.where(lane < count_ref[b], charge_ref[b], 0.0)
        q_ref[b] = q
        x = point_rows(pos_ref, b)
        rel = (0.5 * ROOT3) * x
        tgt = planes(rel, False)
        for unit in range(2):
            f_ref[b, unit] = jnp.concatenate([jnp.where(sub // 4 == unit, part, 0.0) for part in tgt], axis=0).astype(BF)
        zero = jnp.zeros((96, 128), F32)
        src = jnp.concatenate(planes(rel, True) + [zero], axis=0).T.astype(BF)
        first = jnp.concatenate([jnp.where(sub < 4, part, 0.0) for part in tgt] + [zero], axis=0).astype(BF)
        value = stack_kernel(matern(dot(src, first)))
        qs = jnp.concatenate(split(q), axis=0)
        base_ref[b] = fold(dot(jnp.concatenate([qs, qs], axis=1), value)) + q
        return carry

    lax.fori_loop(0, boxes, body, 0, unroll=4)


def goal_kernel(want_ref, served_ref, cen_ref, node_ref, nc_ref, fc_ref, ec_ref, goal_ref, odd_ref):
    lane = iota((128, 128), 1)
    left = lane < HALF
    boxes = cen_ref.shape[1]
    cen = jnp.concatenate([cen_ref[...], jnp.zeros((5, boxes), F32)], axis=0)
    cen = jnp.concatenate([cen, jnp.zeros((8, 128 - boxes), F32)], axis=1)
    cen = jnp.concatenate([cen, jnp.zeros((120, 128), F32)], axis=0).T

    def split3(x, axis):
        high = x.astype(BF)
        rest = x - high.astype(F32)
        mid = rest.astype(BF)
        return jnp.concatenate([high, mid, (rest - mid.astype(F32)).astype(BF)], axis=axis)

    parts = split3(cen, 0)
    want = want_ref[...]
    goal_ref[...] = want.astype(F32).T[16:32].astype(jnp.int32)
    sources = [served_ref[pl.ds(1, 128, stride=2), :], served_ref[pl.ds(0, 128, stride=2), :]]
    halves = [jnp.concatenate([(iota((128, 128), 0) // HALF == h).astype(F32).astype(BF)] * 3, axis=0) for h in range(2)]

    def column(at):
        return jnp.broadcast_to(want[:, at : at + 1], (128, 128))

    def centers(at):
        onehot = (column(at) == lane).astype(F32).astype(BF)
        found = dot(jnp.concatenate([onehot] * 3, axis=1), parts)
        return [jnp.broadcast_to(found[:, d : d + 1], (128, 128)) for d in range(3)]

    def gaps(j):
        mine = lane % HALF == column(4 + j) // 8
        both = [split3(jnp.where(mine, source, 0.0), 1) for source in sources]
        theirs = [dot(both[0], halves[0]), dot(both[0], halves[1]), dot(both[1], halves[1])]
        return [a - b for a, b in zip(centers(20 + j), theirs)]

    nc_ref[...] = jnp.zeros_like(nc_ref)
    fc_ref[...] = jnp.zeros_like(fc_ref)
    ec_ref[...] = jnp.zeros_like(ec_ref)
    for u in range(2):
        first, second = centers(16 + 2 * u), centers(17 + 2 * u)
        for d in range(3):
            nc_ref[pl.ds(4 * u + d, 128, stride=8), :] = jnp.where(left, first[d], second[d])
        first, second = gaps(2 * u), gaps(2 * u + 1)
        for d in range(3):
            fc_ref[pl.ds(4 * u + d, 128, stride=8), :] = jnp.where(left, first[d], second[d]) + node_ref[d : d + 1, :]
    extra = centers(24)
    for d in range(3):
        odd_ref[...] = extra[d]
        even, odd = odd_ref[pl.ds(0, 64, stride=2), :], odd_ref[pl.ds(1, 64, stride=2), :]
        ec_ref[pl.ds(d, 64, stride=8), :] = jnp.where(left[:64], even, odd)


def far_kernel(fc_ref, fn_ref, out_ref):
    group = fc_ref.shape[0]
    tgt = jnp.concatenate(planes(fc_ref[...] * ROOT3, False), axis=1).astype(BF)
    for k in range(group):
        out_ref[k] = stack_kernel(matern(dot(fn_ref[...], tgt[k])))


def send_kernel(member_ref, served_ref, near_ref, far_ref, own_ref, *refs):
    moved, (out_ref, ids_ref, int_ref, ex_ref, buf_ref, sems) = refs[:3], refs[3:]
    peers = ids_ref.shape[1]
    sub = iota((8, 128), 0)
    lane = iota((8, 128), 1)
    left = lane < HALF
    keep = left | (sub < 3)
    second = sub < 5
    int_ref[...] = served_ref[pl.ds(0, peers, stride=2), :].T[:16].astype(jnp.int32)
    copy = pltpu.make_async_copy(int_ref, ids_ref, sems.at[0])
    copy.start()
    half = ex_ref.shape[0] // 16
    packed = moved[0][...] + moved[1][...] + moved[2][...]
    packed = jnp.where(member_ref[0] == 0, own_ref[...], packed)
    for d in range(3):
        rows = packed[(8 + d) * half : (9 + d) * half]
        ex_ref[pl.ds(d, half, stride=8), :] = pltpu.roll(rows, HALF, 1)
        ex_ref[pl.ds(8 * half + d, half, stride=8), :] = rows
    for b in range(half):
        tile = packed[8 * b : 8 * b + 8]
        for at, part in ((8 * b, tile), (8 * (b + half), pltpu.roll(tile, HALF, 1))):
            ex_ref[at : at + 8, :] = jnp.where(left, part, jnp.where(sub < 3, ex_ref[at : at + 8, :], 0.0))
    copy.wait()

    def body(i, carry):
        base = pl.multiple_of(i * 2 * ROWS, 8)
        for k in range(2):
            peer = 2 * i + k
            at = lambda row: pl.ds(base + (k * ROWS + row), 8)
            rows = lambda ref, j, row: ref[pl.ds(pl.multiple_of(ids_ref[j, peer], 8) + row, 8), :]
            q = [rows(near_ref, j, 0) for j in range(4)]
            w = [rows(far_ref, 4 + j, 0) for j in range(4)]
            p = [rows(near_ref, j, 16 if j < 2 else 8) for j in range(4)]
            buf_ref[at(0), :] = jnp.where(left, q[0], q[1])
            buf_ref[at(8), :] = jnp.where(left, q[2], q[3])
            buf_ref[at(16), :] = jnp.where(left, w[0], w[2])
            buf_ref[at(24), :] = jnp.where(left, w[1], w[3])
            buf_ref[at(36), :] = jnp.where(sub == 7, jnp.where(left, p[0], p[1]), jnp.where(left, p[2], p[3]))
            buf_ref[at(32), :] = jnp.where(keep, rows(ex_ref, 8, 0), jnp.where(second, p[1], p[0]))
        return carry

    chunks = 8
    each = peers // chunks
    stores = []
    for c in range(chunks):
        lax.fori_loop(c * each // 2, (c + 1) * each // 2, body, 0, unroll=8)
        at = pl.ds(c * each * ROWS, each * ROWS)
        stores.append(pltpu.make_async_copy(buf_ref.at[at], out_ref.at[at], sems.at[1 + c]))
        stores[-1].start()
    for copy in stores:
        copy.wait()


def duo_kernel(
    scale, got_ref, want_hbm, nc_hbm, ec_hbm, f_hbm, base_hbm, q_hbm, w_hbm, v_hbm, near0_hbm, near1_hbm, far0_hbm, far1_hbm, term_ref,
    tgt_ref, nc_ref, ec_ref, f_ref, base_ref, q_ref, w_ref, v_ref, sems, *bufs
):
    whole = [(want_hbm, tgt_ref), (nc_hbm, nc_ref), (ec_hbm, ec_ref), (f_hbm, f_ref)]
    whole += [(base_hbm, base_ref), (q_hbm, q_ref), (w_hbm, w_ref)]
    loads = [pltpu.make_async_copy(source, target, sems.at[i]) for i, (source, target) in enumerate(whole)]
    for copy in loads[:4]:
        copy.start()
    chunk = v_ref.shape[0] // CHUNKS

    def far_values(c):
        at = pl.ds(c * chunk, chunk)
        return pltpu.make_async_copy(v_hbm.at[at], v_ref.at[at], sems.at[16 + c % AHEAD])

    for c in range(AHEAD):
        far_values(c).start()
    xt_refs, dist_refs, value_refs = bufs[:2], (bufs[2:7], bufs[7:12]), (bufs[12:17], bufs[17:22])
    near_accs, far_accs = bufs[22:24], bufs[24:26]
    duos = ec_ref.shape[0]
    boxes = f_ref.shape[0]
    sub = iota((8, 128), 0)
    lane = iota((8, 128), 1)
    left = lane < HALF
    for ref in value_refs[1] + near_accs + far_accs:
        ref[...] = jnp.zeros_like(ref)
    for ref in dist_refs[1]:
        ref[...] = jnp.full(ref.shape, 1e6, F32)
    def tile(duo, a, row):
        return got_ref[pl.ds(pl.multiple_of(duo * 2 * ROWS, 8) + (a * ROWS + row), 8), :]

    def extra(duo):
        return tile(duo, 0, 32), tile(duo, 1, 32)

    def goals(duo):
        pairs = [(tgt_ref[2 * (k % 2), 2 * duo + k // 2], tgt_ref[2 * (k % 2) + 1, 2 * duo + k // 2]) for k in range(4)]
        return pairs + [(tgt_ref[8, 2 * duo], tgt_ref[8, 2 * duo + 1])]

    def halves(x):
        high = x.astype(BF).astype(F32)
        both = [high, x - high]
        return [jnp.where(left, part, 0.0) for part in both] + [jnp.where(left, 0.0, part) for part in both]

    def products(duo, value):
        ex = extra(duo)
        tiles = [tile(duo, k // 2, 8 * (k % 2)) for k in range(4)]
        tiles.append(jnp.where(left, ex[0], pltpu.roll(ex[1], HALF, 1)))
        for k, goal in enumerate(goals(duo)):
            qs = jnp.concatenate(halves(tiles[k]), axis=0).astype(BF)
            new = dot(jnp.concatenate([qs, qs], axis=1), value[k][...])
            for h in range(2):
                near_accs[h][goal[h]] += fold(new[16 * h : 16 * h + 16])

    def far_products(duo):
        for a in range(2):
            ws = []
            for h in range(2):
                ws += halves(tile(duo, a, 16 + 8 * h))
            ws = jnp.concatenate(ws, axis=0).astype(BF)
            new = dot(jnp.concatenate([ws, ws], axis=1), v_ref[2 * duo + a])
            for h in range(2):
                for u in range(2):
                    at = 32 * h + 16 * u
                    far_accs[h][tgt_ref[4 + 2 * u + h, 2 * duo + a]] += fold(new[at : at + 16])

    def values(dist, value):
        for k in range(5):
            value[k][...] = stack_kernel(matern(dist[k][...]))

    def distances(duo, xt, dist):
        for k, goal in enumerate(goals(duo)):
            v, u = k // 2, k % 2
            for half in range(2):
                pieces = [jnp.zeros((32 * v, 128), BF)] if v else []
                pieces += [f_ref[goal[half], u], jnp.zeros((96 - 32 * v, 128), BF)]
                at = slice(64 * half, 64 * half + 64)
                dist[k][at, :] = dot(xt[at, :], jnp.concatenate(pieces, axis=0))

    def features(duo, xt):
        ex = extra(duo)
        turned = [pltpu.roll(x, HALF, 1) for x in ex]
        feats = []
        for a in range(2):
            full = tile(duo, a, 36)
            split_rows = jnp.where(left, pltpu.roll(turned[a], 4, 0), pltpu.roll(ex[a], 6, 0))
            point = jnp.where(sub >= 4, full, jnp.where(sub == 0, pltpu.roll(full, 1, 0), split_rows))
            feats += planes((point - nc_ref[2 * duo + a]) * ROOT3, True)
        point = jnp.where(left, turned[0], ex[1])
        feats += planes((point - ec_ref[duo]) * ROOT3, True)
        feats.append(jnp.zeros((32, 128), F32))
        xt[...] = jnp.concatenate(feats, axis=0).T.astype(BF)

    turns = duos // UNROLL
    assert turns == CHUNKS

    def body(i, carry):
        far_values(i).wait()

        @pl.when(i + AHEAD < CHUNKS)
        def _():
            far_values(i + AHEAD).start()

        for s in range(UNROLL):
            now, was = s % 2, 1 - s % 2
            step = UNROLL * i + s
            products(jnp.maximum(step - 2, 0), value_refs[was])
            far_products(step)
            values(dist_refs[was], value_refs[now])
            distances(step, xt_refs[was], dist_refs[now])
            features(jnp.minimum(step + 1, duos - 1), xt_refs[now])
        return carry

    for copy in loads[:4]:
        copy.wait()
    features(0, xt_refs[1])
    for copy in loads[4:]:
        copy.start()
    lax.fori_loop(0, turns, body, 0)
    products(duos - 2, value_refs[1])
    values(dist_refs[1], value_refs[0])
    products(duos - 1, value_refs[0])

    sums = (near0_hbm, near1_hbm, far0_hbm, far1_hbm)
    stores = [pltpu.make_async_copy(a, b, sems.at[8 + i]) for i, (a, b) in enumerate(zip(near_accs + far_accs, sums))]
    for copy in stores:
        copy.start()
    for copy in loads[4:]:
        copy.wait()

    def finish(b, total):
        near = near_accs[0][b] + near_accs[1][b] + base_ref[b]
        far = jnp.where(left, far_accs[0][b], far_accs[1][b])
        return total + near * q_ref[b] + far * w_ref[b]

    total = lax.fori_loop(0, boxes, finish, jnp.zeros((8, 128), F32), unroll=16)
    ones = jnp.ones((128, 128), F32)
    sums = lax.dot_general(ones, total, NT, precision=lax.Precision.HIGHEST, preferred_element_type=F32)
    term_ref[...] = jnp.concatenate([sums * scale, jnp.zeros((128, 120), F32)], axis=1)
    for copy in stores:
        copy.wait()


def finish_kernel(count_ref, pos_ref, near0_ref, near1_ref, far0_ref, far1_ref, base_ref, out_ref, basis_ref):
    boxes = base_ref.shape[0]
    lane = iota((8, 128), 1)
    fill_basis(pos_ref, basis_ref)

    def body(b, carry):
        locs = jnp.where(lane < HALF, far0_ref[b], far1_ref[b])
        ls = jnp.concatenate(split(locs), axis=0)
        high, low = split(basis_table(basis_ref, b))
        far = fold(dot(jnp.concatenate([ls, ls], axis=1), jnp.concatenate([high, high, low, low], axis=0)))
        near = near0_ref[b] + near1_ref[b] + base_ref[b]
        out_ref[b] = jnp.where(lane < count_ref[b], near + far, 0.0)
        return carry

    lax.fori_loop(0, boxes, body, 0, unroll=16)


def on_device(local_pos, charges, counts, box_centers, far_list, near_list):
    devices = lax.axis_size("gx") * lax.axis_size("gy")
    boxes, _, slots = local_pos.shape
    struct = jax.ShapeDtypeStruct
    hbm = pltpu.HBM
    stay = lambda x: pltpu.with_memory_space_constraint(x, pltpu.HBM)
    anywhere = pl.BlockSpec(memory_space=pltpu.HBM)
    pos = jnp.transpose(local_pos, (1, 0, 2))
    table = struct((boxes, 8, 128), F32)
    flat = lambda x: x.reshape(-1, 128)
    member = (lax.axis_index("gy") % 4).astype(jnp.int32).reshape(1)
    ex_own = pl.pallas_call(
        upper_kernel,
        out_shape=struct((boxes * 11 // 2, 128), F32),
        in_specs=[vmem(), vmem(), SMEM, vmem()],
        out_specs=vmem(),
        compiler_params=params(8),
        name="upper_halves",
    )(pos, charges, counts, box_centers)
    msg, want = pl.pallas_call(
        start_kernel,
        out_shape=(struct((devices * 2, 128), F32), struct((devices, 128), jnp.int32)),
        in_specs=[vmem()] * 4,
        out_specs=(vmem(), vmem()),
        compiler_params=params(8),
        name="start",
    )(far_list.T, near_list.T, counts.reshape(1, boxes), box_centers)
    moved = [lax.ppermute(ex_own, "gy", [(4 * z, 4 * z + k) for z in range(4)]) for k in range(1, 4)]
    served = flat(exchange(msg.reshape(devices, 2, 128)))

    near_tab, far_tab = pl.pallas_call(
        send_table_kernel,
        out_shape=(struct((boxes, NEAR_ROWS, 128), F32), table),
        in_specs=[vmem(), vmem(), SMEM, SMEM],
        out_specs=(vmem(), vmem()),
        scratch_shapes=[pltpu.VMEM((12, boxes, 128), F32)],
        compiler_params=params(8),
        cost_estimate=pl.CostEstimate(flops=50_000_000, bytes_accessed=1_200_000, transcendentals=0),
        name="send_tables",
    )(pos, charges, counts, box_centers)

    send = pl.pallas_call(
        send_kernel,
        out_shape=hbm((devices * ROWS, 128), F32),
        in_specs=[SMEM] + [vmem()] * 7,
        out_specs=anywhere,
        scratch_shapes=[
            pltpu.SMEM((16, devices), jnp.int32),
            pltpu.VMEM((16, devices), jnp.int32),
            pltpu.VMEM((boxes * 8, 128), F32),
            pltpu.VMEM((devices * ROWS, 128), F32),
            pltpu.SemaphoreType.DMA((9,)),
        ],
        compiler_params=params(12),
        name="send",
    )(member, served, flat(near_tab), flat(far_tab), ex_own, *moved)
    got = flat(exchange(send.reshape(devices, ROWS // 4, 4, 128)))

    q_tab, f_tab, base = pl.pallas_call(
        own_table_kernel,
        out_shape=(hbm((boxes, 8, 128), F32), hbm((boxes, 2, 32, 128), BF), hbm((boxes, 8, 128), F32)),
        in_specs=[vmem(), vmem(), SMEM],
        out_specs=(vmem(), vmem(), vmem()),
        compiler_params=params(8),
        cost_estimate=pl.CostEstimate(flops=200_000_000, bytes_accessed=4_000_000, transcendentals=2_000_000),
        name="own_tables",
    )(pos, charges, counts)

    near_cen, far_gap, ex_cen, goals = pl.pallas_call(
        goal_kernel,
        out_shape=(
            hbm((devices * 8, 128), F32),
            hbm((devices * 8, 128), F32),
            hbm((devices * 4, 128), F32),
            hbm((16, devices), jnp.int32),
        ),
        in_specs=[vmem()] * 4,
        out_specs=(vmem(),) * 4,
        scratch_shapes=[pltpu.VMEM((128, 128), F32)],
        compiler_params=params(8),
        cost_estimate=pl.CostEstimate(flops=50_000_000, bytes_accessed=2_000_000, transcendentals=0),
        name="goals",
    )(want, served, box_centers, jnp.asarray(node_rows()))
    near_cen, far_gap, ex_cen = [x.reshape(-1, 8, 128) for x in (near_cen, far_gap, ex_cen)]
    group = 8
    far_value = pl.pallas_call(
        far_kernel,
        grid=(devices // group,),
        out_shape=hbm((devices, 256, 128), BF),
        in_specs=[vmem((group, 8, 128), lambda i: (i, 0, 0)), vmem()],
        out_specs=vmem((group, 256, 128), lambda i: (i, 0, 0)),
        compiler_params=params(8),
        cost_estimate=pl.CostEstimate(flops=200_000_000, bytes_accessed=9_000_000, transcendentals=4_000_000),
        name="far_values",
    )(far_gap, jnp.asarray(far_sources(), BF))

    big = lambda dtype, rows: pltpu.VMEM((rows, 128), dtype)
    *sums, term = pl.pallas_call(
        functools.partial(duo_kernel, 1.0 / (devices * boxes * slots)),
        out_shape=(hbm((boxes, 8, 128), F32),) * 4 + (struct((devices, 128), F32),),
        in_specs=[vmem()] + [anywhere] * 8,
        out_specs=(anywhere,) * 4 + (vmem(),),
        scratch_shapes=[
            pltpu.SMEM((16, devices), jnp.int32),
            pltpu.VMEM((devices, 8, 128), F32),
            pltpu.VMEM((devices // 2, 8, 128), F32),
            pltpu.VMEM((boxes, 2, 32, 128), BF),
            pltpu.VMEM((boxes, 8, 128), F32),
            pltpu.VMEM((boxes, 8, 128), F32),
            pltpu.VMEM((boxes, 8, 128), F32),
            pltpu.VMEM((devices, 256, 128), BF),
            pltpu.SemaphoreType.DMA((20,)),
        ]
        + [big(BF, 128)] * 2
        + [big(F32, 128)] * 10
        + [big(BF, 256)] * 10
        + [pltpu.VMEM((boxes, 8, 128), F32)] * 4,
        compiler_params=params(28),
        cost_estimate=pl.CostEstimate(flops=1_000_000_000, bytes_accessed=12_000_000, transcendentals=20_000_000),
        name="pairs",
    )(got, *[stay(x) for x in (goals, near_cen, ex_cen, f_tab, base, q_tab, far_tab, far_value)])

    terms = exchange(term.reshape(devices, 1, 128))[:, 0, :8]
    curvature = jnp.sum(terms, axis=0)
    product = pl.pallas_call(
        finish_kernel,
        out_shape=table,
        in_specs=[SMEM] + [vmem()] * 6,
        out_specs=vmem(),
        scratch_shapes=[pltpu.VMEM((12, boxes, 128), F32)],
        compiler_params=params(8),
        cost_estimate=pl.CostEstimate(flops=50_000_000, bytes_accessed=3_000_000, transcendentals=0),
        name="finish",
    )(counts, pos, *[stay(x) for x in (*sums, base)])
    over = jnp.any((served.reshape(devices, 2, 128)[:, 0, 9] > HALF) & (jnp.arange(devices) % 4 != 0))
    whole = (local_pos, charges, counts, box_centers, far_list, near_list)
    return lax.cond(over, lambda: general(*whole), lambda: (product, curvature))


def solution(mesh):
    in_specs = (
        P(AXES, None, None),
        P(AXES, None, None),
        P(AXES),
        P(None, AXES),
        P(AXES, None),
        P(AXES, None),
    )
    out_specs = (P(AXES, None, None), P())
    return jax.shard_map(on_device, mesh=mesh, in_specs=in_specs, out_specs=out_specs, check_vma=False)
```

```python
import functools
import math

import jax
import jax.numpy as jnp
import numpy as np
from jax import lax
from jax.experimental import pallas as pl
from jax.experimental.pallas import tpu as pltpu
from jax.sharding import PartitionSpec as P

AXES = ("gx", "gy")
NODES = 4
ROOT3 = 1.7320508075688772
LOG2E = 1.4426950408889634
BF = jnp.bfloat16
F32 = jnp.float32
NODE = [math.cos((2 * i + 1) * math.pi / 8) for i in range(NODES)]
NT = (((1,), (1,)), ((), ()))
TN = (((0,), (0,)), ((), ()))


def iota(shape, dim):
    return lax.broadcasted_iota(jnp.int32, shape, dim)


def dot(a, b, dims=None):
    if dims is None:
        return jnp.dot(a, b, preferred_element_type=F32)
    return lax.dot_general(a, b, dims, preferred_element_type=F32)


def split(x):
    high = x.astype(BF)
    return high, (x - high.astype(F32)).astype(BF)


def planes(rel, source):
    axis = rel.ndim - 2
    sub = iota(rel.shape, axis) % 4
    last = sub == 3
    rel = jnp.where(last, 0.0, rel)
    high = rel.astype(BF).astype(F32)
    low = (rel - high).astype(BF).astype(F32)
    square = high * (high + 2.0 * low)
    norm = pltpu.roll(square, 1, axis) + pltpu.roll(square, 2, axis) + pltpu.roll(square, 3, axis)
    one = norm.astype(BF).astype(F32)
    rest = norm - one
    two = rest.astype(BF).astype(F32)
    three = (rest - two).astype(BF).astype(F32)
    if source:
        parts = [
            jnp.where(last, one, high),
            jnp.where(last, two, high),
            jnp.where(last, 1.0, low),
            jnp.where(last, three, jnp.where(sub < 2, 1.0, 0.0)),
        ]
    else:
        parts = [
            jnp.where(last, 1.0, -2.0 * high),
            jnp.where(last, 1.0, -2.0 * low),
            jnp.where(last, one, -2.0 * high),
            jnp.where(
                sub == 0,
                pltpu.roll(two, 5, axis),
                jnp.where(sub == 1, pltpu.roll(three, 6, axis), jnp.where(last, 1.0, 0.0)),
            ),
        ]
    return parts


def matern(dist2):
    safe = jnp.maximum(dist2, 1e-12)
    scaled = safe * lax.rsqrt(safe)
    decay = jnp.exp2(scaled * (-LOG2E))
    return decay + scaled * decay


def stack_kernel(value):
    high, low = split(value)
    return jnp.concatenate([high, low], axis=0)


def fold(x):
    return x[0:8] + x[8:16]


def ids_kernel(far_ref, near_ref, want_ref):
    boxes = far_ref.shape[0]
    slots = far_ref.shape[1]
    total = boxes * slots
    lane = iota((total, 128), 1)
    box = iota((total, 128), 0) % boxes
    tri = (iota((total, total), 0) > iota((total, total), 1)).astype(F32).astype(BF)
    result = jnp.zeros((128, 128), F32)
    for ref, first, base in ((near_ref, 1, 0), (far_ref, 0, 4)):
        flat = jnp.concatenate([ref[:, first + j : first + j + 1] for j in range(slots)], axis=0)
        flat = jnp.broadcast_to(flat, (total, 128))
        hit = (flat // boxes) == lane
        onehot = hit.astype(F32).astype(BF)
        before = dot(tri, onehot)
        rank = jnp.sum(jnp.where(hit, before, 0.0), axis=1, keepdims=True).astype(jnp.int32)
        mine = rank == (lane % 4)
        within = jnp.where((lane >= base) & (lane < base + 4), flat % boxes, 0)
        owner = jnp.where((lane >= base + 16) & (lane < base + 20), box, 0)
        value = jnp.where(mine, within + owner, 0).astype(F32).astype(BF)
        result = result + dot(onehot, value, TN)
    want_ref[...] = result.astype(jnp.int32)


def table_kernel(pos_ref, charge_ref, count_ref, cen_ref, q_ref, w_ref, p_ref, f_ref, base_ref, t_ref):
    step = pl.program_id(0)
    group = pos_ref.shape[0]
    sub = iota((8, 128), 0)
    lane = iota((8, 128), 1)

    def body(b, carry):
        box = step * group + b
        live = lane < count_ref[box]
        q = jnp.where(live, charge_ref[b], 0.0)
        q_ref[b] = q
        pos = pos_ref[b]
        zero1 = jnp.zeros((1, 128), F32)
        x4 = jnp.concatenate([pos, zero1], axis=0)
        x = jnp.concatenate([x4, x4], axis=0)
        second = 2.0 * x * x - 1.0
        third = 2.0 * x * second - x
        basis = []
        for i in range(NODES):
            theta = (2 * i + 1) * math.pi / 8
            basis.append(0.25 + 0.5 * (math.cos(theta) * x + math.cos(2 * theta) * second + math.cos(3 * theta) * third))
        row = lambda i, d: jnp.broadcast_to(basis[i][d : d + 1], (8, 128))
        sub4 = sub % 4
        zs = jnp.where(sub4 == 0, row(0, 2), jnp.where(sub4 == 1, row(1, 2), jnp.where(sub4 == 2, row(2, 2), row(3, 2))))
        ys = [jnp.where(sub < 4, row(0, 1), row(1, 1)) * zs, jnp.where(sub < 4, row(2, 1), row(3, 1)) * zs]
        table = jnp.concatenate([row(i, 0) * ys[j] for i in range(NODES) for j in range(2)], axis=0)
        both = stack_kernel(table)
        t_ref[b] = both
        qs = jnp.concatenate(split(q), axis=0)
        weight = fold(dot(qs, both, NT))
        w_ref[b] = weight + pltpu.roll(weight, 64, 1)
        cx, cy, cz = cen_ref[0, box], cen_ref[1, box], cen_ref[2, box]
        lane4 = lane % 4
        far = jnp.where(lane4 == 0, cx, jnp.where(lane4 == 1, cy, cz))
        center = jnp.where(sub4 == 0, cx, jnp.where(sub4 == 1, cy, cz))
        p_ref[b] = jnp.where(sub4 == 3, far, center + 0.5 * x)
        rel = (0.5 * ROOT3) * x
        tgt = planes(rel, False)
        for unit in range(2):
            f_ref[b, unit] = jnp.concatenate([jnp.where(sub // 4 == unit, part, 0.0) for part in tgt], axis=0).astype(BF)
        src = jnp.concatenate(planes(rel, True) + [jnp.zeros((96, 128), F32)], axis=0).T.astype(BF)
        dist2 = dot(src[:, :32], f_ref[b, 0])
        value = stack_kernel(matern(dist2))
        near = fold(dot(jnp.concatenate([qs, qs], axis=1), value))
        base_ref[b] = near + q
        return carry

    lax.fori_loop(0, group, body, 0, unroll=4)


def gather_kernel(ids_ref, q_ref, w_ref, p_ref, out_ref):
    step = pl.program_id(0)
    group = out_ref.shape[0]
    sub4 = iota((8, 128), 0) % 4
    top = iota((8, 128), 0) < 4
    lane = iota((8, 128), 1)
    left = lane < 64

    def body(k, carry):
        peer = step * group + k
        near = [ids_ref[peer, j] for j in range(4)]
        far = [ids_ref[peer, 4 + j] for j in range(4)]
        for j in range(4):
            out_ref[k, 8 * j : 8 * j + 8] = q_ref[near[j]]
        w = [w_ref[far[j]] for j in range(4)]
        out_ref[k, 32:40] = jnp.where(left, w[0], w[2])
        out_ref[k, 40:48] = jnp.where(left, w[1], w[3])
        c = [p_ref[far[j]] for j in range(4)]
        centers = jnp.where(
            left, jnp.where(lane < 4, c[0], c[2]), jnp.where(lane < 68, c[1], c[3])
        )
        s = [p_ref[near[j]] for j in range(4)]
        out_ref[k, 48:56] = jnp.where(sub4 == 3, centers, jnp.where(top, s[0], s[1]))
        out_ref[k, 56:64] = jnp.where(sub4 == 3, centers, jnp.where(top, s[2], s[3]))
        return carry

    lax.fori_loop(0, group, body, 0, unroll=4)


def pair_kernel(
    tgt_ref, count_ref, got_ref, nc_ref, fc_ref, f_ref, fn_ref, base_ref, q_ref, t_ref, out_ref, term_ref, near_acc, far_acc
):
    step = pl.program_id(0)
    steps = pl.num_programs(0)
    group = got_ref.shape[0]
    boxes = f_ref.shape[0]
    sub = iota((8, 128), 0)
    lane = iota((8, 128), 1)
    left = lane < 64

    @pl.when(step == 0)
    def _():
        near_acc[...] = base_ref[...]
        far_acc[...] = jnp.zeros_like(far_acc)

    spread = (iota((128, 128), 0) // 64 == iota((128, 128), 1) // 64).astype(F32).astype(BF)

    def body(k, carry):
        peer = step * group + k
        tn = [tgt_ref[peer, j] for j in range(4)]
        tf = [tgt_ref[peer, 4 + j] for j in range(4)]
        points = [got_ref[k, 48:56], got_ref[k, 56:64]]
        feats = []
        for v in range(2):
            feats += planes((points[v] - nc_ref[k, 8 * v : 8 * v + 8]) * ROOT3, True)
        src = jnp.concatenate(feats + [jnp.zeros((64, 128), F32)], axis=0).T.astype(BF)
        for j in range(4):
            dist2 = dot(src[:, 32 * (j // 2) : 32 * (j // 2) + 32], f_ref[tn[j], j % 2])
            value = stack_kernel(matern(dist2))
            qs = jnp.concatenate(split(got_ref[k, 8 * j : 8 * j + 8]), axis=0)
            near_acc[tn[j]] += fold(dot(jnp.concatenate([qs, qs], axis=1), value))
        row = jnp.broadcast_to(points[0][3:4], (8, 128))
        row = jnp.where(lane % 64 == sub, row, 0.0)
        high = row.astype(BF)
        rest = row - high.astype(F32)
        mid = rest.astype(BF)
        low = (rest - mid.astype(F32)).astype(BF)
        cen = dot(jnp.concatenate([high, mid, low], axis=0), spread)
        rel = (fc_ref[k] - (cen[0:8] + cen[8:16] + cen[16:24])) * ROOT3
        tgt = jnp.concatenate(planes(rel, False), axis=0).astype(BF)
        value = stack_kernel(matern(dot(fn_ref[...], tgt)))
        ws = []
        for h in range(2):
            w = got_ref[k, 32 + 8 * h : 40 + 8 * h]
            for part in (jnp.where(left, w, 0.0), jnp.where(left, 0.0, w)):
                ws += list(split(part))
        ws = jnp.concatenate(ws, axis=0)
        locs = dot(jnp.concatenate([ws, ws], axis=1), value)
        for h in range(2):
            for u in range(2):
                at = 32 * h + 16 * u
                new = fold(locs[at : at + 16])
                far_acc[tf[2 * u + h]] += jnp.where(left if h == 0 else jnp.logical_not(left), new, 0.0)
        return carry

    lax.fori_loop(0, group, body, 0, unroll=2)

    @pl.when(step == steps - 1)
    def _():
        def finish(b, total):
            ls = jnp.concatenate(split(far_acc[b]), axis=0)
            both = t_ref[b]
            high, low = both[0:64], both[64:128]
            table = jnp.concatenate([high, high, low, low], axis=0)
            far = fold(dot(jnp.concatenate([ls, ls], axis=1), table))
            live = lane < count_ref[b]
            product = jnp.where(live, near_acc[b] + far, 0.0)
            out_ref[b] = product
            return total + product * q_ref[b]

        total = lax.fori_loop(0, boxes, finish, jnp.zeros((8, 128), F32), unroll=4)
        ones = jnp.ones((128, 128), F32)
        sums = lax.dot_general(ones, total, NT, precision=lax.Precision.HIGHEST, preferred_element_type=F32)
        term_ref[...] = jnp.concatenate([sums, jnp.zeros((128, 120), F32)], axis=1)


def far_sources():
    x = np.zeros((8, 128), np.float32)
    for n in range(64):
        for d, value in enumerate((NODE[n // 16], NODE[n // 4 % 4], NODE[n % 4])):
            for u in range(2):
                x[4 * u + d, 64 * u + n] = 0.5 * ROOT3 * value
    bf = lambda a: a.astype(jnp.bfloat16).astype(np.float32)
    high = bf(x)
    low = bf(x - high)
    norm = np.zeros_like(x)
    square = high * (high + 2 * low)
    for u in range(2):
        norm[4 * u + 3] = square[4 * u] + square[4 * u + 1] + square[4 * u + 2]
    one = bf(norm)
    two = bf(norm - one)
    three = bf(norm - one - two)
    sub = np.arange(8)[:, None] % 4
    unit = (np.arange(8)[:, None] // 4) == (np.arange(128)[None, :] // 64)
    parts = [
        np.where(sub == 3, one, high),
        np.where(sub == 3, two, high),
        np.where(sub == 3, 1.0, low),
        np.where(sub == 3, three, np.where(sub < 2, 1.0, 0.0)),
    ]
    return np.concatenate([np.where(unit, part, 0.0) for part in parts], axis=0).T.astype(np.float32)


def node_rows():
    out = np.zeros((8, 128), np.float32)
    for m in range(128):
        n = m % 64
        for u in range(2):
            for d, value in enumerate((NODE[n // 16], NODE[n // 4 % 4], NODE[n % 4])):
                out[4 * u + d, m] = 0.5 * value
    return out


def vmem(shape=None, index=None):
    if shape is None:
        return pl.BlockSpec(memory_space=pltpu.VMEM)
    return pl.BlockSpec(shape, index, memory_space=pltpu.VMEM)


SMEM = pl.BlockSpec(memory_space=pltpu.SMEM)


def params(mebibytes=56):
    return pltpu.CompilerParams(vmem_limit_bytes=mebibytes * 1024 * 1024)


def exchange(x):
    return lax.all_to_all(x, AXES, split_axis=0, concat_axis=0, tiled=True)


def general(local_pos, charges, counts, box_centers, far_list, near_list):
    devices = lax.axis_size("gx") * lax.axis_size("gy")
    boxes, _, slots = local_pos.shape
    struct = jax.ShapeDtypeStruct
    want = pl.pallas_call(
        ids_kernel,
        out_shape=struct((devices, 128), jnp.int32),
        in_specs=[vmem(), vmem()],
        out_specs=vmem(),
        compiler_params=params(),
        name="ids",
    )(far_list, near_list)
    served = exchange(want.reshape(devices, 1, 128)).reshape(devices, 128)

    group = 16
    lead = lambda shape: vmem((group,) + shape, lambda i: (i,) + (0,) * len(shape))
    q_tab, w_tab, p_tab, f_tab, base, table = pl.pallas_call(
        table_kernel,
        grid=(boxes // group,),
        out_shape=(
            struct((boxes, 8, 128), F32),
            struct((boxes, 8, 128), F32),
            struct((boxes, 8, 128), F32),
            struct((boxes, 2, 32, 128), BF),
            struct((boxes, 8, 128), F32),
            struct((boxes, 128, 128), BF),
        ),
        in_specs=[lead((3, 128)), lead((8, 128)), SMEM, SMEM],
        out_specs=(lead((8, 128)), lead((8, 128)), lead((8, 128)), lead((2, 32, 128)), lead((8, 128)), lead((128, 128))),
        compiler_params=params(),
        cost_estimate=pl.CostEstimate(flops=200_000_000, bytes_accessed=6_000_000, transcendentals=2_000_000),
        name="tables",
    )(local_pos, charges, counts, box_centers)

    send = pl.pallas_call(
        gather_kernel,
        grid=(devices // group,),
        out_shape=struct((devices, 64, 128), F32),
        in_specs=[SMEM, vmem(), vmem(), vmem()],
        out_specs=lead((64, 128)),
        compiler_params=params(),
        name="gather",
    )(served, q_tab, w_tab, p_tab)
    got = exchange(send)

    tgt = want[:, 16:24]
    centers = box_centers.T
    near_cen = jnp.pad(centers[tgt[:, :4]], ((0, 0), (0, 0), (0, 1))).reshape(devices, 16, 1)
    near_cen = jnp.broadcast_to(near_cen, (devices, 16, 128))
    far_cen = jnp.pad(centers[tgt[:, 4:]], ((0, 0), (0, 0), (0, 1))).reshape(devices, 2, 2, 4)
    far_cen = far_cen.transpose(0, 1, 3, 2).reshape(devices, 8, 2, 1)
    far_cen = jnp.broadcast_to(far_cen, (devices, 8, 2, 64)).reshape(devices, 8, 128) + node_rows()[None]

    product, term = pl.pallas_call(
        pair_kernel,
        grid=(devices // group,),
        out_shape=(struct((boxes, 8, 128), F32), struct((devices, 128), F32)),
        in_specs=[
            SMEM,
            SMEM,
            lead((64, 128)),
            lead((16, 128)),
            lead((8, 128)),
            vmem(),
            vmem(),
            vmem(),
            vmem(),
            vmem(),
        ],
        out_specs=(vmem(), vmem()),
        scratch_shapes=[pltpu.VMEM((boxes, 8, 128), F32), pltpu.VMEM((boxes, 8, 128), F32)],
        compiler_params=params(),
        cost_estimate=pl.CostEstimate(flops=1_000_000_000, bytes_accessed=12_000_000, transcendentals=20_000_000),
        name="pairs",
    )(tgt, counts, got, near_cen, far_cen, f_tab, jnp.asarray(far_sources(), BF), base, q_tab, table)

    terms = exchange(term.reshape(devices, 1, 128))[:, 0, :8]
    curvature = jnp.sum(terms, axis=0) / (devices * boxes * slots)
    return (product, curvature)


HALF = 64
ROWS = 44
NEAR_ROWS = 24
UNROLL = 4
CHUNKS = 16
AHEAD = 4


def upper_kernel(pos_ref, charge_ref, count_ref, row_ref, ex_ref):
    half = charge_ref.shape[0] // 2
    lane = iota((8, 128), 1)
    left = lane < HALF
    center = jnp.concatenate([row_ref[...], jnp.zeros((5, 2 * half), F32)], axis=0)
    center = jnp.concatenate([center, jnp.zeros((8, 128 - 2 * half), F32)], axis=1)
    center = jnp.concatenate([center, jnp.zeros((120, 128), F32)], axis=0).T
    wide = iota((half, 128), 1) < HALF
    for d in range(3):
        first = center[:half, d : d + 1] + 0.5 * pos_ref[d, :half]
        second = center[half : 2 * half, d : d + 1] + 0.5 * pos_ref[d, half:]
        ex_ref[(8 + d) * half : (9 + d) * half, :] = jnp.where(wide, pltpu.roll(first, HALF, 1), second)

    def body(b, carry):
        first = pltpu.roll(jnp.where(lane < count_ref[b], charge_ref[b], 0.0), HALF, 1)
        second = jnp.where(lane < count_ref[b + half], charge_ref[b + half], 0.0)
        ex_ref[pl.ds(pl.multiple_of(8 * b, 8), 8), :] = jnp.where(left, first, second)
        return carry

    lax.fori_loop(0, half, body, 0, unroll=16)


def start_kernel(
    far_ref, near_ref, most_ref, row_ref, count_ref, pos_hbm, charge_hbm, msg_hbm, want_ref, ex_ref,
    pos_ref, charge_ref, msg_ref, sems
):
    loads = [pltpu.make_async_copy(pos_hbm, pos_ref, sems.at[0]), pltpu.make_async_copy(charge_hbm, charge_ref, sems.at[1])]
    for copy in loads:
        copy.start()
    boxes = far_ref.shape[1]
    slots = far_ref.shape[0]
    peer = iota((128, 128), 0)
    line = iota((128, 128), 1)
    tri = (peer < line).astype(F32).astype(BF)
    full = jnp.ones((128, 128), BF)
    row32 = iota((32, 128), 0)
    kind = row32 // 4
    boxrow = iota((32, 128), 1) % boxes
    result = jnp.zeros((128, 32), F32)
    for ref, first, group in ((near_ref, 1, 0), (far_ref, 0, 1)):
        seen = jnp.zeros((128, 128), F32)
        for j in range(0, slots, 2):
            flat = jnp.concatenate([ref[first + j : first + j + 1, :], ref[first + j + 1 : first + j + 2, :]], axis=1)
            hit = jnp.broadcast_to(flat // boxes, (128, 128)) == peer
            onehot = hit.astype(F32).astype(BF)
            before = dot(onehot, tri) + seen
            rank = jnp.sum(jnp.where(hit, before, 0.0), axis=0, keepdims=True).astype(jnp.int32)
            if j + 2 < slots:
                seen = seen + dot(onehot, full)
            within = jnp.broadcast_to(flat % boxes, (32, 128))
            if group == 0:
                value = jnp.where(kind == 0, within * NEAR_ROWS, jnp.where(kind == 2, within * 8, 0))
            else:
                value = jnp.where(kind == 1, within * 8, 0)
            value = jnp.where(kind == 4 + group, boxrow, value)
            value = jnp.where(row32 % 4 == jnp.broadcast_to(rank, (32, 128)), value, 0).astype(F32).astype(BF)
            result = result + dot(onehot, value, NT)
    result = jnp.concatenate([result, jnp.zeros((128, 96), F32)], axis=1)
    heavy = (line == peer - peer % 4).astype(F32).astype(BF)
    first = dot(heavy, result.astype(BF))
    for at, base in ((8, 8), (24, 16)):
        extra = dot(jnp.where(line == base + peer % 4, first, 0.0).astype(BF), full)
        result = jnp.where(line == at, extra, result)
    most = jnp.max(most_ref[...], axis=1, keepdims=True).astype(F32)
    result = jnp.where(line == 9, jnp.broadcast_to(most, (128, 128)), result)
    want_ref[...] = result.astype(jnp.int32)
    rows = [jnp.concatenate([row_ref[d : d + 1, :]] * 2, axis=1) for d in range(3)]
    rows = [jnp.broadcast_to(row, (128, 128)) for row in rows]
    msg_ref[pl.ds(0, 128, stride=2), :] = jnp.where(line < HALF, result, rows[2])
    msg_ref[pl.ds(1, 128, stride=2), :] = jnp.where(line < HALF, rows[0], rows[1])
    store = pltpu.make_async_copy(msg_ref, msg_hbm, sems.at[2])
    store.start()
    for copy in loads:
        copy.wait()
    upper_kernel(pos_ref, charge_ref, count_ref, row_ref, ex_ref)
    store.wait()


def cheb_rows(x):
    sub = iota((8, 128), 0)
    second = 2.0 * x * x - 1.0
    third = 2.0 * x * second - x
    basis = []
    for i in range(NODES):
        theta = (2 * i + 1) * math.pi / 8
        basis.append(0.25 + 0.5 * (math.cos(theta) * x + math.cos(2 * theta) * second + math.cos(3 * theta) * third))
    row = lambda i, d: jnp.broadcast_to(basis[i][d : d + 1], (8, 128))
    sub4 = sub % 4
    zs = jnp.where(sub4 == 0, row(0, 2), jnp.where(sub4 == 1, row(1, 2), jnp.where(sub4 == 2, row(2, 2), row(3, 2))))
    ys = [jnp.where(sub < 4, row(0, 1), row(1, 1)) * zs, jnp.where(sub < 4, row(2, 1), row(3, 1)) * zs]
    return jnp.concatenate([row(i, 0) * ys[j] for i in range(NODES) for j in range(2)], axis=0)


def point_rows(pos_ref, b):
    sub4 = iota((8, 128), 0) % 4
    x = jnp.zeros((8, 128), F32)
    for d in range(3):
        x = jnp.where(sub4 == d, jnp.broadcast_to(pos_ref[d, pl.ds(b, 1), :], (8, 128)), x)
    return x


def doubled(x):
    return jnp.where(iota((8, 128), 1) < HALF, x, pltpu.roll(x, HALF, 1))


def fill_basis(pos_ref, basis_ref):
    for d in range(3):
        x = pos_ref[d]
        second = 2.0 * x * x - 1.0
        third = 2.0 * x * second - x
        for i in range(NODES):
            theta = (2 * i + 1) * math.pi / 8
            value = math.cos(theta) * x + math.cos(2 * theta) * second + math.cos(3 * theta) * third
            basis_ref[4 * d + i] = 0.25 + 0.5 * value


def basis_table(basis_ref, b):
    sub = iota((8, 128), 0)
    row = lambda i, d: jnp.broadcast_to(basis_ref[4 * d + i, pl.ds(b, 1), :], (8, 128))
    sub4 = sub % 4
    zs = jnp.where(sub4 == 0, row(0, 2), jnp.where(sub4 == 1, row(1, 2), jnp.where(sub4 == 2, row(2, 2), row(3, 2))))
    ys = [jnp.where(sub < 4, row(0, 1), row(1, 1)) * zs, jnp.where(sub < 4, row(2, 1), row(3, 1)) * zs]
    return jnp.concatenate([row(i, 0) * ys[j] for i in range(NODES) for j in range(2)], axis=0)


def send_table_kernel(pos_ref, charge_ref, count_ref, cen_ref, near_ref, far_ref, basis_ref):
    boxes = charge_ref.shape[0]
    lane = iota((8, 128), 1)
    sub = iota((8, 128), 0)
    fill_basis(pos_ref, basis_ref)

    def body(b, carry):
        q = jnp.where(lane < count_ref[b], charge_ref[b], 0.0)
        near_ref[b, 0:8] = doubled(q)
        x, y, z = [doubled(cen_ref[d, b] + 0.5 * jnp.broadcast_to(pos_ref[d, pl.ds(b, 1), :], (8, 128))) for d in range(3)]
        near_ref[b, 8:16] = jnp.where(sub == 4, x, jnp.where(sub == 5, y, z))
        near_ref[b, 16:24] = jnp.where(sub == 7, x, jnp.where((sub == 3) | (sub == 5), y, z))
        table = basis_table(basis_ref, b)
        qs = jnp.concatenate(split(q), axis=0)
        weight = fold(dot(qs, stack_kernel(table), NT))
        far_ref[b] = weight + pltpu.roll(weight, 64, 1)
        return carry

    lax.fori_loop(0, boxes, body, 0, unroll=32)


def own_table_kernel(pos_ref, charge_ref, count_ref, q_ref, f_ref, base_ref):
    boxes = charge_ref.shape[0]
    sub = iota((8, 128), 0)
    lane = iota((8, 128), 1)

    def body(b, carry):
        q = jnp.where(lane < count_ref[b], charge_ref[b], 0.0)
        q_ref[b] = q
        x = point_rows(pos_ref, b)
        rel = (0.5 * ROOT3) * x
        tgt = planes(rel, False)
        for unit in range(2):
            f_ref[b, unit] = jnp.concatenate([jnp.where(sub // 4 == unit, part, 0.0) for part in tgt], axis=0).astype(BF)
        zero = jnp.zeros((96, 128), F32)
        src = jnp.concatenate(planes(rel, True) + [zero], axis=0).T.astype(BF)
        first = jnp.concatenate([jnp.where(sub < 4, part, 0.0) for part in tgt] + [zero], axis=0).astype(BF)
        value = stack_kernel(matern(dot(src, first)))
        qs = jnp.concatenate(split(q), axis=0)
        base_ref[b] = fold(dot(jnp.concatenate([qs, qs], axis=1), value)) + q
        return carry

    lax.fori_loop(0, boxes, body, 0, unroll=4)


def goal_kernel(want_ref, served_ref, cen_ref, node_ref, nc_ref, fc_ref, ec_ref, goal_ref, odd_ref):
    lane = iota((128, 128), 1)
    left = lane < HALF
    boxes = cen_ref.shape[1]
    cen = jnp.concatenate([cen_ref[...], jnp.zeros((5, boxes), F32)], axis=0)
    cen = jnp.concatenate([cen, jnp.zeros((8, 128 - boxes), F32)], axis=1)
    cen = jnp.concatenate([cen, jnp.zeros((120, 128), F32)], axis=0).T

    def split3(x, axis):
        high = x.astype(BF)
        rest = x - high.astype(F32)
        mid = rest.astype(BF)
        return jnp.concatenate([high, mid, (rest - mid.astype(F32)).astype(BF)], axis=axis)

    parts = split3(cen, 0)
    want = want_ref[...]
    goal_ref[...] = want.astype(F32).T[16:32].astype(jnp.int32)
    sources = [served_ref[pl.ds(1, 128, stride=2), :], served_ref[pl.ds(0, 128, stride=2), :]]
    halves = [jnp.concatenate([(iota((128, 128), 0) // HALF == h).astype(F32).astype(BF)] * 3, axis=0) for h in range(2)]

    def column(at):
        return jnp.broadcast_to(want[:, at : at + 1], (128, 128))

    def centers(at):
        onehot = (column(at) == lane).astype(F32).astype(BF)
        found = dot(jnp.concatenate([onehot] * 3, axis=1), parts)
        return [jnp.broadcast_to(found[:, d : d + 1], (128, 128)) for d in range(3)]

    def gaps(j):
        mine = lane % HALF == column(4 + j) // 8
        both = [split3(jnp.where(mine, source, 0.0), 1) for source in sources]
        theirs = [dot(both[0], halves[0]), dot(both[0], halves[1]), dot(both[1], halves[1])]
        return [a - b for a, b in zip(centers(20 + j), theirs)]

    nc_ref[...] = jnp.zeros_like(nc_ref)
    fc_ref[...] = jnp.zeros_like(fc_ref)
    ec_ref[...] = jnp.zeros_like(ec_ref)
    for u in range(2):
        first, second = centers(16 + 2 * u), centers(17 + 2 * u)
        for d in range(3):
            nc_ref[pl.ds(4 * u + d, 128, stride=8), :] = jnp.where(left, first[d], second[d])
        first, second = gaps(2 * u), gaps(2 * u + 1)
        for d in range(3):
            fc_ref[pl.ds(4 * u + d, 128, stride=8), :] = jnp.where(left, first[d], second[d]) + node_ref[d : d + 1, :]
    extra = centers(24)
    for d in range(3):
        odd_ref[...] = extra[d]
        even, odd = odd_ref[pl.ds(0, 64, stride=2), :], odd_ref[pl.ds(1, 64, stride=2), :]
        ec_ref[pl.ds(d, 64, stride=8), :] = jnp.where(left[:64], even, odd)


def far_kernel(fc_ref, fn_ref, out_ref):
    group = fc_ref.shape[0]
    tgt = jnp.concatenate(planes(fc_ref[...] * ROOT3, False), axis=1).astype(BF)
    for k in range(group):
        out_ref[k] = stack_kernel(matern(dot(fn_ref[...], tgt[k])))


def send_kernel(member_ref, served_ref, near_ref, far_ref, own_ref, *refs):
    moved, (out_ref, ids_ref, int_ref, ex_ref, buf_ref, sems) = refs[:3], refs[3:]
    peers = ids_ref.shape[1]
    sub = iota((8, 128), 0)
    lane = iota((8, 128), 1)
    left = lane < HALF
    keep = left | (sub < 3)
    second = sub < 5
    int_ref[...] = served_ref[pl.ds(0, peers, stride=2), :].T[:16].astype(jnp.int32)
    copy = pltpu.make_async_copy(int_ref, ids_ref, sems.at[0])
    copy.start()
    half = ex_ref.shape[0] // 16
    packed = moved[0][...] + moved[1][...] + moved[2][...]
    packed = jnp.where(member_ref[0] == 0, own_ref[...], packed)
    for d in range(3):
        rows = packed[(8 + d) * half : (9 + d) * half]
        ex_ref[pl.ds(d, half, stride=8), :] = pltpu.roll(rows, HALF, 1)
        ex_ref[pl.ds(8 * half + d, half, stride=8), :] = rows
    for b in range(half):
        tile = packed[8 * b : 8 * b + 8]
        for at, part in ((8 * b, tile), (8 * (b + half), pltpu.roll(tile, HALF, 1))):
            ex_ref[at : at + 8, :] = jnp.where(left, part, jnp.where(sub < 3, ex_ref[at : at + 8, :], 0.0))
    copy.wait()

    def body(i, carry):
        base = pl.multiple_of(i * 2 * ROWS, 8)
        for k in range(2):
            peer = 2 * i + k
            at = lambda row: pl.ds(base + (k * ROWS + row), 8)
            rows = lambda ref, j, row: ref[pl.ds(pl.multiple_of(ids_ref[j, peer], 8) + row, 8), :]
            q = [rows(near_ref, j, 0) for j in range(4)]
            w = [rows(far_ref, 4 + j, 0) for j in range(4)]
            p = [rows(near_ref, j, 16 if j < 2 else 8) for j in range(4)]
            buf_ref[at(0), :] = jnp.where(left, q[0], q[1])
            buf_ref[at(8), :] = jnp.where(left, q[2], q[3])
            buf_ref[at(16), :] = jnp.where(left, w[0], w[2])
            buf_ref[at(24), :] = jnp.where(left, w[1], w[3])
            buf_ref[at(36), :] = jnp.where(sub == 7, jnp.where(left, p[0], p[1]), jnp.where(left, p[2], p[3]))
            buf_ref[at(32), :] = jnp.where(keep, rows(ex_ref, 8, 0), jnp.where(second, p[1], p[0]))
        return carry

    chunks = 8
    each = peers // chunks
    stores = []
    for c in range(chunks):
        lax.fori_loop(c * each // 2, (c + 1) * each // 2, body, 0, unroll=8)
        at = pl.ds(c * each * ROWS, each * ROWS)
        stores.append(pltpu.make_async_copy(buf_ref.at[at], out_ref.at[at], sems.at[1 + c]))
        stores[-1].start()
    for copy in stores:
        copy.wait()


def duo_kernel(
    scale, got_ref, want_hbm, nc_hbm, ec_hbm, f_hbm, base_hbm, q_hbm, w_hbm, v_hbm, near0_hbm, near1_hbm, far0_hbm, far1_hbm, term_ref,
    tgt_ref, nc_ref, ec_ref, f_ref, base_ref, q_ref, w_ref, v_ref, sems, *bufs
):
    whole = [(want_hbm, tgt_ref), (nc_hbm, nc_ref), (ec_hbm, ec_ref), (f_hbm, f_ref)]
    whole += [(base_hbm, base_ref), (q_hbm, q_ref), (w_hbm, w_ref)]
    loads = [pltpu.make_async_copy(source, target, sems.at[i]) for i, (source, target) in enumerate(whole)]
    for copy in loads[:4]:
        copy.start()
    chunk = v_ref.shape[0] // CHUNKS

    def far_values(c):
        at = pl.ds(c * chunk, chunk)
        return pltpu.make_async_copy(v_hbm.at[at], v_ref.at[at], sems.at[16 + c % AHEAD])

    for c in range(AHEAD):
        far_values(c).start()
    xt_refs, dist_refs, value_refs = bufs[:2], (bufs[2:7], bufs[7:12]), (bufs[12:17], bufs[17:22])
    near_accs, far_accs = bufs[22:24], bufs[24:26]
    duos = ec_ref.shape[0]
    boxes = f_ref.shape[0]
    sub = iota((8, 128), 0)
    lane = iota((8, 128), 1)
    left = lane < HALF
    for ref in value_refs[1] + near_accs + far_accs:
        ref[...] = jnp.zeros_like(ref)
    for ref in dist_refs[1]:
        ref[...] = jnp.full(ref.shape, 1e6, F32)
    def tile(duo, a, row):
        return got_ref[pl.ds(pl.multiple_of(duo * 2 * ROWS, 8) + (a * ROWS + row), 8), :]

    def extra(duo):
        return tile(duo, 0, 32), tile(duo, 1, 32)

    def goals(duo):
        pairs = [(tgt_ref[2 * (k % 2), 2 * duo + k // 2], tgt_ref[2 * (k % 2) + 1, 2 * duo + k // 2]) for k in range(4)]
        return pairs + [(tgt_ref[8, 2 * duo], tgt_ref[8, 2 * duo + 1])]

    def halves(x):
        high = x.astype(BF).astype(F32)
        both = [high, x - high]
        return [jnp.where(left, part, 0.0) for part in both] + [jnp.where(left, 0.0, part) for part in both]

    def products(duo, value):
        ex = extra(duo)
        tiles = [tile(duo, k // 2, 8 * (k % 2)) for k in range(4)]
        tiles.append(jnp.where(left, ex[0], pltpu.roll(ex[1], HALF, 1)))
        for k, goal in enumerate(goals(duo)):
            qs = jnp.concatenate(halves(tiles[k]), axis=0).astype(BF)
            new = dot(jnp.concatenate([qs, qs], axis=1), value[k][...])
            for h in range(2):
                near_accs[h][goal[h]] += fold(new[16 * h : 16 * h + 16])

    def far_products(duo):
        for a in range(2):
            ws = []
            for h in range(2):
                ws += halves(tile(duo, a, 16 + 8 * h))
            ws = jnp.concatenate(ws, axis=0).astype(BF)
            new = dot(jnp.concatenate([ws, ws], axis=1), v_ref[2 * duo + a])
            for h in range(2):
                for u in range(2):
                    at = 32 * h + 16 * u
                    far_accs[h][tgt_ref[4 + 2 * u + h, 2 * duo + a]] += fold(new[at : at + 16])

    def values(dist, value):
        for k in range(5):
            value[k][...] = stack_kernel(matern(dist[k][...]))

    def distances(duo, xt, dist):
        for k, goal in enumerate(goals(duo)):
            v, u = k // 2, k % 2
            for half in range(2):
                pieces = [jnp.zeros((32 * v, 128), BF)] if v else []
                pieces += [f_ref[goal[half], u], jnp.zeros((96 - 32 * v, 128), BF)]
                at = slice(64 * half, 64 * half + 64)
                dist[k][at, :] = dot(xt[at, :], jnp.concatenate(pieces, axis=0))

    def features(duo, xt):
        ex = extra(duo)
        turned = [pltpu.roll(x, HALF, 1) for x in ex]
        feats = []
        for a in range(2):
            full = tile(duo, a, 36)
            split_rows = jnp.where(left, pltpu.roll(turned[a], 4, 0), pltpu.roll(ex[a], 6, 0))
            point = jnp.where(sub >= 4, full, jnp.where(sub == 0, pltpu.roll(full, 1, 0), split_rows))
            feats += planes((point - nc_ref[2 * duo + a]) * ROOT3, True)
        point = jnp.where(left, turned[0], ex[1])
        feats += planes((point - ec_ref[duo]) * ROOT3, True)
        feats.append(jnp.zeros((32, 128), F32))
        xt[...] = jnp.concatenate(feats, axis=0).T.astype(BF)

    turns = duos // UNROLL
    assert turns == CHUNKS

    def body(i, carry):
        far_values(i).wait()

        @pl.when(i + AHEAD < CHUNKS)
        def _():
            far_values(i + AHEAD).start()

        for s in range(UNROLL):
            now, was = s % 2, 1 - s % 2
            step = UNROLL * i + s
            products(jnp.maximum(step - 2, 0), value_refs[was])
            far_products(step)
            values(dist_refs[was], value_refs[now])
            distances(step, xt_refs[was], dist_refs[now])
            features(jnp.minimum(step + 1, duos - 1), xt_refs[now])
        return carry

    for copy in loads[:4]:
        copy.wait()
    features(0, xt_refs[1])
    for copy in loads[4:]:
        copy.start()
    lax.fori_loop(0, turns, body, 0)
    products(duos - 2, value_refs[1])
    values(dist_refs[1], value_refs[0])
    products(duos - 1, value_refs[0])

    sums = (near0_hbm, near1_hbm, far0_hbm, far1_hbm)
    stores = [pltpu.make_async_copy(a, b, sems.at[8 + i]) for i, (a, b) in enumerate(zip(near_accs + far_accs, sums))]
    for copy in stores:
        copy.start()
    for copy in loads[4:]:
        copy.wait()

    def finish(b, total):
        near = near_accs[0][b] + near_accs[1][b] + base_ref[b]
        far = jnp.where(left, far_accs[0][b], far_accs[1][b])
        return total + near * q_ref[b] + far * w_ref[b]

    total = lax.fori_loop(0, boxes, finish, jnp.zeros((8, 128), F32), unroll=16)
    ones = jnp.ones((128, 128), F32)
    sums = lax.dot_general(ones, total, NT, precision=lax.Precision.HIGHEST, preferred_element_type=F32)
    term_ref[...] = jnp.concatenate([sums * scale, jnp.zeros((128, 120), F32)], axis=1)
    for copy in stores:
        copy.wait()


def finish_kernel(count_ref, pos_ref, near0_ref, near1_ref, far0_ref, far1_ref, base_ref, out_ref, basis_ref):
    boxes = base_ref.shape[0]
    lane = iota((8, 128), 1)
    fill_basis(pos_ref, basis_ref)

    def body(b, carry):
        locs = jnp.where(lane < HALF, far0_ref[b], far1_ref[b])
        ls = jnp.concatenate(split(locs), axis=0)
        high, low = split(basis_table(basis_ref, b))
        far = fold(dot(jnp.concatenate([ls, ls], axis=1), jnp.concatenate([high, high, low, low], axis=0)))
        near = near0_ref[b] + near1_ref[b] + base_ref[b]
        out_ref[b] = jnp.where(lane < count_ref[b], near + far, 0.0)
        return carry

    lax.fori_loop(0, boxes, body, 0, unroll=16)


def on_device(local_pos, charges, counts, box_centers, far_list, near_list):
    devices = lax.axis_size("gx") * lax.axis_size("gy")
    boxes, _, slots = local_pos.shape
    struct = jax.ShapeDtypeStruct
    hbm = pltpu.HBM
    stay = lambda x: pltpu.with_memory_space_constraint(x, pltpu.HBM)
    anywhere = pl.BlockSpec(memory_space=pltpu.HBM)
    pos = jnp.transpose(local_pos, (1, 0, 2))
    table = struct((boxes, 8, 128), F32)
    flat = lambda x: x.reshape(-1, 128)
    member = (lax.axis_index("gy") % 4).astype(jnp.int32).reshape(1)
    msg, want, ex_own = pl.pallas_call(
        start_kernel,
        out_shape=(
            hbm((devices * 2, 128), F32),
            struct((devices, 128), jnp.int32),
            struct((boxes * 11 // 2, 128), F32),
        ),
        in_specs=[vmem()] * 4 + [SMEM, anywhere, anywhere],
        out_specs=(anywhere, vmem(), vmem()),
        scratch_shapes=[
            pltpu.VMEM((3, boxes, 128), F32),
            pltpu.VMEM((boxes, 8, 128), F32),
            pltpu.VMEM((devices * 2, 128), F32),
            pltpu.SemaphoreType.DMA((3,)),
        ],
        compiler_params=params(8),
        name="start",
    )(far_list.T, near_list.T, counts.reshape(1, boxes), box_centers, counts, stay(pos), stay(charges))
    moved = [lax.ppermute(ex_own, "gy", [(4 * z, 4 * z + k) for z in range(4)]) for k in range(1, 4)]
    served = flat(exchange(msg.reshape(devices, 2, 128)))

    near_tab, far_tab = pl.pallas_call(
        send_table_kernel,
        out_shape=(struct((boxes, NEAR_ROWS, 128), F32), table),
        in_specs=[vmem(), vmem(), SMEM, SMEM],
        out_specs=(vmem(), vmem()),
        scratch_shapes=[pltpu.VMEM((12, boxes, 128), F32)],
        compiler_params=params(8),
        cost_estimate=pl.CostEstimate(flops=50_000_000, bytes_accessed=1_200_000, transcendentals=0),
        name="send_tables",
    )(pos, charges, counts, box_centers)

    send = pl.pallas_call(
        send_kernel,
        out_shape=hbm((devices * ROWS, 128), F32),
        in_specs=[SMEM] + [vmem()] * 7,
        out_specs=anywhere,
        scratch_shapes=[
            pltpu.SMEM((16, devices), jnp.int32),
            pltpu.VMEM((16, devices), jnp.int32),
            pltpu.VMEM((boxes * 8, 128), F32),
            pltpu.VMEM((devices * ROWS, 128), F32),
            pltpu.SemaphoreType.DMA((9,)),
        ],
        compiler_params=params(12),
        name="send",
    )(member, served, flat(near_tab), flat(far_tab), ex_own, *moved)
    got = flat(exchange(send.reshape(devices, ROWS // 4, 4, 128)))

    q_tab, f_tab, base = pl.pallas_call(
        own_table_kernel,
        out_shape=(hbm((boxes, 8, 128), F32), hbm((boxes, 2, 32, 128), BF), hbm((boxes, 8, 128), F32)),
        in_specs=[vmem(), vmem(), SMEM],
        out_specs=(vmem(), vmem(), vmem()),
        compiler_params=params(8),
        cost_estimate=pl.CostEstimate(flops=200_000_000, bytes_accessed=4_000_000, transcendentals=2_000_000),
        name="own_tables",
    )(pos, charges, counts)

    near_cen, far_gap, ex_cen, goals = pl.pallas_call(
        goal_kernel,
        out_shape=(
            hbm((devices * 8, 128), F32),
            hbm((devices * 8, 128), F32),
            hbm((devices * 4, 128), F32),
            hbm((16, devices), jnp.int32),
        ),
        in_specs=[vmem()] * 4,
        out_specs=(vmem(),) * 4,
        scratch_shapes=[pltpu.VMEM((128, 128), F32)],
        compiler_params=params(8),
        cost_estimate=pl.CostEstimate(flops=50_000_000, bytes_accessed=2_000_000, transcendentals=0),
        name="goals",
    )(want, served, box_centers, jnp.asarray(node_rows()))
    near_cen, far_gap, ex_cen = [x.reshape(-1, 8, 128) for x in (near_cen, far_gap, ex_cen)]
    group = 8
    far_value = pl.pallas_call(
        far_kernel,
        grid=(devices // group,),
        out_shape=hbm((devices, 256, 128), BF),
        in_specs=[vmem((group, 8, 128), lambda i: (i, 0, 0)), vmem()],
        out_specs=vmem((group, 256, 128), lambda i: (i, 0, 0)),
        compiler_params=params(8),
        cost_estimate=pl.CostEstimate(flops=200_000_000, bytes_accessed=9_000_000, transcendentals=4_000_000),
        name="far_values",
    )(far_gap, jnp.asarray(far_sources(), BF))

    big = lambda dtype, rows: pltpu.VMEM((rows, 128), dtype)
    *sums, term = pl.pallas_call(
        functools.partial(duo_kernel, 1.0 / (devices * boxes * slots)),
        out_shape=(hbm((boxes, 8, 128), F32),) * 4 + (struct((devices, 128), F32),),
        in_specs=[vmem()] + [anywhere] * 8,
        out_specs=(anywhere,) * 4 + (vmem(),),
        scratch_shapes=[
            pltpu.SMEM((16, devices), jnp.int32),
            pltpu.VMEM((devices, 8, 128), F32),
            pltpu.VMEM((devices // 2, 8, 128), F32),
            pltpu.VMEM((boxes, 2, 32, 128), BF),
            pltpu.VMEM((boxes, 8, 128), F32),
            pltpu.VMEM((boxes, 8, 128), F32),
            pltpu.VMEM((boxes, 8, 128), F32),
            pltpu.VMEM((devices, 256, 128), BF),
            pltpu.SemaphoreType.DMA((20,)),
        ]
        + [big(BF, 128)] * 2
        + [big(F32, 128)] * 10
        + [big(BF, 256)] * 10
        + [pltpu.VMEM((boxes, 8, 128), F32)] * 4,
        compiler_params=params(28),
        cost_estimate=pl.CostEstimate(flops=1_000_000_000, bytes_accessed=12_000_000, transcendentals=20_000_000),
        name="pairs",
    )(got, *[stay(x) for x in (goals, near_cen, ex_cen, f_tab, base, q_tab, far_tab, far_value)])

    terms = exchange(term.reshape(devices, 1, 128))[:, 0, :8]
    curvature = jnp.sum(terms, axis=0)
    product = pl.pallas_call(
        finish_kernel,
        out_shape=table,
        in_specs=[SMEM] + [vmem()] * 6,
        out_specs=vmem(),
        scratch_shapes=[pltpu.VMEM((12, boxes, 128), F32)],
        compiler_params=params(8),
        cost_estimate=pl.CostEstimate(flops=50_000_000, bytes_accessed=3_000_000, transcendentals=0),
        name="finish",
    )(counts, pos, *[stay(x) for x in (*sums, base)])
    over = jnp.any((served.reshape(devices, 2, 128)[:, 0, 9] > HALF) & (jnp.arange(devices) % 4 != 0))
    whole = (local_pos, charges, counts, box_centers, far_list, near_list)
    return lax.cond(over, lambda: general(*whole), lambda: (product, curvature))


def solution(mesh):
    in_specs = (
        P(AXES, None, None),
        P(AXES, None, None),
        P(AXES),
        P(None, AXES),
        P(AXES, None),
        P(AXES, None),
    )
    out_specs = (P(AXES, None, None), P())
    return jax.shard_map(on_device, mesh=mesh, in_specs=in_specs, out_specs=out_specs, check_vma=False)
```

```python
import functools
import math

import jax
import jax.numpy as jnp
import numpy as np
from jax import lax
from jax.experimental import pallas as pl
from jax.experimental.pallas import tpu as pltpu
from jax.sharding import PartitionSpec as P

AXES = ("gx", "gy")
NODES = 4
ROOT3 = 1.7320508075688772
LOG2E = 1.4426950408889634
BF = jnp.bfloat16
F32 = jnp.float32
NODE = [math.cos((2 * i + 1) * math.pi / 8) for i in range(NODES)]
NT = (((1,), (1,)), ((), ()))
TN = (((0,), (0,)), ((), ()))


def iota(shape, dim):
    return lax.broadcasted_iota(jnp.int32, shape, dim)


def dot(a, b, dims=None):
    if dims is None:
        return jnp.dot(a, b, preferred_element_type=F32)
    return lax.dot_general(a, b, dims, preferred_element_type=F32)


def split(x):
    high = x.astype(BF)
    return high, (x - high.astype(F32)).astype(BF)


def planes(rel, source):
    axis = rel.ndim - 2
    sub = iota(rel.shape, axis) % 4
    last = sub == 3
    rel = jnp.where(last, 0.0, rel)
    high = rel.astype(BF).astype(F32)
    low = (rel - high).astype(BF).astype(F32)
    square = high * (high + 2.0 * low)
    norm = pltpu.roll(square, 1, axis) + pltpu.roll(square, 2, axis) + pltpu.roll(square, 3, axis)
    one = norm.astype(BF).astype(F32)
    rest = norm - one
    two = rest.astype(BF).astype(F32)
    three = (rest - two).astype(BF).astype(F32)
    if source:
        parts = [
            jnp.where(last, one, high),
            jnp.where(last, two, high),
            jnp.where(last, 1.0, low),
            jnp.where(last, three, jnp.where(sub < 2, 1.0, 0.0)),
        ]
    else:
        parts = [
            jnp.where(last, 1.0, -2.0 * high),
            jnp.where(last, 1.0, -2.0 * low),
            jnp.where(last, one, -2.0 * high),
            jnp.where(
                sub == 0,
                pltpu.roll(two, 5, axis),
                jnp.where(sub == 1, pltpu.roll(three, 6, axis), jnp.where(last, 1.0, 0.0)),
            ),
        ]
    return parts


def matern(dist2):
    safe = jnp.maximum(dist2, 1e-12)
    scaled = safe * lax.rsqrt(safe)
    decay = jnp.exp2(scaled * (-LOG2E))
    return decay + scaled * decay


def stack_kernel(value):
    high, low = split(value)
    return jnp.concatenate([high, low], axis=0)


def fold(x):
    return x[0:8] + x[8:16]


def ids_kernel(far_ref, near_ref, want_ref):
    boxes = far_ref.shape[0]
    slots = far_ref.shape[1]
    total = boxes * slots
    lane = iota((total, 128), 1)
    box = iota((total, 128), 0) % boxes
    tri = (iota((total, total), 0) > iota((total, total), 1)).astype(F32).astype(BF)
    result = jnp.zeros((128, 128), F32)
    for ref, first, base in ((near_ref, 1, 0), (far_ref, 0, 4)):
        flat = jnp.concatenate([ref[:, first + j : first + j + 1] for j in range(slots)], axis=0)
        flat = jnp.broadcast_to(flat, (total, 128))
        hit = (flat // boxes) == lane
        onehot = hit.astype(F32).astype(BF)
        before = dot(tri, onehot)
        rank = jnp.sum(jnp.where(hit, before, 0.0), axis=1, keepdims=True).astype(jnp.int32)
        mine = rank == (lane % 4)
        within = jnp.where((lane >= base) & (lane < base + 4), flat % boxes, 0)
        owner = jnp.where((lane >= base + 16) & (lane < base + 20), box, 0)
        value = jnp.where(mine, within + owner, 0).astype(F32).astype(BF)
        result = result + dot(onehot, value, TN)
    want_ref[...] = result.astype(jnp.int32)


def table_kernel(pos_ref, charge_ref, count_ref, cen_ref, q_ref, w_ref, p_ref, f_ref, base_ref, t_ref):
    step = pl.program_id(0)
    group = pos_ref.shape[0]
    sub = iota((8, 128), 0)
    lane = iota((8, 128), 1)

    def body(b, carry):
        box = step * group + b
        live = lane < count_ref[box]
        q = jnp.where(live, charge_ref[b], 0.0)
        q_ref[b] = q
        pos = pos_ref[b]
        zero1 = jnp.zeros((1, 128), F32)
        x4 = jnp.concatenate([pos, zero1], axis=0)
        x = jnp.concatenate([x4, x4], axis=0)
        second = 2.0 * x * x - 1.0
        third = 2.0 * x * second - x
        basis = []
        for i in range(NODES):
            theta = (2 * i + 1) * math.pi / 8
            basis.append(0.25 + 0.5 * (math.cos(theta) * x + math.cos(2 * theta) * second + math.cos(3 * theta) * third))
        row = lambda i, d: jnp.broadcast_to(basis[i][d : d + 1], (8, 128))
        sub4 = sub % 4
        zs = jnp.where(sub4 == 0, row(0, 2), jnp.where(sub4 == 1, row(1, 2), jnp.where(sub4 == 2, row(2, 2), row(3, 2))))
        ys = [jnp.where(sub < 4, row(0, 1), row(1, 1)) * zs, jnp.where(sub < 4, row(2, 1), row(3, 1)) * zs]
        table = jnp.concatenate([row(i, 0) * ys[j] for i in range(NODES) for j in range(2)], axis=0)
        both = stack_kernel(table)
        t_ref[b] = both
        qs = jnp.concatenate(split(q), axis=0)
        weight = fold(dot(qs, both, NT))
        w_ref[b] = weight + pltpu.roll(weight, 64, 1)
        cx, cy, cz = cen_ref[0, box], cen_ref[1, box], cen_ref[2, box]
        lane4 = lane % 4
        far = jnp.where(lane4 == 0, cx, jnp.where(lane4 == 1, cy, cz))
        center = jnp.where(sub4 == 0, cx, jnp.where(sub4 == 1, cy, cz))
        p_ref[b] = jnp.where(sub4 == 3, far, center + 0.5 * x)
        rel = (0.5 * ROOT3) * x
        tgt = planes(rel, False)
        for unit in range(2):
            f_ref[b, unit] = jnp.concatenate([jnp.where(sub // 4 == unit, part, 0.0) for part in tgt], axis=0).astype(BF)
        src = jnp.concatenate(planes(rel, True) + [jnp.zeros((96, 128), F32)], axis=0).T.astype(BF)
        dist2 = dot(src[:, :32], f_ref[b, 0])
        value = stack_kernel(matern(dist2))
        near = fold(dot(jnp.concatenate([qs, qs], axis=1), value))
        base_ref[b] = near + q
        return carry

    lax.fori_loop(0, group, body, 0, unroll=4)


def gather_kernel(ids_ref, q_ref, w_ref, p_ref, out_ref):
    step = pl.program_id(0)
    group = out_ref.shape[0]
    sub4 = iota((8, 128), 0) % 4
    top = iota((8, 128), 0) < 4
    lane = iota((8, 128), 1)
    left = lane < 64

    def body(k, carry):
        peer = step * group + k
        near = [ids_ref[peer, j] for j in range(4)]
        far = [ids_ref[peer, 4 + j] for j in range(4)]
        for j in range(4):
            out_ref[k, 8 * j : 8 * j + 8] = q_ref[near[j]]
        w = [w_ref[far[j]] for j in range(4)]
        out_ref[k, 32:40] = jnp.where(left, w[0], w[2])
        out_ref[k, 40:48] = jnp.where(left, w[1], w[3])
        c = [p_ref[far[j]] for j in range(4)]
        centers = jnp.where(
            left, jnp.where(lane < 4, c[0], c[2]), jnp.where(lane < 68, c[1], c[3])
        )
        s = [p_ref[near[j]] for j in range(4)]
        out_ref[k, 48:56] = jnp.where(sub4 == 3, centers, jnp.where(top, s[0], s[1]))
        out_ref[k, 56:64] = jnp.where(sub4 == 3, centers, jnp.where(top, s[2], s[3]))
        return carry

    lax.fori_loop(0, group, body, 0, unroll=4)


def pair_kernel(
    tgt_ref, count_ref, got_ref, nc_ref, fc_ref, f_ref, fn_ref, base_ref, q_ref, t_ref, out_ref, term_ref, near_acc, far_acc
):
    step = pl.program_id(0)
    steps = pl.num_programs(0)
    group = got_ref.shape[0]
    boxes = f_ref.shape[0]
    sub = iota((8, 128), 0)
    lane = iota((8, 128), 1)
    left = lane < 64

    @pl.when(step == 0)
    def _():
        near_acc[...] = base_ref[...]
        far_acc[...] = jnp.zeros_like(far_acc)

    spread = (iota((128, 128), 0) // 64 == iota((128, 128), 1) // 64).astype(F32).astype(BF)

    def body(k, carry):
        peer = step * group + k
        tn = [tgt_ref[peer, j] for j in range(4)]
        tf = [tgt_ref[peer, 4 + j] for j in range(4)]
        points = [got_ref[k, 48:56], got_ref[k, 56:64]]
        feats = []
        for v in range(2):
            feats += planes((points[v] - nc_ref[k, 8 * v : 8 * v + 8]) * ROOT3, True)
        src = jnp.concatenate(feats + [jnp.zeros((64, 128), F32)], axis=0).T.astype(BF)
        for j in range(4):
            dist2 = dot(src[:, 32 * (j // 2) : 32 * (j // 2) + 32], f_ref[tn[j], j % 2])
            value = stack_kernel(matern(dist2))
            qs = jnp.concatenate(split(got_ref[k, 8 * j : 8 * j + 8]), axis=0)
            near_acc[tn[j]] += fold(dot(jnp.concatenate([qs, qs], axis=1), value))
        row = jnp.broadcast_to(points[0][3:4], (8, 128))
        row = jnp.where(lane % 64 == sub, row, 0.0)
        high = row.astype(BF)
        rest = row - high.astype(F32)
        mid = rest.astype(BF)
        low = (rest - mid.astype(F32)).astype(BF)
        cen = dot(jnp.concatenate([high, mid, low], axis=0), spread)
        rel = (fc_ref[k] - (cen[0:8] + cen[8:16] + cen[16:24])) * ROOT3
        tgt = jnp.concatenate(planes(rel, False), axis=0).astype(BF)
        value = stack_kernel(matern(dot(fn_ref[...], tgt)))
        ws = []
        for h in range(2):
            w = got_ref[k, 32 + 8 * h : 40 + 8 * h]
            for part in (jnp.where(left, w, 0.0), jnp.where(left, 0.0, w)):
                ws += list(split(part))
        ws = jnp.concatenate(ws, axis=0)
        locs = dot(jnp.concatenate([ws, ws], axis=1), value)
        for h in range(2):
            for u in range(2):
                at = 32 * h + 16 * u
                new = fold(locs[at : at + 16])
                far_acc[tf[2 * u + h]] += jnp.where(left if h == 0 else jnp.logical_not(left), new, 0.0)
        return carry

    lax.fori_loop(0, group, body, 0, unroll=2)

    @pl.when(step == steps - 1)
    def _():
        def finish(b, total):
            ls = jnp.concatenate(split(far_acc[b]), axis=0)
            both = t_ref[b]
            high, low = both[0:64], both[64:128]
            table = jnp.concatenate([high, high, low, low], axis=0)
            far = fold(dot(jnp.concatenate([ls, ls], axis=1), table))
            live = lane < count_ref[b]
            product = jnp.where(live, near_acc[b] + far, 0.0)
            out_ref[b] = product
            return total + product * q_ref[b]

        total = lax.fori_loop(0, boxes, finish, jnp.zeros((8, 128), F32), unroll=4)
        ones = jnp.ones((128, 128), F32)
        sums = lax.dot_general(ones, total, NT, precision=lax.Precision.HIGHEST, preferred_element_type=F32)
        term_ref[...] = jnp.concatenate([sums, jnp.zeros((128, 120), F32)], axis=1)


def far_sources():
    x = np.zeros((8, 128), np.float32)
    for n in range(64):
        for d, value in enumerate((NODE[n // 16], NODE[n // 4 % 4], NODE[n % 4])):
            for u in range(2):
                x[4 * u + d, 64 * u + n] = 0.5 * ROOT3 * value
    bf = lambda a: a.astype(jnp.bfloat16).astype(np.float32)
    high = bf(x)
    low = bf(x - high)
    norm = np.zeros_like(x)
    square = high * (high + 2 * low)
    for u in range(2):
        norm[4 * u + 3] = square[4 * u] + square[4 * u + 1] + square[4 * u + 2]
    one = bf(norm)
    two = bf(norm - one)
    three = bf(norm - one - two)
    sub = np.arange(8)[:, None] % 4
    unit = (np.arange(8)[:, None] // 4) == (np.arange(128)[None, :] // 64)
    parts = [
        np.where(sub == 3, one, high),
        np.where(sub == 3, two, high),
        np.where(sub == 3, 1.0, low),
        np.where(sub == 3, three, np.where(sub < 2, 1.0, 0.0)),
    ]
    return np.concatenate([np.where(unit, part, 0.0) for part in parts], axis=0).T.astype(np.float32)


def node_rows():
    out = np.zeros((8, 128), np.float32)
    for m in range(128):
        n = m % 64
        for u in range(2):
            for d, value in enumerate((NODE[n // 16], NODE[n // 4 % 4], NODE[n % 4])):
                out[4 * u + d, m] = 0.5 * value
    return out


def vmem(shape=None, index=None):
    if shape is None:
        return pl.BlockSpec(memory_space=pltpu.VMEM)
    return pl.BlockSpec(shape, index, memory_space=pltpu.VMEM)


SMEM = pl.BlockSpec(memory_space=pltpu.SMEM)


def params(mebibytes=56):
    return pltpu.CompilerParams(vmem_limit_bytes=mebibytes * 1024 * 1024)


def exchange(x):
    return lax.all_to_all(x, AXES, split_axis=0, concat_axis=0, tiled=True)


def general(local_pos, charges, counts, box_centers, far_list, near_list):
    devices = lax.axis_size("gx") * lax.axis_size("gy")
    boxes, _, slots = local_pos.shape
    struct = jax.ShapeDtypeStruct
    want = pl.pallas_call(
        ids_kernel,
        out_shape=struct((devices, 128), jnp.int32),
        in_specs=[vmem(), vmem()],
        out_specs=vmem(),
        compiler_params=params(),
        name="ids",
    )(far_list, near_list)
    served = exchange(want.reshape(devices, 1, 128)).reshape(devices, 128)

    group = 16
    lead = lambda shape: vmem((group,) + shape, lambda i: (i,) + (0,) * len(shape))
    q_tab, w_tab, p_tab, f_tab, base, table = pl.pallas_call(
        table_kernel,
        grid=(boxes // group,),
        out_shape=(
            struct((boxes, 8, 128), F32),
            struct((boxes, 8, 128), F32),
            struct((boxes, 8, 128), F32),
            struct((boxes, 2, 32, 128), BF),
            struct((boxes, 8, 128), F32),
            struct((boxes, 128, 128), BF),
        ),
        in_specs=[lead((3, 128)), lead((8, 128)), SMEM, SMEM],
        out_specs=(lead((8, 128)), lead((8, 128)), lead((8, 128)), lead((2, 32, 128)), lead((8, 128)), lead((128, 128))),
        compiler_params=params(),
        cost_estimate=pl.CostEstimate(flops=200_000_000, bytes_accessed=6_000_000, transcendentals=2_000_000),
        name="tables",
    )(local_pos, charges, counts, box_centers)

    send = pl.pallas_call(
        gather_kernel,
        grid=(devices // group,),
        out_shape=struct((devices, 64, 128), F32),
        in_specs=[SMEM, vmem(), vmem(), vmem()],
        out_specs=lead((64, 128)),
        compiler_params=params(),
        name="gather",
    )(served, q_tab, w_tab, p_tab)
    got = exchange(send)

    tgt = want[:, 16:24]
    centers = box_centers.T
    near_cen = jnp.pad(centers[tgt[:, :4]], ((0, 0), (0, 0), (0, 1))).reshape(devices, 16, 1)
    near_cen = jnp.broadcast_to(near_cen, (devices, 16, 128))
    far_cen = jnp.pad(centers[tgt[:, 4:]], ((0, 0), (0, 0), (0, 1))).reshape(devices, 2, 2, 4)
    far_cen = far_cen.transpose(0, 1, 3, 2).reshape(devices, 8, 2, 1)
    far_cen = jnp.broadcast_to(far_cen, (devices, 8, 2, 64)).reshape(devices, 8, 128) + node_rows()[None]

    product, term = pl.pallas_call(
        pair_kernel,
        grid=(devices // group,),
        out_shape=(struct((boxes, 8, 128), F32), struct((devices, 128), F32)),
        in_specs=[
            SMEM,
            SMEM,
            lead((64, 128)),
            lead((16, 128)),
            lead((8, 128)),
            vmem(),
            vmem(),
            vmem(),
            vmem(),
            vmem(),
        ],
        out_specs=(vmem(), vmem()),
        scratch_shapes=[pltpu.VMEM((boxes, 8, 128), F32), pltpu.VMEM((boxes, 8, 128), F32)],
        compiler_params=params(),
        cost_estimate=pl.CostEstimate(flops=1_000_000_000, bytes_accessed=12_000_000, transcendentals=20_000_000),
        name="pairs",
    )(tgt, counts, got, near_cen, far_cen, f_tab, jnp.asarray(far_sources(), BF), base, q_tab, table)

    terms = exchange(term.reshape(devices, 1, 128))[:, 0, :8]
    curvature = jnp.sum(terms, axis=0) / (devices * boxes * slots)
    return (product, curvature)


HALF = 64
ROWS = 44
NEAR_ROWS = 24
UNROLL = 4
CHUNKS = 16
AHEAD = 4


def upper_kernel(pos_ref, charge_ref, count_ref, row_ref, ex_ref):
    half = charge_ref.shape[0] // 2
    lane = iota((8, 128), 1)
    left = lane < HALF
    center = jnp.concatenate([row_ref[...], jnp.zeros((5, 2 * half), F32)], axis=0)
    center = jnp.concatenate([center, jnp.zeros((8, 128 - 2 * half), F32)], axis=1)
    center = jnp.concatenate([center, jnp.zeros((120, 128), F32)], axis=0).T
    wide = iota((half, 128), 1) < HALF
    for d in range(3):
        first = center[:half, d : d + 1] + 0.5 * pos_ref[d, :half]
        second = center[half : 2 * half, d : d + 1] + 0.5 * pos_ref[d, half:]
        ex_ref[(8 + d) * half : (9 + d) * half, :] = jnp.where(wide, pltpu.roll(first, HALF, 1), second)

    def body(b, carry):
        first = pltpu.roll(jnp.where(lane < count_ref[b], charge_ref[b], 0.0), HALF, 1)
        second = jnp.where(lane < count_ref[b + half], charge_ref[b + half], 0.0)
        ex_ref[pl.ds(pl.multiple_of(8 * b, 8), 8), :] = jnp.where(left, first, second)
        return carry

    lax.fori_loop(0, half, body, 0, unroll=16)


def sort_ids(far_ref, near_ref, most_ref, row_ref, msg_ref, want_ref):
    boxes = far_ref.shape[1]
    slots = far_ref.shape[0]
    peer = iota((128, 128), 0)
    line = iota((128, 128), 1)
    tri = (peer < line).astype(F32).astype(BF)
    full = jnp.ones((128, 128), BF)
    row32 = iota((32, 128), 0)
    kind = row32 // 4
    boxrow = iota((32, 128), 1) % boxes
    result = jnp.zeros((128, 32), F32)
    for ref, first, group in ((near_ref, 1, 0), (far_ref, 0, 1)):
        seen = jnp.zeros((128, 128), F32)
        for j in range(0, slots, 2):
            flat = jnp.concatenate([ref[first + j : first + j + 1, :], ref[first + j + 1 : first + j + 2, :]], axis=1)
            hit = jnp.broadcast_to(flat // boxes, (128, 128)) == peer
            onehot = hit.astype(F32).astype(BF)
            before = dot(onehot, tri) + seen
            rank = jnp.sum(jnp.where(hit, before, 0.0), axis=0, keepdims=True).astype(jnp.int32)
            if j + 2 < slots:
                seen = seen + dot(onehot, full)
            within = jnp.broadcast_to(flat % boxes, (32, 128))
            if group == 0:
                value = jnp.where(kind == 0, within * NEAR_ROWS, jnp.where(kind == 2, within * 8, 0))
            else:
                value = jnp.where(kind == 1, within * 8, 0)
            value = jnp.where(kind == 4 + group, boxrow, value)
            value = jnp.where(row32 % 4 == jnp.broadcast_to(rank, (32, 128)), value, 0).astype(F32).astype(BF)
            result = result + dot(onehot, value, NT)
    result = jnp.concatenate([result, jnp.zeros((128, 96), F32)], axis=1)
    heavy = (line == peer - peer % 4).astype(F32).astype(BF)
    first = dot(heavy, result.astype(BF))
    for at, base in ((8, 8), (24, 16)):
        extra = dot(jnp.where(line == base + peer % 4, first, 0.0).astype(BF), full)
        result = jnp.where(line == at, extra, result)
    most = jnp.max(most_ref[...], axis=1, keepdims=True).astype(F32)
    result = jnp.where(line == 9, jnp.broadcast_to(most, (128, 128)), result)
    want_ref[...] = result.astype(jnp.int32)
    rows = [jnp.concatenate([row_ref[d : d + 1, :]] * 2, axis=1) for d in range(3)]
    rows = [jnp.broadcast_to(row, (128, 128)) for row in rows]
    msg_ref[pl.ds(0, 128, stride=2), :] = jnp.where(line < HALF, result, rows[2])
    msg_ref[pl.ds(1, 128, stride=2), :] = jnp.where(line < HALF, rows[0], rows[1])


def first_kernel(
    member_ref, count_ref, far_ref, near_ref, most_ref, row_ref, pos_hbm, charge_hbm, msg_hbm, want_hbm, ex_ref,
    pos_ref, charge_ref, msg_ref, want_ref, sems
):
    @pl.when(member_ref[0] == 0)
    def _():
        loads = [pltpu.make_async_copy(pos_hbm, pos_ref, sems.at[0]), pltpu.make_async_copy(charge_hbm, charge_ref, sems.at[1])]
        for copy in loads:
            copy.start()
        sort_ids(far_ref, near_ref, most_ref, row_ref, msg_ref, want_ref)
        stores = [pltpu.make_async_copy(msg_ref, msg_hbm, sems.at[2]), pltpu.make_async_copy(want_ref, want_hbm, sems.at[3])]
        for copy in stores:
            copy.start()
        for copy in loads:
            copy.wait()
        upper_kernel(pos_ref, charge_ref, count_ref, row_ref, ex_ref)
        for copy in stores:
            copy.wait()


def second_kernel(
    member_ref, far_ref, near_ref, most_ref, row_ref, msg_in, want_in, msg_hbm, want_hbm, msg_ref, want_ref, sems
):
    @pl.when(member_ref[0] != 0)
    def _():
        sort_ids(far_ref, near_ref, most_ref, row_ref, msg_ref, want_ref)
        stores = [pltpu.make_async_copy(msg_ref, msg_hbm, sems.at[0]), pltpu.make_async_copy(want_ref, want_hbm, sems.at[1])]
        for copy in stores:
            copy.start()
        for copy in stores:
            copy.wait()


def cheb_rows(x):
    sub = iota((8, 128), 0)
    second = 2.0 * x * x - 1.0
    third = 2.0 * x * second - x
    basis = []
    for i in range(NODES):
        theta = (2 * i + 1) * math.pi / 8
        basis.append(0.25 + 0.5 * (math.cos(theta) * x + math.cos(2 * theta) * second + math.cos(3 * theta) * third))
    row = lambda i, d: jnp.broadcast_to(basis[i][d : d + 1], (8, 128))
    sub4 = sub % 4
    zs = jnp.where(sub4 == 0, row(0, 2), jnp.where(sub4 == 1, row(1, 2), jnp.where(sub4 == 2, row(2, 2), row(3, 2))))
    ys = [jnp.where(sub < 4, row(0, 1), row(1, 1)) * zs, jnp.where(sub < 4, row(2, 1), row(3, 1)) * zs]
    return jnp.concatenate([row(i, 0) * ys[j] for i in range(NODES) for j in range(2)], axis=0)


def point_rows(pos_ref, b):
    sub4 = iota((8, 128), 0) % 4
    x = jnp.zeros((8, 128), F32)
    for d in range(3):
        x = jnp.where(sub4 == d, jnp.broadcast_to(pos_ref[d, pl.ds(b, 1), :], (8, 128)), x)
    return x


def doubled(x):
    return jnp.where(iota((8, 128), 1) < HALF, x, pltpu.roll(x, HALF, 1))


def fill_basis(pos_ref, basis_ref):
    for d in range(3):
        x = pos_ref[d]
        second = 2.0 * x * x - 1.0
        third = 2.0 * x * second - x
        for i in range(NODES):
            theta = (2 * i + 1) * math.pi / 8
            value = math.cos(theta) * x + math.cos(2 * theta) * second + math.cos(3 * theta) * third
            basis_ref[4 * d + i] = 0.25 + 0.5 * value


def basis_table(basis_ref, b):
    sub = iota((8, 128), 0)
    row = lambda i, d: jnp.broadcast_to(basis_ref[4 * d + i, pl.ds(b, 1), :], (8, 128))
    sub4 = sub % 4
    zs = jnp.where(sub4 == 0, row(0, 2), jnp.where(sub4 == 1, row(1, 2), jnp.where(sub4 == 2, row(2, 2), row(3, 2))))
    ys = [jnp.where(sub < 4, row(0, 1), row(1, 1)) * zs, jnp.where(sub < 4, row(2, 1), row(3, 1)) * zs]
    return jnp.concatenate([row(i, 0) * ys[j] for i in range(NODES) for j in range(2)], axis=0)


def send_table_kernel(pos_ref, charge_ref, count_ref, cen_ref, near_ref, far_ref, basis_ref):
    boxes = charge_ref.shape[0]
    lane = iota((8, 128), 1)
    sub = iota((8, 128), 0)
    fill_basis(pos_ref, basis_ref)

    def body(b, carry):
        q = jnp.where(lane < count_ref[b], charge_ref[b], 0.0)
        near_ref[b, 0:8] = doubled(q)
        x, y, z = [doubled(cen_ref[d, b] + 0.5 * jnp.broadcast_to(pos_ref[d, pl.ds(b, 1), :], (8, 128))) for d in range(3)]
        near_ref[b, 8:16] = jnp.where(sub == 4, x, jnp.where(sub == 5, y, z))
        near_ref[b, 16:24] = jnp.where(sub == 7, x, jnp.where((sub == 3) | (sub == 5), y, z))
        table = basis_table(basis_ref, b)
        qs = jnp.concatenate(split(q), axis=0)
        weight = fold(dot(qs, stack_kernel(table), NT))
        far_ref[b] = weight + pltpu.roll(weight, 64, 1)
        return carry

    lax.fori_loop(0, boxes, body, 0, unroll=32)


def own_table_kernel(pos_ref, charge_ref, count_ref, q_ref, f_ref, base_ref):
    boxes = charge_ref.shape[0]
    sub = iota((8, 128), 0)
    lane = iota((8, 128), 1)

    def body(b, carry):
        q = jnp.where(lane < count_ref[b], charge_ref[b], 0.0)
        q_ref[b] = q
        x = point_rows(pos_ref, b)
        rel = (0.5 * ROOT3) * x
        tgt = planes(rel, False)
        for unit in range(2):
            f_ref[b, unit] = jnp.concatenate([jnp.where(sub // 4 == unit, part, 0.0) for part in tgt], axis=0).astype(BF)
        zero = jnp.zeros((96, 128), F32)
        src = jnp.concatenate(planes(rel, True) + [zero], axis=0).T.astype(BF)
        first = jnp.concatenate([jnp.where(sub < 4, part, 0.0) for part in tgt] + [zero], axis=0).astype(BF)
        value = stack_kernel(matern(dot(src, first)))
        qs = jnp.concatenate(split(q), axis=0)
        base_ref[b] = fold(dot(jnp.concatenate([qs, qs], axis=1), value)) + q
        return carry

    lax.fori_loop(0, boxes, body, 0, unroll=4)


def goal_kernel(want_ref, served_ref, cen_ref, node_ref, nc_ref, fc_ref, ec_ref, goal_ref, odd_ref):
    lane = iota((128, 128), 1)
    left = lane < HALF
    boxes = cen_ref.shape[1]
    cen = jnp.concatenate([cen_ref[...], jnp.zeros((5, boxes), F32)], axis=0)
    cen = jnp.concatenate([cen, jnp.zeros((8, 128 - boxes), F32)], axis=1)
    cen = jnp.concatenate([cen, jnp.zeros((120, 128), F32)], axis=0).T

    def split3(x, axis):
        high = x.astype(BF)
        rest = x - high.astype(F32)
        mid = rest.astype(BF)
        return jnp.concatenate([high, mid, (rest - mid.astype(F32)).astype(BF)], axis=axis)

    parts = split3(cen, 0)
    want = want_ref[...]
    goal_ref[...] = want.astype(F32).T[16:32].astype(jnp.int32)
    sources = [served_ref[pl.ds(1, 128, stride=2), :], served_ref[pl.ds(0, 128, stride=2), :]]
    halves = [jnp.concatenate([(iota((128, 128), 0) // HALF == h).astype(F32).astype(BF)] * 3, axis=0) for h in range(2)]

    def column(at):
        return jnp.broadcast_to(want[:, at : at + 1], (128, 128))

    def centers(at):
        onehot = (column(at) == lane).astype(F32).astype(BF)
        found = dot(jnp.concatenate([onehot] * 3, axis=1), parts)
        return [jnp.broadcast_to(found[:, d : d + 1], (128, 128)) for d in range(3)]

    def gaps(j):
        mine = lane % HALF == column(4 + j) // 8
        both = [split3(jnp.where(mine, source, 0.0), 1) for source in sources]
        theirs = [dot(both[0], halves[0]), dot(both[0], halves[1]), dot(both[1], halves[1])]
        return [a - b for a, b in zip(centers(20 + j), theirs)]

    nc_ref[...] = jnp.zeros_like(nc_ref)
    fc_ref[...] = jnp.zeros_like(fc_ref)
    ec_ref[...] = jnp.zeros_like(ec_ref)
    for u in range(2):
        first, second = centers(16 + 2 * u), centers(17 + 2 * u)
        for d in range(3):
            nc_ref[pl.ds(4 * u + d, 128, stride=8), :] = jnp.where(left, first[d], second[d])
        first, second = gaps(2 * u), gaps(2 * u + 1)
        for d in range(3):
            fc_ref[pl.ds(4 * u + d, 128, stride=8), :] = jnp.where(left, first[d], second[d]) + node_ref[d : d + 1, :]
    extra = centers(24)
    for d in range(3):
        odd_ref[...] = extra[d]
        even, odd = odd_ref[pl.ds(0, 64, stride=2), :], odd_ref[pl.ds(1, 64, stride=2), :]
        ec_ref[pl.ds(d, 64, stride=8), :] = jnp.where(left[:64], even, odd)


def far_kernel(fc_ref, fn_ref, out_ref):
    group = fc_ref.shape[0]
    tgt = jnp.concatenate(planes(fc_ref[...] * ROOT3, False), axis=1).astype(BF)
    for k in range(group):
        out_ref[k] = stack_kernel(matern(dot(fn_ref[...], tgt[k])))


def send_kernel(member_ref, served_ref, near_ref, far_ref, own_ref, *refs):
    moved, (out_ref, ids_ref, int_ref, ex_ref, buf_ref, sems) = refs[:3], refs[3:]
    peers = ids_ref.shape[1]
    sub = iota((8, 128), 0)
    lane = iota((8, 128), 1)
    left = lane < HALF
    keep = left | (sub < 3)
    second = sub < 5
    int_ref[...] = served_ref[pl.ds(0, peers, stride=2), :].T[:16].astype(jnp.int32)
    copy = pltpu.make_async_copy(int_ref, ids_ref, sems.at[0])
    copy.start()
    half = ex_ref.shape[0] // 16
    packed = moved[0][...] + moved[1][...] + moved[2][...]
    packed = jnp.where(member_ref[0] == 0, own_ref[...], packed)
    for d in range(3):
        rows = packed[(8 + d) * half : (9 + d) * half]
        ex_ref[pl.ds(d, half, stride=8), :] = pltpu.roll(rows, HALF, 1)
        ex_ref[pl.ds(8 * half + d, half, stride=8), :] = rows
    for b in range(half):
        tile = packed[8 * b : 8 * b + 8]
        for at, part in ((8 * b, tile), (8 * (b + half), pltpu.roll(tile, HALF, 1))):
            ex_ref[at : at + 8, :] = jnp.where(left, part, jnp.where(sub < 3, ex_ref[at : at + 8, :], 0.0))
    copy.wait()

    def body(i, carry):
        base = pl.multiple_of(i * 2 * ROWS, 8)
        for k in range(2):
            peer = 2 * i + k
            at = lambda row: pl.ds(base + (k * ROWS + row), 8)
            rows = lambda ref, j, row: ref[pl.ds(pl.multiple_of(ids_ref[j, peer], 8) + row, 8), :]
            q = [rows(near_ref, j, 0) for j in range(4)]
            w = [rows(far_ref, 4 + j, 0) for j in range(4)]
            p = [rows(near_ref, j, 16 if j < 2 else 8) for j in range(4)]
            buf_ref[at(0), :] = jnp.where(left, q[0], q[1])
            buf_ref[at(8), :] = jnp.where(left, q[2], q[3])
            buf_ref[at(16), :] = jnp.where(left, w[0], w[2])
            buf_ref[at(24), :] = jnp.where(left, w[1], w[3])
            buf_ref[at(36), :] = jnp.where(sub == 7, jnp.where(left, p[0], p[1]), jnp.where(left, p[2], p[3]))
            buf_ref[at(32), :] = jnp.where(keep, rows(ex_ref, 8, 0), jnp.where(second, p[1], p[0]))
        return carry

    chunks = 8
    each = peers // chunks
    stores = []
    for c in range(chunks):
        lax.fori_loop(c * each // 2, (c + 1) * each // 2, body, 0, unroll=8)
        at = pl.ds(c * each * ROWS, each * ROWS)
        stores.append(pltpu.make_async_copy(buf_ref.at[at], out_ref.at[at], sems.at[1 + c]))
        stores[-1].start()
    for copy in stores:
        copy.wait()


def duo_kernel(
    scale, got_ref, want_hbm, nc_hbm, ec_hbm, f_hbm, base_hbm, q_hbm, w_hbm, v_hbm, near0_hbm, near1_hbm, far0_hbm, far1_hbm, term_hbm,
    tgt_ref, nc_ref, ec_ref, f_ref, base_ref, q_ref, w_ref, v_ref, term_ref, sems, *bufs
):
    whole = [(want_hbm, tgt_ref), (nc_hbm, nc_ref), (ec_hbm, ec_ref), (f_hbm, f_ref)]
    whole += [(base_hbm, base_ref), (q_hbm, q_ref), (w_hbm, w_ref)]
    loads = [pltpu.make_async_copy(source, target, sems.at[i]) for i, (source, target) in enumerate(whole)]
    for copy in loads[:4]:
        copy.start()
    chunk = v_ref.shape[0] // CHUNKS

    def far_values(c):
        at = pl.ds(c * chunk, chunk)
        return pltpu.make_async_copy(v_hbm.at[at], v_ref.at[at], sems.at[16 + c % AHEAD])

    for c in range(AHEAD):
        far_values(c).start()
    xt_refs, dist_refs, value_refs = bufs[:2], (bufs[2:7], bufs[7:12]), (bufs[12:17], bufs[17:22])
    near_accs, far_accs = bufs[22:24], bufs[24:26]
    duos = ec_ref.shape[0]
    boxes = f_ref.shape[0]
    sub = iota((8, 128), 0)
    lane = iota((8, 128), 1)
    left = lane < HALF
    for ref in value_refs[1] + near_accs + far_accs:
        ref[...] = jnp.zeros_like(ref)
    for ref in dist_refs[1]:
        ref[...] = jnp.full(ref.shape, 1e6, F32)
    def tile(duo, a, row):
        return got_ref[pl.ds(pl.multiple_of(duo * 2 * ROWS, 8) + (a * ROWS + row), 8), :]

    def extra(duo):
        return tile(duo, 0, 32), tile(duo, 1, 32)

    def goals(duo):
        pairs = [(tgt_ref[2 * (k % 2), 2 * duo + k // 2], tgt_ref[2 * (k % 2) + 1, 2 * duo + k // 2]) for k in range(4)]
        return pairs + [(tgt_ref[8, 2 * duo], tgt_ref[8, 2 * duo + 1])]

    def halves(x):
        high = x.astype(BF).astype(F32)
        both = [high, x - high]
        return [jnp.where(left, part, 0.0) for part in both] + [jnp.where(left, 0.0, part) for part in both]

    def products(duo, value):
        ex = extra(duo)
        tiles = [tile(duo, k // 2, 8 * (k % 2)) for k in range(4)]
        tiles.append(jnp.where(left, ex[0], pltpu.roll(ex[1], HALF, 1)))
        for k, goal in enumerate(goals(duo)):
            qs = jnp.concatenate(halves(tiles[k]), axis=0).astype(BF)
            new = dot(jnp.concatenate([qs, qs], axis=1), value[k][...])
            for h in range(2):
                near_accs[h][goal[h]] += fold(new[16 * h : 16 * h + 16])

    def far_products(duo):
        for a in range(2):
            ws = []
            for h in range(2):
                ws += halves(tile(duo, a, 16 + 8 * h))
            ws = jnp.concatenate(ws, axis=0).astype(BF)
            new = dot(jnp.concatenate([ws, ws], axis=1), v_ref[2 * duo + a])
            for h in range(2):
                for u in range(2):
                    at = 32 * h + 16 * u
                    far_accs[h][tgt_ref[4 + 2 * u + h, 2 * duo + a]] += fold(new[at : at + 16])

    def values(dist, value):
        for k in range(5):
            value[k][...] = stack_kernel(matern(dist[k][...]))

    def distances(duo, xt, dist):
        for k, goal in enumerate(goals(duo)):
            v, u = k // 2, k % 2
            for half in range(2):
                pieces = [jnp.zeros((32 * v, 128), BF)] if v else []
                pieces += [f_ref[goal[half], u], jnp.zeros((96 - 32 * v, 128), BF)]
                at = slice(64 * half, 64 * half + 64)
                dist[k][at, :] = dot(xt[at, :], jnp.concatenate(pieces, axis=0))

    def features(duo, xt):
        ex = extra(duo)
        turned = [pltpu.roll(x, HALF, 1) for x in ex]
        feats = []
        for a in range(2):
            full = tile(duo, a, 36)
            split_rows = jnp.where(left, pltpu.roll(turned[a], 4, 0), pltpu.roll(ex[a], 6, 0))
            point = jnp.where(sub >= 4, full, jnp.where(sub == 0, pltpu.roll(full, 1, 0), split_rows))
            feats += planes((point - nc_ref[2 * duo + a]) * ROOT3, True)
        point = jnp.where(left, turned[0], ex[1])
        feats += planes((point - ec_ref[duo]) * ROOT3, True)
        feats.append(jnp.zeros((32, 128), F32))
        xt[...] = jnp.concatenate(feats, axis=0).T.astype(BF)

    turns = duos // UNROLL
    assert turns == CHUNKS

    def body(i, carry):
        far_values(i).wait()

        @pl.when(i + AHEAD < CHUNKS)
        def _():
            far_values(i + AHEAD).start()

        for s in range(UNROLL):
            now, was = s % 2, 1 - s % 2
            step = UNROLL * i + s
            products(jnp.maximum(step - 2, 0), value_refs[was])
            far_products(step)
            values(dist_refs[was], value_refs[now])
            distances(step, xt_refs[was], dist_refs[now])
            features(jnp.minimum(step + 1, duos - 1), xt_refs[now])
        return carry

    for copy in loads[:4]:
        copy.wait()
    features(0, xt_refs[1])
    for copy in loads[4:]:
        copy.start()
    lax.fori_loop(0, turns, body, 0)
    products(duos - 2, value_refs[1])
    values(dist_refs[1], value_refs[0])
    products(duos - 1, value_refs[0])

    sums = (near0_hbm, near1_hbm, far0_hbm, far1_hbm)
    stores = [pltpu.make_async_copy(a, b, sems.at[8 + i]) for i, (a, b) in enumerate(zip(near_accs + far_accs, sums))]
    for copy in stores:
        copy.start()
    for copy in loads[4:]:
        copy.wait()

    def finish(b, total):
        near = near_accs[0][b] + near_accs[1][b] + base_ref[b]
        far = jnp.where(left, far_accs[0][b], far_accs[1][b])
        return total + near * q_ref[b] + far * w_ref[b]

    total = lax.fori_loop(0, boxes, finish, jnp.zeros((8, 128), F32), unroll=16)
    high = total.astype(BF)
    rest = total - high.astype(F32)
    mid = rest.astype(BF)
    parts = jnp.concatenate([high, mid, (rest - mid.astype(F32)).astype(BF)], axis=1)
    sums = dot(jnp.ones((128, 384), BF), parts, NT)
    term_ref[...] = jnp.concatenate([sums * scale, jnp.zeros((128, 120), F32)], axis=1)
    stores.append(pltpu.make_async_copy(term_ref, term_hbm, sems.at[12]))
    stores[-1].start()
    for copy in stores:
        copy.wait()


def finish_kernel(count_ref, pos_ref, near0_ref, near1_ref, far0_ref, far1_ref, base_ref, out_ref, basis_ref):
    boxes = base_ref.shape[0]
    lane = iota((8, 128), 1)
    fill_basis(pos_ref, basis_ref)

    def body(b, carry):
        locs = jnp.where(lane < HALF, far0_ref[b], far1_ref[b])
        ls = jnp.concatenate(split(locs), axis=0)
        high, low = split(basis_table(basis_ref, b))
        far = fold(dot(jnp.concatenate([ls, ls], axis=1), jnp.concatenate([high, high, low, low], axis=0)))
        near = near0_ref[b] + near1_ref[b] + base_ref[b]
        out_ref[b] = jnp.where(lane < count_ref[b], near + far, 0.0)
        return carry

    lax.fori_loop(0, boxes, body, 0, unroll=16)


def on_device(local_pos, charges, counts, box_centers, far_list, near_list):
    devices = lax.axis_size("gx") * lax.axis_size("gy")
    boxes, _, slots = local_pos.shape
    struct = jax.ShapeDtypeStruct
    hbm = pltpu.HBM
    stay = lambda x: pltpu.with_memory_space_constraint(x, pltpu.HBM)
    anywhere = pl.BlockSpec(memory_space=pltpu.HBM)
    pos = jnp.transpose(local_pos, (1, 0, 2))
    table = struct((boxes, 8, 128), F32)
    flat = lambda x: x.reshape(-1, 128)
    member = (lax.axis_index("gy") % 4).astype(jnp.int32).reshape(1)
    lists = (far_list.T, near_list.T, counts.reshape(1, boxes), box_centers)
    ids_shape = (hbm((devices * 2, 128), F32), hbm((devices, 128), jnp.int32))
    ids_scratch = [pltpu.VMEM((devices * 2, 128), F32), pltpu.VMEM((devices, 128), jnp.int32)]
    msg, want, ex_own = pl.pallas_call(
        first_kernel,
        out_shape=ids_shape + (struct((boxes * 11 // 2, 128), F32),),
        in_specs=[SMEM, SMEM] + [vmem()] * 4 + [anywhere] * 2,
        out_specs=(anywhere, anywhere, vmem()),
        scratch_shapes=[pltpu.VMEM((3, boxes, 128), F32), pltpu.VMEM((boxes, 8, 128), F32)]
        + ids_scratch
        + [pltpu.SemaphoreType.DMA((4,))],
        compiler_params=params(8),
        name="first",
    )(member, counts, *lists, stay(pos), stay(charges))
    msg, want = pl.pallas_call(
        second_kernel,
        out_shape=ids_shape,
        in_specs=[SMEM] + [vmem()] * 4 + [anywhere] * 2,
        out_specs=(anywhere, anywhere),
        scratch_shapes=ids_scratch + [pltpu.SemaphoreType.DMA((2,))],
        input_output_aliases={5: 0, 6: 1},
        compiler_params=params(8),
        name="second",
    )(member, *lists, stay(msg), stay(want))
    moved = [lax.ppermute(ex_own, "gy", [(4 * z, 4 * z + k) for z in range(4)]) for k in range(1, 4)]
    served = flat(exchange(msg.reshape(devices, 2, 128)))

    near_tab, far_tab = pl.pallas_call(
        send_table_kernel,
        out_shape=(struct((boxes, NEAR_ROWS, 128), F32), table),
        in_specs=[vmem(), vmem(), SMEM, SMEM],
        out_specs=(vmem(), vmem()),
        scratch_shapes=[pltpu.VMEM((12, boxes, 128), F32)],
        compiler_params=params(8),
        cost_estimate=pl.CostEstimate(flops=50_000_000, bytes_accessed=1_200_000, transcendentals=0),
        name="send_tables",
    )(pos, charges, counts, box_centers)

    send = pl.pallas_call(
        send_kernel,
        out_shape=hbm((devices * ROWS, 128), F32),
        in_specs=[SMEM] + [vmem()] * 7,
        out_specs=anywhere,
        scratch_shapes=[
            pltpu.SMEM((16, devices), jnp.int32),
            pltpu.VMEM((16, devices), jnp.int32),
            pltpu.VMEM((boxes * 8, 128), F32),
            pltpu.VMEM((devices * ROWS, 128), F32),
            pltpu.SemaphoreType.DMA((9,)),
        ],
        compiler_params=params(12),
        name="send",
    )(member, served, flat(near_tab), flat(far_tab), ex_own, *moved)
    got = flat(exchange(send.reshape(devices, ROWS // 4, 4, 128)))

    q_tab, f_tab, base = pl.pallas_call(
        own_table_kernel,
        out_shape=(hbm((boxes, 8, 128), F32), hbm((boxes, 2, 32, 128), BF), hbm((boxes, 8, 128), F32)),
        in_specs=[vmem(), vmem(), SMEM],
        out_specs=(vmem(), vmem(), vmem()),
        compiler_params=params(8),
        cost_estimate=pl.CostEstimate(flops=200_000_000, bytes_accessed=4_000_000, transcendentals=2_000_000),
        name="own_tables",
    )(pos, charges, counts)

    near_cen, far_gap, ex_cen, goals = pl.pallas_call(
        goal_kernel,
        out_shape=(
            hbm((devices * 8, 128), F32),
            hbm((devices * 8, 128), F32),
            hbm((devices * 4, 128), F32),
            hbm((16, devices), jnp.int32),
        ),
        in_specs=[vmem()] * 4,
        out_specs=(vmem(),) * 4,
        scratch_shapes=[pltpu.VMEM((128, 128), F32)],
        compiler_params=params(8),
        cost_estimate=pl.CostEstimate(flops=50_000_000, bytes_accessed=2_000_000, transcendentals=0),
        name="goals",
    )(want, served, box_centers, jnp.asarray(node_rows()))
    near_cen, far_gap, ex_cen = [x.reshape(-1, 8, 128) for x in (near_cen, far_gap, ex_cen)]
    group = 8
    far_value = pl.pallas_call(
        far_kernel,
        grid=(devices // group,),
        out_shape=hbm((devices, 256, 128), BF),
        in_specs=[vmem((group, 8, 128), lambda i: (i, 0, 0)), vmem()],
        out_specs=vmem((group, 256, 128), lambda i: (i, 0, 0)),
        compiler_params=params(8),
        cost_estimate=pl.CostEstimate(flops=200_000_000, bytes_accessed=9_000_000, transcendentals=4_000_000),
        name="far_values",
    )(far_gap, jnp.asarray(far_sources(), BF))

    big = lambda dtype, rows: pltpu.VMEM((rows, 128), dtype)
    *sums, term = pl.pallas_call(
        functools.partial(duo_kernel, 1.0 / (devices * boxes * slots)),
        out_shape=(hbm((boxes, 8, 128), F32),) * 4 + (hbm((devices, 128), F32),),
        in_specs=[vmem()] + [anywhere] * 8,
        out_specs=(anywhere,) * 5,
        scratch_shapes=[
            pltpu.SMEM((16, devices), jnp.int32),
            pltpu.VMEM((devices, 8, 128), F32),
            pltpu.VMEM((devices // 2, 8, 128), F32),
            pltpu.VMEM((boxes, 2, 32, 128), BF),
            pltpu.VMEM((boxes, 8, 128), F32),
            pltpu.VMEM((boxes, 8, 128), F32),
            pltpu.VMEM((boxes, 8, 128), F32),
            pltpu.VMEM((devices, 256, 128), BF),
            pltpu.VMEM((devices, 128), F32),
            pltpu.SemaphoreType.DMA((20,)),
        ]
        + [big(BF, 128)] * 2
        + [big(F32, 128)] * 10
        + [big(BF, 256)] * 10
        + [pltpu.VMEM((boxes, 8, 128), F32)] * 4,
        compiler_params=params(28),
        cost_estimate=pl.CostEstimate(flops=1_000_000_000, bytes_accessed=12_000_000, transcendentals=20_000_000),
        name="pairs",
    )(got, *[stay(x) for x in (goals, near_cen, ex_cen, f_tab, base, q_tab, far_tab, far_value)])

    terms = exchange(term.reshape(devices, 1, 128))[:, 0, :8]
    curvature = jnp.sum(terms, axis=0)
    product = pl.pallas_call(
        finish_kernel,
        out_shape=table,
        in_specs=[SMEM] + [vmem()] * 6,
        out_specs=vmem(),
        scratch_shapes=[pltpu.VMEM((12, boxes, 128), F32)],
        compiler_params=params(8),
        cost_estimate=pl.CostEstimate(flops=50_000_000, bytes_accessed=3_000_000, transcendentals=0),
        name="finish",
    )(counts, pos, *[stay(x) for x in (*sums, base)])
    over = jnp.any((served.reshape(devices, 2, 128)[:, 0, 9] > HALF) & (jnp.arange(devices) % 4 != 0))
    whole = (local_pos, charges, counts, box_centers, far_list, near_list)
    return lax.cond(over, lambda: general(*whole), lambda: (product, curvature))


def solution(mesh):
    in_specs = (
        P(AXES, None, None),
        P(AXES, None, None),
        P(AXES),
        P(None, AXES),
        P(AXES, None),
        P(AXES, None),
    )
    out_specs = (P(AXES, None, None), P())
    return jax.shard_map(on_device, mesh=mesh, in_specs=in_specs, out_specs=out_specs, check_vma=False)
```

```python
import functools
import math

import jax
import jax.numpy as jnp
import numpy as np
from jax import lax
from jax.experimental import pallas as pl
from jax.experimental.pallas import tpu as pltpu
from jax.sharding import PartitionSpec as P

AXES = ("gx", "gy")
NODES = 4
ROOT3 = 1.7320508075688772
LOG2E = 1.4426950408889634
BF = jnp.bfloat16
F32 = jnp.float32
NODE = [math.cos((2 * i + 1) * math.pi / 8) for i in range(NODES)]
NT = (((1,), (1,)), ((), ()))
TN = (((0,), (0,)), ((), ()))


def iota(shape, dim):
    return lax.broadcasted_iota(jnp.int32, shape, dim)


def dot(a, b, dims=None):
    if dims is None:
        return jnp.dot(a, b, preferred_element_type=F32)
    return lax.dot_general(a, b, dims, preferred_element_type=F32)


def split(x):
    high = x.astype(BF)
    return high, (x - high.astype(F32)).astype(BF)


def planes(rel, source):
    axis = rel.ndim - 2
    sub = iota(rel.shape, axis) % 4
    last = sub == 3
    rel = jnp.where(last, 0.0, rel)
    high = rel.astype(BF).astype(F32)
    low = (rel - high).astype(BF).astype(F32)
    square = high * (high + 2.0 * low)
    norm = pltpu.roll(square, 1, axis) + pltpu.roll(square, 2, axis) + pltpu.roll(square, 3, axis)
    one = norm.astype(BF).astype(F32)
    rest = norm - one
    two = rest.astype(BF).astype(F32)
    three = (rest - two).astype(BF).astype(F32)
    if source:
        parts = [
            jnp.where(last, one, high),
            jnp.where(last, two, high),
            jnp.where(last, 1.0, low),
            jnp.where(last, three, jnp.where(sub < 2, 1.0, 0.0)),
        ]
    else:
        parts = [
            jnp.where(last, 1.0, -2.0 * high),
            jnp.where(last, 1.0, -2.0 * low),
            jnp.where(last, one, -2.0 * high),
            jnp.where(
                sub == 0,
                pltpu.roll(two, 5, axis),
                jnp.where(sub == 1, pltpu.roll(three, 6, axis), jnp.where(last, 1.0, 0.0)),
            ),
        ]
    return parts


def matern(dist2):
    safe = jnp.maximum(dist2, 1e-12)
    scaled = safe * lax.rsqrt(safe)
    decay = jnp.exp2(scaled * (-LOG2E))
    return decay + scaled * decay


def stack_kernel(value):
    high, low = split(value)
    return jnp.concatenate([high, low], axis=0)


def fold(x):
    return x[0:8] + x[8:16]


def ids_kernel(far_ref, near_ref, want_ref):
    boxes = far_ref.shape[0]
    slots = far_ref.shape[1]
    total = boxes * slots
    lane = iota((total, 128), 1)
    box = iota((total, 128), 0) % boxes
    tri = (iota((total, total), 0) > iota((total, total), 1)).astype(F32).astype(BF)
    result = jnp.zeros((128, 128), F32)
    for ref, first, base in ((near_ref, 1, 0), (far_ref, 0, 4)):
        flat = jnp.concatenate([ref[:, first + j : first + j + 1] for j in range(slots)], axis=0)
        flat = jnp.broadcast_to(flat, (total, 128))
        hit = (flat // boxes) == lane
        onehot = hit.astype(F32).astype(BF)
        before = dot(tri, onehot)
        rank = jnp.sum(jnp.where(hit, before, 0.0), axis=1, keepdims=True).astype(jnp.int32)
        mine = rank == (lane % 4)
        within = jnp.where((lane >= base) & (lane < base + 4), flat % boxes, 0)
        owner = jnp.where((lane >= base + 16) & (lane < base + 20), box, 0)
        value = jnp.where(mine, within + owner, 0).astype(F32).astype(BF)
        result = result + dot(onehot, value, TN)
    want_ref[...] = result.astype(jnp.int32)


def table_kernel(pos_ref, charge_ref, count_ref, cen_ref, q_ref, w_ref, p_ref, f_ref, base_ref, t_ref):
    step = pl.program_id(0)
    group = pos_ref.shape[0]
    sub = iota((8, 128), 0)
    lane = iota((8, 128), 1)

    def body(b, carry):
        box = step * group + b
        live = lane < count_ref[box]
        q = jnp.where(live, charge_ref[b], 0.0)
        q_ref[b] = q
        pos = pos_ref[b]
        zero1 = jnp.zeros((1, 128), F32)
        x4 = jnp.concatenate([pos, zero1], axis=0)
        x = jnp.concatenate([x4, x4], axis=0)
        second = 2.0 * x * x - 1.0
        third = 2.0 * x * second - x
        basis = []
        for i in range(NODES):
            theta = (2 * i + 1) * math.pi / 8
            basis.append(0.25 + 0.5 * (math.cos(theta) * x + math.cos(2 * theta) * second + math.cos(3 * theta) * third))
        row = lambda i, d: jnp.broadcast_to(basis[i][d : d + 1], (8, 128))
        sub4 = sub % 4
        zs = jnp.where(sub4 == 0, row(0, 2), jnp.where(sub4 == 1, row(1, 2), jnp.where(sub4 == 2, row(2, 2), row(3, 2))))
        ys = [jnp.where(sub < 4, row(0, 1), row(1, 1)) * zs, jnp.where(sub < 4, row(2, 1), row(3, 1)) * zs]
        table = jnp.concatenate([row(i, 0) * ys[j] for i in range(NODES) for j in range(2)], axis=0)
        both = stack_kernel(table)
        t_ref[b] = both
        qs = jnp.concatenate(split(q), axis=0)
        weight = fold(dot(qs, both, NT))
        w_ref[b] = weight + pltpu.roll(weight, 64, 1)
        cx, cy, cz = cen_ref[0, box], cen_ref[1, box], cen_ref[2, box]
        lane4 = lane % 4
        far = jnp.where(lane4 == 0, cx, jnp.where(lane4 == 1, cy, cz))
        center = jnp.where(sub4 == 0, cx, jnp.where(sub4 == 1, cy, cz))
        p_ref[b] = jnp.where(sub4 == 3, far, center + 0.5 * x)
        rel = (0.5 * ROOT3) * x
        tgt = planes(rel, False)
        for unit in range(2):
            f_ref[b, unit] = jnp.concatenate([jnp.where(sub // 4 == unit, part, 0.0) for part in tgt], axis=0).astype(BF)
        src = jnp.concatenate(planes(rel, True) + [jnp.zeros((96, 128), F32)], axis=0).T.astype(BF)
        dist2 = dot(src[:, :32], f_ref[b, 0])
        value = stack_kernel(matern(dist2))
        near = fold(dot(jnp.concatenate([qs, qs], axis=1), value))
        base_ref[b] = near + q
        return carry

    lax.fori_loop(0, group, body, 0, unroll=4)


def gather_kernel(ids_ref, q_ref, w_ref, p_ref, out_ref):
    step = pl.program_id(0)
    group = out_ref.shape[0]
    sub4 = iota((8, 128), 0) % 4
    top = iota((8, 128), 0) < 4
    lane = iota((8, 128), 1)
    left = lane < 64

    def body(k, carry):
        peer = step * group + k
        near = [ids_ref[peer, j] for j in range(4)]
        far = [ids_ref[peer, 4 + j] for j in range(4)]
        for j in range(4):
            out_ref[k, 8 * j : 8 * j + 8] = q_ref[near[j]]
        w = [w_ref[far[j]] for j in range(4)]
        out_ref[k, 32:40] = jnp.where(left, w[0], w[2])
        out_ref[k, 40:48] = jnp.where(left, w[1], w[3])
        c = [p_ref[far[j]] for j in range(4)]
        centers = jnp.where(
            left, jnp.where(lane < 4, c[0], c[2]), jnp.where(lane < 68, c[1], c[3])
        )
        s = [p_ref[near[j]] for j in range(4)]
        out_ref[k, 48:56] = jnp.where(sub4 == 3, centers, jnp.where(top, s[0], s[1]))
        out_ref[k, 56:64] = jnp.where(sub4 == 3, centers, jnp.where(top, s[2], s[3]))
        return carry

    lax.fori_loop(0, group, body, 0, unroll=4)


def pair_kernel(
    tgt_ref, count_ref, got_ref, nc_ref, fc_ref, f_ref, fn_ref, base_ref, q_ref, t_ref, out_ref, term_ref, near_acc, far_acc
):
    step = pl.program_id(0)
    steps = pl.num_programs(0)
    group = got_ref.shape[0]
    boxes = f_ref.shape[0]
    sub = iota((8, 128), 0)
    lane = iota((8, 128), 1)
    left = lane < 64

    @pl.when(step == 0)
    def _():
        near_acc[...] = base_ref[...]
        far_acc[...] = jnp.zeros_like(far_acc)

    spread = (iota((128, 128), 0) // 64 == iota((128, 128), 1) // 64).astype(F32).astype(BF)

    def body(k, carry):
        peer = step * group + k
        tn = [tgt_ref[peer, j] for j in range(4)]
        tf = [tgt_ref[peer, 4 + j] for j in range(4)]
        points = [got_ref[k, 48:56], got_ref[k, 56:64]]
        feats = []
        for v in range(2):
            feats += planes((points[v] - nc_ref[k, 8 * v : 8 * v + 8]) * ROOT3, True)
        src = jnp.concatenate(feats + [jnp.zeros((64, 128), F32)], axis=0).T.astype(BF)
        for j in range(4):
            dist2 = dot(src[:, 32 * (j // 2) : 32 * (j // 2) + 32], f_ref[tn[j], j % 2])
            value = stack_kernel(matern(dist2))
            qs = jnp.concatenate(split(got_ref[k, 8 * j : 8 * j + 8]), axis=0)
            near_acc[tn[j]] += fold(dot(jnp.concatenate([qs, qs], axis=1), value))
        row = jnp.broadcast_to(points[0][3:4], (8, 128))
        row = jnp.where(lane % 64 == sub, row, 0.0)
        high = row.astype(BF)
        rest = row - high.astype(F32)
        mid = rest.astype(BF)
        low = (rest - mid.astype(F32)).astype(BF)
        cen = dot(jnp.concatenate([high, mid, low], axis=0), spread)
        rel = (fc_ref[k] - (cen[0:8] + cen[8:16] + cen[16:24])) * ROOT3
        tgt = jnp.concatenate(planes(rel, False), axis=0).astype(BF)
        value = stack_kernel(matern(dot(fn_ref[...], tgt)))
        ws = []
        for h in range(2):
            w = got_ref[k, 32 + 8 * h : 40 + 8 * h]
            for part in (jnp.where(left, w, 0.0), jnp.where(left, 0.0, w)):
                ws += list(split(part))
        ws = jnp.concatenate(ws, axis=0)
        locs = dot(jnp.concatenate([ws, ws], axis=1), value)
        for h in range(2):
            for u in range(2):
                at = 32 * h + 16 * u
                new = fold(locs[at : at + 16])
                far_acc[tf[2 * u + h]] += jnp.where(left if h == 0 else jnp.logical_not(left), new, 0.0)
        return carry

    lax.fori_loop(0, group, body, 0, unroll=2)

    @pl.when(step == steps - 1)
    def _():
        def finish(b, total):
            ls = jnp.concatenate(split(far_acc[b]), axis=0)
            both = t_ref[b]
            high, low = both[0:64], both[64:128]
            table = jnp.concatenate([high, high, low, low], axis=0)
            far = fold(dot(jnp.concatenate([ls, ls], axis=1), table))
            live = lane < count_ref[b]
            product = jnp.where(live, near_acc[b] + far, 0.0)
            out_ref[b] = product
            return total + product * q_ref[b]

        total = lax.fori_loop(0, boxes, finish, jnp.zeros((8, 128), F32), unroll=4)
        ones = jnp.ones((128, 128), F32)
        sums = lax.dot_general(ones, total, NT, precision=lax.Precision.HIGHEST, preferred_element_type=F32)
        term_ref[...] = jnp.concatenate([sums, jnp.zeros((128, 120), F32)], axis=1)


def far_sources():
    x = np.zeros((8, 128), np.float32)
    for n in range(64):
        for d, value in enumerate((NODE[n // 16], NODE[n // 4 % 4], NODE[n % 4])):
            for u in range(2):
                x[4 * u + d, 64 * u + n] = 0.5 * ROOT3 * value
    bf = lambda a: a.astype(jnp.bfloat16).astype(np.float32)
    high = bf(x)
    low = bf(x - high)
    norm = np.zeros_like(x)
    square = high * (high + 2 * low)
    for u in range(2):
        norm[4 * u + 3] = square[4 * u] + square[4 * u + 1] + square[4 * u + 2]
    one = bf(norm)
    two = bf(norm - one)
    three = bf(norm - one - two)
    sub = np.arange(8)[:, None] % 4
    unit = (np.arange(8)[:, None] // 4) == (np.arange(128)[None, :] // 64)
    parts = [
        np.where(sub == 3, one, high),
        np.where(sub == 3, two, high),
        np.where(sub == 3, 1.0, low),
        np.where(sub == 3, three, np.where(sub < 2, 1.0, 0.0)),
    ]
    return np.concatenate([np.where(unit, part, 0.0) for part in parts], axis=0).T.astype(np.float32)


def node_rows():
    out = np.zeros((8, 128), np.float32)
    for m in range(128):
        n = m % 64
        for u in range(2):
            for d, value in enumerate((NODE[n // 16], NODE[n // 4 % 4], NODE[n % 4])):
                out[4 * u + d, m] = 0.5 * value
    return out


def vmem(shape=None, index=None):
    if shape is None:
        return pl.BlockSpec(memory_space=pltpu.VMEM)
    return pl.BlockSpec(shape, index, memory_space=pltpu.VMEM)


SMEM = pl.BlockSpec(memory_space=pltpu.SMEM)


def params(mebibytes=56):
    return pltpu.CompilerParams(vmem_limit_bytes=mebibytes * 1024 * 1024)


def exchange(x):
    return lax.all_to_all(x, AXES, split_axis=0, concat_axis=0, tiled=True)


def general(local_pos, charges, counts, box_centers, far_list, near_list):
    devices = lax.axis_size("gx") * lax.axis_size("gy")
    boxes, _, slots = local_pos.shape
    struct = jax.ShapeDtypeStruct
    want = pl.pallas_call(
        ids_kernel,
        out_shape=struct((devices, 128), jnp.int32),
        in_specs=[vmem(), vmem()],
        out_specs=vmem(),
        compiler_params=params(),
        name="ids",
    )(far_list, near_list)
    served = exchange(want.reshape(devices, 1, 128)).reshape(devices, 128)

    group = 16
    lead = lambda shape: vmem((group,) + shape, lambda i: (i,) + (0,) * len(shape))
    q_tab, w_tab, p_tab, f_tab, base, table = pl.pallas_call(
        table_kernel,
        grid=(boxes // group,),
        out_shape=(
            struct((boxes, 8, 128), F32),
            struct((boxes, 8, 128), F32),
            struct((boxes, 8, 128), F32),
            struct((boxes, 2, 32, 128), BF),
            struct((boxes, 8, 128), F32),
            struct((boxes, 128, 128), BF),
        ),
        in_specs=[lead((3, 128)), lead((8, 128)), SMEM, SMEM],
        out_specs=(lead((8, 128)), lead((8, 128)), lead((8, 128)), lead((2, 32, 128)), lead((8, 128)), lead((128, 128))),
        compiler_params=params(),
        cost_estimate=pl.CostEstimate(flops=200_000_000, bytes_accessed=6_000_000, transcendentals=2_000_000),
        name="tables",
    )(local_pos, charges, counts, box_centers)

    send = pl.pallas_call(
        gather_kernel,
        grid=(devices // group,),
        out_shape=struct((devices, 64, 128), F32),
        in_specs=[SMEM, vmem(), vmem(), vmem()],
        out_specs=lead((64, 128)),
        compiler_params=params(),
        name="gather",
    )(served, q_tab, w_tab, p_tab)
    got = exchange(send)

    tgt = want[:, 16:24]
    centers = box_centers.T
    near_cen = jnp.pad(centers[tgt[:, :4]], ((0, 0), (0, 0), (0, 1))).reshape(devices, 16, 1)
    near_cen = jnp.broadcast_to(near_cen, (devices, 16, 128))
    far_cen = jnp.pad(centers[tgt[:, 4:]], ((0, 0), (0, 0), (0, 1))).reshape(devices, 2, 2, 4)
    far_cen = far_cen.transpose(0, 1, 3, 2).reshape(devices, 8, 2, 1)
    far_cen = jnp.broadcast_to(far_cen, (devices, 8, 2, 64)).reshape(devices, 8, 128) + node_rows()[None]

    product, term = pl.pallas_call(
        pair_kernel,
        grid=(devices // group,),
        out_shape=(struct((boxes, 8, 128), F32), struct((devices, 128), F32)),
        in_specs=[
            SMEM,
            SMEM,
            lead((64, 128)),
            lead((16, 128)),
            lead((8, 128)),
            vmem(),
            vmem(),
            vmem(),
            vmem(),
            vmem(),
        ],
        out_specs=(vmem(), vmem()),
        scratch_shapes=[pltpu.VMEM((boxes, 8, 128), F32), pltpu.VMEM((boxes, 8, 128), F32)],
        compiler_params=params(),
        cost_estimate=pl.CostEstimate(flops=1_000_000_000, bytes_accessed=12_000_000, transcendentals=20_000_000),
        name="pairs",
    )(tgt, counts, got, near_cen, far_cen, f_tab, jnp.asarray(far_sources(), BF), base, q_tab, table)

    terms = exchange(term.reshape(devices, 1, 128))[:, 0, :8]
    curvature = jnp.sum(terms, axis=0) / (devices * boxes * slots)
    return (product, curvature)


HALF = 64
ROWS = 44
NEAR_ROWS = 24
UNROLL = 16
CHUNKS = 4
AHEAD = 1


def upper_kernel(pos_ref, charge_ref, count_ref, row_ref, ex_ref):
    half = charge_ref.shape[0] // 2
    lane = iota((8, 128), 1)
    left = lane < HALF
    center = jnp.concatenate([row_ref[...], jnp.zeros((5, 2 * half), F32)], axis=0)
    center = jnp.concatenate([center, jnp.zeros((8, 128 - 2 * half), F32)], axis=1)
    center = jnp.concatenate([center, jnp.zeros((120, 128), F32)], axis=0).T
    wide = iota((half, 128), 1) < HALF
    for d in range(3):
        first = center[:half, d : d + 1] + 0.5 * pos_ref[d, :half]
        second = center[half : 2 * half, d : d + 1] + 0.5 * pos_ref[d, half:]
        ex_ref[(8 + d) * half : (9 + d) * half, :] = jnp.where(wide, pltpu.roll(first, HALF, 1), second)

    def body(b, carry):
        first = pltpu.roll(jnp.where(lane < count_ref[b], charge_ref[b], 0.0), HALF, 1)
        second = jnp.where(lane < count_ref[b + half], charge_ref[b + half], 0.0)
        ex_ref[pl.ds(pl.multiple_of(8 * b, 8), 8), :] = jnp.where(left, first, second)
        return carry

    lax.fori_loop(0, half, body, 0, unroll=16)


def sort_ids(far_ref, near_ref, most_ref, row_ref, msg_ref, want_ref):
    boxes = far_ref.shape[1]
    slots = far_ref.shape[0]
    peer = iota((128, 128), 0)
    line = iota((128, 128), 1)
    tri = (peer < line).astype(F32).astype(BF)
    full = jnp.ones((128, 128), BF)
    row32 = iota((32, 128), 0)
    kind = row32 // 4
    boxrow = iota((32, 128), 1) % boxes
    result = jnp.zeros((128, 32), F32)
    for ref, first, group in ((near_ref, 1, 0), (far_ref, 0, 1)):
        seen = jnp.zeros((128, 128), F32)
        for j in range(0, slots, 2):
            flat = jnp.concatenate([ref[first + j : first + j + 1, :], ref[first + j + 1 : first + j + 2, :]], axis=1)
            hit = jnp.broadcast_to(flat // boxes, (128, 128)) == peer
            onehot = hit.astype(F32).astype(BF)
            before = dot(onehot, tri) + seen
            rank = jnp.sum(jnp.where(hit, before, 0.0), axis=0, keepdims=True).astype(jnp.int32)
            if j + 2 < slots:
                seen = seen + dot(onehot, full)
            within = jnp.broadcast_to(flat % boxes, (32, 128))
            if group == 0:
                value = jnp.where(kind == 0, within * NEAR_ROWS, jnp.where(kind == 2, within * 8, 0))
            else:
                value = jnp.where(kind == 1, within * 8, 0)
            value = jnp.where(kind == 4 + group, boxrow, value)
            value = jnp.where(row32 % 4 == jnp.broadcast_to(rank, (32, 128)), value, 0).astype(F32).astype(BF)
            result = result + dot(onehot, value, NT)
    result = jnp.concatenate([result, jnp.zeros((128, 96), F32)], axis=1)
    heavy = (line == peer - peer % 4).astype(F32).astype(BF)
    first = dot(heavy, result.astype(BF))
    for at, base in ((8, 8), (24, 16)):
        extra = dot(jnp.where(line == base + peer % 4, first, 0.0).astype(BF), full)
        result = jnp.where(line == at, extra, result)
    most = jnp.max(most_ref[...], axis=1, keepdims=True).astype(F32)
    result = jnp.where(line == 9, jnp.broadcast_to(most, (128, 128)), result)
    want_ref[...] = result.astype(jnp.int32)
    rows = [jnp.concatenate([row_ref[d : d + 1, :]] * 2, axis=1) for d in range(3)]
    rows = [jnp.broadcast_to(row, (128, 128)) for row in rows]
    msg_ref[pl.ds(0, 128, stride=2), :] = jnp.where(line < HALF, result, rows[2])
    msg_ref[pl.ds(1, 128, stride=2), :] = jnp.where(line < HALF, rows[0], rows[1])


def first_kernel(
    member_ref, count_ref, far_ref, near_ref, most_ref, row_ref, pos_hbm, charge_hbm, msg_hbm, want_hbm, ex_ref,
    pos_ref, charge_ref, msg_ref, want_ref, sems
):
    @pl.when(member_ref[0] == 0)
    def _():
        loads = [pltpu.make_async_copy(pos_hbm, pos_ref, sems.at[0]), pltpu.make_async_copy(charge_hbm, charge_ref, sems.at[1])]
        for copy in loads:
            copy.start()
        sort_ids(far_ref, near_ref, most_ref, row_ref, msg_ref, want_ref)
        stores = [pltpu.make_async_copy(msg_ref, msg_hbm, sems.at[2]), pltpu.make_async_copy(want_ref, want_hbm, sems.at[3])]
        for copy in stores:
            copy.start()
        for copy in loads:
            copy.wait()
        upper_kernel(pos_ref, charge_ref, count_ref, row_ref, ex_ref)
        for copy in stores:
            copy.wait()


def second_kernel(
    member_ref, far_ref, near_ref, most_ref, row_ref, msg_in, want_in, msg_hbm, want_hbm, msg_ref, want_ref, sems
):
    @pl.when(member_ref[0] != 0)
    def _():
        sort_ids(far_ref, near_ref, most_ref, row_ref, msg_ref, want_ref)
        stores = [pltpu.make_async_copy(msg_ref, msg_hbm, sems.at[0]), pltpu.make_async_copy(want_ref, want_hbm, sems.at[1])]
        for copy in stores:
            copy.start()
        for copy in stores:
            copy.wait()


def cheb_rows(x):
    sub = iota((8, 128), 0)
    second = 2.0 * x * x - 1.0
    third = 2.0 * x * second - x
    basis = []
    for i in range(NODES):
        theta = (2 * i + 1) * math.pi / 8
        basis.append(0.25 + 0.5 * (math.cos(theta) * x + math.cos(2 * theta) * second + math.cos(3 * theta) * third))
    row = lambda i, d: jnp.broadcast_to(basis[i][d : d + 1], (8, 128))
    sub4 = sub % 4
    zs = jnp.where(sub4 == 0, row(0, 2), jnp.where(sub4 == 1, row(1, 2), jnp.where(sub4 == 2, row(2, 2), row(3, 2))))
    ys = [jnp.where(sub < 4, row(0, 1), row(1, 1)) * zs, jnp.where(sub < 4, row(2, 1), row(3, 1)) * zs]
    return jnp.concatenate([row(i, 0) * ys[j] for i in range(NODES) for j in range(2)], axis=0)


def point_rows(pos_ref, b):
    sub4 = iota((8, 128), 0) % 4
    x = jnp.zeros((8, 128), F32)
    for d in range(3):
        x = jnp.where(sub4 == d, jnp.broadcast_to(pos_ref[d, pl.ds(b, 1), :], (8, 128)), x)
    return x


def doubled(x):
    return jnp.where(iota((8, 128), 1) < HALF, x, pltpu.roll(x, HALF, 1))


def fill_basis(pos_ref, basis_ref):
    for d in range(3):
        x = pos_ref[d]
        second = 2.0 * x * x - 1.0
        third = 2.0 * x * second - x
        for i in range(NODES):
            theta = (2 * i + 1) * math.pi / 8
            value = math.cos(theta) * x + math.cos(2 * theta) * second + math.cos(3 * theta) * third
            basis_ref[4 * d + i] = 0.25 + 0.5 * value


def basis_table(basis_ref, b):
    sub = iota((8, 128), 0)
    row = lambda i, d: jnp.broadcast_to(basis_ref[4 * d + i, pl.ds(b, 1), :], (8, 128))
    sub4 = sub % 4
    zs = jnp.where(sub4 == 0, row(0, 2), jnp.where(sub4 == 1, row(1, 2), jnp.where(sub4 == 2, row(2, 2), row(3, 2))))
    ys = [jnp.where(sub < 4, row(0, 1), row(1, 1)) * zs, jnp.where(sub < 4, row(2, 1), row(3, 1)) * zs]
    return jnp.concatenate([row(i, 0) * ys[j] for i in range(NODES) for j in range(2)], axis=0)


def send_table_kernel(pos_ref, charge_ref, count_ref, cen_ref, near_ref, far_ref, basis_ref):
    boxes = charge_ref.shape[0]
    lane = iota((8, 128), 1)
    sub = iota((8, 128), 0)
    fill_basis(pos_ref, basis_ref)

    def body(b, carry):
        q = jnp.where(lane < count_ref[b], charge_ref[b], 0.0)
        near_ref[b, 0:8] = doubled(q)
        x, y, z = [doubled(cen_ref[d, b] + 0.5 * jnp.broadcast_to(pos_ref[d, pl.ds(b, 1), :], (8, 128))) for d in range(3)]
        near_ref[b, 8:16] = jnp.where(sub == 4, x, jnp.where(sub == 5, y, z))
        near_ref[b, 16:24] = jnp.where(sub == 7, x, jnp.where((sub == 3) | (sub == 5), y, z))
        table = basis_table(basis_ref, b)
        qs = jnp.concatenate(split(q), axis=0)
        weight = fold(dot(qs, stack_kernel(table), NT))
        far_ref[b] = weight + pltpu.roll(weight, 64, 1)
        return carry

    lax.fori_loop(0, boxes, body, 0, unroll=32)


def own_table_kernel(pos_ref, charge_ref, count_ref, q_ref, f_ref, base_ref):
    boxes = charge_ref.shape[0]
    sub = iota((8, 128), 0)
    lane = iota((8, 128), 1)

    def body(b, carry):
        q = jnp.where(lane < count_ref[b], charge_ref[b], 0.0)
        q_ref[b] = q
        x = point_rows(pos_ref, b)
        rel = (0.5 * ROOT3) * x
        tgt = planes(rel, False)
        for unit in range(2):
            f_ref[b, unit] = jnp.concatenate([jnp.where(sub // 4 == unit, part, 0.0) for part in tgt], axis=0).astype(BF)
        zero = jnp.zeros((96, 128), F32)
        src = jnp.concatenate(planes(rel, True) + [zero], axis=0).T.astype(BF)
        first = jnp.concatenate([jnp.where(sub < 4, part, 0.0) for part in tgt] + [zero], axis=0).astype(BF)
        value = stack_kernel(matern(dot(src, first)))
        qs = jnp.concatenate(split(q), axis=0)
        base_ref[b] = fold(dot(jnp.concatenate([qs, qs], axis=1), value)) + q
        return carry

    lax.fori_loop(0, boxes, body, 0, unroll=4)


def goal_kernel(want_ref, served_ref, cen_ref, node_ref, nc_ref, fc_ref, ec_ref, goal_ref, odd_ref):
    lane = iota((128, 128), 1)
    left = lane < HALF
    boxes = cen_ref.shape[1]
    cen = jnp.concatenate([cen_ref[...], jnp.zeros((5, boxes), F32)], axis=0)
    cen = jnp.concatenate([cen, jnp.zeros((8, 128 - boxes), F32)], axis=1)
    cen = jnp.concatenate([cen, jnp.zeros((120, 128), F32)], axis=0).T

    def split3(x, axis):
        high = x.astype(BF)
        rest = x - high.astype(F32)
        mid = rest.astype(BF)
        return jnp.concatenate([high, mid, (rest - mid.astype(F32)).astype(BF)], axis=axis)

    parts = split3(cen, 0)
    want = want_ref[...]
    goal_ref[...] = want.astype(F32).T[16:32].astype(jnp.int32)
    sources = [served_ref[pl.ds(1, 128, stride=2), :], served_ref[pl.ds(0, 128, stride=2), :]]
    halves = [jnp.concatenate([(iota((128, 128), 0) // HALF == h).astype(F32).astype(BF)] * 3, axis=0) for h in range(2)]

    def column(at):
        return jnp.broadcast_to(want[:, at : at + 1], (128, 128))

    def centers(at):
        onehot = (column(at) == lane).astype(F32).astype(BF)
        found = dot(jnp.concatenate([onehot] * 3, axis=1), parts)
        return [jnp.broadcast_to(found[:, d : d + 1], (128, 128)) for d in range(3)]

    def gaps(j):
        mine = lane % HALF == column(4 + j) // 8
        both = [split3(jnp.where(mine, source, 0.0), 1) for source in sources]
        theirs = [dot(both[0], halves[0]), dot(both[0], halves[1]), dot(both[1], halves[1])]
        return [a - b for a, b in zip(centers(20 + j), theirs)]

    nc_ref[...] = jnp.zeros_like(nc_ref)
    fc_ref[...] = jnp.zeros_like(fc_ref)
    ec_ref[...] = jnp.zeros_like(ec_ref)
    for u in range(2):
        first, second = centers(16 + 2 * u), centers(17 + 2 * u)
        for d in range(3):
            nc_ref[pl.ds(4 * u + d, 128, stride=8), :] = jnp.where(left, first[d], second[d])
        first, second = gaps(2 * u), gaps(2 * u + 1)
        for d in range(3):
            fc_ref[pl.ds(4 * u + d, 128, stride=8), :] = jnp.where(left, first[d], second[d]) + node_ref[d : d + 1, :]
    extra = centers(24)
    for d in range(3):
        odd_ref[...] = extra[d]
        even, odd = odd_ref[pl.ds(0, 64, stride=2), :], odd_ref[pl.ds(1, 64, stride=2), :]
        ec_ref[pl.ds(d, 64, stride=8), :] = jnp.where(left[:64], even, odd)


def far_kernel(fc_ref, fn_ref, out_ref):
    group = fc_ref.shape[0]
    tgt = jnp.concatenate(planes(fc_ref[...] * ROOT3, False), axis=1).astype(BF)
    for k in range(group):
        out_ref[k] = stack_kernel(matern(dot(fn_ref[...], tgt[k])))


def send_kernel(member_ref, served_ref, near_ref, far_ref, own_ref, *refs):
    moved, (out_ref, ids_ref, int_ref, ex_ref, buf_ref, sems) = refs[:3], refs[3:]
    peers = ids_ref.shape[1]
    sub = iota((8, 128), 0)
    lane = iota((8, 128), 1)
    left = lane < HALF
    keep = left | (sub < 3)
    second = sub < 5
    int_ref[...] = served_ref[pl.ds(0, peers, stride=2), :].T[:16].astype(jnp.int32)
    copy = pltpu.make_async_copy(int_ref, ids_ref, sems.at[0])
    copy.start()
    half = ex_ref.shape[0] // 16
    packed = moved[0][...] + moved[1][...] + moved[2][...]
    packed = jnp.where(member_ref[0] == 0, own_ref[...], packed)
    for d in range(3):
        rows = packed[(8 + d) * half : (9 + d) * half]
        ex_ref[pl.ds(d, half, stride=8), :] = pltpu.roll(rows, HALF, 1)
        ex_ref[pl.ds(8 * half + d, half, stride=8), :] = rows
    for b in range(half):
        tile = packed[8 * b : 8 * b + 8]
        for at, part in ((8 * b, tile), (8 * (b + half), pltpu.roll(tile, HALF, 1))):
            ex_ref[at : at + 8, :] = jnp.where(left, part, jnp.where(sub < 3, ex_ref[at : at + 8, :], 0.0))
    copy.wait()

    def body(i, carry):
        base = pl.multiple_of(i * 2 * ROWS, 8)
        for k in range(2):
            peer = 2 * i + k
            at = lambda row: pl.ds(base + (k * ROWS + row), 8)
            rows = lambda ref, j, row: ref[pl.ds(pl.multiple_of(ids_ref[j, peer], 8) + row, 8), :]
            q = [rows(near_ref, j, 0) for j in range(4)]
            w = [rows(far_ref, 4 + j, 0) for j in range(4)]
            p = [rows(near_ref, j, 16 if j < 2 else 8) for j in range(4)]
            buf_ref[at(0), :] = jnp.where(left, q[0], q[1])
            buf_ref[at(8), :] = jnp.where(left, q[2], q[3])
            buf_ref[at(16), :] = jnp.where(left, w[0], w[2])
            buf_ref[at(24), :] = jnp.where(left, w[1], w[3])
            buf_ref[at(36), :] = jnp.where(sub == 7, jnp.where(left, p[0], p[1]), jnp.where(left, p[2], p[3]))
            buf_ref[at(32), :] = jnp.where(keep, rows(ex_ref, 8, 0), jnp.where(second, p[1], p[0]))
        return carry

    chunks = 8
    each = peers // chunks
    stores = []
    for c in range(chunks):
        lax.fori_loop(c * each // 2, (c + 1) * each // 2, body, 0, unroll=8)
        at = pl.ds(c * each * ROWS, each * ROWS)
        stores.append(pltpu.make_async_copy(buf_ref.at[at], out_ref.at[at], sems.at[1 + c]))
        stores[-1].start()
    for copy in stores:
        copy.wait()


def duo_kernel(
    scale, got_ref, want_hbm, nc_hbm, ec_hbm, f_hbm, base_hbm, q_hbm, w_hbm, v_hbm, near0_hbm, near1_hbm, far0_hbm, far1_hbm, term_hbm,
    tgt_ref, nc_ref, ec_ref, f_ref, base_ref, q_ref, w_ref, v_ref, term_ref, sems, *bufs
):
    whole = [(want_hbm, tgt_ref), (nc_hbm, nc_ref), (ec_hbm, ec_ref), (f_hbm, f_ref)]
    whole += [(base_hbm, base_ref), (q_hbm, q_ref), (w_hbm, w_ref)]
    loads = [pltpu.make_async_copy(source, target, sems.at[i]) for i, (source, target) in enumerate(whole)]
    for copy in loads[:4]:
        copy.start()
    chunk = v_ref.shape[0] // CHUNKS

    def far_values(c):
        at = pl.ds(c * chunk, chunk)
        return pltpu.make_async_copy(v_hbm.at[at], v_ref.at[at], sems.at[16 + c % AHEAD])

    for c in range(AHEAD):
        far_values(c).start()
    xt_refs, dist_refs, value_refs = bufs[:2], (bufs[2:7], bufs[7:12]), (bufs[12:17], bufs[17:22])
    near_accs, far_accs = bufs[22:24], bufs[24:26]
    duos = ec_ref.shape[0]
    boxes = f_ref.shape[0]
    sub = iota((8, 128), 0)
    lane = iota((8, 128), 1)
    left = lane < HALF
    for ref in value_refs[1] + near_accs + far_accs:
        ref[...] = jnp.zeros_like(ref)
    for ref in dist_refs[1]:
        ref[...] = jnp.full(ref.shape, 1e6, F32)
    def tile(duo, a, row):
        return got_ref[pl.ds(pl.multiple_of(duo * 2 * ROWS, 8) + (a * ROWS + row), 8), :]

    def extra(duo):
        return tile(duo, 0, 32), tile(duo, 1, 32)

    def goals(duo):
        pairs = [(tgt_ref[2 * (k % 2), 2 * duo + k // 2], tgt_ref[2 * (k % 2) + 1, 2 * duo + k // 2]) for k in range(4)]
        return pairs + [(tgt_ref[8, 2 * duo], tgt_ref[8, 2 * duo + 1])]

    def halves(x):
        high = x.astype(BF).astype(F32)
        both = [high, x - high]
        return [jnp.where(left, part, 0.0) for part in both] + [jnp.where(left, 0.0, part) for part in both]

    def products(duo, value):
        ex = extra(duo)
        tiles = [tile(duo, k // 2, 8 * (k % 2)) for k in range(4)]
        tiles.append(jnp.where(left, ex[0], pltpu.roll(ex[1], HALF, 1)))
        for k, goal in enumerate(goals(duo)):
            qs = jnp.concatenate(halves(tiles[k]), axis=0).astype(BF)
            new = dot(jnp.concatenate([qs, qs], axis=1), value[k][...])
            for h in range(2):
                near_accs[h][goal[h]] += fold(new[16 * h : 16 * h + 16])

    def far_products(duo):
        for a in range(2):
            ws = []
            for h in range(2):
                ws += halves(tile(duo, a, 16 + 8 * h))
            ws = jnp.concatenate(ws, axis=0).astype(BF)
            new = dot(jnp.concatenate([ws, ws], axis=1), v_ref[2 * duo + a])
            for h in range(2):
                for u in range(2):
                    at = 32 * h + 16 * u
                    far_accs[h][tgt_ref[4 + 2 * u + h, 2 * duo + a]] += fold(new[at : at + 16])

    def values(dist, value):
        for k in range(5):
            value[k][...] = stack_kernel(matern(dist[k][...]))

    def distances(duo, xt, dist):
        for k, goal in enumerate(goals(duo)):
            v, u = k // 2, k % 2
            for half in range(2):
                pieces = [jnp.zeros((32 * v, 128), BF)] if v else []
                pieces += [f_ref[goal[half], u], jnp.zeros((96 - 32 * v, 128), BF)]
                at = slice(64 * half, 64 * half + 64)
                dist[k][at, :] = dot(xt[at, :], jnp.concatenate(pieces, axis=0))

    def features(duo, xt):
        ex = extra(duo)
        turned = [pltpu.roll(x, HALF, 1) for x in ex]
        feats = []
        for a in range(2):
            full = tile(duo, a, 36)
            split_rows = jnp.where(left, pltpu.roll(turned[a], 4, 0), pltpu.roll(ex[a], 6, 0))
            point = jnp.where(sub >= 4, full, jnp.where(sub == 0, pltpu.roll(full, 1, 0), split_rows))
            feats += planes((point - nc_ref[2 * duo + a]) * ROOT3, True)
        point = jnp.where(left, turned[0], ex[1])
        feats += planes((point - ec_ref[duo]) * ROOT3, True)
        feats.append(jnp.zeros((32, 128), F32))
        xt[...] = jnp.concatenate(feats, axis=0).T.astype(BF)

    turns = duos // UNROLL
    assert turns == CHUNKS

    def body(i, carry):
        far_values(i).wait()

        @pl.when(i + AHEAD < CHUNKS)
        def _():
            far_values(i + AHEAD).start()

        for s in range(UNROLL):
            now, was = s % 2, 1 - s % 2
            step = UNROLL * i + s
            products(jnp.maximum(step - 2, 0), value_refs[was])
            far_products(step)
            values(dist_refs[was], value_refs[now])
            distances(step, xt_refs[was], dist_refs[now])
            features(jnp.minimum(step + 1, duos - 1), xt_refs[now])
        return carry

    for copy in loads[:4]:
        copy.wait()
    features(0, xt_refs[1])
    for copy in loads[4:]:
        copy.start()
    lax.fori_loop(0, turns, body, 0)
    products(duos - 2, value_refs[1])
    values(dist_refs[1], value_refs[0])
    products(duos - 1, value_refs[0])

    sums = (near0_hbm, near1_hbm, far0_hbm, far1_hbm)
    stores = [pltpu.make_async_copy(a, b, sems.at[8 + i]) for i, (a, b) in enumerate(zip(near_accs + far_accs, sums))]
    for copy in stores:
        copy.start()
    for copy in loads[4:]:
        copy.wait()

    def finish(b, total):
        near = near_accs[0][b] + near_accs[1][b] + base_ref[b]
        far = jnp.where(left, far_accs[0][b], far_accs[1][b])
        return total + near * q_ref[b] + far * w_ref[b]

    total = lax.fori_loop(0, boxes, finish, jnp.zeros((8, 128), F32), unroll=16)
    high = total.astype(BF)
    rest = total - high.astype(F32)
    mid = rest.astype(BF)
    parts = jnp.concatenate([high, mid, (rest - mid.astype(F32)).astype(BF)], axis=1)
    sums = dot(jnp.ones((128, 384), BF), parts, NT)
    term_ref[...] = jnp.concatenate([sums * scale, jnp.zeros((128, 120), F32)], axis=1)
    stores.append(pltpu.make_async_copy(term_ref, term_hbm, sems.at[12]))
    stores[-1].start()
    for copy in stores:
        copy.wait()


def finish_kernel(count_ref, pos_ref, near0_ref, near1_ref, far0_ref, far1_ref, base_ref, out_ref, basis_ref):
    boxes = base_ref.shape[0]
    lane = iota((8, 128), 1)
    fill_basis(pos_ref, basis_ref)

    def body(b, carry):
        locs = jnp.where(lane < HALF, far0_ref[b], far1_ref[b])
        ls = jnp.concatenate(split(locs), axis=0)
        high, low = split(basis_table(basis_ref, b))
        far = fold(dot(jnp.concatenate([ls, ls], axis=1), jnp.concatenate([high, high, low, low], axis=0)))
        near = near0_ref[b] + near1_ref[b] + base_ref[b]
        out_ref[b] = jnp.where(lane < count_ref[b], near + far, 0.0)
        return carry

    lax.fori_loop(0, boxes, body, 0, unroll=16)


def on_device(local_pos, charges, counts, box_centers, far_list, near_list):
    devices = lax.axis_size("gx") * lax.axis_size("gy")
    boxes, _, slots = local_pos.shape
    struct = jax.ShapeDtypeStruct
    hbm = pltpu.HBM
    stay = lambda x: pltpu.with_memory_space_constraint(x, pltpu.HBM)
    anywhere = pl.BlockSpec(memory_space=pltpu.HBM)
    pos = jnp.transpose(local_pos, (1, 0, 2))
    table = struct((boxes, 8, 128), F32)
    flat = lambda x: x.reshape(-1, 128)
    member = (lax.axis_index("gy") % 4).astype(jnp.int32).reshape(1)
    lists = (far_list.T, near_list.T, counts.reshape(1, boxes), box_centers)
    ids_shape = (hbm((devices * 2, 128), F32), hbm((devices, 128), jnp.int32))
    ids_scratch = [pltpu.VMEM((devices * 2, 128), F32), pltpu.VMEM((devices, 128), jnp.int32)]
    msg, want, ex_own = pl.pallas_call(
        first_kernel,
        out_shape=ids_shape + (struct((boxes * 11 // 2, 128), F32),),
        in_specs=[SMEM, SMEM] + [vmem()] * 4 + [anywhere] * 2,
        out_specs=(anywhere, anywhere, vmem()),
        scratch_shapes=[pltpu.VMEM((3, boxes, 128), F32), pltpu.VMEM((boxes, 8, 128), F32)]
        + ids_scratch
        + [pltpu.SemaphoreType.DMA((4,))],
        compiler_params=params(8),
        name="first",
    )(member, counts, *lists, stay(pos), stay(charges))
    msg, want = pl.pallas_call(
        second_kernel,
        out_shape=ids_shape,
        in_specs=[SMEM] + [vmem()] * 4 + [anywhere] * 2,
        out_specs=(anywhere, anywhere),
        scratch_shapes=ids_scratch + [pltpu.SemaphoreType.DMA((2,))],
        input_output_aliases={5: 0, 6: 1},
        compiler_params=params(8),
        name="second",
    )(member, *lists, stay(msg), stay(want))
    moved = [lax.ppermute(ex_own, "gy", [(4 * z, 4 * z + k) for z in range(4)]) for k in range(1, 4)]
    served = flat(exchange(msg.reshape(devices, 2, 128)))

    near_tab, far_tab = pl.pallas_call(
        send_table_kernel,
        out_shape=(struct((boxes, NEAR_ROWS, 128), F32), table),
        in_specs=[vmem(), vmem(), SMEM, SMEM],
        out_specs=(vmem(), vmem()),
        scratch_shapes=[pltpu.VMEM((12, boxes, 128), F32)],
        compiler_params=params(8),
        cost_estimate=pl.CostEstimate(flops=50_000_000, bytes_accessed=1_200_000, transcendentals=0),
        name="send_tables",
    )(pos, charges, counts, box_centers)

    send = pl.pallas_call(
        send_kernel,
        out_shape=hbm((devices * ROWS, 128), F32),
        in_specs=[SMEM] + [vmem()] * 7,
        out_specs=anywhere,
        scratch_shapes=[
            pltpu.SMEM((16, devices), jnp.int32),
            pltpu.VMEM((16, devices), jnp.int32),
            pltpu.VMEM((boxes * 8, 128), F32),
            pltpu.VMEM((devices * ROWS, 128), F32),
            pltpu.SemaphoreType.DMA((9,)),
        ],
        compiler_params=params(12),
        name="send",
    )(member, served, flat(near_tab), flat(far_tab), ex_own, *moved)
    got = flat(exchange(send.reshape(devices, ROWS // 4, 4, 128)))

    q_tab, f_tab, base = pl.pallas_call(
        own_table_kernel,
        out_shape=(hbm((boxes, 8, 128), F32), hbm((boxes, 2, 32, 128), BF), hbm((boxes, 8, 128), F32)),
        in_specs=[vmem(), vmem(), SMEM],
        out_specs=(vmem(), vmem(), vmem()),
        compiler_params=params(8),
        cost_estimate=pl.CostEstimate(flops=200_000_000, bytes_accessed=4_000_000, transcendentals=2_000_000),
        name="own_tables",
    )(pos, charges, counts)

    near_cen, far_gap, ex_cen, goals = pl.pallas_call(
        goal_kernel,
        out_shape=(
            hbm((devices * 8, 128), F32),
            hbm((devices * 8, 128), F32),
            hbm((devices * 4, 128), F32),
            hbm((16, devices), jnp.int32),
        ),
        in_specs=[vmem()] * 4,
        out_specs=(vmem(),) * 4,
        scratch_shapes=[pltpu.VMEM((128, 128), F32)],
        compiler_params=params(8),
        cost_estimate=pl.CostEstimate(flops=50_000_000, bytes_accessed=2_000_000, transcendentals=0),
        name="goals",
    )(want, served, box_centers, jnp.asarray(node_rows()))
    near_cen, far_gap, ex_cen = [x.reshape(-1, 8, 128) for x in (near_cen, far_gap, ex_cen)]
    group = 8
    far_value = pl.pallas_call(
        far_kernel,
        grid=(devices // group,),
        out_shape=hbm((devices, 256, 128), BF),
        in_specs=[vmem((group, 8, 128), lambda i: (i, 0, 0)), vmem()],
        out_specs=vmem((group, 256, 128), lambda i: (i, 0, 0)),
        compiler_params=params(8),
        cost_estimate=pl.CostEstimate(flops=200_000_000, bytes_accessed=9_000_000, transcendentals=4_000_000),
        name="far_values",
    )(far_gap, jnp.asarray(far_sources(), BF))

    big = lambda dtype, rows: pltpu.VMEM((rows, 128), dtype)
    *sums, term = pl.pallas_call(
        functools.partial(duo_kernel, 1.0 / (devices * boxes * slots)),
        out_shape=(hbm((boxes, 8, 128), F32),) * 4 + (hbm((devices, 128), F32),),
        in_specs=[vmem()] + [anywhere] * 8,
        out_specs=(anywhere,) * 5,
        scratch_shapes=[
            pltpu.SMEM((16, devices), jnp.int32),
            pltpu.VMEM((devices, 8, 128), F32),
            pltpu.VMEM((devices // 2, 8, 128), F32),
            pltpu.VMEM((boxes, 2, 32, 128), BF),
            pltpu.VMEM((boxes, 8, 128), F32),
            pltpu.VMEM((boxes, 8, 128), F32),
            pltpu.VMEM((boxes, 8, 128), F32),
            pltpu.VMEM((devices, 256, 128), BF),
            pltpu.VMEM((devices, 128), F32),
            pltpu.SemaphoreType.DMA((20,)),
        ]
        + [big(BF, 128)] * 2
        + [big(F32, 128)] * 10
        + [big(BF, 256)] * 10
        + [pltpu.VMEM((boxes, 8, 128), F32)] * 4,
        compiler_params=params(28),
        cost_estimate=pl.CostEstimate(flops=1_000_000_000, bytes_accessed=12_000_000, transcendentals=20_000_000),
        name="pairs",
    )(got, *[stay(x) for x in (goals, near_cen, ex_cen, f_tab, base, q_tab, far_tab, far_value)])

    terms = exchange(term.reshape(devices, 1, 128))[:, 0, :8]
    curvature = jnp.sum(terms, axis=0)
    product = pl.pallas_call(
        finish_kernel,
        out_shape=table,
        in_specs=[SMEM] + [vmem()] * 6,
        out_specs=vmem(),
        scratch_shapes=[pltpu.VMEM((12, boxes, 128), F32)],
        compiler_params=params(8),
        cost_estimate=pl.CostEstimate(flops=50_000_000, bytes_accessed=3_000_000, transcendentals=0),
        name="finish",
    )(counts, pos, *[stay(x) for x in (*sums, base)])
    over = jnp.any((served.reshape(devices, 2, 128)[:, 0, 9] > HALF) & (jnp.arange(devices) % 4 != 0))
    whole = (local_pos, charges, counts, box_centers, far_list, near_list)
    return lax.cond(over, lambda: general(*whole), lambda: (product, curvature))


def solution(mesh):
    in_specs = (
        P(AXES, None, None),
        P(AXES, None, None),
        P(AXES),
        P(None, AXES),
        P(AXES, None),
        P(AXES, None),
    )
    out_specs = (P(AXES, None, None), P())
    return jax.shard_map(on_device, mesh=mesh, in_specs=in_specs, out_specs=out_specs, check_vma=False)
```

```python
import functools
import math

import jax
import jax.numpy as jnp
import numpy as np
from jax import lax
from jax.experimental import pallas as pl
from jax.experimental.pallas import tpu as pltpu
from jax.sharding import PartitionSpec as P

AXES = ("gx", "gy")
NODES = 4
ROOT3 = 1.7320508075688772
LOG2E = 1.4426950408889634
BF = jnp.bfloat16
F32 = jnp.float32
NODE = [math.cos((2 * i + 1) * math.pi / 8) for i in range(NODES)]
NT = (((1,), (1,)), ((), ()))
TN = (((0,), (0,)), ((), ()))


def iota(shape, dim):
    return lax.broadcasted_iota(jnp.int32, shape, dim)


def dot(a, b, dims=None):
    if dims is None:
        return jnp.dot(a, b, preferred_element_type=F32)
    return lax.dot_general(a, b, dims, preferred_element_type=F32)


def split(x):
    high = x.astype(BF)
    return high, (x - high.astype(F32)).astype(BF)


def planes(rel, source):
    axis = rel.ndim - 2
    sub = iota(rel.shape, axis) % 4
    last = sub == 3
    rel = jnp.where(last, 0.0, rel)
    high = rel.astype(BF).astype(F32)
    low = (rel - high).astype(BF).astype(F32)
    square = high * (high + 2.0 * low)
    norm = pltpu.roll(square, 1, axis) + pltpu.roll(square, 2, axis) + pltpu.roll(square, 3, axis)
    one = norm.astype(BF).astype(F32)
    rest = norm - one
    two = rest.astype(BF).astype(F32)
    three = (rest - two).astype(BF).astype(F32)
    if source:
        parts = [
            jnp.where(last, one, high),
            jnp.where(last, two, high),
            jnp.where(last, 1.0, low),
            jnp.where(last, three, jnp.where(sub < 2, 1.0, 0.0)),
        ]
    else:
        parts = [
            jnp.where(last, 1.0, -2.0 * high),
            jnp.where(last, 1.0, -2.0 * low),
            jnp.where(last, one, -2.0 * high),
            jnp.where(
                sub == 0,
                pltpu.roll(two, 5, axis),
                jnp.where(sub == 1, pltpu.roll(three, 6, axis), jnp.where(last, 1.0, 0.0)),
            ),
        ]
    return parts


def matern(dist2):
    safe = jnp.maximum(dist2, 1e-12)
    scaled = safe * lax.rsqrt(safe)
    decay = jnp.exp2(scaled * (-LOG2E))
    return decay + scaled * decay


def stack_kernel(value):
    high, low = split(value)
    return jnp.concatenate([high, low], axis=0)


def fold(x):
    return x[0:8] + x[8:16]


def ids_kernel(far_ref, near_ref, want_ref):
    boxes = far_ref.shape[0]
    slots = far_ref.shape[1]
    total = boxes * slots
    lane = iota((total, 128), 1)
    box = iota((total, 128), 0) % boxes
    tri = (iota((total, total), 0) > iota((total, total), 1)).astype(F32).astype(BF)
    result = jnp.zeros((128, 128), F32)
    for ref, first, base in ((near_ref, 1, 0), (far_ref, 0, 4)):
        flat = jnp.concatenate([ref[:, first + j : first + j + 1] for j in range(slots)], axis=0)
        flat = jnp.broadcast_to(flat, (total, 128))
        hit = (flat // boxes) == lane
        onehot = hit.astype(F32).astype(BF)
        before = dot(tri, onehot)
        rank = jnp.sum(jnp.where(hit, before, 0.0), axis=1, keepdims=True).astype(jnp.int32)
        mine = rank == (lane % 4)
        within = jnp.where((lane >= base) & (lane < base + 4), flat % boxes, 0)
        owner = jnp.where((lane >= base + 16) & (lane < base + 20), box, 0)
        value = jnp.where(mine, within + owner, 0).astype(F32).astype(BF)
        result = result + dot(onehot, value, TN)
    want_ref[...] = result.astype(jnp.int32)


def table_kernel(pos_ref, charge_ref, count_ref, cen_ref, q_ref, w_ref, p_ref, f_ref, base_ref, t_ref):
    step = pl.program_id(0)
    group = pos_ref.shape[0]
    sub = iota((8, 128), 0)
    lane = iota((8, 128), 1)

    def body(b, carry):
        box = step * group + b
        live = lane < count_ref[box]
        q = jnp.where(live, charge_ref[b], 0.0)
        q_ref[b] = q
        pos = pos_ref[b]
        zero1 = jnp.zeros((1, 128), F32)
        x4 = jnp.concatenate([pos, zero1], axis=0)
        x = jnp.concatenate([x4, x4], axis=0)
        second = 2.0 * x * x - 1.0
        third = 2.0 * x * second - x
        basis = []
        for i in range(NODES):
            theta = (2 * i + 1) * math.pi / 8
            basis.append(0.25 + 0.5 * (math.cos(theta) * x + math.cos(2 * theta) * second + math.cos(3 * theta) * third))
        row = lambda i, d: jnp.broadcast_to(basis[i][d : d + 1], (8, 128))
        sub4 = sub % 4
        zs = jnp.where(sub4 == 0, row(0, 2), jnp.where(sub4 == 1, row(1, 2), jnp.where(sub4 == 2, row(2, 2), row(3, 2))))
        ys = [jnp.where(sub < 4, row(0, 1), row(1, 1)) * zs, jnp.where(sub < 4, row(2, 1), row(3, 1)) * zs]
        table = jnp.concatenate([row(i, 0) * ys[j] for i in range(NODES) for j in range(2)], axis=0)
        both = stack_kernel(table)
        t_ref[b] = both
        qs = jnp.concatenate(split(q), axis=0)
        weight = fold(dot(qs, both, NT))
        w_ref[b] = weight + pltpu.roll(weight, 64, 1)
        cx, cy, cz = cen_ref[0, box], cen_ref[1, box], cen_ref[2, box]
        lane4 = lane % 4
        far = jnp.where(lane4 == 0, cx, jnp.where(lane4 == 1, cy, cz))
        center = jnp.where(sub4 == 0, cx, jnp.where(sub4 == 1, cy, cz))
        p_ref[b] = jnp.where(sub4 == 3, far, center + 0.5 * x)
        rel = (0.5 * ROOT3) * x
        tgt = planes(rel, False)
        for unit in range(2):
            f_ref[b, unit] = jnp.concatenate([jnp.where(sub // 4 == unit, part, 0.0) for part in tgt], axis=0).astype(BF)
        src = jnp.concatenate(planes(rel, True) + [jnp.zeros((96, 128), F32)], axis=0).T.astype(BF)
        dist2 = dot(src[:, :32], f_ref[b, 0])
        value = stack_kernel(matern(dist2))
        near = fold(dot(jnp.concatenate([qs, qs], axis=1), value))
        base_ref[b] = near + q
        return carry

    lax.fori_loop(0, group, body, 0, unroll=4)


def gather_kernel(ids_ref, q_ref, w_ref, p_ref, out_ref):
    step = pl.program_id(0)
    group = out_ref.shape[0]
    sub4 = iota((8, 128), 0) % 4
    top = iota((8, 128), 0) < 4
    lane = iota((8, 128), 1)
    left = lane < 64

    def body(k, carry):
        peer = step * group + k
        near = [ids_ref[peer, j] for j in range(4)]
        far = [ids_ref[peer, 4 + j] for j in range(4)]
        for j in range(4):
            out_ref[k, 8 * j : 8 * j + 8] = q_ref[near[j]]
        w = [w_ref[far[j]] for j in range(4)]
        out_ref[k, 32:40] = jnp.where(left, w[0], w[2])
        out_ref[k, 40:48] = jnp.where(left, w[1], w[3])
        c = [p_ref[far[j]] for j in range(4)]
        centers = jnp.where(
            left, jnp.where(lane < 4, c[0], c[2]), jnp.where(lane < 68, c[1], c[3])
        )
        s = [p_ref[near[j]] for j in range(4)]
        out_ref[k, 48:56] = jnp.where(sub4 == 3, centers, jnp.where(top, s[0], s[1]))
        out_ref[k, 56:64] = jnp.where(sub4 == 3, centers, jnp.where(top, s[2], s[3]))
        return carry

    lax.fori_loop(0, group, body, 0, unroll=4)


def pair_kernel(
    tgt_ref, count_ref, got_ref, nc_ref, fc_ref, f_ref, fn_ref, base_ref, q_ref, t_ref, out_ref, term_ref, near_acc, far_acc
):
    step = pl.program_id(0)
    steps = pl.num_programs(0)
    group = got_ref.shape[0]
    boxes = f_ref.shape[0]
    sub = iota((8, 128), 0)
    lane = iota((8, 128), 1)
    left = lane < 64

    @pl.when(step == 0)
    def _():
        near_acc[...] = base_ref[...]
        far_acc[...] = jnp.zeros_like(far_acc)

    spread = (iota((128, 128), 0) // 64 == iota((128, 128), 1) // 64).astype(F32).astype(BF)

    def body(k, carry):
        peer = step * group + k
        tn = [tgt_ref[peer, j] for j in range(4)]
        tf = [tgt_ref[peer, 4 + j] for j in range(4)]
        points = [got_ref[k, 48:56], got_ref[k, 56:64]]
        feats = []
        for v in range(2):
            feats += planes((points[v] - nc_ref[k, 8 * v : 8 * v + 8]) * ROOT3, True)
        src = jnp.concatenate(feats + [jnp.zeros((64, 128), F32)], axis=0).T.astype(BF)
        for j in range(4):
            dist2 = dot(src[:, 32 * (j // 2) : 32 * (j // 2) + 32], f_ref[tn[j], j % 2])
            value = stack_kernel(matern(dist2))
            qs = jnp.concatenate(split(got_ref[k, 8 * j : 8 * j + 8]), axis=0)
            near_acc[tn[j]] += fold(dot(jnp.concatenate([qs, qs], axis=1), value))
        row = jnp.broadcast_to(points[0][3:4], (8, 128))
        row = jnp.where(lane % 64 == sub, row, 0.0)
        high = row.astype(BF)
        rest = row - high.astype(F32)
        mid = rest.astype(BF)
        low = (rest - mid.astype(F32)).astype(BF)
        cen = dot(jnp.concatenate([high, mid, low], axis=0), spread)
        rel = (fc_ref[k] - (cen[0:8] + cen[8:16] + cen[16:24])) * ROOT3
        tgt = jnp.concatenate(planes(rel, False), axis=0).astype(BF)
        value = stack_kernel(matern(dot(fn_ref[...], tgt)))
        ws = []
        for h in range(2):
            w = got_ref[k, 32 + 8 * h : 40 + 8 * h]
            for part in (jnp.where(left, w, 0.0), jnp.where(left, 0.0, w)):
                ws += list(split(part))
        ws = jnp.concatenate(ws, axis=0)
        locs = dot(jnp.concatenate([ws, ws], axis=1), value)
        for h in range(2):
            for u in range(2):
                at = 32 * h + 16 * u
                new = fold(locs[at : at + 16])
                far_acc[tf[2 * u + h]] += jnp.where(left if h == 0 else jnp.logical_not(left), new, 0.0)
        return carry

    lax.fori_loop(0, group, body, 0, unroll=2)

    @pl.when(step == steps - 1)
    def _():
        def finish(b, total):
            ls = jnp.concatenate(split(far_acc[b]), axis=0)
            both = t_ref[b]
            high, low = both[0:64], both[64:128]
            table = jnp.concatenate([high, high, low, low], axis=0)
            far = fold(dot(jnp.concatenate([ls, ls], axis=1), table))
            live = lane < count_ref[b]
            product = jnp.where(live, near_acc[b] + far, 0.0)
            out_ref[b] = product
            return total + product * q_ref[b]

        total = lax.fori_loop(0, boxes, finish, jnp.zeros((8, 128), F32), unroll=4)
        ones = jnp.ones((128, 128), F32)
        sums = lax.dot_general(ones, total, NT, precision=lax.Precision.HIGHEST, preferred_element_type=F32)
        term_ref[...] = jnp.concatenate([sums, jnp.zeros((128, 120), F32)], axis=1)


def far_sources():
    x = np.zeros((8, 128), np.float32)
    for n in range(64):
        for d, value in enumerate((NODE[n // 16], NODE[n // 4 % 4], NODE[n % 4])):
            for u in range(2):
                x[4 * u + d, 64 * u + n] = 0.5 * ROOT3 * value
    bf = lambda a: a.astype(jnp.bfloat16).astype(np.float32)
    high = bf(x)
    low = bf(x - high)
    norm = np.zeros_like(x)
    square = high * (high + 2 * low)
    for u in range(2):
        norm[4 * u + 3] = square[4 * u] + square[4 * u + 1] + square[4 * u + 2]
    one = bf(norm)
    two = bf(norm - one)
    three = bf(norm - one - two)
    sub = np.arange(8)[:, None] % 4
    unit = (np.arange(8)[:, None] // 4) == (np.arange(128)[None, :] // 64)
    parts = [
        np.where(sub == 3, one, high),
        np.where(sub == 3, two, high),
        np.where(sub == 3, 1.0, low),
        np.where(sub == 3, three, np.where(sub < 2, 1.0, 0.0)),
    ]
    return np.concatenate([np.where(unit, part, 0.0) for part in parts], axis=0).T.astype(np.float32)


def node_rows():
    out = np.zeros((8, 128), np.float32)
    for m in range(128):
        n = m % 64
        for u in range(2):
            for d, value in enumerate((NODE[n // 16], NODE[n // 4 % 4], NODE[n % 4])):
                out[4 * u + d, m] = 0.5 * value
    return out


def vmem(shape=None, index=None):
    if shape is None:
        return pl.BlockSpec(memory_space=pltpu.VMEM)
    return pl.BlockSpec(shape, index, memory_space=pltpu.VMEM)


SMEM = pl.BlockSpec(memory_space=pltpu.SMEM)


def params(mebibytes=56):
    return pltpu.CompilerParams(vmem_limit_bytes=mebibytes * 1024 * 1024)


def exchange(x):
    return lax.all_to_all(x, AXES, split_axis=0, concat_axis=0, tiled=True)


def general(local_pos, charges, counts, box_centers, far_list, near_list):
    devices = lax.axis_size("gx") * lax.axis_size("gy")
    boxes, _, slots = local_pos.shape
    struct = jax.ShapeDtypeStruct
    want = pl.pallas_call(
        ids_kernel,
        out_shape=struct((devices, 128), jnp.int32),
        in_specs=[vmem(), vmem()],
        out_specs=vmem(),
        compiler_params=params(),
        name="ids",
    )(far_list, near_list)
    served = exchange(want.reshape(devices, 1, 128)).reshape(devices, 128)

    group = 16
    lead = lambda shape: vmem((group,) + shape, lambda i: (i,) + (0,) * len(shape))
    q_tab, w_tab, p_tab, f_tab, base, table = pl.pallas_call(
        table_kernel,
        grid=(boxes // group,),
        out_shape=(
            struct((boxes, 8, 128), F32),
            struct((boxes, 8, 128), F32),
            struct((boxes, 8, 128), F32),
            struct((boxes, 2, 32, 128), BF),
            struct((boxes, 8, 128), F32),
            struct((boxes, 128, 128), BF),
        ),
        in_specs=[lead((3, 128)), lead((8, 128)), SMEM, SMEM],
        out_specs=(lead((8, 128)), lead((8, 128)), lead((8, 128)), lead((2, 32, 128)), lead((8, 128)), lead((128, 128))),
        compiler_params=params(),
        cost_estimate=pl.CostEstimate(flops=200_000_000, bytes_accessed=6_000_000, transcendentals=2_000_000),
        name="tables",
    )(local_pos, charges, counts, box_centers)

    send = pl.pallas_call(
        gather_kernel,
        grid=(devices // group,),
        out_shape=struct((devices, 64, 128), F32),
        in_specs=[SMEM, vmem(), vmem(), vmem()],
        out_specs=lead((64, 128)),
        compiler_params=params(),
        name="gather",
    )(served, q_tab, w_tab, p_tab)
    got = exchange(send)

    tgt = want[:, 16:24]
    centers = box_centers.T
    near_cen = jnp.pad(centers[tgt[:, :4]], ((0, 0), (0, 0), (0, 1))).reshape(devices, 16, 1)
    near_cen = jnp.broadcast_to(near_cen, (devices, 16, 128))
    far_cen = jnp.pad(centers[tgt[:, 4:]], ((0, 0), (0, 0), (0, 1))).reshape(devices, 2, 2, 4)
    far_cen = far_cen.transpose(0, 1, 3, 2).reshape(devices, 8, 2, 1)
    far_cen = jnp.broadcast_to(far_cen, (devices, 8, 2, 64)).reshape(devices, 8, 128) + node_rows()[None]

    product, term = pl.pallas_call(
        pair_kernel,
        grid=(devices // group,),
        out_shape=(struct((boxes, 8, 128), F32), struct((devices, 128), F32)),
        in_specs=[
            SMEM,
            SMEM,
            lead((64, 128)),
            lead((16, 128)),
            lead((8, 128)),
            vmem(),
            vmem(),
            vmem(),
            vmem(),
            vmem(),
        ],
        out_specs=(vmem(), vmem()),
        scratch_shapes=[pltpu.VMEM((boxes, 8, 128), F32), pltpu.VMEM((boxes, 8, 128), F32)],
        compiler_params=params(),
        cost_estimate=pl.CostEstimate(flops=1_000_000_000, bytes_accessed=12_000_000, transcendentals=20_000_000),
        name="pairs",
    )(tgt, counts, got, near_cen, far_cen, f_tab, jnp.asarray(far_sources(), BF), base, q_tab, table)

    terms = exchange(term.reshape(devices, 1, 128))[:, 0, :8]
    curvature = jnp.sum(terms, axis=0) / (devices * boxes * slots)
    return (product, curvature)


HALF = 64
ROWS = 44
NEAR_ROWS = 24
UNROLL = 16
CHUNKS = 4
AHEAD = 1


def upper_kernel(pos_ref, charge_ref, count_ref, row_ref, ex_ref):
    half = charge_ref.shape[0] // 2
    lane = iota((8, 128), 1)
    left = lane < HALF
    center = jnp.concatenate([row_ref[...], jnp.zeros((5, 2 * half), F32)], axis=0)
    center = jnp.concatenate([center, jnp.zeros((8, 128 - 2 * half), F32)], axis=1)
    center = jnp.concatenate([center, jnp.zeros((120, 128), F32)], axis=0).T
    wide = iota((half, 128), 1) < HALF
    for d in range(3):
        first = center[:half, d : d + 1] + 0.5 * pos_ref[d, :half]
        second = center[half : 2 * half, d : d + 1] + 0.5 * pos_ref[d, half:]
        ex_ref[(8 + d) * half : (9 + d) * half, :] = jnp.where(wide, pltpu.roll(first, HALF, 1), second)

    def body(b, carry):
        first = pltpu.roll(jnp.where(lane < count_ref[b], charge_ref[b], 0.0), HALF, 1)
        second = jnp.where(lane < count_ref[b + half], charge_ref[b + half], 0.0)
        ex_ref[pl.ds(pl.multiple_of(8 * b, 8), 8), :] = jnp.where(left, first, second)
        return carry

    lax.fori_loop(0, half, body, 0, unroll=16)


def sort_ids(far_ref, near_ref, most_ref, row_ref, msg_ref, want_ref):
    boxes = far_ref.shape[1]
    slots = far_ref.shape[0]
    peer = iota((128, 128), 0)
    line = iota((128, 128), 1)
    tri = (peer < line).astype(F32).astype(BF)
    full = jnp.ones((128, 128), BF)
    row32 = iota((32, 128), 0)
    kind = row32 // 4
    boxrow = iota((32, 128), 1) % boxes
    result = jnp.zeros((128, 32), F32)
    for ref, first, group in ((near_ref, 1, 0), (far_ref, 0, 1)):
        seen = jnp.zeros((128, 128), F32)
        for j in range(0, slots, 2):
            flat = jnp.concatenate([ref[first + j : first + j + 1, :], ref[first + j + 1 : first + j + 2, :]], axis=1)
            hit = jnp.broadcast_to(flat // boxes, (128, 128)) == peer
            onehot = hit.astype(F32).astype(BF)
            before = dot(onehot, tri) + seen
            rank = jnp.sum(jnp.where(hit, before, 0.0), axis=0, keepdims=True).astype(jnp.int32)
            if j + 2 < slots:
                seen = seen + dot(onehot, full)
            within = jnp.broadcast_to(flat % boxes, (32, 128))
            if group == 0:
                value = jnp.where(kind == 0, within * NEAR_ROWS, jnp.where(kind == 2, within * 8, 0))
            else:
                value = jnp.where(kind == 1, within * 8, 0)
            value = jnp.where(kind == 4 + group, boxrow, value)
            value = jnp.where(row32 % 4 == jnp.broadcast_to(rank, (32, 128)), value, 0).astype(F32).astype(BF)
            result = result + dot(onehot, value, NT)
    result = jnp.concatenate([result, jnp.zeros((128, 96), F32)], axis=1)
    heavy = (line == peer - peer % 4).astype(F32).astype(BF)
    first = dot(heavy, result.astype(BF))
    for at, base in ((8, 8), (24, 16)):
        extra = dot(jnp.where(line == base + peer % 4, first, 0.0).astype(BF), full)
        result = jnp.where(line == at, extra, result)
    most = jnp.max(most_ref[...], axis=1, keepdims=True).astype(F32)
    result = jnp.where(line == 9, jnp.broadcast_to(most, (128, 128)), result)
    want_ref[...] = result.astype(jnp.int32)
    rows = [jnp.concatenate([row_ref[d : d + 1, :]] * 2, axis=1) for d in range(3)]
    rows = [jnp.broadcast_to(row, (128, 128)) for row in rows]
    msg_ref[pl.ds(0, 128, stride=2), :] = jnp.where(line < HALF, result, rows[2])
    msg_ref[pl.ds(1, 128, stride=2), :] = jnp.where(line < HALF, rows[0], rows[1])


def first_kernel(
    member_ref, count_ref, far_ref, near_ref, most_ref, row_ref, pos_hbm, charge_hbm, msg_hbm, want_hbm, ex_ref,
    pos_ref, charge_ref, msg_ref, want_ref, sems
):
    @pl.when(member_ref[0] == 0)
    def _():
        loads = [pltpu.make_async_copy(pos_hbm, pos_ref, sems.at[0]), pltpu.make_async_copy(charge_hbm, charge_ref, sems.at[1])]
        for copy in loads:
            copy.start()
        sort_ids(far_ref, near_ref, most_ref, row_ref, msg_ref, want_ref)
        stores = [pltpu.make_async_copy(msg_ref, msg_hbm, sems.at[2]), pltpu.make_async_copy(want_ref, want_hbm, sems.at[3])]
        for copy in stores:
            copy.start()
        for copy in loads:
            copy.wait()
        upper_kernel(pos_ref, charge_ref, count_ref, row_ref, ex_ref)
        for copy in stores:
            copy.wait()


def second_kernel(
    member_ref, far_ref, near_ref, most_ref, row_ref, msg_in, want_in, msg_hbm, want_hbm, msg_ref, want_ref, sems
):
    @pl.when(member_ref[0] != 0)
    def _():
        sort_ids(far_ref, near_ref, most_ref, row_ref, msg_ref, want_ref)
        stores = [pltpu.make_async_copy(msg_ref, msg_hbm, sems.at[0]), pltpu.make_async_copy(want_ref, want_hbm, sems.at[1])]
        for copy in stores:
            copy.start()
        for copy in stores:
            copy.wait()


def cheb_rows(x):
    sub = iota((8, 128), 0)
    second = 2.0 * x * x - 1.0
    third = 2.0 * x * second - x
    basis = []
    for i in range(NODES):
        theta = (2 * i + 1) * math.pi / 8
        basis.append(0.25 + 0.5 * (math.cos(theta) * x + math.cos(2 * theta) * second + math.cos(3 * theta) * third))
    row = lambda i, d: jnp.broadcast_to(basis[i][d : d + 1], (8, 128))
    sub4 = sub % 4
    zs = jnp.where(sub4 == 0, row(0, 2), jnp.where(sub4 == 1, row(1, 2), jnp.where(sub4 == 2, row(2, 2), row(3, 2))))
    ys = [jnp.where(sub < 4, row(0, 1), row(1, 1)) * zs, jnp.where(sub < 4, row(2, 1), row(3, 1)) * zs]
    return jnp.concatenate([row(i, 0) * ys[j] for i in range(NODES) for j in range(2)], axis=0)


def point_rows(pos_ref, b):
    sub4 = iota((8, 128), 0) % 4
    x = jnp.zeros((8, 128), F32)
    for d in range(3):
        x = jnp.where(sub4 == d, jnp.broadcast_to(pos_ref[d, pl.ds(b, 1), :], (8, 128)), x)
    return x


def doubled(x):
    return jnp.where(iota((8, 128), 1) < HALF, x, pltpu.roll(x, HALF, 1))


def fill_basis(pos_ref, basis_ref):
    for d in range(3):
        x = pos_ref[d]
        second = 2.0 * x * x - 1.0
        third = 2.0 * x * second - x
        for i in range(NODES):
            theta = (2 * i + 1) * math.pi / 8
            value = math.cos(theta) * x + math.cos(2 * theta) * second + math.cos(3 * theta) * third
            basis_ref[4 * d + i] = 0.25 + 0.5 * value


def basis_table(basis_ref, b):
    sub = iota((8, 128), 0)
    row = lambda i, d: jnp.broadcast_to(basis_ref[4 * d + i, pl.ds(b, 1), :], (8, 128))
    sub4 = sub % 4
    zs = jnp.where(sub4 == 0, row(0, 2), jnp.where(sub4 == 1, row(1, 2), jnp.where(sub4 == 2, row(2, 2), row(3, 2))))
    ys = [jnp.where(sub < 4, row(0, 1), row(1, 1)) * zs, jnp.where(sub < 4, row(2, 1), row(3, 1)) * zs]
    return jnp.concatenate([row(i, 0) * ys[j] for i in range(NODES) for j in range(2)], axis=0)


def send_table_kernel(pos_ref, charge_ref, count_ref, cen_ref, near_ref, far_ref, basis_ref):
    boxes = charge_ref.shape[0]
    lane = iota((8, 128), 1)
    sub = iota((8, 128), 0)
    fill_basis(pos_ref, basis_ref)

    def body(b, carry):
        q = jnp.where(lane < count_ref[b], charge_ref[b], 0.0)
        near_ref[b, 0:8] = doubled(q)
        x, y, z = [doubled(cen_ref[d, b] + 0.5 * jnp.broadcast_to(pos_ref[d, pl.ds(b, 1), :], (8, 128))) for d in range(3)]
        near_ref[b, 8:16] = jnp.where(sub == 4, x, jnp.where(sub == 5, y, z))
        near_ref[b, 16:24] = jnp.where(sub == 7, x, jnp.where((sub == 3) | (sub == 5), y, z))
        table = basis_table(basis_ref, b)
        qs = jnp.concatenate(split(q), axis=0)
        weight = fold(dot(qs, stack_kernel(table), NT))
        far_ref[b] = weight + pltpu.roll(weight, 64, 1)
        return carry

    lax.fori_loop(0, boxes, body, 0, unroll=32)


def own_table_kernel(pos_ref, charge_ref, count_ref, q_ref, f_ref, base_ref):
    boxes = charge_ref.shape[0]
    sub = iota((8, 128), 0)
    lane = iota((8, 128), 1)

    def body(b, carry):
        q = jnp.where(lane < count_ref[b], charge_ref[b], 0.0)
        q_ref[b] = q
        x = point_rows(pos_ref, b)
        rel = (0.5 * ROOT3) * x
        tgt = planes(rel, False)
        for unit in range(2):
            f_ref[b, unit] = jnp.concatenate([jnp.where(sub // 4 == unit, part, 0.0) for part in tgt], axis=0).astype(BF)
        zero = jnp.zeros((96, 128), F32)
        src = jnp.concatenate(planes(rel, True) + [zero], axis=0).T.astype(BF)
        first = jnp.concatenate([jnp.where(sub < 4, part, 0.0) for part in tgt] + [zero], axis=0).astype(BF)
        value = stack_kernel(matern(dot(src, first)))
        qs = jnp.concatenate(split(q), axis=0)
        base_ref[b] = fold(dot(jnp.concatenate([qs, qs], axis=1), value)) + q
        return carry

    lax.fori_loop(0, boxes, body, 0, unroll=4)


def goal_kernel(want_ref, served_ref, cen_ref, node_ref, nc_ref, fc_ref, ec_ref, goal_ref, odd_ref):
    lane = iota((128, 128), 1)
    left = lane < HALF
    boxes = cen_ref.shape[1]
    cen = jnp.concatenate([cen_ref[...], jnp.zeros((5, boxes), F32)], axis=0)
    cen = jnp.concatenate([cen, jnp.zeros((8, 128 - boxes), F32)], axis=1)
    cen = jnp.concatenate([cen, jnp.zeros((120, 128), F32)], axis=0).T

    def split3(x, axis):
        high = x.astype(BF)
        rest = x - high.astype(F32)
        mid = rest.astype(BF)
        return jnp.concatenate([high, mid, (rest - mid.astype(F32)).astype(BF)], axis=axis)

    parts = split3(cen, 0)
    want = want_ref[...]
    goal_ref[...] = want.astype(F32).T[16:32].astype(jnp.int32)
    sources = [served_ref[pl.ds(1, 128, stride=2), :], served_ref[pl.ds(0, 128, stride=2), :]]
    halves = [jnp.concatenate([(iota((128, 128), 0) // HALF == h).astype(F32).astype(BF)] * 3, axis=0) for h in range(2)]

    def column(at):
        return jnp.broadcast_to(want[:, at : at + 1], (128, 128))

    def centers(at):
        onehot = (column(at) == lane).astype(F32).astype(BF)
        found = dot(jnp.concatenate([onehot] * 3, axis=1), parts)
        return [jnp.broadcast_to(found[:, d : d + 1], (128, 128)) for d in range(3)]

    def gaps(j):
        mine = lane % HALF == column(4 + j) // 8
        both = [split3(jnp.where(mine, source, 0.0), 1) for source in sources]
        theirs = [dot(both[0], halves[0]), dot(both[0], halves[1]), dot(both[1], halves[1])]
        return [a - b for a, b in zip(centers(20 + j), theirs)]

    nc_ref[...] = jnp.zeros_like(nc_ref)
    fc_ref[...] = jnp.zeros_like(fc_ref)
    ec_ref[...] = jnp.zeros_like(ec_ref)
    for u in range(2):
        first, second = centers(16 + 2 * u), centers(17 + 2 * u)
        for d in range(3):
            nc_ref[pl.ds(4 * u + d, 128, stride=8), :] = jnp.where(left, first[d], second[d])
        first, second = gaps(2 * u), gaps(2 * u + 1)
        for d in range(3):
            fc_ref[pl.ds(4 * u + d, 128, stride=8), :] = jnp.where(left, first[d], second[d]) + node_ref[d : d + 1, :]
    extra = centers(24)
    for d in range(3):
        odd_ref[...] = extra[d]
        even, odd = odd_ref[pl.ds(0, 64, stride=2), :], odd_ref[pl.ds(1, 64, stride=2), :]
        ec_ref[pl.ds(d, 64, stride=8), :] = jnp.where(left[:64], even, odd)


def far_kernel(fc_ref, fn_ref, out_ref):
    group = fc_ref.shape[0]
    tgt = jnp.concatenate(planes(fc_ref[...] * ROOT3, False), axis=1).astype(BF)
    for k in range(group):
        out_ref[k] = stack_kernel(matern(dot(fn_ref[...], tgt[k])))


def send_kernel(member_ref, served_ref, near_ref, far_ref, own_ref, *refs):
    moved, (out_ref, ids_ref, int_ref, ex_ref, buf_ref, sems) = refs[:3], refs[3:]
    peers = ids_ref.shape[1]
    sub = iota((8, 128), 0)
    lane = iota((8, 128), 1)
    left = lane < HALF
    keep = left | (sub < 3)
    second = sub < 5
    int_ref[...] = served_ref[pl.ds(0, peers, stride=2), :].T[:16].astype(jnp.int32)
    copy = pltpu.make_async_copy(int_ref, ids_ref, sems.at[0])
    copy.start()
    half = ex_ref.shape[0] // 16
    packed = moved[0][...] + moved[1][...] + moved[2][...]
    packed = jnp.where(member_ref[0] == 0, own_ref[...], packed)
    for d in range(3):
        rows = packed[(8 + d) * half : (9 + d) * half]
        ex_ref[pl.ds(d, half, stride=8), :] = pltpu.roll(rows, HALF, 1)
        ex_ref[pl.ds(8 * half + d, half, stride=8), :] = rows
    for b in range(half):
        tile = packed[8 * b : 8 * b + 8]
        for at, part in ((8 * b, tile), (8 * (b + half), pltpu.roll(tile, HALF, 1))):
            ex_ref[at : at + 8, :] = jnp.where(left, part, jnp.where(sub < 3, ex_ref[at : at + 8, :], 0.0))
    copy.wait()

    def body(i, carry):
        base = pl.multiple_of(i * 2 * ROWS, 8)
        for k in range(2):
            peer = 2 * i + k
            at = lambda row: pl.ds(base + (k * ROWS + row), 8)
            rows = lambda ref, j, row: ref[pl.ds(pl.multiple_of(ids_ref[j, peer], 8) + row, 8), :]
            q = [rows(near_ref, j, 0) for j in range(4)]
            w = [rows(far_ref, 4 + j, 0) for j in range(4)]
            p = [rows(near_ref, j, 16 if j < 2 else 8) for j in range(4)]
            buf_ref[at(0), :] = jnp.where(left, q[0], q[1])
            buf_ref[at(8), :] = jnp.where(left, q[2], q[3])
            buf_ref[at(16), :] = jnp.where(left, w[0], w[2])
            buf_ref[at(24), :] = jnp.where(left, w[1], w[3])
            buf_ref[at(36), :] = jnp.where(sub == 7, jnp.where(left, p[0], p[1]), jnp.where(left, p[2], p[3]))
            buf_ref[at(32), :] = jnp.where(keep, rows(ex_ref, 8, 0), jnp.where(second, p[1], p[0]))
        return carry

    chunks = 8
    each = peers // chunks
    stores = []
    for c in range(chunks):
        lax.fori_loop(c * each // 2, (c + 1) * each // 2, body, 0, unroll=8)
        at = pl.ds(c * each * ROWS, each * ROWS)
        stores.append(pltpu.make_async_copy(buf_ref.at[at], out_ref.at[at], sems.at[1 + c]))
        stores[-1].start()
    for copy in stores:
        copy.wait()


def duo_kernel(
    scale, got_ref, want_hbm, nc_hbm, ec_hbm, f_hbm, base_hbm, q_hbm, w_hbm, v_hbm, near0_hbm, near1_hbm, far0_hbm, far1_hbm, term_hbm,
    tgt_ref, nc_ref, ec_ref, f_ref, base_ref, q_ref, w_ref, v_ref, term_ref, sems, *bufs
):
    whole = [(want_hbm, tgt_ref), (nc_hbm, nc_ref), (ec_hbm, ec_ref), (f_hbm, f_ref)]
    whole += [(base_hbm, base_ref), (q_hbm, q_ref), (w_hbm, w_ref)]
    loads = [pltpu.make_async_copy(source, target, sems.at[i]) for i, (source, target) in enumerate(whole)]
    for copy in loads[:4]:
        copy.start()
    chunk = v_ref.shape[0] // CHUNKS

    def far_values(c):
        at = pl.ds(c * chunk, chunk)
        return pltpu.make_async_copy(v_hbm.at[at], v_ref.at[at], sems.at[16 + c % AHEAD])

    for c in range(AHEAD):
        far_values(c).start()
    xt_refs, dist_refs, value_refs = bufs[:2], (bufs[2:7], bufs[7:12]), (bufs[12:17], bufs[17:22])
    near_accs, far_accs = bufs[22:24], bufs[24:26]
    duos = ec_ref.shape[0]
    boxes = f_ref.shape[0]
    sub = iota((8, 128), 0)
    lane = iota((8, 128), 1)
    left = lane < HALF
    for ref in value_refs[1] + near_accs + far_accs:
        ref[...] = jnp.zeros_like(ref)
    for ref in dist_refs[1]:
        ref[...] = jnp.full(ref.shape, 1e6, F32)
    def tile(duo, a, row):
        return got_ref[pl.ds(pl.multiple_of(duo * 2 * ROWS, 8) + (a * ROWS + row), 8), :]

    def extra(duo):
        return tile(duo, 0, 32), tile(duo, 1, 32)

    def goals(duo):
        pairs = [(tgt_ref[2 * (k % 2), 2 * duo + k // 2], tgt_ref[2 * (k % 2) + 1, 2 * duo + k // 2]) for k in range(4)]
        return pairs + [(tgt_ref[8, 2 * duo], tgt_ref[8, 2 * duo + 1])]

    def halves(x):
        high = x.astype(BF).astype(F32)
        both = [high, x - high]
        return [jnp.where(left, part, 0.0) for part in both] + [jnp.where(left, 0.0, part) for part in both]

    def products(duo, value):
        ex = extra(duo)
        tiles = [tile(duo, k // 2, 8 * (k % 2)) for k in range(4)]
        tiles.append(jnp.where(left, ex[0], pltpu.roll(ex[1], HALF, 1)))
        for k, goal in enumerate(goals(duo)):
            qs = jnp.concatenate(halves(tiles[k]), axis=0).astype(BF)
            new = dot(jnp.concatenate([qs, qs], axis=1), value[k][...])
            for h in range(2):
                near_accs[h][goal[h]] += fold(new[16 * h : 16 * h + 16])

    def far_products(duo):
        for a in range(2):
            ws = []
            for h in range(2):
                ws += halves(tile(duo, a, 16 + 8 * h))
            ws = jnp.concatenate(ws, axis=0).astype(BF)
            new = dot(jnp.concatenate([ws, ws], axis=1), v_ref[2 * duo + a])
            for h in range(2):
                for u in range(2):
                    at = 32 * h + 16 * u
                    far_accs[h][tgt_ref[4 + 2 * u + h, 2 * duo + a]] += fold(new[at : at + 16])

    def values(dist, value):
        for k in range(5):
            value[k][...] = stack_kernel(matern(dist[k][...]))

    def distances(duo, xt, dist):
        for k, goal in enumerate(goals(duo)):
            v, u = k // 2, k % 2
            for half in range(2):
                pieces = [jnp.zeros((32 * v, 128), BF)] if v else []
                pieces += [f_ref[goal[half], u], jnp.zeros((96 - 32 * v, 128), BF)]
                at = slice(64 * half, 64 * half + 64)
                dist[k][at, :] = dot(xt[at, :], jnp.concatenate(pieces, axis=0))

    def features(duo, xt):
        ex = extra(duo)
        turned = [pltpu.roll(x, HALF, 1) for x in ex]
        feats = []
        for a in range(2):
            full = tile(duo, a, 36)
            split_rows = jnp.where(left, pltpu.roll(turned[a], 4, 0), pltpu.roll(ex[a], 6, 0))
            point = jnp.where(sub >= 4, full, jnp.where(sub == 0, pltpu.roll(full, 1, 0), split_rows))
            feats += planes((point - nc_ref[2 * duo + a]) * ROOT3, True)
        point = jnp.where(left, turned[0], ex[1])
        feats += planes((point - ec_ref[duo]) * ROOT3, True)
        feats.append(jnp.zeros((32, 128), F32))
        xt[...] = jnp.concatenate(feats, axis=0).T.astype(BF)

    turns = duos // UNROLL
    assert turns == CHUNKS

    def body(i, carry):
        far_values(i).wait()

        @pl.when(i + AHEAD < CHUNKS)
        def _():
            far_values(i + AHEAD).start()

        for s in range(UNROLL):
            now, was = s % 2, 1 - s % 2
            step = UNROLL * i + s
            products(jnp.maximum(step - 2, 0), value_refs[was])
            far_products(step)
            values(dist_refs[was], value_refs[now])
            distances(step, xt_refs[was], dist_refs[now])
            features(jnp.minimum(step + 1, duos - 1), xt_refs[now])
        return carry

    for copy in loads[:4]:
        copy.wait()
    features(0, xt_refs[1])
    for copy in loads[4:]:
        copy.start()
    lax.fori_loop(0, turns, body, 0)
    products(duos - 2, value_refs[1])
    values(dist_refs[1], value_refs[0])
    products(duos - 1, value_refs[0])

    sums = (near0_hbm, near1_hbm, far0_hbm, far1_hbm)
    stores = [pltpu.make_async_copy(a, b, sems.at[8 + i]) for i, (a, b) in enumerate(zip(near_accs + far_accs, sums))]
    for copy in stores:
        copy.start()
    for copy in loads[4:]:
        copy.wait()

    def finish(b, total):
        near = near_accs[0][b] + near_accs[1][b] + base_ref[b]
        far = jnp.where(left, far_accs[0][b], far_accs[1][b])
        return total + near * q_ref[b] + far * w_ref[b]

    total = lax.fori_loop(0, boxes, finish, jnp.zeros((8, 128), F32), unroll=16)
    high = total.astype(BF)
    rest = total - high.astype(F32)
    mid = rest.astype(BF)
    parts = jnp.concatenate([high, mid, (rest - mid.astype(F32)).astype(BF)], axis=1)
    sums = dot(jnp.ones((128, 384), BF), parts, NT)
    term_ref[...] = jnp.concatenate([sums * scale, jnp.zeros((128, 120), F32)], axis=1)
    stores.append(pltpu.make_async_copy(term_ref, term_hbm, sems.at[12]))
    stores[-1].start()
    for copy in stores:
        copy.wait()


def finish_kernel(count_ref, pos_ref, near0_ref, near1_ref, far0_ref, far1_ref, base_ref, out_ref, basis_ref):
    boxes = base_ref.shape[0]
    lane = iota((8, 128), 1)
    fill_basis(pos_ref, basis_ref)

    def body(b, carry):
        locs = jnp.where(lane < HALF, far0_ref[b], far1_ref[b])
        ls = jnp.concatenate(split(locs), axis=0)
        high, low = split(basis_table(basis_ref, b))
        far = fold(dot(jnp.concatenate([ls, ls], axis=1), jnp.concatenate([high, high, low, low], axis=0)))
        near = near0_ref[b] + near1_ref[b] + base_ref[b]
        out_ref[b] = jnp.where(lane < count_ref[b], near + far, 0.0)
        return carry

    lax.fori_loop(0, boxes, body, 0, unroll=32)


def on_device(local_pos, charges, counts, box_centers, far_list, near_list):
    devices = lax.axis_size("gx") * lax.axis_size("gy")
    boxes, _, slots = local_pos.shape
    struct = jax.ShapeDtypeStruct
    hbm = pltpu.HBM
    stay = lambda x: pltpu.with_memory_space_constraint(x, pltpu.HBM)
    anywhere = pl.BlockSpec(memory_space=pltpu.HBM)
    pos = jnp.transpose(local_pos, (1, 0, 2))
    table = struct((boxes, 8, 128), F32)
    flat = lambda x: x.reshape(-1, 128)
    member = (lax.axis_index("gy") % 4).astype(jnp.int32).reshape(1)
    lists = (far_list.T, near_list.T, counts.reshape(1, boxes), box_centers)
    ids_shape = (hbm((devices * 2, 128), F32), hbm((devices, 128), jnp.int32))
    ids_scratch = [pltpu.VMEM((devices * 2, 128), F32), pltpu.VMEM((devices, 128), jnp.int32)]
    msg, want, ex_own = pl.pallas_call(
        first_kernel,
        out_shape=ids_shape + (struct((boxes * 11 // 2, 128), F32),),
        in_specs=[SMEM, SMEM] + [vmem()] * 4 + [anywhere] * 2,
        out_specs=(anywhere, anywhere, vmem()),
        scratch_shapes=[pltpu.VMEM((3, boxes, 128), F32), pltpu.VMEM((boxes, 8, 128), F32)]
        + ids_scratch
        + [pltpu.SemaphoreType.DMA((4,))],
        compiler_params=params(8),
        name="first",
    )(member, counts, *lists, stay(pos), stay(charges))
    msg, want = pl.pallas_call(
        second_kernel,
        out_shape=ids_shape,
        in_specs=[SMEM] + [vmem()] * 4 + [anywhere] * 2,
        out_specs=(anywhere, anywhere),
        scratch_shapes=ids_scratch + [pltpu.SemaphoreType.DMA((2,))],
        input_output_aliases={5: 0, 6: 1},
        compiler_params=params(8),
        name="second",
    )(member, *lists, stay(msg), stay(want))
    moved = [lax.ppermute(ex_own, "gy", [(4 * z, 4 * z + k) for z in range(4)]) for k in range(1, 4)]
    served = flat(exchange(msg.reshape(devices, 2, 128)))

    near_tab, far_tab = pl.pallas_call(
        send_table_kernel,
        out_shape=(struct((boxes, NEAR_ROWS, 128), F32), table),
        in_specs=[vmem(), vmem(), SMEM, SMEM],
        out_specs=(vmem(), vmem()),
        scratch_shapes=[pltpu.VMEM((12, boxes, 128), F32)],
        compiler_params=params(8),
        cost_estimate=pl.CostEstimate(flops=50_000_000, bytes_accessed=1_200_000, transcendentals=0),
        name="send_tables",
    )(pos, charges, counts, box_centers)

    send = pl.pallas_call(
        send_kernel,
        out_shape=hbm((devices * ROWS, 128), F32),
        in_specs=[SMEM] + [vmem()] * 7,
        out_specs=anywhere,
        scratch_shapes=[
            pltpu.SMEM((16, devices), jnp.int32),
            pltpu.VMEM((16, devices), jnp.int32),
            pltpu.VMEM((boxes * 8, 128), F32),
            pltpu.VMEM((devices * ROWS, 128), F32),
            pltpu.SemaphoreType.DMA((9,)),
        ],
        compiler_params=params(12),
        name="send",
    )(member, served, flat(near_tab), flat(far_tab), ex_own, *moved)
    got = flat(exchange(send.reshape(devices, ROWS // 4, 4, 128)))

    q_tab, f_tab, base = pl.pallas_call(
        own_table_kernel,
        out_shape=(hbm((boxes, 8, 128), F32), hbm((boxes, 2, 32, 128), BF), hbm((boxes, 8, 128), F32)),
        in_specs=[vmem(), vmem(), SMEM],
        out_specs=(vmem(), vmem(), vmem()),
        compiler_params=params(8),
        cost_estimate=pl.CostEstimate(flops=200_000_000, bytes_accessed=4_000_000, transcendentals=2_000_000),
        name="own_tables",
    )(pos, charges, counts)

    near_cen, far_gap, ex_cen, goals = pl.pallas_call(
        goal_kernel,
        out_shape=(
            hbm((devices * 8, 128), F32),
            hbm((devices * 8, 128), F32),
            hbm((devices * 4, 128), F32),
            hbm((16, devices), jnp.int32),
        ),
        in_specs=[vmem()] * 4,
        out_specs=(vmem(),) * 4,
        scratch_shapes=[pltpu.VMEM((128, 128), F32)],
        compiler_params=params(8),
        cost_estimate=pl.CostEstimate(flops=50_000_000, bytes_accessed=2_000_000, transcendentals=0),
        name="goals",
    )(want, served, box_centers, jnp.asarray(node_rows()))
    near_cen, far_gap, ex_cen = [x.reshape(-1, 8, 128) for x in (near_cen, far_gap, ex_cen)]
    group = 8
    far_value = pl.pallas_call(
        far_kernel,
        grid=(devices // group,),
        out_shape=hbm((devices, 256, 128), BF),
        in_specs=[vmem((group, 8, 128), lambda i: (i, 0, 0)), vmem()],
        out_specs=vmem((group, 256, 128), lambda i: (i, 0, 0)),
        compiler_params=params(8),
        cost_estimate=pl.CostEstimate(flops=200_000_000, bytes_accessed=9_000_000, transcendentals=4_000_000),
        name="far_values",
    )(far_gap, jnp.asarray(far_sources(), BF))

    big = lambda dtype, rows: pltpu.VMEM((rows, 128), dtype)
    *sums, term = pl.pallas_call(
        functools.partial(duo_kernel, 1.0 / (devices * boxes * slots)),
        out_shape=(hbm((boxes, 8, 128), F32),) * 4 + (hbm((devices, 128), F32),),
        in_specs=[vmem()] + [anywhere] * 8,
        out_specs=(anywhere,) * 5,
        scratch_shapes=[
            pltpu.SMEM((16, devices), jnp.int32),
            pltpu.VMEM((devices, 8, 128), F32),
            pltpu.VMEM((devices // 2, 8, 128), F32),
            pltpu.VMEM((boxes, 2, 32, 128), BF),
            pltpu.VMEM((boxes, 8, 128), F32),
            pltpu.VMEM((boxes, 8, 128), F32),
            pltpu.VMEM((boxes, 8, 128), F32),
            pltpu.VMEM((devices, 256, 128), BF),
            pltpu.VMEM((devices, 128), F32),
            pltpu.SemaphoreType.DMA((20,)),
        ]
        + [big(BF, 128)] * 2
        + [big(F32, 128)] * 10
        + [big(BF, 256)] * 10
        + [pltpu.VMEM((boxes, 8, 128), F32)] * 4,
        compiler_params=params(28),
        cost_estimate=pl.CostEstimate(flops=1_000_000_000, bytes_accessed=12_000_000, transcendentals=20_000_000),
        name="pairs",
    )(got, *[stay(x) for x in (goals, near_cen, ex_cen, f_tab, base, q_tab, far_tab, far_value)])

    terms = exchange(term.reshape(devices, 1, 128))[:, 0, :8]
    curvature = jnp.sum(terms, axis=0)
    product = pl.pallas_call(
        finish_kernel,
        out_shape=table,
        in_specs=[SMEM] + [vmem()] * 6,
        out_specs=vmem(),
        scratch_shapes=[pltpu.VMEM((12, boxes, 128), F32)],
        compiler_params=params(8),
        cost_estimate=pl.CostEstimate(flops=50_000_000, bytes_accessed=3_000_000, transcendentals=0),
        name="finish",
    )(counts, pos, *[stay(x) for x in (*sums, base)])
    over = jnp.any((served.reshape(devices, 2, 128)[:, 0, 9] > HALF) & (jnp.arange(devices) % 4 != 0))
    whole = (local_pos, charges, counts, box_centers, far_list, near_list)
    return lax.cond(over, lambda: general(*whole), lambda: (product, curvature))


def solution(mesh):
    in_specs = (
        P(AXES, None, None),
        P(AXES, None, None),
        P(AXES),
        P(None, AXES),
        P(AXES, None),
        P(AXES, None),
    )
    out_specs = (P(AXES, None, None), P())
    return jax.shard_map(on_device, mesh=mesh, in_specs=in_specs, out_specs=out_specs, check_vma=False)
```
